32 devices in a mesh: parts: 2 (over y), ctx: 4 (over z), mp: 4 (over x, core).
Axes of the slice: x: 2, y: 2, z: 4, core: 2. Of those that a mesh axis runs over, the one named last changes fastest.
Arguments:
- inputs: bfloat16 [1024, 3, 4096], P(('parts', 'ctx'), None, 'mp'), parts along dimension 0, may hold values from -6 to 6
- short_filter: bfloat16 [3, 3, 4096], P(None, None, 'mp'), may hold values from -3.5 to 3.5
- long_filter: bfloat16 [256, 128], P('mp'), may hold values from -0.5 to 0.5
- skip_gain: float32 [4096], P('mp'), may hold values from -1 to 1
- queries: bfloat16 [1024, 4096], P(('parts', 'ctx'), 'mp'), parts along dimension 0, may hold values from -6 to 6
- key_rows: bfloat16 [1024, 4096], P(('parts', 'ctx'), 'mp'), parts along dimension 0, may hold values from -6 to 6
- out_weight: bfloat16 [4096, 4096], P('mp'), may hold values from -0.25 to 0.25
Outputs:
- block_output: bfloat16 [1024, 4096], P(('parts', 'ctx'), 'mp'), parts along dimension 0
The draws below stay inside these ranges and needn't reach their ends.
There are 2 independent parts, one for each index of `parts`. The reference program is written for one: setup_inputs(seed, part) draws one part's arguments, and reference() takes and returns one part's arrays. A program takes and returns all parts, laid end to end along the dimension named above; an argument that names none is the same for every part. Nothing has to cross between parts.
All inputs are finite; a program needn't handle non-finite values.
Results may differ from the reference program's by a relative error of at most 0.014.
Values may be sent and summed in bfloat16 or wider, within the bound.
No kernel may reach another device: no remote copies, remote signals or barrier semaphores. Data moves between devices by JAX's collectives and lax.ppermute only.
A program may use at most 64 MiB of HBM per device.

```python
import jax
import jax.numpy as jnp
from jax import lax

D = 4096
HEAD_DIM = 128
GROUP = 16
SHORT_K = 3
LONG_K = 128
GROUPS = 256
WINDOW = 512


def drawn_values(key, salt):
    return 1.5 * jax.random.truncated_normal(jax.random.fold_in(key, salt), -4.0, 4.0, (WINDOW, D), jnp.float32)


def draw_queries(key, part):
    values_drawn = drawn_values(key, 1)
    return values_drawn.astype(jnp.bfloat16)


def draw_key_rows(key, part):
    values_drawn = drawn_values(key, 2)
    return values_drawn.astype(jnp.bfloat16)


def raised(array, key, source, target, parts, factor):
    def block_of(position):
        return (jnp.arange(array.shape[position]) // (array.shape[position] // parts)).reshape((-1,) + (1,) * (array.ndim - 1 - position))

    first = jax.random.permutation(key, parts)[block_of(target)]
    other_side = (block_of(target) + parts // 2) % parts
    return jnp.where((block_of(source) == first) | (block_of(source) == other_side), factor * array, array)


def steps_of(rng, shape, cuts, smallest, largest):
    level, own = 1.0, jax.random.fold_in(rng, 6)
    for dim, shards_of in cuts:
        steps = jnp.exp(jax.random.uniform(jax.random.fold_in(own, dim), (shards_of,), jnp.float32, smallest / len(cuts), largest / len(cuts)))
        level = level * jnp.repeat(steps, shape[dim] // shards_of).reshape([-1 if axis == dim else 1 for axis in range(len(shape))])
    return level


def centred(own_key, dims, scale, reach, split=(), dtype=jnp.bfloat16):
    array = jax.random.normal(own_key, dims, jnp.float32) * scale
    if len(split) > 0:
        array = steps_of(own_key, dims, split, -0.22, 0.18) * array
    return jnp.clip(array, min=-reach, max=reach).astype(dtype)


def bell_draw_with(key, dims, width, limit, pieces, heavy, kind=jnp.bfloat16):
    values = width * jax.random.normal(key, dims, jnp.float32)
    if pieces:
        values = values * steps_of(key, dims, pieces, -0.22, 0.18)
    return jnp.clip(raised(values, jax.random.fold_in(key, 3), *heavy), -limit, limit).astype(kind)


def setup_inputs(seed: int = 0, part: int = 0) -> dict:
    splits = jax.random.split(jax.random.key(seed), 8)
    part_keys = jax.random.split(jax.random.fold_in(splits[7], part), 8)
    inputs = centred(part_keys[0], (WINDOW, 3, D), 1.0, 6.0, ((0, 4), (2, 4)))
    short_filter = centred(splits[1], (SHORT_K, 3, D), SHORT_K ** -0.5, 3.5, ((2, 4),))
    long_filter = centred(splits[2], (GROUPS, LONG_K), LONG_K ** -0.5, 0.5, ((0, 4),))
    skip_gain = jnp.clip(jax.random.uniform(splits[3], (D,), jnp.float32, -1.0, 1.0) * steps_of(splits[3], (D,), ((0, 4),), -0.4, 0.0), -1.0, 1.0)
    queries = draw_queries(jax.random.fold_in(jax.random.fold_in(splits[7], part), 71), part)
    key_rows = draw_key_rows(jax.random.fold_in(jax.random.fold_in(splits[7], part), 71), part)
    out_weight = bell_draw_with(splits[6], (D, D), (D // 4) ** -0.5, 0.25, ((0, 4),), (0, 1, 4, 2.0))
    return {"inputs": inputs, "short_filter": short_filter, "long_filter": long_filter, "skip_gain": skip_gain, "queries": queries, "key_rows": key_rows, "out_weight": out_weight}


def reference(inputs, short_filter, long_filter, skip_gain, queries, key_rows, out_weight):
    window = inputs.shape[0]
    signal = inputs.astype(jnp.float32)
    features = jnp.zeros(signal.shape, jnp.float32)
    for lag_index in range(SHORT_K):
        delayed = jnp.pad(signal, ((lag_index, 0), (0, 0), (0, 0)))[:window]
        features = features + short_filter[lag_index].astype(jnp.float32)[None] * delayed
    gate_product = (features[:, 1] * features[:, 2]).astype(jnp.bfloat16)
    gate_float = gate_product.astype(jnp.float32)
    filters = jnp.repeat(long_filter.astype(jnp.float32), GROUP, axis=0)
    padded = jnp.pad(gate_float, ((LONG_K - 1, 0), (0, 0)))

    def add_tap(tap_index, filtered):
        column = lax.dynamic_slice_in_dim(filters, tap_index, 1, 1)[:, 0]
        delayed = lax.dynamic_slice_in_dim(padded, LONG_K - 1 - tap_index, window, 0)
        return filtered + column[None] * delayed

    filtered = lax.fori_loop(0, LONG_K, add_tap, jnp.zeros((window, D), jnp.float32))
    values = (features[:, 0] * (filtered + skip_gain[None] * gate_float)).astype(jnp.bfloat16)
    head_count = D // HEAD_DIM
    head_queries = queries.reshape(window, head_count, HEAD_DIM).transpose(1, 0, 2)
    head_keys = key_rows.reshape(window, head_count, HEAD_DIM).transpose(1, 0, 2)
    head_values = values.reshape(window, head_count, HEAD_DIM).transpose(1, 0, 2)
    causal = jnp.tril(jnp.ones((window, window), jnp.bool_))

    def one_head(operands):
        head_query, head_key, head_value = operands
        scores = jnp.dot(head_query, head_key.T, preferred_element_type=jnp.float32) * (HEAD_DIM ** -0.5)
        new_max = jnp.max(jnp.where(causal, scores, -1e30), axis=1)
        probabilities = jnp.where(causal, jnp.exp(scores - new_max[:, None]), 0.0)
        weight_sum = jnp.sum(probabilities, axis=1)
        mixed = jnp.dot(probabilities.astype(jnp.bfloat16), head_value, preferred_element_type=jnp.float32)
        return (mixed / weight_sum[:, None]).astype(jnp.bfloat16)

    attended = lax.map(one_head, (head_queries, head_keys, head_values))
    attended = attended.transpose(1, 0, 2).reshape(window, D)
    return jnp.dot(attended, out_weight, preferred_element_type=jnp.float32).astype(jnp.bfloat16)
```

```python
import jax
import jax.numpy as jnp
from jax import lax
from jax.sharding import PartitionSpec as P

HEAD_DIM = 128


masked_score = -1e30


def passed_along(value, axis, steps):
    count = lax.axis_size(axis)
    initial, last = (max(0, -steps), min(count, count - steps))
    return lax.ppermute(value, axis, [(source, source + steps) for source in range(initial, last)])


def toeplitz_taps(filters, row_count):
    group_count = filters.shape[0]
    tap_count = filters.shape[1]
    span = row_count + tap_count - 1
    flipped = filters[:, ::-1]
    padded_taps = jnp.concatenate(
        [flipped, jnp.zeros((group_count, row_count), filters.dtype)], axis=1
    )
    repeated = jnp.tile(padded_taps, (1, row_count))
    return repeated[:, : row_count * span].reshape(group_count, row_count, span)


def short_features(extended, short_filter, row_count):
    tap_count = short_filter.shape[0]
    features = jnp.zeros((row_count,) + extended.shape[1:], jnp.float32)
    for lag_index in range(tap_count):
        delayed = extended[
            tap_count - 1 - lag_index : tap_count - 1 - lag_index + row_count
        ].astype(jnp.float32)
        features = features + short_filter[lag_index].astype(jnp.float32)[None] * delayed
    return features


def attend(head_queries, query_pos, key_piece, value_piece):
    key_count = key_piece.shape[0]
    head_count = head_queries.shape[1]
    key_heads = key_piece.reshape(key_count, head_count, -1)
    value_heads = value_piece.reshape(key_count, head_count, -1)
    scores = jnp.einsum(
        "qhd,khd->hqk", head_queries, key_heads, preferred_element_type=jnp.float32
    ) * head_queries.shape[2] ** (-0.5)
    key_pos = lax.iota(jnp.int32, key_count)
    allowed = (key_pos[None, :] <= query_pos[:, None])[None]
    peak = jnp.max(jnp.where(allowed, scores, masked_score), axis=2)
    probabilities = jnp.where(allowed, jnp.exp(scores - peak[..., None]), 0.0)
    weight_sum = jnp.sum(probabilities, axis=2)
    mixed = jnp.einsum(
        "hqk,khd->hqd",
        probabilities.astype(jnp.bfloat16),
        value_heads,
        preferred_element_type=jnp.float32,
    )
    result = mixed / weight_sum[..., None]
    return jnp.transpose(result, (1, 0, 2)).reshape(result.shape[1], -1).astype(jnp.bfloat16)


def by_rows(inputs, short_filter, long_filter, skip_gain, queries, key_rows):
    row_count = inputs.shape[0]
    channels = inputs.shape[2]
    groups = long_filter.shape[0]
    tap_count = long_filter.shape[1]
    short_reach = short_filter.shape[0] - 1
    position = lax.axis_index("ctx")
    rim = passed_along(inputs[row_count - short_reach :], "ctx", 1)
    extended = jnp.concatenate([rim, inputs], axis=0)
    features = short_features(extended, short_filter, row_count)
    gate_product = (features[:, 1] * features[:, 2]).astype(jnp.bfloat16)
    gate_prev = passed_along(gate_product[row_count - (tap_count - 1) :], "ctx", 1)
    gate_ext = jnp.concatenate([gate_prev, gate_product], axis=0)
    toeplitz = toeplitz_taps(long_filter, row_count)
    filtered = jnp.einsum(
        "gtr,rgc->tgc",
        toeplitz,
        gate_ext.reshape(row_count + tap_count - 1, groups, channels // groups),
        preferred_element_type=jnp.float32,
    ).reshape(row_count, channels)
    values = (
        features[:, 0] * (filtered + skip_gain[None] * gate_product.astype(jnp.float32))
    ).astype(jnp.bfloat16)
    head_count = channels // HEAD_DIM
    head_queries = queries.reshape(row_count, head_count, HEAD_DIM)
    query_pos = position * row_count + lax.iota(jnp.int32, row_count)
    return attend(
        head_queries,
        query_pos,
        lax.all_gather(key_rows, "ctx", axis=0, tiled=True),
        lax.all_gather(values, "ctx", axis=0, tiled=True),
    )


def by_heads(inputs, short_filter, long_filter, skip_gain, queries, key_rows):
    count = lax.axis_size("ctx")
    position = lax.axis_index("ctx")
    row_count, streams, channels = inputs.shape
    own = channels // count
    groups, tap_count = long_filter.shape
    own_groups = groups // count
    window = row_count * count
    arrays = [inputs[:, 1], inputs[:, 2], inputs[:, 0], queries, key_rows]
    sent = jnp.stack(
        [jnp.transpose(a.reshape(row_count, count, own), (1, 0, 2)) for a in arrays], axis=1
    )
    got = lax.all_to_all(sent, "ctx", 0, 0)
    got = jnp.transpose(got, (1, 0, 2, 3)).reshape(len(arrays), window, own)
    own_short = lax.dynamic_slice_in_dim(short_filter, position * own, own, 2).astype(jnp.float32)
    own_long = lax.dynamic_slice_in_dim(long_filter, position * own_groups, own_groups, 0)
    own_gain = lax.dynamic_slice_in_dim(skip_gain, position * own, own, 0)

    def feature(stream, which):
        signal = got[which].astype(jnp.float32)
        total = own_short[0, stream][None] * signal
        for lag in range(1, short_filter.shape[0]):
            total = total + own_short[lag, stream][None] * jnp.pad(signal, ((lag, 0), (0, 0)))[:window]
        return total

    gate = (feature(1, 0) * feature(2, 1)).astype(jnp.bfloat16)
    blocks = gate.reshape(count, row_count, own_groups, own // own_groups)
    earlier = jnp.concatenate([jnp.zeros_like(blocks[:1]), blocks[:-1]], axis=0)[:, row_count - tap_count + 1 :]
    extended = jnp.concatenate([earlier, blocks], axis=1)
    filtered = jnp.einsum(
        "gtr,brgc->btgc",
        toeplitz_taps(own_long, row_count),
        extended,
        preferred_element_type=jnp.float32,
    ).reshape(window, own)
    values = (feature(0, 2) * (filtered + own_gain[None] * gate.astype(jnp.float32))).astype(jnp.bfloat16)
    attended = attend(
        got[3].reshape(window, own // HEAD_DIM, HEAD_DIM),
        lax.iota(jnp.int32, window),
        got[4],
        values,
    )
    back = lax.all_to_all(attended.reshape(count, row_count, own), "ctx", 0, 0)
    return jnp.transpose(back, (1, 0, 2)).reshape(row_count, channels)


def per_device(inputs, short_filter, long_filter, skip_gain, queries, key_rows, out_weight):
    row_count, _, channels = inputs.shape
    count = lax.axis_size("ctx")
    splits = channels % (count * HEAD_DIM) == 0 and row_count + 1 >= long_filter.shape[1]
    mix = by_heads if splits else by_rows
    attended = mix(inputs, short_filter, long_filter, skip_gain, queries, key_rows)
    partial_out = jnp.dot(attended, out_weight, preferred_element_type=jnp.float32)
    return lax.psum_scatter(partial_out.astype(jnp.bfloat16), "mp", scatter_dimension=1, tiled=True)


def solution(mesh):
    placed = (
        P(("parts", "ctx"), None, "mp"),
        P(None, None, "mp"),
        P("mp", None),
        P("mp"),
        P(("parts", "ctx"), "mp"),
        P(("parts", "ctx"), "mp"),
        P("mp", None),
    )
    return jax.shard_map(
        per_device, mesh=mesh, in_specs=placed, out_specs=P(("parts", "ctx"), "mp"), check_vma=False
    )
```

```python
import jax
import jax.numpy as jnp
from jax import lax
from jax.experimental import pallas as pl
from jax.experimental.pallas import tpu as pltpu
from jax.sharding import PartitionSpec as P

HEAD_DIM = 128


masked_score = -1e30


def passed_along(value, axis, steps):
    count = lax.axis_size(axis)
    initial, last = (max(0, -steps), min(count, count - steps))
    return lax.ppermute(value, axis, [(source, source + steps) for source in range(initial, last)])


def toeplitz_taps(filters, row_count):
    group_count = filters.shape[0]
    tap_count = filters.shape[1]
    span = row_count + tap_count - 1
    flipped = filters[:, ::-1]
    padded_taps = jnp.concatenate(
        [flipped, jnp.zeros((group_count, row_count), filters.dtype)], axis=1
    )
    repeated = jnp.tile(padded_taps, (1, row_count))
    return repeated[:, : row_count * span].reshape(group_count, row_count, span)


def short_features(extended, short_filter, row_count):
    tap_count = short_filter.shape[0]
    features = jnp.zeros((row_count,) + extended.shape[1:], jnp.float32)
    for lag_index in range(tap_count):
        delayed = extended[
            tap_count - 1 - lag_index : tap_count - 1 - lag_index + row_count
        ].astype(jnp.float32)
        features = features + short_filter[lag_index].astype(jnp.float32)[None] * delayed
    return features


def attend(head_queries, query_pos, key_piece, value_piece):
    key_count = key_piece.shape[0]
    head_count = head_queries.shape[1]
    key_heads = key_piece.reshape(key_count, head_count, -1)
    value_heads = value_piece.reshape(key_count, head_count, -1)
    scores = jnp.einsum(
        "qhd,khd->hqk", head_queries, key_heads, preferred_element_type=jnp.float32
    ) * head_queries.shape[2] ** (-0.5)
    key_pos = lax.iota(jnp.int32, key_count)
    allowed = (key_pos[None, :] <= query_pos[:, None])[None]
    peak = jnp.max(jnp.where(allowed, scores, masked_score), axis=2)
    probabilities = jnp.where(allowed, jnp.exp(scores - peak[..., None]), 0.0)
    weight_sum = jnp.sum(probabilities, axis=2)
    mixed = jnp.einsum(
        "hqk,khd->hqd",
        probabilities.astype(jnp.bfloat16),
        value_heads,
        preferred_element_type=jnp.float32,
    )
    result = mixed / weight_sum[..., None]
    return jnp.transpose(result, (1, 0, 2)).reshape(result.shape[1], -1).astype(jnp.bfloat16)


def by_rows(inputs, short_filter, long_filter, skip_gain, queries, key_rows):
    row_count = inputs.shape[0]
    channels = inputs.shape[2]
    groups = long_filter.shape[0]
    tap_count = long_filter.shape[1]
    short_reach = short_filter.shape[0] - 1
    position = lax.axis_index("ctx")
    rim = passed_along(inputs[row_count - short_reach :], "ctx", 1)
    extended = jnp.concatenate([rim, inputs], axis=0)
    features = short_features(extended, short_filter, row_count)
    gate_product = (features[:, 1] * features[:, 2]).astype(jnp.bfloat16)
    gate_prev = passed_along(gate_product[row_count - (tap_count - 1) :], "ctx", 1)
    gate_ext = jnp.concatenate([gate_prev, gate_product], axis=0)
    toeplitz = toeplitz_taps(long_filter, row_count)
    filtered = jnp.einsum(
        "gtr,rgc->tgc",
        toeplitz,
        gate_ext.reshape(row_count + tap_count - 1, groups, channels // groups),
        preferred_element_type=jnp.float32,
    ).reshape(row_count, channels)
    values = (
        features[:, 0] * (filtered + skip_gain[None] * gate_product.astype(jnp.float32))
    ).astype(jnp.bfloat16)
    head_count = channels // HEAD_DIM
    head_queries = queries.reshape(row_count, head_count, HEAD_DIM)
    query_pos = position * row_count + lax.iota(jnp.int32, row_count)
    return attend(
        head_queries,
        query_pos,
        lax.all_gather(key_rows, "ctx", axis=0, tiled=True),
        lax.all_gather(values, "ctx", axis=0, tiled=True),
    )


def delayed(signal, lag):
    if lag == 0:
        return signal
    row = lax.broadcasted_iota(jnp.int32, signal.shape, 0)
    return jnp.where(row < lag, 0.0, pltpu.roll(signal, lag, 0))


def featured(signal, taps):
    total = taps[0] * signal
    for lag in range(1, len(taps)):
        total = total + taps[lag] * delayed(signal, lag)
    return total


def pack_kernel(inputs_ref, short_ref, queries_ref, keys_ref, out_ref):
    count, _, own = out_ref.shape
    rows = queries_ref.shape[0]
    edge_row = lax.broadcasted_iota(jnp.int32, (8, own), 0)
    for target in range(count):
        columns = slice(target * own, (target + 1) * own)
        features, edges = [], []
        for stream in (1, 2):
            signal = inputs_ref[stream, :, columns].astype(jnp.float32)
            taps = [short_ref[lag, stream : stream + 1, columns].astype(jnp.float32) for lag in range(3)]
            features.append(featured(signal, taps))
            last = pltpu.roll(signal[rows - 8 :], 4, 0)
            edges.append(jnp.where(edge_row < 2, signal[:8], jnp.where(edge_row < 4, last, 0.0)))
        out_ref[target, 0:rows] = (features[0] * features[1]).astype(jnp.bfloat16)
        out_ref[target, rows : 2 * rows] = inputs_ref[0, :, columns]
        out_ref[target, 2 * rows : 3 * rows] = queries_ref[:, columns]
        out_ref[target, 3 * rows : 4 * rows] = keys_ref[:, columns]
        out_ref[target, 4 * rows :] = jnp.concatenate(edges, axis=0).astype(jnp.bfloat16)


def band_kernel(_, filter_ref, out_ref):
    groups, taps = filter_ref.shape
    span = out_ref.shape[1]
    source = lax.broadcasted_iota(jnp.int32, (taps, span), 0)
    target = lax.broadcasted_iota(jnp.int32, (taps, span), 1)
    flip = (source + target == taps).astype(jnp.bfloat16)
    first = jnp.dot(filter_ref[...], flip, preferred_element_type=jnp.float32)
    for group in range(groups):
        repeated = jnp.broadcast_to(first[group : group + 1], (taps, span))
        banded = pltpu.roll(repeated, 0, 1, stride=1, stride_axis=0)
        out_ref[group * taps : (group + 1) * taps] = banded.astype(jnp.bfloat16)


def mixer_kernel(_, got_ref, band_ref, short_ref, gain_ref, out_ref, gate_s, value_s):
    count, rows, own = out_ref.shape
    window = count * rows
    groups = band_ref.shape[0] // rows
    per_group = own // groups
    taps = [[short_ref[lag, stream : stream + 1].astype(jnp.float32) for lag in range(3)] for stream in range(3)]
    gate_s[0:rows] = jnp.zeros((rows, own), jnp.bfloat16)
    edge_row = lax.broadcasted_iota(jnp.int32, (8, own), 0)
    head_row = lax.broadcasted_iota(jnp.int32, (16, own), 0)
    for block in range(count):
        gate_s[(block + 1) * rows : (block + 2) * rows] = got_ref[block, 0:rows]
        if block == 0:
            continue
        fixed = 1.0
        before = got_ref[block - 1, 4 * rows :].astype(jnp.float32)
        here = got_ref[block, 4 * rows :].astype(jnp.float32)
        for which, stream in enumerate((1, 2)):
            old = pltpu.roll(before[8 * which : 8 * which + 8], 6, 0)
            new = pltpu.roll(here[8 * which : 8 * which + 8], 2, 0)
            joined = jnp.where(edge_row < 2, old, new)
            fixed = fixed * (
                taps[stream][0] * pltpu.roll(joined, 6, 0)
                + taps[stream][1] * pltpu.roll(joined, 7, 0)
                + taps[stream][2] * joined
            )
        head = got_ref[block, 0:16].astype(jnp.float32)
        head = jnp.where(head_row < 2, jnp.concatenate([fixed, fixed], axis=0), head)
        gate_s[(block + 1) * rows : (block + 1) * rows + 16] = head.astype(jnp.bfloat16)
    signal = jnp.concatenate([got_ref[block, rows : 2 * rows] for block in range(count)], axis=0)
    feature = featured(signal.astype(jnp.float32), taps[0])
    gain = gain_ref[...]
    per_tile = HEAD_DIM // per_group
    lane = lax.broadcasted_iota(jnp.int32, (rows, HEAD_DIM), 1) // per_group
    for block in range(count):
        for tile in range(own // HEAD_DIM):
            columns = slice(tile * HEAD_DIM, (tile + 1) * HEAD_DIM)
            mixed = jnp.dot(
                band_ref[tile * per_tile * rows : (tile + 1) * per_tile * rows],
                gate_s[block * rows : (block + 2) * rows, columns],
                preferred_element_type=jnp.float32,
            )
            filtered = mixed[:rows]
            for group in range(1, per_tile):
                filtered = jnp.where(lane == group, mixed[group * rows : (group + 1) * rows], filtered)
            here = slice(block * rows, (block + 1) * rows)
            gate = gate_s[(block + 1) * rows : (block + 2) * rows, columns].astype(jnp.float32)
            value_s[here, columns] = (
                feature[here, columns] * (filtered + gain[:, columns] * gate)
            ).astype(jnp.bfloat16)
    causal = lax.broadcasted_iota(jnp.int32, (rows, rows), 1) <= lax.broadcasted_iota(jnp.int32, (rows, rows), 0)
    for head in range(own // HEAD_DIM):
        columns = slice(head * HEAD_DIM, (head + 1) * HEAD_DIM)
        for block in range(count):
            query = got_ref[block, 2 * rows : 3 * rows, columns]
            keys = jnp.concatenate(
                [got_ref[other, 3 * rows : 4 * rows, columns] for other in range(block + 1)], axis=0
            )
            scores = lax.dot_general(
                query, keys, (((1,), (1,)), ((), ())), preferred_element_type=jnp.float32
            ) * HEAD_DIM ** (-0.5)
            own_scores = jnp.where(causal, scores[:, block * rows :], masked_score)
            pieces = [scores[:, : block * rows], own_scores] if block else [own_scores]
            scores = jnp.concatenate(pieces, axis=1)
            peak = jnp.max(scores, axis=1, keepdims=True)
            weights = jnp.exp(scores - peak)
            total = jnp.sum(weights, axis=1, keepdims=True)
            mixed = jnp.dot(
                weights.astype(jnp.bfloat16),
                value_s[0 : (block + 1) * rows, columns],
                preferred_element_type=jnp.float32,
            )
            out_ref[block, :, columns] = (mixed / total).astype(jnp.bfloat16)


def project_kernel(_, attended_ref, weight_ref, out_ref):
    count, rows, own = attended_ref.shape
    attended = jnp.concatenate([attended_ref[source] for source in range(count)], axis=1)
    out_ref[0] = jnp.dot(attended, weight_ref[...], preferred_element_type=jnp.float32).astype(jnp.bfloat16)


VMEM_LIMIT = 40 * 1024 * 1024


def whole(array):
    shape = array.shape
    return pl.BlockSpec(shape, lambda *_: (0,) * len(shape))


def by_heads(inputs, short_filter, long_filter, skip_gain, queries, key_rows):
    count = lax.axis_size("ctx")
    position = lax.axis_index("ctx").reshape(1)
    rows, streams, channels = inputs.shape
    own = channels // count
    groups, taps = long_filter.shape
    own_groups = groups // count
    params = pltpu.CompilerParams(vmem_limit_bytes=VMEM_LIMIT)
    sent = pl.pallas_call(
        pack_kernel,
        out_shape=jax.ShapeDtypeStruct((count, 4 * rows + 16, own), jnp.bfloat16),
        compiler_params=params,
        name="pack",
    )(jnp.transpose(inputs, (1, 0, 2)), short_filter, queries, key_rows)
    got = lax.all_to_all(sent, "ctx", 0, 0)
    band = pl.pallas_call(
        band_kernel,
        out_shape=jax.ShapeDtypeStruct((own_groups * taps, 2 * taps), jnp.bfloat16),
        grid_spec=pltpu.PrefetchScalarGridSpec(
            num_scalar_prefetch=1,
            grid=(1,),
            in_specs=[pl.BlockSpec((own_groups, taps), lambda _, at: (at[0], 0))],
            out_specs=pl.BlockSpec((own_groups * taps, 2 * taps), lambda _, at: (0, 0)),
        ),
        compiler_params=params,
        name="band",
    )(position, long_filter)
    attended = pl.pallas_call(
        mixer_kernel,
        out_shape=jax.ShapeDtypeStruct((count, rows, own), jnp.bfloat16),
        grid_spec=pltpu.PrefetchScalarGridSpec(
            num_scalar_prefetch=1,
            grid=(1,),
            in_specs=[
                whole(got),
                whole(band),
                pl.BlockSpec((3, streams, own), lambda _, at: (0, 0, at[0])),
                pl.BlockSpec((1, own), lambda _, at: (0, at[0])),
            ],
            out_specs=pl.BlockSpec((count, rows, own), lambda _, at: (0, 0, 0)),
            scratch_shapes=[
                pltpu.VMEM(((count + 1) * rows, own), jnp.bfloat16),
                pltpu.VMEM((count * rows, own), jnp.bfloat16),
            ],
        ),
        compiler_params=params,
        name="mixer",
    )(position, got, band, short_filter, skip_gain.reshape(1, channels))
    return lax.all_to_all(attended, "ctx", 0, 0)


def projected(attended, out_weight, blocks, width):
    count, rows, own = attended.shape
    chunk = width // 2
    number = blocks.shape[0]
    return pl.pallas_call(
        project_kernel,
        out_shape=jax.ShapeDtypeStruct((number, rows, width), jnp.bfloat16),
        grid_spec=pltpu.PrefetchScalarGridSpec(
            num_scalar_prefetch=1,
            grid=(number * 2,),
            in_specs=[
                whole(attended),
                pl.BlockSpec((count * own, chunk), lambda step, at: (0, at[step // 2] * 2 + step % 2)),
            ],
            out_specs=pl.BlockSpec((1, rows, chunk), lambda step, at: (step // 2, 0, step % 2)),
        ),
        compiler_params=pltpu.CompilerParams(vmem_limit_bytes=VMEM_LIMIT),
        name="project",
    )(blocks, attended, out_weight)


def added(*terms):
    total = terms[0].astype(jnp.float32)
    for term in terms[1:]:
        total = total + term.astype(jnp.float32)
    return total.astype(jnp.bfloat16)


def crossed(value, step):
    return lax.ppermute(value, "mp", [(source, source ^ step) for source in range(lax.axis_size("mp"))])


def project_and_share(attended, out_weight):
    width = out_weight.shape[1] // lax.axis_size("mp")
    here = lax.axis_index("mp")
    far = projected(attended, out_weight, jnp.stack([here ^ 3, here ^ 2]), width)
    far_given = crossed(far[0], 1)
    near = projected(attended, out_weight, jnp.stack([here ^ 1, here]), width)
    far_sum = added(far[1], far_given)
    near_given = crossed(near[0], 1)
    far_got = crossed(far_sum, 2)
    return added(near[1], near_given, far_got)


def per_device(inputs, short_filter, long_filter, skip_gain, queries, key_rows, out_weight):
    rows, _, channels = inputs.shape
    count = lax.axis_size("ctx")
    taps = long_filter.shape[1]
    splits = channels % (count * HEAD_DIM) == 0 and count <= 4 and rows == taps
    if splits and lax.axis_size("mp") == 4:
        attended = by_heads(inputs, short_filter, long_filter, skip_gain, queries, key_rows)
        return project_and_share(attended, out_weight)
    attended = by_rows(inputs, short_filter, long_filter, skip_gain, queries, key_rows)
    partial_out = jnp.dot(attended, out_weight, preferred_element_type=jnp.float32)
    return lax.psum_scatter(partial_out.astype(jnp.bfloat16), "mp", scatter_dimension=1, tiled=True)


def solution(mesh):
    placed = (
        P(("parts", "ctx"), None, "mp"),
        P(None, None, "mp"),
        P("mp", None),
        P("mp"),
        P(("parts", "ctx"), "mp"),
        P(("parts", "ctx"), "mp"),
        P("mp", None),
    )
    return jax.shard_map(
        per_device, mesh=mesh, in_specs=placed, out_specs=P(("parts", "ctx"), "mp"), check_vma=False
    )
```

```python
import functools

import jax
import jax.numpy as jnp
from jax import lax
from jax.experimental import pallas as pl
from jax.experimental.pallas import tpu as pltpu
from jax.sharding import PartitionSpec as P

HEAD_DIM = 128


masked_score = -1e30


def passed_along(value, axis, steps):
    count = lax.axis_size(axis)
    initial, last = (max(0, -steps), min(count, count - steps))
    return lax.ppermute(value, axis, [(source, source + steps) for source in range(initial, last)])


def toeplitz_taps(filters, row_count):
    group_count = filters.shape[0]
    tap_count = filters.shape[1]
    span = row_count + tap_count - 1
    flipped = filters[:, ::-1]
    padded_taps = jnp.concatenate(
        [flipped, jnp.zeros((group_count, row_count), filters.dtype)], axis=1
    )
    repeated = jnp.tile(padded_taps, (1, row_count))
    return repeated[:, : row_count * span].reshape(group_count, row_count, span)


def short_features(extended, short_filter, row_count):
    tap_count = short_filter.shape[0]
    features = jnp.zeros((row_count,) + extended.shape[1:], jnp.float32)
    for lag_index in range(tap_count):
        delayed = extended[
            tap_count - 1 - lag_index : tap_count - 1 - lag_index + row_count
        ].astype(jnp.float32)
        features = features + short_filter[lag_index].astype(jnp.float32)[None] * delayed
    return features


def attend(head_queries, query_pos, key_piece, value_piece):
    key_count = key_piece.shape[0]
    head_count = head_queries.shape[1]
    key_heads = key_piece.reshape(key_count, head_count, -1)
    value_heads = value_piece.reshape(key_count, head_count, -1)
    scores = jnp.einsum(
        "qhd,khd->hqk", head_queries, key_heads, preferred_element_type=jnp.float32
    ) * head_queries.shape[2] ** (-0.5)
    key_pos = lax.iota(jnp.int32, key_count)
    allowed = (key_pos[None, :] <= query_pos[:, None])[None]
    peak = jnp.max(jnp.where(allowed, scores, masked_score), axis=2)
    probabilities = jnp.where(allowed, jnp.exp(scores - peak[..., None]), 0.0)
    weight_sum = jnp.sum(probabilities, axis=2)
    mixed = jnp.einsum(
        "hqk,khd->hqd",
        probabilities.astype(jnp.bfloat16),
        value_heads,
        preferred_element_type=jnp.float32,
    )
    result = mixed / weight_sum[..., None]
    return jnp.transpose(result, (1, 0, 2)).reshape(result.shape[1], -1).astype(jnp.bfloat16)


def by_rows(inputs, short_filter, long_filter, skip_gain, queries, key_rows):
    row_count = inputs.shape[0]
    channels = inputs.shape[2]
    groups = long_filter.shape[0]
    tap_count = long_filter.shape[1]
    short_reach = short_filter.shape[0] - 1
    position = lax.axis_index("ctx")
    rim = passed_along(inputs[row_count - short_reach :], "ctx", 1)
    extended = jnp.concatenate([rim, inputs], axis=0)
    features = short_features(extended, short_filter, row_count)
    gate_product = (features[:, 1] * features[:, 2]).astype(jnp.bfloat16)
    gate_prev = passed_along(gate_product[row_count - (tap_count - 1) :], "ctx", 1)
    gate_ext = jnp.concatenate([gate_prev, gate_product], axis=0)
    toeplitz = toeplitz_taps(long_filter, row_count)
    filtered = jnp.einsum(
        "gtr,rgc->tgc",
        toeplitz,
        gate_ext.reshape(row_count + tap_count - 1, groups, channels // groups),
        preferred_element_type=jnp.float32,
    ).reshape(row_count, channels)
    values = (
        features[:, 0] * (filtered + skip_gain[None] * gate_product.astype(jnp.float32))
    ).astype(jnp.bfloat16)
    head_count = channels // HEAD_DIM
    head_queries = queries.reshape(row_count, head_count, HEAD_DIM)
    query_pos = position * row_count + lax.iota(jnp.int32, row_count)
    return attend(
        head_queries,
        query_pos,
        lax.all_gather(key_rows, "ctx", axis=0, tiled=True),
        lax.all_gather(values, "ctx", axis=0, tiled=True),
    )


def delayed(signal, lag):
    if lag == 0:
        return signal
    row = lax.broadcasted_iota(jnp.int32, signal.shape, 0)
    return jnp.where(row < lag, 0.0, pltpu.roll(signal, lag, 0))


def featured(signal, taps):
    total = taps[0] * signal
    for lag in range(1, len(taps)):
        total = total + taps[lag] * delayed(signal, lag)
    return total


def pack_kernel(inputs_any, short_any, queries_any, keys_any, *refs):
    count = 4
    first_refs, second_refs = refs[:count], refs[count : 2 * count]
    signal_s, short_s, gate_s, in_sems, gate_sems, plain_sems = refs[2 * count :]
    rows, own = signal_s.shape[2:]
    edged = gate_s.shape[1]
    position = lax.axis_index("ctx")
    columns = [pl.ds(pl.multiple_of((position ^ step) * own, own), own) for step in range(count)]
    order = (3, 2, 1, 0)
    load_short = pltpu.make_async_copy(short_any, short_s, in_sems.at[count])
    load_short.start()
    loads = [
        pltpu.make_async_copy(inputs_any.at[1:3, :, columns[step]], signal_s.at[step], in_sems.at[step])
        for step in range(count)
    ]
    for step in order:
        loads[step].start()
    plain = []
    for step in order:
        for index, (source, target) in enumerate(
            (
                (inputs_any.at[0, :, columns[step]], first_refs[step].at[edged:]),
                (queries_any.at[:, columns[step]], second_refs[step].at[0:rows]),
                (keys_any.at[:, columns[step]], second_refs[step].at[rows:]),
            )
        ):
            plain.append(pltpu.make_async_copy(source, target, plain_sems.at[3 * step + index]))
    for copy in plain:
        copy.start()
    edge_row = lax.broadcasted_iota(jnp.int32, (8, own), 0)
    load_short.wait()
    stores = []
    for step in order:
        loads[step].wait()
        features, edges = [], []
        for stream in (1, 2):
            signal = signal_s[step, stream - 1].astype(jnp.float32)
            taps = [short_s[lag, stream : stream + 1, columns[step]].astype(jnp.float32) for lag in range(3)]
            features.append(featured(signal, taps))
            last = pltpu.roll(signal[rows - 8 :], 4, 0)
            edges.append(jnp.where(edge_row < 2, signal[:8], jnp.where(edge_row < 4, last, 0.0)))
        gate_s[step, 0:rows] = (features[0] * features[1]).astype(jnp.bfloat16)
        gate_s[step, rows:] = jnp.concatenate(edges, axis=0).astype(jnp.bfloat16)
        store = pltpu.make_async_copy(gate_s.at[step], first_refs[step].at[0:edged], gate_sems.at[step])
        store.start()
        stores.append(store)
    for copy in plain + stores:
        copy.wait()


def ready_kernel(filter_ref, weight_any, band_ref, weight_ref, sem):
    rows, span = band_ref.shape
    taps = filter_ref.shape[1]
    groups = rows // taps
    weights = pltpu.make_async_copy(weight_any, weight_ref, sem)
    weights.start()
    source = lax.broadcasted_iota(jnp.int32, (taps, span), 0)
    target = lax.broadcasted_iota(jnp.int32, (taps, span), 1)
    flip = (source + target == taps).astype(jnp.bfloat16)
    first_group = pl.multiple_of(lax.axis_index("ctx") * groups, groups)
    first = jnp.dot(filter_ref[pl.ds(first_group, groups)], flip, preferred_element_type=jnp.float32)
    for group in range(groups):
        repeated = jnp.broadcast_to(first[group : group + 1], (taps, span))
        banded = pltpu.roll(repeated, 0, 1, stride=1, stride_axis=0)
        band_ref[group * taps : (group + 1) * taps] = banded.astype(jnp.bfloat16)
    weights.wait()


def values_kernel(at, *refs):
    count = 4
    given = refs[:count]
    band_ref, short_ref, gain_ref, out_ref, got_s, gate_s = refs[count:]
    own = out_ref.shape[1]
    rows = out_ref.shape[0] // count
    groups = band_ref.shape[0] // rows
    per_group = own // groups
    position = at[0]
    for step in range(count):
        got_s[position ^ step] = given[step][...]
    taps = [[short_ref[lag, stream : stream + 1].astype(jnp.float32) for lag in range(3)] for stream in range(3)]
    gate_s[0:rows] = jnp.zeros((rows, own), jnp.bfloat16)
    edge_row = lax.broadcasted_iota(jnp.int32, (8, own), 0)
    head_row = lax.broadcasted_iota(jnp.int32, (16, own), 0)
    for block in range(count):
        gate_s[(block + 1) * rows : (block + 2) * rows] = got_s[block, 0:rows]
        if block == 0:
            continue
        fixed = 1.0
        before = got_s[block - 1, rows : rows + 16].astype(jnp.float32)
        here = got_s[block, rows : rows + 16].astype(jnp.float32)
        for which, stream in enumerate((1, 2)):
            old = pltpu.roll(before[8 * which : 8 * which + 8], 6, 0)
            new = pltpu.roll(here[8 * which : 8 * which + 8], 2, 0)
            joined = jnp.where(edge_row < 2, old, new)
            fixed = fixed * (
                taps[stream][0] * pltpu.roll(joined, 6, 0)
                + taps[stream][1] * pltpu.roll(joined, 7, 0)
                + taps[stream][2] * joined
            )
        head = got_s[block, 0:16].astype(jnp.float32)
        head = jnp.where(head_row < 2, jnp.concatenate([fixed, fixed], axis=0), head)
        gate_s[(block + 1) * rows : (block + 1) * rows + 16] = head.astype(jnp.bfloat16)
    signal = jnp.concatenate([got_s[block, rows + 16 :] for block in range(count)], axis=0)
    feature = featured(signal.astype(jnp.float32), taps[0])
    gain = gain_ref[...]
    per_tile = HEAD_DIM // per_group
    lane = lax.broadcasted_iota(jnp.int32, (rows, HEAD_DIM), 1) // per_group
    for block in range(count):
        for tile in range(own // HEAD_DIM):
            columns = slice(tile * HEAD_DIM, (tile + 1) * HEAD_DIM)
            mixed = jnp.dot(
                band_ref[tile * per_tile * rows : (tile + 1) * per_tile * rows],
                gate_s[block * rows : (block + 2) * rows, columns],
                preferred_element_type=jnp.float32,
            )
            filtered = mixed[:rows]
            for group in range(1, per_tile):
                filtered = jnp.where(lane == group, mixed[group * rows : (group + 1) * rows], filtered)
            here = slice(block * rows, (block + 1) * rows)
            gate = gate_s[(block + 1) * rows : (block + 2) * rows, columns].astype(jnp.float32)
            out_ref[here, columns] = (
                feature[here, columns] * (filtered + gain[:, columns] * gate)
            ).astype(jnp.bfloat16)


def attend_kernel(*refs):
    count = 4
    given, value_ref = refs[:count], refs[count]
    out_refs = refs[count + 1 : 2 * count + 1]
    query_s, key_s, out_s = refs[2 * count + 1 :]
    rows, own = query_s.shape[1:]
    position = lax.axis_index("ctx")
    for step in range(count):
        query_s[position ^ step] = given[step][0:rows]
        key_s[pl.ds(pl.multiple_of((position ^ step) * rows, rows), rows)] = given[step][rows:]
    causal = lax.broadcasted_iota(jnp.int32, (rows, rows), 1) <= lax.broadcasted_iota(jnp.int32, (rows, rows), 0)
    for head in range(own // HEAD_DIM):
        columns = slice(head * HEAD_DIM, (head + 1) * HEAD_DIM)
        for block in range(count):
            scores = lax.dot_general(
                query_s[block, :, columns],
                key_s[0 : (block + 1) * rows, columns],
                (((1,), (1,)), ((), ())),
                preferred_element_type=jnp.float32,
            ) * HEAD_DIM ** (-0.5)
            own_scores = jnp.where(causal, scores[:, block * rows :], masked_score)
            pieces = [scores[:, : block * rows], own_scores] if block else [own_scores]
            scores = jnp.concatenate(pieces, axis=1)
            peak = jnp.max(scores, axis=1, keepdims=True)
            weights = jnp.exp(scores - peak)
            total = jnp.sum(weights, axis=1, keepdims=True)
            mixed = jnp.dot(
                weights.astype(jnp.bfloat16),
                value_ref[0 : (block + 1) * rows, columns],
                preferred_element_type=jnp.float32,
            )
            out_s[block, :, columns] = (mixed / total).astype(jnp.bfloat16)
    for step in range(count):
        out_refs[step][...] = out_s[position ^ step]


def project_kernel(masks, *refs):
    count = 4
    given, weight_ref = refs[:count], refs[count]
    out_refs, attended_s = refs[count + 1 : -1], refs[-1]
    own = given[0].shape[1]
    width = out_refs[0].shape[1]
    position, here = lax.axis_index("ctx"), lax.axis_index("mp")
    for step in range(count):
        attended_s[:, pl.ds(pl.multiple_of((position ^ step) * own, own), own)] = given[step][...]
    for mask, out_ref in zip(masks, out_refs):
        columns = pl.ds(pl.multiple_of((here ^ mask) * width, width), width)
        out_ref[...] = jnp.dot(
            attended_s[...], weight_ref[:, columns], preferred_element_type=jnp.float32
        ).astype(jnp.bfloat16)


VMEM_LIMIT = 40 * 1024 * 1024
WIDE_LIMIT = 60 * 1024 * 1024
IN_HBM = pl.BlockSpec(memory_space=pl.ANY)
IN_VMEM = pl.BlockSpec(memory_space=pltpu.VMEM)


def whole(array):
    shape = array.shape
    return pl.BlockSpec(shape, lambda *_: (0,) * len(shape))


def swapped(value, axis, step):
    return lax.ppermute(value, axis, [(source, source ^ step) for source in range(lax.axis_size(axis))])


def exchanged(pieces, axis):
    sent = {step: swapped(pieces[step], axis, step) for step in (3, 2, 1)}
    return [pieces[0]] + [sent[step] for step in (1, 2, 3)]


def by_heads(inputs, short_filter, long_filter, skip_gain, queries, key_rows, out_weight):
    count = lax.axis_size("ctx")
    position = lax.axis_index("ctx").reshape(1)
    rows, streams, channels = inputs.shape
    own = channels // count
    groups, taps = long_filter.shape
    own_groups = groups // count
    params = pltpu.CompilerParams(vmem_limit_bytes=VMEM_LIMIT)
    first = jax.ShapeDtypeStruct((2 * rows + 16, own), jnp.bfloat16)
    second = jax.ShapeDtypeStruct((2 * rows, own), jnp.bfloat16)
    piece = jax.ShapeDtypeStruct((rows, own), jnp.bfloat16)
    sent = pl.pallas_call(
        pack_kernel,
        out_shape=[first] * count + [second] * count,
        in_specs=[IN_HBM] * 4,
        out_specs=[IN_HBM] * (2 * count),
        scratch_shapes=[
            pltpu.VMEM((count, 2, rows, own), jnp.bfloat16),
            pltpu.VMEM(short_filter.shape, jnp.bfloat16),
            pltpu.VMEM((count, rows + 16, own), jnp.bfloat16),
            pltpu.SemaphoreType.DMA((count + 1,)),
            pltpu.SemaphoreType.DMA((count,)),
            pltpu.SemaphoreType.DMA((3 * count,)),
        ],
        compiler_params=pltpu.CompilerParams(vmem_limit_bytes=WIDE_LIMIT),
        name="pack",
    )(jnp.transpose(inputs, (1, 0, 2)), short_filter, queries, key_rows)
    first_got = exchanged(sent[:count], "ctx")
    second_got = exchanged(sent[count:], "ctx")
    band, weight = pl.pallas_call(
        ready_kernel,
        out_shape=[
            jax.ShapeDtypeStruct((own_groups * taps, 2 * taps), jnp.bfloat16),
            jax.ShapeDtypeStruct(out_weight.shape, jnp.bfloat16),
        ],
        in_specs=[IN_VMEM, IN_HBM],
        out_specs=[IN_VMEM] * 2,
        scratch_shapes=[pltpu.SemaphoreType.DMA],
        compiler_params=params,
        name="ready",
    )(long_filter, out_weight)
    values = pl.pallas_call(
        values_kernel,
        out_shape=jax.ShapeDtypeStruct((count * rows, own), jnp.bfloat16),
        grid_spec=pltpu.PrefetchScalarGridSpec(
            num_scalar_prefetch=1,
            grid=(1,),
            in_specs=[whole(first)] * count
            + [
                whole(band),
                pl.BlockSpec((3, streams, own), lambda _, at: (0, 0, at[0])),
                pl.BlockSpec((1, own), lambda _, at: (0, at[0])),
            ],
            out_specs=pl.BlockSpec((count * rows, own), lambda _, at: (0, 0)),
            scratch_shapes=[
                pltpu.VMEM((count, 2 * rows + 16, own), jnp.bfloat16),
                pltpu.VMEM(((count + 1) * rows, own), jnp.bfloat16),
            ],
        ),
        compiler_params=params,
        cost_estimate=pl.CostEstimate(flops=2 * count * rows * own * 8 * 2 * taps, bytes_accessed=2**21, transcendentals=0),
        name="values",
    )(position, *first_got, band, short_filter, skip_gain.reshape(1, channels))
    attended = pl.pallas_call(
        attend_kernel,
        out_shape=[piece] * count,
        in_specs=[IN_VMEM] * (count + 1),
        out_specs=[IN_VMEM] * count,
        scratch_shapes=[
            pltpu.VMEM((count, rows, own), jnp.bfloat16),
            pltpu.VMEM((count * rows, own), jnp.bfloat16),
            pltpu.VMEM((count, rows, own), jnp.bfloat16),
        ],
        compiler_params=params,
        name="attend",
    )(*second_got, values)
    return project_and_share(exchanged(attended, "ctx"), weight)


def projected(attended, out_weight, masks):
    rows = attended[0].shape[0]
    width = out_weight.shape[1] // lax.axis_size("mp")
    return pl.pallas_call(
        functools.partial(project_kernel, masks),
        out_shape=[jax.ShapeDtypeStruct((rows, width), jnp.bfloat16)] * len(masks),
        in_specs=[IN_VMEM] * (len(attended) + 1),
        out_specs=[IN_VMEM] * len(masks),
        scratch_shapes=[pltpu.VMEM((rows, out_weight.shape[0]), jnp.bfloat16)],
        compiler_params=pltpu.CompilerParams(vmem_limit_bytes=VMEM_LIMIT),
        cost_estimate=pl.CostEstimate(
            flops=2 * rows * out_weight.shape[0] * width * len(masks), bytes_accessed=2**22, transcendentals=0
        ),
        name="project",
    )(*attended, out_weight)


def added(*terms):
    total = terms[0].astype(jnp.float32)
    for term in terms[1:]:
        total = total + term.astype(jnp.float32)
    return total.astype(jnp.bfloat16)


def project_and_share(attended, out_weight):
    far_given, far_kept = projected(attended, out_weight, (3, 2))
    far_got = swapped(far_given, "mp", 1)
    near_given, near_kept = projected(attended, out_weight, (1, 0))
    far_sum = added(far_kept, far_got)
    near_got = swapped(near_given, "mp", 1)
    return added(near_kept, near_got, swapped(far_sum, "mp", 2))


def per_device(inputs, short_filter, long_filter, skip_gain, queries, key_rows, out_weight):
    rows, _, channels = inputs.shape
    count = lax.axis_size("ctx")
    taps = long_filter.shape[1]
    splits = channels % (count * HEAD_DIM) == 0 and count == 4 and rows == taps
    if splits and lax.axis_size("mp") == 4:
        return by_heads(inputs, short_filter, long_filter, skip_gain, queries, key_rows, out_weight)
    attended = by_rows(inputs, short_filter, long_filter, skip_gain, queries, key_rows)
    partial_out = jnp.dot(attended, out_weight, preferred_element_type=jnp.float32)
    return lax.psum_scatter(partial_out.astype(jnp.bfloat16), "mp", scatter_dimension=1, tiled=True)


def solution(mesh):
    placed = (
        P(("parts", "ctx"), None, "mp"),
        P(None, None, "mp"),
        P("mp", None),
        P("mp"),
        P(("parts", "ctx"), "mp"),
        P(("parts", "ctx"), "mp"),
        P("mp", None),
    )
    return jax.shard_map(
        per_device, mesh=mesh, in_specs=placed, out_specs=P(("parts", "ctx"), "mp"), check_vma=False
    )
```

```python
import functools

import jax
import jax.numpy as jnp
from jax import lax
from jax.experimental import pallas as pl
from jax.experimental.pallas import tpu as pltpu
from jax.sharding import PartitionSpec as P

HEAD_DIM = 128


masked_score = -1e30


def passed_along(value, axis, steps):
    count = lax.axis_size(axis)
    initial, last = (max(0, -steps), min(count, count - steps))
    return lax.ppermute(value, axis, [(source, source + steps) for source in range(initial, last)])


def toeplitz_taps(filters, row_count):
    group_count = filters.shape[0]
    tap_count = filters.shape[1]
    span = row_count + tap_count - 1
    flipped = filters[:, ::-1]
    padded_taps = jnp.concatenate(
        [flipped, jnp.zeros((group_count, row_count), filters.dtype)], axis=1
    )
    repeated = jnp.tile(padded_taps, (1, row_count))
    return repeated[:, : row_count * span].reshape(group_count, row_count, span)


def short_features(extended, short_filter, row_count):
    tap_count = short_filter.shape[0]
    features = jnp.zeros((row_count,) + extended.shape[1:], jnp.float32)
    for lag_index in range(tap_count):
        delayed = extended[
            tap_count - 1 - lag_index : tap_count - 1 - lag_index + row_count
        ].astype(jnp.float32)
        features = features + short_filter[lag_index].astype(jnp.float32)[None] * delayed
    return features


def attend(head_queries, query_pos, key_piece, value_piece):
    key_count = key_piece.shape[0]
    head_count = head_queries.shape[1]
    key_heads = key_piece.reshape(key_count, head_count, -1)
    value_heads = value_piece.reshape(key_count, head_count, -1)
    scores = jnp.einsum(
        "qhd,khd->hqk", head_queries, key_heads, preferred_element_type=jnp.float32
    ) * head_queries.shape[2] ** (-0.5)
    key_pos = lax.iota(jnp.int32, key_count)
    allowed = (key_pos[None, :] <= query_pos[:, None])[None]
    peak = jnp.max(jnp.where(allowed, scores, masked_score), axis=2)
    probabilities = jnp.where(allowed, jnp.exp(scores - peak[..., None]), 0.0)
    weight_sum = jnp.sum(probabilities, axis=2)
    mixed = jnp.einsum(
        "hqk,khd->hqd",
        probabilities.astype(jnp.bfloat16),
        value_heads,
        preferred_element_type=jnp.float32,
    )
    result = mixed / weight_sum[..., None]
    return jnp.transpose(result, (1, 0, 2)).reshape(result.shape[1], -1).astype(jnp.bfloat16)


def by_rows(inputs, short_filter, long_filter, skip_gain, queries, key_rows):
    row_count = inputs.shape[0]
    channels = inputs.shape[2]
    groups = long_filter.shape[0]
    tap_count = long_filter.shape[1]
    short_reach = short_filter.shape[0] - 1
    position = lax.axis_index("ctx")
    rim = passed_along(inputs[row_count - short_reach :], "ctx", 1)
    extended = jnp.concatenate([rim, inputs], axis=0)
    features = short_features(extended, short_filter, row_count)
    gate_product = (features[:, 1] * features[:, 2]).astype(jnp.bfloat16)
    gate_prev = passed_along(gate_product[row_count - (tap_count - 1) :], "ctx", 1)
    gate_ext = jnp.concatenate([gate_prev, gate_product], axis=0)
    toeplitz = toeplitz_taps(long_filter, row_count)
    filtered = jnp.einsum(
        "gtr,rgc->tgc",
        toeplitz,
        gate_ext.reshape(row_count + tap_count - 1, groups, channels // groups),
        preferred_element_type=jnp.float32,
    ).reshape(row_count, channels)
    values = (
        features[:, 0] * (filtered + skip_gain[None] * gate_product.astype(jnp.float32))
    ).astype(jnp.bfloat16)
    head_count = channels // HEAD_DIM
    head_queries = queries.reshape(row_count, head_count, HEAD_DIM)
    query_pos = position * row_count + lax.iota(jnp.int32, row_count)
    return attend(
        head_queries,
        query_pos,
        lax.all_gather(key_rows, "ctx", axis=0, tiled=True),
        lax.all_gather(values, "ctx", axis=0, tiled=True),
    )


def delayed(signal, lag):
    if lag == 0:
        return signal
    row = lax.broadcasted_iota(jnp.int32, signal.shape, 0)
    return jnp.where(row < lag, 0.0, pltpu.roll(signal, lag, 0))


def featured(signal, taps):
    total = taps[0] * signal
    for lag in range(1, len(taps)):
        total = total + taps[lag] * delayed(signal, lag)
    return total


def pack_kernel(inputs_any, short_any, queries_any, keys_any, *refs):
    count = 4
    first_refs, second_refs = refs[:count], refs[count : 2 * count]
    inputs_s, short_s, queries_s, keys_s, in_sems = refs[2 * count :]
    rows, own = second_refs[0].shape[0] // 2, second_refs[0].shape[1]
    edged = rows + 16
    position = lax.axis_index("ctx")
    columns = [pl.ds(pl.multiple_of((position ^ step) * own, own), own) for step in range(count)]
    order = (3, 2, 1, 0)
    loads = [
        pltpu.make_async_copy(source, held, in_sems.at[index])
        for index, (source, held) in enumerate(
            (
                (short_any, short_s),
                (inputs_any.at[1], inputs_s.at[1]),
                (inputs_any.at[2], inputs_s.at[2]),
                (inputs_any.at[0], inputs_s.at[0]),
                (queries_any, queries_s),
                (keys_any, keys_s),
            )
        )
    ]
    for load in loads:
        load.start()
    edge_row = lax.broadcasted_iota(jnp.int32, (8, own), 0)
    for load in loads[:4]:
        load.wait()
    for step in order:
        features, edges = [], []
        for stream in (1, 2):
            signal = inputs_s[stream, :, columns[step]].astype(jnp.float32)
            taps = [short_s[lag, stream : stream + 1, columns[step]].astype(jnp.float32) for lag in range(3)]
            features.append(featured(signal, taps))
            last = pltpu.roll(signal[rows - 8 :], 4, 0)
            edges.append(jnp.where(edge_row < 2, signal[:8], jnp.where(edge_row < 4, last, 0.0)))
        first_refs[step][0:rows] = (features[0] * features[1]).astype(jnp.bfloat16)
        first_refs[step][rows:edged] = jnp.concatenate(edges, axis=0).astype(jnp.bfloat16)
        first_refs[step][edged:] = inputs_s[0, :, columns[step]]
    for load in loads[4:]:
        load.wait()
    for step in order:
        second_refs[step][0:rows] = queries_s[:, columns[step]]
        second_refs[step][rows:] = keys_s[:, columns[step]]


def ready_kernel(filter_ref, weight_any, band_ref, weight_ref, sem):
    rows, span = band_ref.shape
    taps = filter_ref.shape[1]
    groups = rows // taps
    weights = pltpu.make_async_copy(weight_any, weight_ref, sem)
    weights.start()
    source = lax.broadcasted_iota(jnp.int32, (taps, span), 0)
    target = lax.broadcasted_iota(jnp.int32, (taps, span), 1)
    flip = (source + target == taps).astype(jnp.bfloat16)
    first_group = pl.multiple_of(lax.axis_index("ctx") * groups, groups)
    first = jnp.dot(filter_ref[pl.ds(first_group, groups)], flip, preferred_element_type=jnp.float32)
    for group in range(groups):
        repeated = jnp.broadcast_to(first[group : group + 1], (taps, span))
        banded = pltpu.roll(repeated, 0, 1, stride=1, stride_axis=0)
        band_ref[group * taps : (group + 1) * taps] = banded.astype(jnp.bfloat16)
    weights.wait()


def values_kernel(at, *refs):
    count = 4
    given = refs[:count]
    band_ref, short_ref, gain_ref, out_ref, got_s, gate_s = refs[count:]
    own = out_ref.shape[1]
    rows = out_ref.shape[0] // count
    groups = band_ref.shape[0] // rows
    per_group = own // groups
    position = at[0]
    for step in range(count):
        got_s[position ^ step] = given[step][...]
    taps = [[short_ref[lag, stream : stream + 1].astype(jnp.float32) for lag in range(3)] for stream in range(3)]
    gate_s[0:rows] = jnp.zeros((rows, own), jnp.bfloat16)
    edge_row = lax.broadcasted_iota(jnp.int32, (8, own), 0)
    head_row = lax.broadcasted_iota(jnp.int32, (16, own), 0)
    for block in range(count):
        gate_s[(block + 1) * rows : (block + 2) * rows] = got_s[block, 0:rows]
        if block == 0:
            continue
        fixed = 1.0
        before = got_s[block - 1, rows : rows + 16].astype(jnp.float32)
        here = got_s[block, rows : rows + 16].astype(jnp.float32)
        for which, stream in enumerate((1, 2)):
            old = pltpu.roll(before[8 * which : 8 * which + 8], 6, 0)
            new = pltpu.roll(here[8 * which : 8 * which + 8], 2, 0)
            joined = jnp.where(edge_row < 2, old, new)
            fixed = fixed * (
                taps[stream][0] * pltpu.roll(joined, 6, 0)
                + taps[stream][1] * pltpu.roll(joined, 7, 0)
                + taps[stream][2] * joined
            )
        head = got_s[block, 0:16].astype(jnp.float32)
        head = jnp.where(head_row < 2, jnp.concatenate([fixed, fixed], axis=0), head)
        gate_s[(block + 1) * rows : (block + 1) * rows + 16] = head.astype(jnp.bfloat16)
    signal = jnp.concatenate([got_s[block, rows + 16 :] for block in range(count)], axis=0)
    feature = featured(signal.astype(jnp.float32), taps[0])
    gain = gain_ref[...]
    per_tile = HEAD_DIM // per_group
    lane = lax.broadcasted_iota(jnp.int32, (rows, HEAD_DIM), 1) // per_group
    for block in range(count):
        for tile in range(own // HEAD_DIM):
            columns = slice(tile * HEAD_DIM, (tile + 1) * HEAD_DIM)
            mixed = jnp.dot(
                band_ref[tile * per_tile * rows : (tile + 1) * per_tile * rows],
                gate_s[block * rows : (block + 2) * rows, columns],
                preferred_element_type=jnp.float32,
            )
            filtered = mixed[:rows]
            for group in range(1, per_tile):
                filtered = jnp.where(lane == group, mixed[group * rows : (group + 1) * rows], filtered)
            here = slice(block * rows, (block + 1) * rows)
            gate = gate_s[(block + 1) * rows : (block + 2) * rows, columns].astype(jnp.float32)
            out_ref[here, columns] = (
                feature[here, columns] * (filtered + gain[:, columns] * gate)
            ).astype(jnp.bfloat16)


def attend_kernel(*refs):
    count = 4
    given, value_ref = refs[:count], refs[count]
    out_refs = refs[count + 1 : 2 * count + 1]
    query_s, key_s, out_s = refs[2 * count + 1 :]
    rows, own = query_s.shape[1:]
    position = lax.axis_index("ctx")
    for step in range(count):
        query_s[position ^ step] = given[step][0:rows]
        key_s[pl.ds(pl.multiple_of((position ^ step) * rows, rows), rows)] = given[step][rows:]
    causal = lax.broadcasted_iota(jnp.int32, (rows, rows), 1) <= lax.broadcasted_iota(jnp.int32, (rows, rows), 0)
    for head in range(own // HEAD_DIM):
        columns = slice(head * HEAD_DIM, (head + 1) * HEAD_DIM)
        for block in range(count):
            scores = lax.dot_general(
                query_s[block, :, columns],
                key_s[0 : (block + 1) * rows, columns],
                (((1,), (1,)), ((), ())),
                preferred_element_type=jnp.float32,
            ) * HEAD_DIM ** (-0.5)
            own_scores = jnp.where(causal, scores[:, block * rows :], masked_score)
            pieces = [scores[:, : block * rows], own_scores] if block else [own_scores]
            scores = jnp.concatenate(pieces, axis=1)
            peak = jnp.max(scores, axis=1, keepdims=True)
            weights = jnp.exp(scores - peak)
            total = jnp.sum(weights, axis=1, keepdims=True)
            mixed = jnp.dot(
                weights.astype(jnp.bfloat16),
                value_ref[0 : (block + 1) * rows, columns],
                preferred_element_type=jnp.float32,
            )
            out_s[block, :, columns] = (mixed / total).astype(jnp.bfloat16)
    for step in range(count):
        out_refs[step][...] = out_s[position ^ step]


def project_kernel(masks, *refs):
    count = 4
    given, weight_ref = refs[:count], refs[count]
    out_refs, attended_s = refs[count + 1 : -1], refs[-1]
    own = given[0].shape[1]
    width = out_refs[0].shape[1]
    position, here = lax.axis_index("ctx"), lax.axis_index("mp")
    for step in range(count):
        attended_s[:, pl.ds(pl.multiple_of((position ^ step) * own, own), own)] = given[step][...]
    for mask, out_ref in zip(masks, out_refs):
        columns = pl.ds(pl.multiple_of((here ^ mask) * width, width), width)
        out_ref[...] = jnp.dot(
            attended_s[...], weight_ref[:, columns], preferred_element_type=jnp.float32
        ).astype(jnp.bfloat16)


VMEM_LIMIT = 40 * 1024 * 1024
WIDE_LIMIT = 60 * 1024 * 1024
IN_HBM = pl.BlockSpec(memory_space=pl.ANY)
IN_VMEM = pl.BlockSpec(memory_space=pltpu.VMEM)


def whole(array):
    shape = array.shape
    return pl.BlockSpec(shape, lambda *_: (0,) * len(shape))


def swapped(value, axis, step):
    return lax.ppermute(value, axis, [(source, source ^ step) for source in range(lax.axis_size(axis))])


def exchanged(pieces, axis):
    sent = {step: swapped(pieces[step], axis, step) for step in (3, 2, 1)}
    return [pieces[0]] + [sent[step] for step in (1, 2, 3)]


def by_heads(inputs, short_filter, long_filter, skip_gain, queries, key_rows, out_weight):
    count = lax.axis_size("ctx")
    position = lax.axis_index("ctx").reshape(1)
    rows, streams, channels = inputs.shape
    own = channels // count
    groups, taps = long_filter.shape
    own_groups = groups // count
    params = pltpu.CompilerParams(vmem_limit_bytes=VMEM_LIMIT)
    first = jax.ShapeDtypeStruct((2 * rows + 16, own), jnp.bfloat16)
    second = jax.ShapeDtypeStruct((2 * rows, own), jnp.bfloat16)
    piece = jax.ShapeDtypeStruct((rows, own), jnp.bfloat16)
    sent = pl.pallas_call(
        pack_kernel,
        out_shape=[first] * count + [second] * count,
        in_specs=[IN_HBM] * 4,
        out_specs=[IN_VMEM] * (2 * count),
        scratch_shapes=[
            pltpu.VMEM((streams, rows, channels), jnp.bfloat16),
            pltpu.VMEM(short_filter.shape, jnp.bfloat16),
            pltpu.VMEM(queries.shape, jnp.bfloat16),
            pltpu.VMEM(key_rows.shape, jnp.bfloat16),
            pltpu.SemaphoreType.DMA((6,)),
        ],
        compiler_params=pltpu.CompilerParams(vmem_limit_bytes=WIDE_LIMIT),
        name="pack",
    )(jnp.transpose(inputs, (1, 0, 2)), short_filter, queries, key_rows)
    first_got = exchanged(sent[:count], "ctx")
    second_got = exchanged(sent[count:], "ctx")
    band, weight = pl.pallas_call(
        ready_kernel,
        out_shape=[
            jax.ShapeDtypeStruct((own_groups * taps, 2 * taps), jnp.bfloat16),
            jax.ShapeDtypeStruct(out_weight.shape, jnp.bfloat16),
        ],
        in_specs=[IN_VMEM, IN_HBM],
        out_specs=[IN_VMEM] * 2,
        scratch_shapes=[pltpu.SemaphoreType.DMA],
        compiler_params=params,
        name="ready",
    )(long_filter, out_weight)
    values = pl.pallas_call(
        values_kernel,
        out_shape=jax.ShapeDtypeStruct((count * rows, own), jnp.bfloat16),
        grid_spec=pltpu.PrefetchScalarGridSpec(
            num_scalar_prefetch=1,
            grid=(1,),
            in_specs=[whole(first)] * count
            + [
                whole(band),
                pl.BlockSpec((3, streams, own), lambda _, at: (0, 0, at[0])),
                pl.BlockSpec((1, own), lambda _, at: (0, at[0])),
            ],
            out_specs=pl.BlockSpec((count * rows, own), lambda _, at: (0, 0)),
            scratch_shapes=[
                pltpu.VMEM((count, 2 * rows + 16, own), jnp.bfloat16),
                pltpu.VMEM(((count + 1) * rows, own), jnp.bfloat16),
            ],
        ),
        compiler_params=params,
        cost_estimate=pl.CostEstimate(flops=2 * count * rows * own * 8 * 2 * taps, bytes_accessed=2**21, transcendentals=0),
        name="values",
    )(position, *first_got, band, short_filter, skip_gain.reshape(1, channels))
    attended = pl.pallas_call(
        attend_kernel,
        out_shape=[piece] * count,
        in_specs=[IN_VMEM] * (count + 1),
        out_specs=[IN_VMEM] * count,
        scratch_shapes=[
            pltpu.VMEM((count, rows, own), jnp.bfloat16),
            pltpu.VMEM((count * rows, own), jnp.bfloat16),
            pltpu.VMEM((count, rows, own), jnp.bfloat16),
        ],
        compiler_params=params,
        name="attend",
    )(*second_got, values)
    return project_and_share(exchanged(attended, "ctx"), weight)


def projected(attended, out_weight, masks):
    rows = attended[0].shape[0]
    width = out_weight.shape[1] // lax.axis_size("mp")
    return pl.pallas_call(
        functools.partial(project_kernel, masks),
        out_shape=[jax.ShapeDtypeStruct((rows, width), jnp.bfloat16)] * len(masks),
        in_specs=[IN_VMEM] * (len(attended) + 1),
        out_specs=[IN_VMEM] * len(masks),
        scratch_shapes=[pltpu.VMEM((rows, out_weight.shape[0]), jnp.bfloat16)],
        compiler_params=pltpu.CompilerParams(vmem_limit_bytes=VMEM_LIMIT),
        cost_estimate=pl.CostEstimate(
            flops=2 * rows * out_weight.shape[0] * width * len(masks), bytes_accessed=2**22, transcendentals=0
        ),
        name="project",
    )(*attended, out_weight)


def added(*terms):
    total = terms[0].astype(jnp.float32)
    for term in terms[1:]:
        total = total + term.astype(jnp.float32)
    return total.astype(jnp.bfloat16)


def project_and_share(attended, out_weight):
    far_given, far_kept = projected(attended, out_weight, (3, 2))
    far_got = swapped(far_given, "mp", 1)
    near_given, near_kept = projected(attended, out_weight, (1, 0))
    far_sum = added(far_kept, far_got)
    near_got = swapped(near_given, "mp", 1)
    return added(near_kept, near_got, swapped(far_sum, "mp", 2))


def per_device(inputs, short_filter, long_filter, skip_gain, queries, key_rows, out_weight):
    rows, _, channels = inputs.shape
    count = lax.axis_size("ctx")
    taps = long_filter.shape[1]
    splits = channels % (count * HEAD_DIM) == 0 and count == 4 and rows == taps
    if splits and lax.axis_size("mp") == 4:
        return by_heads(inputs, short_filter, long_filter, skip_gain, queries, key_rows, out_weight)
    attended = by_rows(inputs, short_filter, long_filter, skip_gain, queries, key_rows)
    partial_out = jnp.dot(attended, out_weight, preferred_element_type=jnp.float32)
    return lax.psum_scatter(partial_out.astype(jnp.bfloat16), "mp", scatter_dimension=1, tiled=True)


def solution(mesh):
    placed = (
        P(("parts", "ctx"), None, "mp"),
        P(None, None, "mp"),
        P("mp", None),
        P("mp"),
        P(("parts", "ctx"), "mp"),
        P(("parts", "ctx"), "mp"),
        P("mp", None),
    )
    return jax.shard_map(
        per_device, mesh=mesh, in_specs=placed, out_specs=P(("parts", "ctx"), "mp"), check_vma=False
    )
```

```python
import functools

import jax
import jax.numpy as jnp
from jax import lax
from jax.experimental import pallas as pl
from jax.experimental.pallas import tpu as pltpu
from jax.sharding import PartitionSpec as P

HEAD_DIM = 128
COUNT = 4
EDGE = 16


masked_score = -1e30


def passed_along(value, axis, steps):
    count = lax.axis_size(axis)
    initial, last = (max(0, -steps), min(count, count - steps))
    return lax.ppermute(value, axis, [(source, source + steps) for source in range(initial, last)])


def toeplitz_taps(filters, row_count):
    group_count = filters.shape[0]
    tap_count = filters.shape[1]
    span = row_count + tap_count - 1
    flipped = filters[:, ::-1]
    padded_taps = jnp.concatenate(
        [flipped, jnp.zeros((group_count, row_count), filters.dtype)], axis=1
    )
    repeated = jnp.tile(padded_taps, (1, row_count))
    return repeated[:, : row_count * span].reshape(group_count, row_count, span)


def short_features(extended, short_filter, row_count):
    tap_count = short_filter.shape[0]
    features = jnp.zeros((row_count,) + extended.shape[1:], jnp.float32)
    for lag_index in range(tap_count):
        delayed = extended[
            tap_count - 1 - lag_index : tap_count - 1 - lag_index + row_count
        ].astype(jnp.float32)
        features = features + short_filter[lag_index].astype(jnp.float32)[None] * delayed
    return features


def attend(head_queries, query_pos, key_piece, value_piece):
    key_count = key_piece.shape[0]
    head_count = head_queries.shape[1]
    key_heads = key_piece.reshape(key_count, head_count, -1)
    value_heads = value_piece.reshape(key_count, head_count, -1)
    scores = jnp.einsum(
        "qhd,khd->hqk", head_queries, key_heads, preferred_element_type=jnp.float32
    ) * head_queries.shape[2] ** (-0.5)
    key_pos = lax.iota(jnp.int32, key_count)
    allowed = (key_pos[None, :] <= query_pos[:, None])[None]
    peak = jnp.max(jnp.where(allowed, scores, masked_score), axis=2)
    probabilities = jnp.where(allowed, jnp.exp(scores - peak[..., None]), 0.0)
    weight_sum = jnp.sum(probabilities, axis=2)
    mixed = jnp.einsum(
        "hqk,khd->hqd",
        probabilities.astype(jnp.bfloat16),
        value_heads,
        preferred_element_type=jnp.float32,
    )
    result = mixed / weight_sum[..., None]
    return jnp.transpose(result, (1, 0, 2)).reshape(result.shape[1], -1).astype(jnp.bfloat16)


def by_rows(inputs, short_filter, long_filter, skip_gain, queries, key_rows):
    row_count = inputs.shape[0]
    channels = inputs.shape[2]
    groups = long_filter.shape[0]
    tap_count = long_filter.shape[1]
    short_reach = short_filter.shape[0] - 1
    position = lax.axis_index("ctx")
    rim = passed_along(inputs[row_count - short_reach :], "ctx", 1)
    extended = jnp.concatenate([rim, inputs], axis=0)
    features = short_features(extended, short_filter, row_count)
    gate_product = (features[:, 1] * features[:, 2]).astype(jnp.bfloat16)
    gate_prev = passed_along(gate_product[row_count - (tap_count - 1) :], "ctx", 1)
    gate_ext = jnp.concatenate([gate_prev, gate_product], axis=0)
    toeplitz = toeplitz_taps(long_filter, row_count)
    filtered = jnp.einsum(
        "gtr,rgc->tgc",
        toeplitz,
        gate_ext.reshape(row_count + tap_count - 1, groups, channels // groups),
        preferred_element_type=jnp.float32,
    ).reshape(row_count, channels)
    values = (
        features[:, 0] * (filtered + skip_gain[None] * gate_product.astype(jnp.float32))
    ).astype(jnp.bfloat16)
    head_count = channels // HEAD_DIM
    head_queries = queries.reshape(row_count, head_count, HEAD_DIM)
    query_pos = position * row_count + lax.iota(jnp.int32, row_count)
    return attend(
        head_queries,
        query_pos,
        lax.all_gather(key_rows, "ctx", axis=0, tiled=True),
        lax.all_gather(values, "ctx", axis=0, tiled=True),
    )


def delayed(signal, lag):
    if lag == 0:
        return signal
    row = lax.broadcasted_iota(jnp.int32, signal.shape, 0)
    return jnp.where(row < lag, 0.0, pltpu.roll(signal, lag, 0))


def featured(signal, taps):
    total = taps[0] * signal
    for lag in range(1, len(taps)):
        total = total + taps[lag] * delayed(signal, lag)
    return total


def columns_of(block, width):
    return pl.ds(pl.multiple_of(block * width, width), width)


def write_gate(signals, taps, out_ref):
    rows, own = signals[0].shape
    edge_row = lax.broadcasted_iota(jnp.int32, (8, own), 0)
    features = [featured(signal, tap) for signal, tap in zip(signals, taps)]
    edges = [
        jnp.where(edge_row < 2, signal[:8], jnp.where(edge_row < 4, pltpu.roll(signal[rows - 8 :], 4, 0), 0.0))
        for signal in signals
    ]
    out_ref[0:rows] = (features[0] * features[1]).astype(jnp.bfloat16)
    out_ref[rows : rows + EDGE] = jnp.concatenate(edges, axis=0).astype(jnp.bfloat16)


def far_heads_kernel(queries_any, keys_any, *refs):
    out_refs, sems = refs[:-1], refs[-1]
    rows, own = queries_any.shape[0], out_refs[0].shape[1]
    position = lax.axis_index("ctx")
    copies = []
    for step, out_ref in zip((3, 2), out_refs):
        columns = columns_of(position ^ step, own)
        for index, source in enumerate((queries_any, keys_any)):
            target = out_ref.at[index * rows : (index + 1) * rows]
            copies.append(pltpu.make_async_copy(source.at[:, columns], target, sems.at[len(copies)]))
    for copy in copies:
        copy.start()
    for copy in copies:
        copy.wait()


def far_gate_kernel(inputs_any, short_any, _, *refs):
    out_refs, (signal_s, short_s, sems) = refs[:2], refs[2:]
    rows, own = inputs_any.shape[1], out_refs[0].shape[1]
    position = lax.axis_index("ctx")
    pair = (position ^ 2) // 2
    copies = [
        pltpu.make_async_copy(inputs_any.at[1:3, :, columns_of(pair, 2 * own)], signal_s, sems.at[0]),
        pltpu.make_async_copy(short_any.at[:, :, columns_of(pair, 2 * own)], short_s, sems.at[1]),
    ]
    for step, out_ref in zip((3, 2), out_refs):
        target = out_ref.at[rows + EDGE :]
        source = inputs_any.at[0, :, columns_of(position ^ step, own)]
        copies.append(pltpu.make_async_copy(source, target, sems.at[step]))
    for copy in copies:
        copy.start()
    for copy in copies[:2]:
        copy.wait()
    for step, out_ref in zip((3, 2), out_refs):
        columns = columns_of((position ^ step) % 2, own)
        signals = [signal_s[stream, :, columns].astype(jnp.float32) for stream in range(2)]
        taps = [
            [short_s[lag, stream : stream + 1, columns].astype(jnp.float32) for lag in range(3)] for stream in (1, 2)
        ]
        write_gate(signals, taps, out_ref)
    for copy in copies[2:]:
        copy.wait()


def near_kernel(inputs_any, short_any, queries_any, keys_any, _, *refs):
    (all_ref, gate_ref, heads_ref), (signal_s, short_s, sems) = refs[:3], refs[3:]
    rows, own = inputs_any.shape[1], all_ref.shape[1]
    position = lax.axis_index("ctx")
    pair = position // 2
    edged = rows + EDGE
    mine, other = columns_of(position, own), columns_of(position ^ 1, own)
    moves = (
        (inputs_any.at[1:3, :, columns_of(pair, 2 * own)], signal_s),
        (short_any.at[:, :, columns_of(pair, 2 * own)], short_s),
        (inputs_any.at[0, :, other], all_ref.at[edged : edged + rows]),
        (queries_any.at[:, other], all_ref.at[edged + rows : edged + 2 * rows]),
        (keys_any.at[:, other], all_ref.at[edged + 2 * rows :]),
        (inputs_any.at[0, :, mine], gate_ref.at[edged:]),
        (queries_any.at[:, mine], heads_ref.at[0:rows]),
        (keys_any.at[:, mine], heads_ref.at[rows:]),
    )
    copies = [pltpu.make_async_copy(*move, sems.at[index]) for index, move in enumerate(moves)]
    for copy in copies:
        copy.start()
    for copy in copies[:2]:
        copy.wait()
    for step, out_ref in ((1, all_ref), (0, gate_ref)):
        columns = columns_of((position ^ step) % 2, own)
        signals = [signal_s[stream, :, columns].astype(jnp.float32) for stream in range(2)]
        taps = [
            [short_s[lag, stream : stream + 1, columns].astype(jnp.float32) for lag in range(3)] for stream in (1, 2)
        ]
        write_gate(signals, taps, out_ref)
    for copy in copies[2:]:
        copy.wait()


def ready_kernel(filter_ref, weight_any, band_ref, weight_ref, sem):
    rows, span = band_ref.shape
    taps = filter_ref.shape[1]
    groups = rows // taps
    weights = pltpu.make_async_copy(weight_any, weight_ref, sem)
    weights.start()
    source = lax.broadcasted_iota(jnp.int32, (taps, span), 0)
    target = lax.broadcasted_iota(jnp.int32, (taps, span), 1)
    flip = (source + target == taps).astype(jnp.bfloat16)
    first_group = pl.multiple_of(lax.axis_index("ctx") * groups, groups)
    first = jnp.dot(filter_ref[pl.ds(first_group, groups)], flip, preferred_element_type=jnp.float32)
    for group in range(groups):
        repeated = jnp.broadcast_to(first[group : group + 1], (taps, span))
        banded = pltpu.roll(repeated, 0, 1, stride=1, stride_axis=0)
        band_ref[group * taps : (group + 1) * taps] = banded.astype(jnp.bfloat16)
    weights.wait()


def weights_kernel(own_ref, near_ref, second_ref, third_ref, weight_ref, total_ref, query_s, key_s):
    count = COUNT
    rows, own = own_ref.shape[0] // 2, own_ref.shape[1]
    position = lax.axis_index("ctx")
    skip = near_ref.shape[0] - 2 * rows
    for step, (given, start) in enumerate(((own_ref, 0), (near_ref, skip), (second_ref, 0), (third_ref, 0))):
        query_s[position ^ step] = given[start : start + rows]
        key_s[columns_of(position ^ step, rows)] = given[start + rows : start + 2 * rows]
    causal = lax.broadcasted_iota(jnp.int32, (rows, rows), 1) <= lax.broadcasted_iota(jnp.int32, (rows, rows), 0)
    for head in range(own // HEAD_DIM):
        columns = slice(head * HEAD_DIM, (head + 1) * HEAD_DIM)
        for block in range(count):
            here, seen = slice(block * rows, (block + 1) * rows), (block + 1) * rows
            scores = lax.dot_general(
                query_s[block, :, columns],
                key_s[0:seen, columns],
                (((1,), (1,)), ((), ())),
                preferred_element_type=jnp.float32,
            ) * HEAD_DIM ** (-0.5)
            own_scores = jnp.where(causal, scores[:, block * rows :], masked_score)
            pieces = [scores[:, : block * rows], own_scores] if block else [own_scores]
            scores = jnp.concatenate(pieces, axis=1)
            weights = jnp.exp(scores - jnp.max(scores, axis=1, keepdims=True))
            total_ref[here, head : head + 1] = jnp.sum(weights, axis=1, keepdims=True)
            weight_ref[head, here, 0:seen] = weights.astype(jnp.bfloat16)
            if seen < count * rows:
                weight_ref[head, here, seen:] = jnp.zeros((rows, count * rows - seen), jnp.bfloat16)


def mix_rows(block, weight_ref, total_ref, value_ref, out_ref):
    rows = out_ref.shape[0]
    here = columns_of(block, rows)
    for head in range(out_ref.shape[1] // HEAD_DIM):
        columns = slice(head * HEAD_DIM, (head + 1) * HEAD_DIM)
        mixed = jnp.dot(weight_ref[head, here], value_ref[:, columns], preferred_element_type=jnp.float32)
        out_ref[:, columns] = (mixed / total_ref[here, head : head + 1]).astype(jnp.bfloat16)


def values_kernel(*refs):
    count = COUNT
    given = refs[:count]
    band_ref, short_ref, gain_ref, weight_ref, total_ref = refs[count : count + 5]
    third_ref, second_ref, value_ref = refs[count + 5 : count + 8]
    got_s, gate_s = refs[count + 8 :]
    rows, own = second_ref.shape
    edged = rows + EDGE
    per_group = own * rows // band_ref.shape[0]
    position = lax.axis_index("ctx")
    mine = columns_of(position, own)
    for step in range(count):
        got_s[position ^ step] = given[step][0 : edged + rows]
    taps = [
        [short_ref[lag, stream : stream + 1, mine].astype(jnp.float32) for lag in range(3)] for stream in range(3)
    ]
    gate_s[0:rows] = jnp.zeros((rows, own), jnp.bfloat16)
    edge_row = lax.broadcasted_iota(jnp.int32, (8, own), 0)
    head_row = lax.broadcasted_iota(jnp.int32, (16, own), 0)
    for block in range(count):
        gate_s[(block + 1) * rows : (block + 2) * rows] = got_s[block, 0:rows]
        if block == 0:
            continue
        fixed = 1.0
        before = got_s[block - 1, rows:edged].astype(jnp.float32)
        here = got_s[block, rows:edged].astype(jnp.float32)
        for which, stream in enumerate((1, 2)):
            old = pltpu.roll(before[8 * which : 8 * which + 8], 6, 0)
            new = pltpu.roll(here[8 * which : 8 * which + 8], 2, 0)
            joined = jnp.where(edge_row < 2, old, new)
            fixed = fixed * (
                taps[stream][0] * pltpu.roll(joined, 6, 0)
                + taps[stream][1] * pltpu.roll(joined, 7, 0)
                + taps[stream][2] * joined
            )
        head = got_s[block, 0:16].astype(jnp.float32)
        head = jnp.where(head_row < 2, jnp.concatenate([fixed, fixed], axis=0), head)
        gate_s[(block + 1) * rows : (block + 1) * rows + 16] = head.astype(jnp.bfloat16)
    signal = jnp.concatenate([got_s[block, edged:] for block in range(count)], axis=0)
    feature = featured(signal.astype(jnp.float32), taps[0])
    gain = gain_ref[:, mine]
    per_tile = HEAD_DIM // per_group
    lane = lax.broadcasted_iota(jnp.int32, (rows, 2 * HEAD_DIM), 1) % HEAD_DIM // per_group
    for tile in range(own // HEAD_DIM):
        columns = slice(tile * HEAD_DIM, (tile + 1) * HEAD_DIM)
        for block in range(0, count, 2):
            windows = [gate_s[other * rows : (other + 2) * rows, columns] for other in (block, block + 1)]
            mixed = jnp.dot(
                band_ref[tile * per_tile * rows : (tile + 1) * per_tile * rows],
                jnp.concatenate(windows, axis=1),
                preferred_element_type=jnp.float32,
            )
            filtered = mixed[:rows]
            for group in range(1, per_tile):
                filtered = jnp.where(lane == group, mixed[group * rows : (group + 1) * rows], filtered)
            for index in range(2):
                here = slice((block + index) * rows, (block + index + 1) * rows)
                gate = gate_s[(block + index + 1) * rows : (block + index + 2) * rows, columns].astype(jnp.float32)
                part = filtered[:, index * HEAD_DIM : (index + 1) * HEAD_DIM]
                value_ref[here, columns] = (
                    feature[here, columns] * (part + gain[:, columns] * gate)
                ).astype(jnp.bfloat16)
    for step, out_ref in ((3, third_ref), (2, second_ref)):
        mix_rows(position ^ step, weight_ref, total_ref, value_ref, out_ref)


def near_rows_kernel(weight_ref, total_ref, value_ref, near_ref, own_ref):
    position = lax.axis_index("ctx")
    for step, out_ref in ((1, near_ref), (0, own_ref)):
        mix_rows(position ^ step, weight_ref, total_ref, value_ref, out_ref)


def project_kernel(masks, *refs):
    count = COUNT
    given, weight_ref = refs[:count], refs[count]
    out_refs, attended_s = refs[count + 1 : -1], refs[-1]
    own = given[0].shape[1]
    width = out_refs[0].shape[1]
    position, here = lax.axis_index("ctx"), lax.axis_index("mp")
    for step in range(count):
        attended_s[:, pl.ds(pl.multiple_of((position ^ step) * own, own), own)] = given[step][...]
    for mask, out_ref in zip(masks, out_refs):
        columns = pl.ds(pl.multiple_of((here ^ mask) * width, width), width)
        out_ref[...] = jnp.dot(
            attended_s[...], weight_ref[:, columns], preferred_element_type=jnp.float32
        ).astype(jnp.bfloat16)


VMEM_LIMIT = 40 * 1024 * 1024
WIDE_LIMIT = 60 * 1024 * 1024
IN_HBM = pl.BlockSpec(memory_space=pltpu.HBM)
IN_VMEM = pl.BlockSpec(memory_space=pltpu.VMEM)


def run_kernel(kernel, operands, outputs, scratch=(), spaces=None, limit=VMEM_LIMIT, cost=10**6):
    return pl.pallas_call(
        kernel,
        out_shape=[jax.ShapeDtypeStruct(shape, dtype) for shape, dtype in outputs],
        in_specs=spaces or [IN_VMEM] * len(operands),
        out_specs=[IN_VMEM] * len(outputs),
        scratch_shapes=scratch,
        compiler_params=pltpu.CompilerParams(vmem_limit_bytes=limit),
        cost_estimate=pl.CostEstimate(flops=cost, bytes_accessed=2**20, transcendentals=0),
        name=getattr(kernel, "func", kernel).__name__,
    )(*operands)


def swapped(value, axis, step):
    return lax.ppermute(value, axis, [(source, source ^ step) for source in range(lax.axis_size(axis))])


def by_heads(inputs, short_filter, long_filter, skip_gain, queries, key_rows, out_weight):
    rows, streams, channels = inputs.shape
    own = channels // COUNT
    groups, taps = long_filter.shape
    half = jnp.bfloat16
    gate_shape, heads_shape = ((2 * rows + EDGE, own), half), ((2 * rows, own), half)
    piece, window = ((rows, own), half), COUNT * rows
    streamed = jnp.transpose(inputs, (1, 0, 2))
    staging = [
        pltpu.VMEM((2, rows, 2 * own), half),
        pltpu.VMEM((3, streams, 2 * own), half),
    ]
    heads = run_kernel(
        far_heads_kernel,
        (queries, key_rows),
        [heads_shape] * 2,
        [pltpu.SemaphoreType.DMA((4,))],
        [IN_HBM] * 2,
        WIDE_LIMIT,
    )
    heads_third, heads_second = swapped(heads[0], "ctx", 3), swapped(heads[1], "ctx", 2)
    gates = run_kernel(
        far_gate_kernel,
        (streamed, short_filter, heads[0]),
        [gate_shape] * 2,
        staging + [pltpu.SemaphoreType.DMA((4,))],
        [IN_HBM] * 3,
        WIDE_LIMIT,
    )
    gate_third, gate_second = swapped(gates[0], "ctx", 3), swapped(gates[1], "ctx", 2)
    near_all, own_gate, own_heads = run_kernel(
        near_kernel,
        (streamed, short_filter, queries, key_rows, gates[0]),
        [((4 * rows + EDGE, own), half), gate_shape, heads_shape],
        staging + [pltpu.SemaphoreType.DMA((8,))],
        [IN_HBM] * 5,
        WIDE_LIMIT,
    )
    near_got = swapped(near_all, "ctx", 1)
    band, weight = run_kernel(
        ready_kernel,
        (long_filter, out_weight),
        [((groups // COUNT * taps, 2 * taps), half), (out_weight.shape, half)],
        [pltpu.SemaphoreType.DMA],
        [IN_VMEM, IN_HBM],
    )
    soft, totals = run_kernel(
        weights_kernel,
        (own_heads, near_got, heads_second, heads_third),
        [((own // HEAD_DIM, window, window), half), ((window, HEAD_DIM), jnp.float32)],
        [pltpu.VMEM((COUNT, rows, own), half), pltpu.VMEM((window, own), half)],
    )
    third, second, values = run_kernel(
        values_kernel,
        (own_gate, near_got, gate_second, gate_third, band, short_filter, skip_gain.reshape(1, channels), soft, totals),
        [piece, piece, ((window, own), half)],
        [pltpu.VMEM((COUNT,) + gate_shape[0], half), pltpu.VMEM((window + rows, own), half)],
    )
    third_got, second_got = swapped(third, "ctx", 3), swapped(second, "ctx", 2)
    near, mine = run_kernel(near_rows_kernel, (soft, totals, values), [piece] * 2)
    attended = [mine, swapped(near, "ctx", 1), second_got, third_got]
    return project_and_share(attended, weight)


def projected(attended, out_weight, masks):
    rows = attended[0].shape[0]
    width = out_weight.shape[1] // lax.axis_size("mp")
    return run_kernel(
        functools.partial(project_kernel, masks),
        (*attended, out_weight),
        [((rows, width), jnp.bfloat16)] * len(masks),
        [pltpu.VMEM((rows, out_weight.shape[0]), jnp.bfloat16)],
        cost=2 * rows * out_weight.shape[0] * width * len(masks),
    )


def added(*terms):
    total = terms[0].astype(jnp.float32)
    for term in terms[1:]:
        total = total + term.astype(jnp.float32)
    return total.astype(jnp.bfloat16)


def project_and_share(attended, out_weight):
    far_given, far_kept = projected(attended, out_weight, (3, 2))
    far_got = swapped(far_given, "mp", 1)
    near_given, near_kept = projected(attended, out_weight, (1, 0))
    far_sum = added(far_kept, far_got)
    near_got = swapped(near_given, "mp", 1)
    return added(near_kept, near_got, swapped(far_sum, "mp", 2))


def per_device(inputs, short_filter, long_filter, skip_gain, queries, key_rows, out_weight):
    rows, _, channels = inputs.shape
    count = lax.axis_size("ctx")
    taps = long_filter.shape[1]
    splits = channels % (count * HEAD_DIM) == 0 and count == COUNT and rows == taps
    if splits and lax.axis_size("mp") == 4:
        return by_heads(inputs, short_filter, long_filter, skip_gain, queries, key_rows, out_weight)
    attended = by_rows(inputs, short_filter, long_filter, skip_gain, queries, key_rows)
    partial_out = jnp.dot(attended, out_weight, preferred_element_type=jnp.float32)
    return lax.psum_scatter(partial_out.astype(jnp.bfloat16), "mp", scatter_dimension=1, tiled=True)


def solution(mesh):
    placed = (
        P(("parts", "ctx"), None, "mp"),
        P(None, None, "mp"),
        P("mp", None),
        P("mp"),
        P(("parts", "ctx"), "mp"),
        P(("parts", "ctx"), "mp"),
        P("mp", None),
    )
    return jax.shard_map(
        per_device, mesh=mesh, in_specs=placed, out_specs=P(("parts", "ctx"), "mp"), check_vma=False
    )
```

```python
import functools

import jax
import jax.numpy as jnp
from jax import lax
from jax.experimental import pallas as pl
from jax.experimental.pallas import tpu as pltpu
from jax.sharding import PartitionSpec as P

HEAD_DIM = 128
COUNT = 4
ORDER = (3, 2, 1, 0)
EDGE = 16


masked_score = -1e30


def passed_along(value, axis, steps):
    count = lax.axis_size(axis)
    initial, last = (max(0, -steps), min(count, count - steps))
    return lax.ppermute(value, axis, [(source, source + steps) for source in range(initial, last)])


def toeplitz_taps(filters, row_count):
    group_count = filters.shape[0]
    tap_count = filters.shape[1]
    span = row_count + tap_count - 1
    flipped = filters[:, ::-1]
    padded_taps = jnp.concatenate(
        [flipped, jnp.zeros((group_count, row_count), filters.dtype)], axis=1
    )
    repeated = jnp.tile(padded_taps, (1, row_count))
    return repeated[:, : row_count * span].reshape(group_count, row_count, span)


def short_features(extended, short_filter, row_count):
    tap_count = short_filter.shape[0]
    features = jnp.zeros((row_count,) + extended.shape[1:], jnp.float32)
    for lag_index in range(tap_count):
        delayed = extended[
            tap_count - 1 - lag_index : tap_count - 1 - lag_index + row_count
        ].astype(jnp.float32)
        features = features + short_filter[lag_index].astype(jnp.float32)[None] * delayed
    return features


def attend(head_queries, query_pos, key_piece, value_piece):
    key_count = key_piece.shape[0]
    head_count = head_queries.shape[1]
    key_heads = key_piece.reshape(key_count, head_count, -1)
    value_heads = value_piece.reshape(key_count, head_count, -1)
    scores = jnp.einsum(
        "qhd,khd->hqk", head_queries, key_heads, preferred_element_type=jnp.float32
    ) * head_queries.shape[2] ** (-0.5)
    key_pos = lax.iota(jnp.int32, key_count)
    allowed = (key_pos[None, :] <= query_pos[:, None])[None]
    peak = jnp.max(jnp.where(allowed, scores, masked_score), axis=2)
    probabilities = jnp.where(allowed, jnp.exp(scores - peak[..., None]), 0.0)
    weight_sum = jnp.sum(probabilities, axis=2)
    mixed = jnp.einsum(
        "hqk,khd->hqd",
        probabilities.astype(jnp.bfloat16),
        value_heads,
        preferred_element_type=jnp.float32,
    )
    result = mixed / weight_sum[..., None]
    return jnp.transpose(result, (1, 0, 2)).reshape(result.shape[1], -1).astype(jnp.bfloat16)


def by_rows(inputs, short_filter, long_filter, skip_gain, queries, key_rows):
    row_count = inputs.shape[0]
    channels = inputs.shape[2]
    groups = long_filter.shape[0]
    tap_count = long_filter.shape[1]
    short_reach = short_filter.shape[0] - 1
    position = lax.axis_index("ctx")
    rim = passed_along(inputs[row_count - short_reach :], "ctx", 1)
    extended = jnp.concatenate([rim, inputs], axis=0)
    features = short_features(extended, short_filter, row_count)
    gate_product = (features[:, 1] * features[:, 2]).astype(jnp.bfloat16)
    gate_prev = passed_along(gate_product[row_count - (tap_count - 1) :], "ctx", 1)
    gate_ext = jnp.concatenate([gate_prev, gate_product], axis=0)
    toeplitz = toeplitz_taps(long_filter, row_count)
    filtered = jnp.einsum(
        "gtr,rgc->tgc",
        toeplitz,
        gate_ext.reshape(row_count + tap_count - 1, groups, channels // groups),
        preferred_element_type=jnp.float32,
    ).reshape(row_count, channels)
    values = (
        features[:, 0] * (filtered + skip_gain[None] * gate_product.astype(jnp.float32))
    ).astype(jnp.bfloat16)
    head_count = channels // HEAD_DIM
    head_queries = queries.reshape(row_count, head_count, HEAD_DIM)
    query_pos = position * row_count + lax.iota(jnp.int32, row_count)
    return attend(
        head_queries,
        query_pos,
        lax.all_gather(key_rows, "ctx", axis=0, tiled=True),
        lax.all_gather(values, "ctx", axis=0, tiled=True),
    )


def delayed(signal, lag):
    if lag == 0:
        return signal
    row = lax.broadcasted_iota(jnp.int32, signal.shape, 0)
    return jnp.where(row < lag, 0.0, pltpu.roll(signal, lag, 0))


def featured(signal, taps):
    total = taps[0] * signal
    for lag in range(1, len(taps)):
        total = total + taps[lag] * delayed(signal, lag)
    return total


def columns_of(block, width):
    return pl.ds(pl.multiple_of(block * width, width), width)


def write_gate(signals, taps, out_ref):
    rows, own = signals[0].shape
    edge_row = lax.broadcasted_iota(jnp.int32, (8, own), 0)
    features = [featured(signal, tap) for signal, tap in zip(signals, taps)]
    edges = [
        jnp.where(edge_row < 2, signal[:8], jnp.where(edge_row < 4, pltpu.roll(signal[rows - 8 :], 4, 0), 0.0))
        for signal in signals
    ]
    out_ref[0:rows] = (features[0] * features[1]).astype(jnp.bfloat16)
    out_ref[rows : rows + EDGE] = jnp.concatenate(edges, axis=0).astype(jnp.bfloat16)


def pack_kernel(inputs_any, short_any, queries_any, keys_any, *refs):
    plain_refs, gate_refs = refs[:COUNT], refs[COUNT : 2 * COUNT]
    signal_s, short_s, sems = refs[2 * COUNT :]
    rows, own = inputs_any.shape[1], plain_refs[0].shape[1]
    position = lax.axis_index("ctx")
    loads = [
        pltpu.make_async_copy(short_any, short_s, sems.at[0]),
        pltpu.make_async_copy(inputs_any.at[1:3], signal_s, sems.at[1]),
    ]
    for step in ORDER:
        columns = columns_of(position ^ step, own)
        for index, source in enumerate((queries_any, keys_any, inputs_any.at[0])):
            target = plain_refs[step].at[index * rows : (index + 1) * rows]
            loads.append(pltpu.make_async_copy(source.at[:, columns], target, sems.at[len(loads)]))
    for load in loads:
        load.start()
    for load in loads[:2]:
        load.wait()
    for step in ORDER:
        columns = columns_of(position ^ step, own)
        signals = [signal_s[stream, :, columns].astype(jnp.float32) for stream in range(2)]
        taps = [
            [short_s[lag, stream : stream + 1, columns].astype(jnp.float32) for lag in range(3)] for stream in (1, 2)
        ]
        write_gate(signals, taps, gate_refs[step])
    for load in loads[2:]:
        load.wait()


def ready_kernel(filter_ref, weight_any, band_ref, weight_ref, sem):
    rows, span = band_ref.shape
    taps = filter_ref.shape[1]
    groups = rows // taps
    weights = pltpu.make_async_copy(weight_any, weight_ref, sem)
    weights.start()
    source = lax.broadcasted_iota(jnp.int32, (taps, span), 0)
    target = lax.broadcasted_iota(jnp.int32, (taps, span), 1)
    flip = (source + target == taps).astype(jnp.bfloat16)
    first_group = pl.multiple_of(lax.axis_index("ctx") * groups, groups)
    first = jnp.dot(filter_ref[pl.ds(first_group, groups)], flip, preferred_element_type=jnp.float32)
    for group in range(groups):
        repeated = jnp.broadcast_to(first[group : group + 1], (taps, span))
        banded = pltpu.roll(repeated, 0, 1, stride=1, stride_axis=0)
        band_ref[group * taps : (group + 1) * taps] = banded.astype(jnp.bfloat16)
    weights.wait()


def weights_kernel(third_ref, second_ref, near_ref, own_ref, weight_ref, total_ref, query_s, key_s):
    count = COUNT
    rows, own = query_s.shape[1:]
    position = lax.axis_index("ctx")
    for step, given in zip(ORDER, (third_ref, second_ref, near_ref, own_ref)):
        query_s[position ^ step] = given[0:rows]
        key_s[columns_of(position ^ step, rows)] = given[rows : 2 * rows]
    causal = lax.broadcasted_iota(jnp.int32, (rows, rows), 1) <= lax.broadcasted_iota(jnp.int32, (rows, rows), 0)
    for head in range(own // HEAD_DIM):
        columns = slice(head * HEAD_DIM, (head + 1) * HEAD_DIM)
        for block in range(count):
            here, seen = slice(block * rows, (block + 1) * rows), (block + 1) * rows
            scores = lax.dot_general(
                query_s[block, :, columns],
                key_s[0:seen, columns],
                (((1,), (1,)), ((), ())),
                preferred_element_type=jnp.float32,
            ) * HEAD_DIM ** (-0.5)
            own_scores = jnp.where(causal, scores[:, block * rows :], masked_score)
            pieces = [scores[:, : block * rows], own_scores] if block else [own_scores]
            scores = jnp.concatenate(pieces, axis=1)
            weights = jnp.exp(scores - jnp.max(scores, axis=1, keepdims=True))
            total_ref[here, head : head + 1] = jnp.sum(weights, axis=1, keepdims=True)
            weight_ref[head, here, 0:seen] = weights.astype(jnp.bfloat16)
            if seen < count * rows:
                weight_ref[head, here, seen:] = jnp.zeros((rows, count * rows - seen), jnp.bfloat16)


def mix_rows(block, weight_ref, total_ref, value_ref, out_ref):
    rows = out_ref.shape[0]
    here = columns_of(block, rows)
    for head in range(out_ref.shape[1] // HEAD_DIM):
        columns = slice(head * HEAD_DIM, (head + 1) * HEAD_DIM)
        mixed = jnp.dot(weight_ref[head, here], value_ref[:, columns], preferred_element_type=jnp.float32)
        out_ref[:, columns] = (mixed / total_ref[here, head : head + 1]).astype(jnp.bfloat16)


def values_kernel(*refs):
    count = COUNT
    plain, gates = refs[:count], refs[count : 2 * count]
    band_ref, short_ref, gain_ref, weight_ref, total_ref = refs[2 * count : 2 * count + 5]
    third_ref, second_ref, value_ref = refs[2 * count + 5 : 2 * count + 8]
    signal_s, gates_s, gate_s = refs[2 * count + 8 :]
    rows, own = second_ref.shape
    per_group = own * rows // band_ref.shape[0]
    position = lax.axis_index("ctx")
    mine = columns_of(position, own)
    for step, given, gate in zip(ORDER, plain, gates):
        signal_s[columns_of(position ^ step, rows)] = given[2 * rows :]
        gates_s[position ^ step] = gate[...]
    taps = [
        [short_ref[lag, stream : stream + 1, mine].astype(jnp.float32) for lag in range(3)] for stream in range(3)
    ]
    gate_s[0:rows] = jnp.zeros((rows, own), jnp.bfloat16)
    edge_row = lax.broadcasted_iota(jnp.int32, (8, own), 0)
    head_row = lax.broadcasted_iota(jnp.int32, (16, own), 0)
    for block in range(count):
        gate_s[(block + 1) * rows : (block + 2) * rows] = gates_s[block, 0:rows]
        if block == 0:
            continue
        fixed = 1.0
        before = gates_s[block - 1, rows:].astype(jnp.float32)
        here = gates_s[block, rows:].astype(jnp.float32)
        for which, stream in enumerate((1, 2)):
            old = pltpu.roll(before[8 * which : 8 * which + 8], 6, 0)
            new = pltpu.roll(here[8 * which : 8 * which + 8], 2, 0)
            joined = jnp.where(edge_row < 2, old, new)
            fixed = fixed * (
                taps[stream][0] * pltpu.roll(joined, 6, 0)
                + taps[stream][1] * pltpu.roll(joined, 7, 0)
                + taps[stream][2] * joined
            )
        head = gates_s[block, 0:16].astype(jnp.float32)
        head = jnp.where(head_row < 2, jnp.concatenate([fixed, fixed], axis=0), head)
        gate_s[(block + 1) * rows : (block + 1) * rows + 16] = head.astype(jnp.bfloat16)
    feature = featured(signal_s[...].astype(jnp.float32), taps[0])
    gain = gain_ref[:, mine]
    per_tile = HEAD_DIM // per_group
    lane = lax.broadcasted_iota(jnp.int32, (rows, 2 * HEAD_DIM), 1) % HEAD_DIM // per_group
    for tile in range(own // HEAD_DIM):
        columns = slice(tile * HEAD_DIM, (tile + 1) * HEAD_DIM)
        for block in range(0, count, 2):
            windows = [gate_s[other * rows : (other + 2) * rows, columns] for other in (block, block + 1)]
            mixed = jnp.dot(
                band_ref[tile * per_tile * rows : (tile + 1) * per_tile * rows],
                jnp.concatenate(windows, axis=1),
                preferred_element_type=jnp.float32,
            )
            filtered = mixed[:rows]
            for group in range(1, per_tile):
                filtered = jnp.where(lane == group, mixed[group * rows : (group + 1) * rows], filtered)
            for index in range(2):
                here = slice((block + index) * rows, (block + index + 1) * rows)
                gate = gate_s[(block + index + 1) * rows : (block + index + 2) * rows, columns].astype(jnp.float32)
                part = filtered[:, index * HEAD_DIM : (index + 1) * HEAD_DIM]
                value_ref[here, columns] = (
                    feature[here, columns] * (part + gain[:, columns] * gate)
                ).astype(jnp.bfloat16)
    for step, out_ref in ((3, third_ref), (2, second_ref)):
        mix_rows(position ^ step, weight_ref, total_ref, value_ref, out_ref)


def near_rows_kernel(weight_ref, total_ref, value_ref, *refs):
    upper_ref, lower_ref, own_ref, near_s = refs
    half = upper_ref.shape[0]
    position = lax.axis_index("ctx")
    mix_rows(position ^ 1, weight_ref, total_ref, value_ref, near_s)
    upper_ref[...] = near_s[0:half]
    lower_ref[...] = near_s[half:]
    mix_rows(position, weight_ref, total_ref, value_ref, own_ref)


def project_kernel(masks, *refs):
    given, weight_ref = refs[:5], refs[5]
    out_refs, attended_s = refs[6:-1], refs[-1]
    own = given[0].shape[1]
    width = out_refs[0].shape[1]
    position, here = lax.axis_index("ctx"), lax.axis_index("mp")
    third, second, upper, lower, mine = given
    half = upper.shape[0]
    attended_s[0:half, columns_of(position ^ 1, own)] = upper[...]
    attended_s[half:, columns_of(position ^ 1, own)] = lower[...]
    for step, piece in ((0, mine), (2, second), (3, third)):
        attended_s[:, columns_of(position ^ step, own)] = piece[...]
    for mask, out_ref in zip(masks, out_refs):
        columns = pl.ds(pl.multiple_of((here ^ mask) * width, width), width)
        out_ref[...] = jnp.dot(
            attended_s[...], weight_ref[:, columns], preferred_element_type=jnp.float32
        ).astype(jnp.bfloat16)


VMEM_LIMIT = 40 * 1024 * 1024
WIDE_LIMIT = 60 * 1024 * 1024
IN_HBM = pl.BlockSpec(memory_space=pltpu.HBM)
IN_VMEM = pl.BlockSpec(memory_space=pltpu.VMEM)


def run_kernel(kernel, operands, outputs, scratch=(), spaces=None, limit=VMEM_LIMIT, cost=10**6):
    return pl.pallas_call(
        kernel,
        out_shape=[jax.ShapeDtypeStruct(shape, dtype) for shape, dtype in outputs],
        in_specs=spaces or [IN_VMEM] * len(operands),
        out_specs=[IN_VMEM] * len(outputs),
        scratch_shapes=scratch,
        compiler_params=pltpu.CompilerParams(vmem_limit_bytes=limit),
        cost_estimate=pl.CostEstimate(flops=cost, bytes_accessed=2**20, transcendentals=0),
        name=getattr(kernel, "func", kernel).__name__,
    )(*operands)


def swapped(value, axis, step):
    return lax.ppermute(value, axis, [(source, source ^ step) for source in range(lax.axis_size(axis))])


def by_heads(inputs, short_filter, long_filter, skip_gain, queries, key_rows, out_weight):
    rows, streams, channels = inputs.shape
    own = channels // COUNT
    groups, taps = long_filter.shape
    half = jnp.bfloat16
    piece, window = ((rows, own), half), COUNT * rows
    packed = run_kernel(
        pack_kernel,
        (jnp.transpose(inputs, (1, 0, 2)), short_filter, queries, key_rows),
        [((3 * rows, own), half)] * COUNT + [((rows + EDGE, own), half)] * COUNT,
        [
            pltpu.VMEM((2, rows, channels), half),
            pltpu.VMEM(short_filter.shape, half),
            pltpu.SemaphoreType.DMA((3 * COUNT + 2,)),
        ],
        [IN_HBM] * 4,
        WIDE_LIMIT,
    )
    plain, gates = packed[:COUNT], packed[COUNT:]
    plain = [swapped(plain[step], "ctx", step) for step in ORDER[:3]] + [plain[0]]
    gates = [swapped(gates[step], "ctx", step) for step in ORDER[:3]] + [gates[0]]
    band, weight = run_kernel(
        ready_kernel,
        (long_filter, out_weight),
        [((groups // COUNT * taps, 2 * taps), half), (out_weight.shape, half)],
        [pltpu.SemaphoreType.DMA],
        [IN_VMEM, IN_HBM],
    )
    soft, totals = run_kernel(
        weights_kernel,
        plain,
        [((own // HEAD_DIM, window, window), half), ((window, HEAD_DIM), jnp.float32)],
        [pltpu.VMEM((COUNT, rows, own), half), pltpu.VMEM((window, own), half)],
    )
    third, second, values = run_kernel(
        values_kernel,
        (*plain, *gates, band, short_filter, skip_gain.reshape(1, channels), soft, totals),
        [piece, piece, ((window, own), half)],
        [
            pltpu.VMEM((window, own), half),
            pltpu.VMEM((COUNT, rows + EDGE, own), half),
            pltpu.VMEM((window + rows, own), half),
        ],
    )
    third_got, second_got = swapped(third, "ctx", 3), swapped(second, "ctx", 2)
    upper, lower, mine = run_kernel(
        near_rows_kernel,
        (soft, totals, values),
        [((rows // 2, own), half)] * 2 + [piece],
        [pltpu.VMEM((rows, own), half)],
    )
    near = (swapped(upper, "ctx", 1), swapped(lower, "ctx", 1))
    return project_and_share((third_got, second_got, *near, mine), weight)


def projected(attended, out_weight, masks):
    rows = attended[0].shape[0]
    width = out_weight.shape[1] // lax.axis_size("mp")
    return run_kernel(
        functools.partial(project_kernel, masks),
        (*attended, out_weight),
        [((rows, width), jnp.bfloat16)] * len(masks),
        [pltpu.VMEM((rows, out_weight.shape[0]), jnp.bfloat16)],
        cost=2 * rows * out_weight.shape[0] * width * len(masks),
    )


def added(*terms):
    total = terms[0].astype(jnp.float32)
    for term in terms[1:]:
        total = total + term.astype(jnp.float32)
    return total.astype(jnp.bfloat16)


def project_and_share(attended, out_weight):
    far_given, far_kept = projected(attended, out_weight, (3, 2))
    far_got = swapped(far_given, "mp", 1)
    near_given, near_kept = projected(attended, out_weight, (1, 0))
    far_sum = added(far_kept, far_got)
    near_got = swapped(near_given, "mp", 1)
    return added(near_kept, near_got, swapped(far_sum, "mp", 2))


def per_device(inputs, short_filter, long_filter, skip_gain, queries, key_rows, out_weight):
    rows, _, channels = inputs.shape
    count = lax.axis_size("ctx")
    taps = long_filter.shape[1]
    splits = channels % (count * HEAD_DIM) == 0 and count == COUNT and rows == taps
    if splits and lax.axis_size("mp") == 4:
        return by_heads(inputs, short_filter, long_filter, skip_gain, queries, key_rows, out_weight)
    attended = by_rows(inputs, short_filter, long_filter, skip_gain, queries, key_rows)
    partial_out = jnp.dot(attended, out_weight, preferred_element_type=jnp.float32)
    return lax.psum_scatter(partial_out.astype(jnp.bfloat16), "mp", scatter_dimension=1, tiled=True)


def solution(mesh):
    placed = (
        P(("parts", "ctx"), None, "mp"),
        P(None, None, "mp"),
        P("mp", None),
        P("mp"),
        P(("parts", "ctx"), "mp"),
        P(("parts", "ctx"), "mp"),
        P("mp", None),
    )
    return jax.shard_map(
        per_device, mesh=mesh, in_specs=placed, out_specs=P(("parts", "ctx"), "mp"), check_vma=False
    )
```

```python
import functools

import jax
import jax.numpy as jnp
from jax import lax
from jax.experimental import pallas as pl
from jax.experimental.pallas import tpu as pltpu
from jax.sharding import PartitionSpec as P

HEAD_DIM = 128
COUNT = 4
ORDER = (3, 2, 1, 0)
EDGE = 16


masked_score = -1e30


def passed_along(value, axis, steps):
    count = lax.axis_size(axis)
    initial, last = (max(0, -steps), min(count, count - steps))
    return lax.ppermute(value, axis, [(source, source + steps) for source in range(initial, last)])


def toeplitz_taps(filters, row_count):
    group_count = filters.shape[0]
    tap_count = filters.shape[1]
    span = row_count + tap_count - 1
    flipped = filters[:, ::-1]
    padded_taps = jnp.concatenate(
        [flipped, jnp.zeros((group_count, row_count), filters.dtype)], axis=1
    )
    repeated = jnp.tile(padded_taps, (1, row_count))
    return repeated[:, : row_count * span].reshape(group_count, row_count, span)


def short_features(extended, short_filter, row_count):
    tap_count = short_filter.shape[0]
    features = jnp.zeros((row_count,) + extended.shape[1:], jnp.float32)
    for lag_index in range(tap_count):
        delayed = extended[
            tap_count - 1 - lag_index : tap_count - 1 - lag_index + row_count
        ].astype(jnp.float32)
        features = features + short_filter[lag_index].astype(jnp.float32)[None] * delayed
    return features


def attend(head_queries, query_pos, key_piece, value_piece):
    key_count = key_piece.shape[0]
    head_count = head_queries.shape[1]
    key_heads = key_piece.reshape(key_count, head_count, -1)
    value_heads = value_piece.reshape(key_count, head_count, -1)
    scores = jnp.einsum(
        "qhd,khd->hqk", head_queries, key_heads, preferred_element_type=jnp.float32
    ) * head_queries.shape[2] ** (-0.5)
    key_pos = lax.iota(jnp.int32, key_count)
    allowed = (key_pos[None, :] <= query_pos[:, None])[None]
    peak = jnp.max(jnp.where(allowed, scores, masked_score), axis=2)
    probabilities = jnp.where(allowed, jnp.exp(scores - peak[..., None]), 0.0)
    weight_sum = jnp.sum(probabilities, axis=2)
    mixed = jnp.einsum(
        "hqk,khd->hqd",
        probabilities.astype(jnp.bfloat16),
        value_heads,
        preferred_element_type=jnp.float32,
    )
    result = mixed / weight_sum[..., None]
    return jnp.transpose(result, (1, 0, 2)).reshape(result.shape[1], -1).astype(jnp.bfloat16)


def by_rows(inputs, short_filter, long_filter, skip_gain, queries, key_rows):
    row_count = inputs.shape[0]
    channels = inputs.shape[2]
    groups = long_filter.shape[0]
    tap_count = long_filter.shape[1]
    short_reach = short_filter.shape[0] - 1
    position = lax.axis_index("ctx")
    rim = passed_along(inputs[row_count - short_reach :], "ctx", 1)
    extended = jnp.concatenate([rim, inputs], axis=0)
    features = short_features(extended, short_filter, row_count)
    gate_product = (features[:, 1] * features[:, 2]).astype(jnp.bfloat16)
    gate_prev = passed_along(gate_product[row_count - (tap_count - 1) :], "ctx", 1)
    gate_ext = jnp.concatenate([gate_prev, gate_product], axis=0)
    toeplitz = toeplitz_taps(long_filter, row_count)
    filtered = jnp.einsum(
        "gtr,rgc->tgc",
        toeplitz,
        gate_ext.reshape(row_count + tap_count - 1, groups, channels // groups),
        preferred_element_type=jnp.float32,
    ).reshape(row_count, channels)
    values = (
        features[:, 0] * (filtered + skip_gain[None] * gate_product.astype(jnp.float32))
    ).astype(jnp.bfloat16)
    head_count = channels // HEAD_DIM
    head_queries = queries.reshape(row_count, head_count, HEAD_DIM)
    query_pos = position * row_count + lax.iota(jnp.int32, row_count)
    return attend(
        head_queries,
        query_pos,
        lax.all_gather(key_rows, "ctx", axis=0, tiled=True),
        lax.all_gather(values, "ctx", axis=0, tiled=True),
    )


def delayed(signal, lag):
    if lag == 0:
        return signal
    row = lax.broadcasted_iota(jnp.int32, signal.shape, 0)
    return jnp.where(row < lag, 0.0, pltpu.roll(signal, lag, 0))


def featured(signal, taps):
    total = taps[0] * signal
    for lag in range(1, len(taps)):
        total = total + taps[lag] * delayed(signal, lag)
    return total


def columns_of(block, width):
    return pl.ds(pl.multiple_of(block * width, width), width)


def write_gate(signals, taps, out_ref):
    rows, own = signals[0].shape
    edge_row = lax.broadcasted_iota(jnp.int32, (8, own), 0)
    features = [featured(signal, tap) for signal, tap in zip(signals, taps)]
    edges = [
        jnp.where(edge_row < 2, signal[:8], jnp.where(edge_row < 4, pltpu.roll(signal[rows - 8 :], 4, 0), 0.0))
        for signal in signals
    ]
    out_ref[0:rows] = (features[0] * features[1]).astype(jnp.bfloat16)
    out_ref[rows : rows + EDGE] = jnp.concatenate(edges, axis=0).astype(jnp.bfloat16)


def plain_kernel(inputs_any, queries_any, keys_any, *refs):
    out_refs, sems = refs[:COUNT], refs[COUNT]
    rows, own = queries_any.shape[0], out_refs[0].shape[1]
    position = lax.axis_index("ctx")
    copies = []
    for step in ORDER:
        columns = columns_of(position ^ step, own)
        for index, source in enumerate((queries_any, keys_any, inputs_any.at[0])):
            target = out_refs[step].at[index * rows : (index + 1) * rows]
            copies.append(pltpu.make_async_copy(source.at[:, columns], target, sems.at[len(copies)]))
    for copy in copies:
        copy.start()
    for copy in copies:
        copy.wait()


def gate_kernel(inputs_any, short_any, *refs):
    out_refs, (signal_s, short_s, sems) = refs[:COUNT], refs[COUNT:]
    own = out_refs[0].shape[1]
    position = lax.axis_index("ctx")
    copies = [
        pltpu.make_async_copy(short_any, short_s, sems.at[0]),
        pltpu.make_async_copy(inputs_any.at[1:3], signal_s, sems.at[1]),
    ]
    for copy in copies:
        copy.start()
    for copy in copies:
        copy.wait()
    for step in ORDER:
        columns = columns_of(position ^ step, own)
        signals = [signal_s[stream, :, columns].astype(jnp.float32) for stream in range(2)]
        taps = [
            [short_s[lag, stream : stream + 1, columns].astype(jnp.float32) for lag in range(3)] for stream in (1, 2)
        ]
        write_gate(signals, taps, out_refs[step])


def ready_kernel(filter_ref, weight_any, band_ref, weight_ref, sem):
    rows, span = band_ref.shape
    taps = filter_ref.shape[1]
    groups = rows // taps
    weights = pltpu.make_async_copy(weight_any, weight_ref, sem)
    weights.start()
    source = lax.broadcasted_iota(jnp.int32, (taps, span), 0)
    target = lax.broadcasted_iota(jnp.int32, (taps, span), 1)
    flip = (source + target == taps).astype(jnp.bfloat16)
    first_group = pl.multiple_of(lax.axis_index("ctx") * groups, groups)
    first = jnp.dot(filter_ref[pl.ds(first_group, groups)], flip, preferred_element_type=jnp.float32)
    for group in range(groups):
        repeated = jnp.broadcast_to(first[group : group + 1], (taps, span))
        banded = pltpu.roll(repeated, 0, 1, stride=1, stride_axis=0)
        band_ref[group * taps : (group + 1) * taps] = banded.astype(jnp.bfloat16)
    weights.wait()


def weights_kernel(third_ref, second_ref, near_ref, own_ref, weight_ref, total_ref, query_s, key_s):
    count = COUNT
    rows, own = query_s.shape[1:]
    position = lax.axis_index("ctx")
    for step, given in zip(ORDER, (third_ref, second_ref, near_ref, own_ref)):
        query_s[position ^ step] = given[0:rows]
        key_s[columns_of(position ^ step, rows)] = given[rows : 2 * rows]
    causal = lax.broadcasted_iota(jnp.int32, (rows, rows), 1) <= lax.broadcasted_iota(jnp.int32, (rows, rows), 0)
    for head in range(own // HEAD_DIM):
        columns = slice(head * HEAD_DIM, (head + 1) * HEAD_DIM)
        for block in range(count):
            here, seen = slice(block * rows, (block + 1) * rows), (block + 1) * rows
            scores = lax.dot_general(
                query_s[block, :, columns],
                key_s[0:seen, columns],
                (((1,), (1,)), ((), ())),
                preferred_element_type=jnp.float32,
            ) * HEAD_DIM ** (-0.5)
            own_scores = jnp.where(causal, scores[:, block * rows :], masked_score)
            pieces = [scores[:, : block * rows], own_scores] if block else [own_scores]
            scores = jnp.concatenate(pieces, axis=1)
            weights = jnp.exp(scores - jnp.max(scores, axis=1, keepdims=True))
            total_ref[here, head : head + 1] = jnp.sum(weights, axis=1, keepdims=True)
            weight_ref[head, here, 0:seen] = weights.astype(jnp.bfloat16)
            if seen < count * rows:
                weight_ref[head, here, seen:] = jnp.zeros((rows, count * rows - seen), jnp.bfloat16)


def mix_rows(block, weight_ref, total_ref, value_ref, out_ref):
    rows = out_ref.shape[0]
    here = columns_of(block, rows)
    for head in range(out_ref.shape[1] // HEAD_DIM):
        columns = slice(head * HEAD_DIM, (head + 1) * HEAD_DIM)
        mixed = jnp.dot(weight_ref[head, here], value_ref[:, columns], preferred_element_type=jnp.float32)
        out_ref[:, columns] = (mixed / total_ref[here, head : head + 1]).astype(jnp.bfloat16)


def values_kernel(*refs):
    count = COUNT
    plain, gates = refs[:count], refs[count : 2 * count]
    band_ref, short_ref, gain_ref, weight_ref, total_ref = refs[2 * count : 2 * count + 5]
    third_ref, second_ref, value_ref = refs[2 * count + 5 : 2 * count + 8]
    signal_s, gates_s, gate_s = refs[2 * count + 8 :]
    rows, own = second_ref.shape
    per_group = own * rows // band_ref.shape[0]
    position = lax.axis_index("ctx")
    mine = columns_of(position, own)
    for step, given, gate in zip(ORDER, plain, gates):
        signal_s[columns_of(position ^ step, rows)] = given[2 * rows :]
        gates_s[position ^ step] = gate[...]
    taps = [
        [short_ref[lag, stream : stream + 1, mine].astype(jnp.float32) for lag in range(3)] for stream in range(3)
    ]
    gate_s[0:rows] = jnp.zeros((rows, own), jnp.bfloat16)
    edge_row = lax.broadcasted_iota(jnp.int32, (8, own), 0)
    head_row = lax.broadcasted_iota(jnp.int32, (16, own), 0)
    for block in range(count):
        gate_s[(block + 1) * rows : (block + 2) * rows] = gates_s[block, 0:rows]
        if block == 0:
            continue
        fixed = 1.0
        before = gates_s[block - 1, rows:].astype(jnp.float32)
        here = gates_s[block, rows:].astype(jnp.float32)
        for which, stream in enumerate((1, 2)):
            old = pltpu.roll(before[8 * which : 8 * which + 8], 6, 0)
            new = pltpu.roll(here[8 * which : 8 * which + 8], 2, 0)
            joined = jnp.where(edge_row < 2, old, new)
            fixed = fixed * (
                taps[stream][0] * pltpu.roll(joined, 6, 0)
                + taps[stream][1] * pltpu.roll(joined, 7, 0)
                + taps[stream][2] * joined
            )
        head = gates_s[block, 0:16].astype(jnp.float32)
        head = jnp.where(head_row < 2, jnp.concatenate([fixed, fixed], axis=0), head)
        gate_s[(block + 1) * rows : (block + 1) * rows + 16] = head.astype(jnp.bfloat16)
    feature = featured(signal_s[...].astype(jnp.float32), taps[0])
    gain = gain_ref[:, mine]
    per_tile = HEAD_DIM // per_group
    lane = lax.broadcasted_iota(jnp.int32, (rows, 2 * HEAD_DIM), 1) % HEAD_DIM // per_group
    for tile in range(own // HEAD_DIM):
        columns = slice(tile * HEAD_DIM, (tile + 1) * HEAD_DIM)
        for block in range(0, count, 2):
            windows = [gate_s[other * rows : (other + 2) * rows, columns] for other in (block, block + 1)]
            mixed = jnp.dot(
                band_ref[tile * per_tile * rows : (tile + 1) * per_tile * rows],
                jnp.concatenate(windows, axis=1),
                preferred_element_type=jnp.float32,
            )
            filtered = mixed[:rows]
            for group in range(1, per_tile):
                filtered = jnp.where(lane == group, mixed[group * rows : (group + 1) * rows], filtered)
            for index in range(2):
                here = slice((block + index) * rows, (block + index + 1) * rows)
                gate = gate_s[(block + index + 1) * rows : (block + index + 2) * rows, columns].astype(jnp.float32)
                part = filtered[:, index * HEAD_DIM : (index + 1) * HEAD_DIM]
                value_ref[here, columns] = (
                    feature[here, columns] * (part + gain[:, columns] * gate)
                ).astype(jnp.bfloat16)
    for step, out_ref in ((3, third_ref), (2, second_ref)):
        mix_rows(position ^ step, weight_ref, total_ref, value_ref, out_ref)


def near_rows_kernel(weight_ref, total_ref, value_ref, *refs):
    upper_ref, lower_ref, own_ref, near_s = refs
    half = upper_ref.shape[0]
    position = lax.axis_index("ctx")
    mix_rows(position ^ 1, weight_ref, total_ref, value_ref, near_s)
    upper_ref[...] = near_s[0:half]
    lower_ref[...] = near_s[half:]
    mix_rows(position, weight_ref, total_ref, value_ref, own_ref)


def project_kernel(masks, *refs):
    given, weight_ref = refs[:5], refs[5]
    out_refs, attended_s = refs[6:-1], refs[-1]
    own = given[0].shape[1]
    width = out_refs[0].shape[1]
    position, here = lax.axis_index("ctx"), lax.axis_index("mp")
    third, second, upper, lower, mine = given
    half = upper.shape[0]
    attended_s[0:half, columns_of(position ^ 1, own)] = upper[...]
    attended_s[half:, columns_of(position ^ 1, own)] = lower[...]
    for step, piece in ((0, mine), (2, second), (3, third)):
        attended_s[:, columns_of(position ^ step, own)] = piece[...]
    for mask, out_ref in zip(masks, out_refs):
        columns = pl.ds(pl.multiple_of((here ^ mask) * width, width), width)
        out_ref[...] = jnp.dot(
            attended_s[...], weight_ref[:, columns], preferred_element_type=jnp.float32
        ).astype(jnp.bfloat16)


VMEM_LIMIT = 40 * 1024 * 1024
PLAIN_LIMIT = 53 * 1024 * 1024
GATE_LIMIT = 60 * 1024 * 1024
IN_HBM = pl.BlockSpec(memory_space=pltpu.HBM)
IN_VMEM = pl.BlockSpec(memory_space=pltpu.VMEM)


def run_kernel(kernel, operands, outputs, scratch=(), spaces=None, limit=VMEM_LIMIT, cost=10**6):
    return pl.pallas_call(
        kernel,
        out_shape=[jax.ShapeDtypeStruct(shape, dtype) for shape, dtype in outputs],
        in_specs=spaces or [IN_VMEM] * len(operands),
        out_specs=[IN_VMEM] * len(outputs),
        scratch_shapes=scratch,
        compiler_params=pltpu.CompilerParams(vmem_limit_bytes=limit),
        cost_estimate=pl.CostEstimate(flops=cost, bytes_accessed=2**20, transcendentals=0),
        name=getattr(kernel, "func", kernel).__name__,
    )(*operands)


def swapped(value, axis, step):
    return lax.ppermute(value, axis, [(source, source ^ step) for source in range(lax.axis_size(axis))])


def by_heads(inputs, short_filter, long_filter, skip_gain, queries, key_rows, out_weight):
    rows, streams, channels = inputs.shape
    own = channels // COUNT
    groups, taps = long_filter.shape
    half = jnp.bfloat16
    piece, window = ((rows, own), half), COUNT * rows
    streamed = jnp.transpose(inputs, (1, 0, 2))
    plain = run_kernel(
        plain_kernel,
        (streamed, queries, key_rows),
        [((3 * rows, own), half)] * COUNT,
        [pltpu.SemaphoreType.DMA((3 * COUNT,))],
        [IN_HBM] * 3,
        PLAIN_LIMIT,
    )
    gates = run_kernel(
        gate_kernel,
        (streamed, short_filter),
        [((rows + EDGE, own), half)] * COUNT,
        [
            pltpu.VMEM((2, rows, channels), half),
            pltpu.VMEM(short_filter.shape, half),
            pltpu.SemaphoreType.DMA((2,)),
        ],
        [IN_HBM] * 2,
        GATE_LIMIT,
    )
    plain = [swapped(plain[step], "ctx", step) for step in ORDER[:3]] + [plain[0]]
    gates = [swapped(gates[step], "ctx", step) for step in ORDER[:3]] + [gates[0]]
    band, weight = run_kernel(
        ready_kernel,
        (long_filter, out_weight),
        [((groups // COUNT * taps, 2 * taps), half), (out_weight.shape, half)],
        [pltpu.SemaphoreType.DMA],
        [IN_VMEM, IN_HBM],
    )
    soft, totals = run_kernel(
        weights_kernel,
        plain,
        [((own // HEAD_DIM, window, window), half), ((window, HEAD_DIM), jnp.float32)],
        [pltpu.VMEM((COUNT, rows, own), half), pltpu.VMEM((window, own), half)],
    )
    third, second, values = run_kernel(
        values_kernel,
        (*plain, *gates, band, short_filter, skip_gain.reshape(1, channels), soft, totals),
        [piece, piece, ((window, own), half)],
        [
            pltpu.VMEM((window, own), half),
            pltpu.VMEM((COUNT, rows + EDGE, own), half),
            pltpu.VMEM((window + rows, own), half),
        ],
    )
    third_got, second_got = swapped(third, "ctx", 3), swapped(second, "ctx", 2)
    upper, lower, mine = run_kernel(
        near_rows_kernel,
        (soft, totals, values),
        [((rows // 2, own), half)] * 2 + [piece],
        [pltpu.VMEM((rows, own), half)],
    )
    near = (swapped(upper, "ctx", 1), swapped(lower, "ctx", 1))
    return project_and_share((third_got, second_got, *near, mine), weight)


def projected(attended, out_weight, masks):
    rows = attended[0].shape[0]
    width = out_weight.shape[1] // lax.axis_size("mp")
    return run_kernel(
        functools.partial(project_kernel, masks),
        (*attended, out_weight),
        [((rows, width), jnp.bfloat16)] * len(masks),
        [pltpu.VMEM((rows, out_weight.shape[0]), jnp.bfloat16)],
        cost=2 * rows * out_weight.shape[0] * width * len(masks),
    )


def added(*terms):
    total = terms[0].astype(jnp.float32)
    for term in terms[1:]:
        total = total + term.astype(jnp.float32)
    return total.astype(jnp.bfloat16)


def project_and_share(attended, out_weight):
    far_given, far_kept = projected(attended, out_weight, (3, 2))
    far_got = swapped(far_given, "mp", 1)
    near_given, near_kept = projected(attended, out_weight, (1, 0))
    far_sum = added(far_kept, far_got)
    near_got = swapped(near_given, "mp", 1)
    return added(near_kept, near_got, swapped(far_sum, "mp", 2))


def per_device(inputs, short_filter, long_filter, skip_gain, queries, key_rows, out_weight):
    rows, _, channels = inputs.shape
    count = lax.axis_size("ctx")
    taps = long_filter.shape[1]
    splits = channels % (count * HEAD_DIM) == 0 and count == COUNT and rows == taps
    if splits and lax.axis_size("mp") == 4:
        return by_heads(inputs, short_filter, long_filter, skip_gain, queries, key_rows, out_weight)
    attended = by_rows(inputs, short_filter, long_filter, skip_gain, queries, key_rows)
    partial_out = jnp.dot(attended, out_weight, preferred_element_type=jnp.float32)
    return lax.psum_scatter(partial_out.astype(jnp.bfloat16), "mp", scatter_dimension=1, tiled=True)


def solution(mesh):
    placed = (
        P(("parts", "ctx"), None, "mp"),
        P(None, None, "mp"),
        P("mp", None),
        P("mp"),
        P(("parts", "ctx"), "mp"),
        P(("parts", "ctx"), "mp"),
        P("mp", None),
    )
    return jax.shard_map(
        per_device, mesh=mesh, in_specs=placed, out_specs=P(("parts", "ctx"), "mp"), check_vma=False
    )
```

```python
import functools

import jax
import jax.numpy as jnp
from jax import lax
from jax.experimental import pallas as pl
from jax.experimental.pallas import tpu as pltpu
from jax.sharding import PartitionSpec as P

HEAD_DIM = 128
COUNT = 4
ORDER = (3, 2, 1, 0)
EDGE = 16


masked_score = -1e30


def passed_along(value, axis, steps):
    count = lax.axis_size(axis)
    initial, last = (max(0, -steps), min(count, count - steps))
    return lax.ppermute(value, axis, [(source, source + steps) for source in range(initial, last)])


def toeplitz_taps(filters, row_count):
    group_count = filters.shape[0]
    tap_count = filters.shape[1]
    span = row_count + tap_count - 1
    flipped = filters[:, ::-1]
    padded_taps = jnp.concatenate(
        [flipped, jnp.zeros((group_count, row_count), filters.dtype)], axis=1
    )
    repeated = jnp.tile(padded_taps, (1, row_count))
    return repeated[:, : row_count * span].reshape(group_count, row_count, span)


def short_features(extended, short_filter, row_count):
    tap_count = short_filter.shape[0]
    features = jnp.zeros((row_count,) + extended.shape[1:], jnp.float32)
    for lag_index in range(tap_count):
        delayed = extended[
            tap_count - 1 - lag_index : tap_count - 1 - lag_index + row_count
        ].astype(jnp.float32)
        features = features + short_filter[lag_index].astype(jnp.float32)[None] * delayed
    return features


def attend(head_queries, query_pos, key_piece, value_piece):
    key_count = key_piece.shape[0]
    head_count = head_queries.shape[1]
    key_heads = key_piece.reshape(key_count, head_count, -1)
    value_heads = value_piece.reshape(key_count, head_count, -1)
    scores = jnp.einsum(
        "qhd,khd->hqk", head_queries, key_heads, preferred_element_type=jnp.float32
    ) * head_queries.shape[2] ** (-0.5)
    key_pos = lax.iota(jnp.int32, key_count)
    allowed = (key_pos[None, :] <= query_pos[:, None])[None]
    peak = jnp.max(jnp.where(allowed, scores, masked_score), axis=2)
    probabilities = jnp.where(allowed, jnp.exp(scores - peak[..., None]), 0.0)
    weight_sum = jnp.sum(probabilities, axis=2)
    mixed = jnp.einsum(
        "hqk,khd->hqd",
        probabilities.astype(jnp.bfloat16),
        value_heads,
        preferred_element_type=jnp.float32,
    )
    result = mixed / weight_sum[..., None]
    return jnp.transpose(result, (1, 0, 2)).reshape(result.shape[1], -1).astype(jnp.bfloat16)


def by_rows(inputs, short_filter, long_filter, skip_gain, queries, key_rows):
    row_count = inputs.shape[0]
    channels = inputs.shape[2]
    groups = long_filter.shape[0]
    tap_count = long_filter.shape[1]
    short_reach = short_filter.shape[0] - 1
    position = lax.axis_index("ctx")
    rim = passed_along(inputs[row_count - short_reach :], "ctx", 1)
    extended = jnp.concatenate([rim, inputs], axis=0)
    features = short_features(extended, short_filter, row_count)
    gate_product = (features[:, 1] * features[:, 2]).astype(jnp.bfloat16)
    gate_prev = passed_along(gate_product[row_count - (tap_count - 1) :], "ctx", 1)
    gate_ext = jnp.concatenate([gate_prev, gate_product], axis=0)
    toeplitz = toeplitz_taps(long_filter, row_count)
    filtered = jnp.einsum(
        "gtr,rgc->tgc",
        toeplitz,
        gate_ext.reshape(row_count + tap_count - 1, groups, channels // groups),
        preferred_element_type=jnp.float32,
    ).reshape(row_count, channels)
    values = (
        features[:, 0] * (filtered + skip_gain[None] * gate_product.astype(jnp.float32))
    ).astype(jnp.bfloat16)
    head_count = channels // HEAD_DIM
    head_queries = queries.reshape(row_count, head_count, HEAD_DIM)
    query_pos = position * row_count + lax.iota(jnp.int32, row_count)
    return attend(
        head_queries,
        query_pos,
        lax.all_gather(key_rows, "ctx", axis=0, tiled=True),
        lax.all_gather(values, "ctx", axis=0, tiled=True),
    )


def delayed(signal, lag):
    if lag == 0:
        return signal
    row = lax.broadcasted_iota(jnp.int32, signal.shape, 0)
    return jnp.where(row < lag, 0.0, pltpu.roll(signal, lag, 0))


def featured(signal, taps):
    total = taps[0] * signal
    for lag in range(1, len(taps)):
        total = total + taps[lag] * delayed(signal, lag)
    return total


def columns_of(block, width):
    return pl.ds(pl.multiple_of(block * width, width), width)


def write_gate(signals, taps, out_ref):
    rows, own = signals[0].shape
    edge_row = lax.broadcasted_iota(jnp.int32, (8, own), 0)
    features = [featured(signal, tap) for signal, tap in zip(signals, taps)]
    edges = [
        jnp.where(edge_row < 2, signal[:8], jnp.where(edge_row < 4, pltpu.roll(signal[rows - 8 :], 4, 0), 0.0))
        for signal in signals
    ]
    out_ref[0:rows] = (features[0] * features[1]).astype(jnp.bfloat16)
    out_ref[rows : rows + EDGE] = jnp.concatenate(edges, axis=0).astype(jnp.bfloat16)


def plain_kernel(inputs_any, queries_any, keys_any, *refs):
    out_refs, sems = refs[:COUNT], refs[COUNT]
    rows, own = queries_any.shape[0], out_refs[0].shape[1]
    position = lax.axis_index("ctx")
    copies = []
    for step in ORDER:
        columns = columns_of(position ^ step, own)
        for index, source in enumerate((queries_any, keys_any, inputs_any.at[0])):
            target = out_refs[step].at[index * rows : (index + 1) * rows]
            copies.append(pltpu.make_async_copy(source.at[:, columns], target, sems.at[len(copies)]))
    for copy in copies:
        copy.start()
    for copy in copies:
        copy.wait()


def gate_kernel(inputs_any, short_any, *refs):
    out_refs, (signal_s, short_s, sems) = refs[:COUNT], refs[COUNT:]
    own = out_refs[0].shape[1]
    position = lax.axis_index("ctx")
    copies = [
        pltpu.make_async_copy(short_any, short_s, sems.at[0]),
        pltpu.make_async_copy(inputs_any.at[1:3], signal_s, sems.at[1]),
    ]
    for copy in copies:
        copy.start()
    for copy in copies:
        copy.wait()
    for step in ORDER:
        columns = columns_of(position ^ step, own)
        signals = [signal_s[stream, :, columns].astype(jnp.float32) for stream in range(2)]
        taps = [
            [short_s[lag, stream : stream + 1, columns].astype(jnp.float32) for lag in range(3)] for stream in (1, 2)
        ]
        write_gate(signals, taps, out_refs[step])


def ready_kernel(filter_ref, weight_any, band_ref, weight_ref, sem):
    rows, span = band_ref.shape
    taps = filter_ref.shape[1]
    groups = rows // taps
    weights = pltpu.make_async_copy(weight_any, weight_ref, sem)
    weights.start()
    source = lax.broadcasted_iota(jnp.int32, (taps, span), 0)
    target = lax.broadcasted_iota(jnp.int32, (taps, span), 1)
    flip = (source + target == taps).astype(jnp.bfloat16)
    first_group = pl.multiple_of(lax.axis_index("ctx") * groups, groups)
    first = jnp.dot(filter_ref[pl.ds(first_group, groups)], flip, preferred_element_type=jnp.float32)
    for group in range(groups):
        repeated = jnp.broadcast_to(first[group : group + 1], (taps, span))
        banded = pltpu.roll(repeated, 0, 1, stride=1, stride_axis=0)
        band_ref[group * taps : (group + 1) * taps] = banded.astype(jnp.bfloat16)
    weights.wait()


def weights_kernel(third_ref, second_ref, near_ref, own_ref, weight_ref, total_ref, query_s, key_s):
    count = COUNT
    rows, own = query_s.shape[1:]
    position = lax.axis_index("ctx")
    for step, given in zip(ORDER, (third_ref, second_ref, near_ref, own_ref)):
        query_s[position ^ step] = given[0:rows]
        key_s[columns_of(position ^ step, rows)] = given[rows : 2 * rows]
    causal = lax.broadcasted_iota(jnp.int32, (rows, rows), 1) <= lax.broadcasted_iota(jnp.int32, (rows, rows), 0)
    for head in range(own // HEAD_DIM):
        columns = slice(head * HEAD_DIM, (head + 1) * HEAD_DIM)
        for block in range(count):
            here, seen = slice(block * rows, (block + 1) * rows), (block + 1) * rows
            scores = lax.dot_general(
                query_s[block, :, columns],
                key_s[0:seen, columns],
                (((1,), (1,)), ((), ())),
                preferred_element_type=jnp.float32,
            ) * HEAD_DIM ** (-0.5)
            own_scores = jnp.where(causal, scores[:, block * rows :], masked_score)
            pieces = [scores[:, : block * rows], own_scores] if block else [own_scores]
            scores = jnp.concatenate(pieces, axis=1)
            weights = jnp.exp(scores - jnp.max(scores, axis=1, keepdims=True))
            total_ref[here, head : head + 1] = jnp.sum(weights, axis=1, keepdims=True)
            weight_ref[head, here, 0:seen] = weights.astype(jnp.bfloat16)
            if seen < count * rows:
                weight_ref[head, here, seen:] = jnp.zeros((rows, count * rows - seen), jnp.bfloat16)


def mix_rows(block, weight_ref, total_ref, value_ref, out_ref):
    rows = out_ref.shape[0]
    here = columns_of(block, rows)
    for head in range(out_ref.shape[1] // HEAD_DIM):
        columns = slice(head * HEAD_DIM, (head + 1) * HEAD_DIM)
        mixed = jnp.dot(weight_ref[head, here], value_ref[:, columns], preferred_element_type=jnp.float32)
        out_ref[:, columns] = (mixed / total_ref[here, head : head + 1]).astype(jnp.bfloat16)


def values_kernel(*refs):
    count = COUNT
    plain, gates = refs[:count], refs[count : 2 * count]
    band_ref, short_ref, gain_ref, weight_ref, total_ref = refs[2 * count : 2 * count + 5]
    third_ref, second_ref, value_ref = refs[2 * count + 5 : 2 * count + 8]
    signal_s, gates_s, gate_s = refs[2 * count + 8 :]
    rows, own = second_ref.shape
    per_group = own * rows // band_ref.shape[0]
    position = lax.axis_index("ctx")
    mine = columns_of(position, own)
    for step, given, gate in zip(ORDER, plain, gates):
        signal_s[columns_of(position ^ step, rows)] = given[2 * rows :]
        gates_s[position ^ step] = gate[...]
    taps = [
        [short_ref[lag, stream : stream + 1, mine].astype(jnp.float32) for lag in range(3)] for stream in range(3)
    ]
    gate_s[0:rows] = jnp.zeros((rows, own), jnp.bfloat16)
    edge_row = lax.broadcasted_iota(jnp.int32, (8, own), 0)
    head_row = lax.broadcasted_iota(jnp.int32, (16, own), 0)
    for block in range(count):
        gate_s[(block + 1) * rows : (block + 2) * rows] = gates_s[block, 0:rows]
        if block == 0:
            continue
        fixed = 1.0
        before = gates_s[block - 1, rows:].astype(jnp.float32)
        here = gates_s[block, rows:].astype(jnp.float32)
        for which, stream in enumerate((1, 2)):
            old = pltpu.roll(before[8 * which : 8 * which + 8], 6, 0)
            new = pltpu.roll(here[8 * which : 8 * which + 8], 2, 0)
            joined = jnp.where(edge_row < 2, old, new)
            fixed = fixed * (
                taps[stream][0] * pltpu.roll(joined, 6, 0)
                + taps[stream][1] * pltpu.roll(joined, 7, 0)
                + taps[stream][2] * joined
            )
        head = gates_s[block, 0:16].astype(jnp.float32)
        head = jnp.where(head_row < 2, jnp.concatenate([fixed, fixed], axis=0), head)
        gate_s[(block + 1) * rows : (block + 1) * rows + 16] = head.astype(jnp.bfloat16)
    feature = featured(signal_s[...].astype(jnp.float32), taps[0])
    gain = gain_ref[:, mine]
    per_tile = HEAD_DIM // per_group
    lane = lax.broadcasted_iota(jnp.int32, (rows, 2 * HEAD_DIM), 1) % HEAD_DIM // per_group
    for tile in range(own // HEAD_DIM):
        columns = slice(tile * HEAD_DIM, (tile + 1) * HEAD_DIM)
        for block in range(0, count, 2):
            windows = [gate_s[other * rows : (other + 2) * rows, columns] for other in (block, block + 1)]
            mixed = jnp.dot(
                band_ref[tile * per_tile * rows : (tile + 1) * per_tile * rows],
                jnp.concatenate(windows, axis=1),
                preferred_element_type=jnp.float32,
            )
            filtered = mixed[:rows]
            for group in range(1, per_tile):
                filtered = jnp.where(lane == group, mixed[group * rows : (group + 1) * rows], filtered)
            for index in range(2):
                here = slice((block + index) * rows, (block + index + 1) * rows)
                gate = gate_s[(block + index + 1) * rows : (block + index + 2) * rows, columns].astype(jnp.float32)
                part = filtered[:, index * HEAD_DIM : (index + 1) * HEAD_DIM]
                value_ref[here, columns] = (
                    feature[here, columns] * (part + gain[:, columns] * gate)
                ).astype(jnp.bfloat16)
    for step, out_ref in ((3, third_ref), (2, second_ref)):
        mix_rows(position ^ step, weight_ref, total_ref, value_ref, out_ref)


def near_rows_kernel(weight_ref, total_ref, value_ref, *refs):
    upper_ref, lower_ref, own_ref, near_s = refs
    half = upper_ref.shape[0]
    position = lax.axis_index("ctx")
    mix_rows(position ^ 1, weight_ref, total_ref, value_ref, near_s)
    upper_ref[...] = near_s[0:half]
    lower_ref[...] = near_s[half:]
    mix_rows(position, weight_ref, total_ref, value_ref, own_ref)


def project_kernel(masks, *refs):
    given, weight_ref = refs[:5], refs[5]
    out_refs, attended_s = refs[-1 - len(masks) : -1], refs[-1]
    own = given[0].shape[1]
    width = out_refs[0].shape[1]
    position, here = lax.axis_index("ctx"), lax.axis_index("mp")
    second, third, upper, lower, mine = given
    half = upper.shape[0]
    attended_s[0:half, columns_of(position ^ 1, own)] = upper[...]
    attended_s[half:, columns_of(position ^ 1, own)] = lower[...]
    for step, piece in ((0, mine), (2, second), (3, third)):
        attended_s[:, columns_of(position ^ step, own)] = piece[...]
    for mask, out_ref in zip(masks, out_refs):
        columns = pl.ds(pl.multiple_of((here ^ mask) * width, width), width)
        out_ref[...] = jnp.dot(
            attended_s[...], weight_ref[:, columns], preferred_element_type=jnp.float32
        ).astype(jnp.bfloat16)


VMEM_LIMIT = 40 * 1024 * 1024
PLAIN_LIMIT = 53 * 1024 * 1024
GATE_LIMIT = 60 * 1024 * 1024
IN_HBM = pl.BlockSpec(memory_space=pltpu.HBM)
IN_VMEM = pl.BlockSpec(memory_space=pltpu.VMEM)
ANYWHERE = pl.BlockSpec(memory_space=pl.ANY)


def run_kernel(kernel, operands, outputs, scratch=(), spaces=None, limit=VMEM_LIMIT, cost=10**6):
    return pl.pallas_call(
        kernel,
        out_shape=[jax.ShapeDtypeStruct(shape, dtype) for shape, dtype in outputs],
        in_specs=spaces or [IN_VMEM] * len(operands),
        out_specs=[IN_VMEM] * len(outputs),
        scratch_shapes=scratch,
        compiler_params=pltpu.CompilerParams(vmem_limit_bytes=limit),
        cost_estimate=pl.CostEstimate(flops=cost, bytes_accessed=2**20, transcendentals=0),
        name=getattr(kernel, "func", kernel).__name__,
    )(*operands)


def swapped(value, axis, step):
    return lax.ppermute(value, axis, [(source, source ^ step) for source in range(lax.axis_size(axis))])


def by_heads(inputs, short_filter, long_filter, skip_gain, queries, key_rows, out_weight):
    rows, streams, channels = inputs.shape
    own = channels // COUNT
    groups, taps = long_filter.shape
    half = jnp.bfloat16
    piece, window = ((rows, own), half), COUNT * rows
    streamed = jnp.transpose(inputs, (1, 0, 2))
    plain = run_kernel(
        plain_kernel,
        (streamed, queries, key_rows),
        [((3 * rows, own), half)] * COUNT,
        [pltpu.SemaphoreType.DMA((3 * COUNT,))],
        [IN_HBM] * 3,
        PLAIN_LIMIT,
    )
    gates = run_kernel(
        gate_kernel,
        (streamed, short_filter),
        [((rows + EDGE, own), half)] * COUNT,
        [
            pltpu.VMEM((2, rows, channels), half),
            pltpu.VMEM(short_filter.shape, half),
            pltpu.SemaphoreType.DMA((2,)),
        ],
        [IN_HBM] * 2,
        GATE_LIMIT,
    )
    plain = [swapped(plain[step], "ctx", step) for step in ORDER[:3]] + [plain[0]]
    gates = [swapped(gates[step], "ctx", step) for step in ORDER[:3]] + [gates[0]]
    band, weight = run_kernel(
        ready_kernel,
        (long_filter, out_weight),
        [((groups // COUNT * taps, 2 * taps), half), (out_weight.shape, half)],
        [pltpu.SemaphoreType.DMA],
        [IN_VMEM, IN_HBM],
    )
    soft, totals = run_kernel(
        weights_kernel,
        plain,
        [((own // HEAD_DIM, window, window), half), ((window, HEAD_DIM), jnp.float32)],
        [pltpu.VMEM((COUNT, rows, own), half), pltpu.VMEM((window, own), half)],
    )
    third, second, values = run_kernel(
        values_kernel,
        (*plain, *gates, band, short_filter, skip_gain.reshape(1, channels), soft, totals),
        [piece, piece, ((window, own), half)],
        [
            pltpu.VMEM((window, own), half),
            pltpu.VMEM((COUNT, rows + EDGE, own), half),
            pltpu.VMEM((window + rows, own), half),
        ],
    )
    third_got, second_got = swapped(third, "ctx", 3), swapped(second, "ctx", 2)
    upper, lower, mine = run_kernel(
        near_rows_kernel,
        (soft, totals, values),
        [((rows // 2, own), half)] * 2 + [piece],
        [pltpu.VMEM((rows, own), half)],
    )
    near = (swapped(upper, "ctx", 1), swapped(lower, "ctx", 1))
    return project_and_share((second_got, third_got, *near, mine), weight)


def projected(attended, out_weight, masks, after=()):
    rows = attended[0].shape[0]
    width = out_weight.shape[1] // lax.axis_size("mp")
    return run_kernel(
        functools.partial(project_kernel, masks),
        (*attended, out_weight, *after),
        [((rows, width), jnp.bfloat16)] * len(masks),
        [pltpu.VMEM((rows, out_weight.shape[0]), jnp.bfloat16)],
        [IN_VMEM] * (len(attended) + 1) + [ANYWHERE] * len(after),
        cost=2 * rows * out_weight.shape[0] * width * len(masks),
    )


def added(*terms):
    total = terms[0].astype(jnp.float32)
    for term in terms[1:]:
        total = total + term.astype(jnp.float32)
    return total.astype(jnp.bfloat16)


def project_and_share(attended, out_weight):
    (far_given,) = projected(attended, out_weight, (3,))
    far_got = swapped(far_given, "mp", 1)
    (far_kept,) = projected(attended, out_weight, (2,))
    far_sum = added(far_kept, far_got)
    near_given, near_kept = projected(attended, out_weight, (1, 0), (far_sum,))
    half = near_given.shape[0] // 2
    near_got = jnp.concatenate([swapped(near_given[:half], "mp", 1), swapped(near_given[half:], "mp", 1)])
    return added(near_kept, near_got, swapped(far_sum, "mp", 2))


def per_device(inputs, short_filter, long_filter, skip_gain, queries, key_rows, out_weight):
    rows, _, channels = inputs.shape
    count = lax.axis_size("ctx")
    taps = long_filter.shape[1]
    splits = channels % (count * HEAD_DIM) == 0 and count == COUNT and rows == taps
    if splits and lax.axis_size("mp") == 4:
        return by_heads(inputs, short_filter, long_filter, skip_gain, queries, key_rows, out_weight)
    attended = by_rows(inputs, short_filter, long_filter, skip_gain, queries, key_rows)
    partial_out = jnp.dot(attended, out_weight, preferred_element_type=jnp.float32)
    return lax.psum_scatter(partial_out.astype(jnp.bfloat16), "mp", scatter_dimension=1, tiled=True)


def solution(mesh):
    placed = (
        P(("parts", "ctx"), None, "mp"),
        P(None, None, "mp"),
        P("mp", None),
        P("mp"),
        P(("parts", "ctx"), "mp"),
        P(("parts", "ctx"), "mp"),
        P("mp", None),
    )
    return jax.shard_map(
        per_device, mesh=mesh, in_specs=placed, out_specs=P(("parts", "ctx"), "mp"), check_vma=False
    )
```

```python
import functools

import jax
import jax.numpy as jnp
from jax import lax
from jax.experimental import pallas as pl
from jax.experimental.pallas import tpu as pltpu
from jax.sharding import PartitionSpec as P

HEAD_DIM = 128
COUNT = 4
ORDER = (3, 2, 1, 0)
BACK = (2, 3, 1, 0)
EDGE = 16


masked_score = -1e30


def passed_along(value, axis, steps):
    count = lax.axis_size(axis)
    initial, last = (max(0, -steps), min(count, count - steps))
    return lax.ppermute(value, axis, [(source, source + steps) for source in range(initial, last)])


def toeplitz_taps(filters, row_count):
    group_count = filters.shape[0]
    tap_count = filters.shape[1]
    span = row_count + tap_count - 1
    flipped = filters[:, ::-1]
    padded_taps = jnp.concatenate(
        [flipped, jnp.zeros((group_count, row_count), filters.dtype)], axis=1
    )
    repeated = jnp.tile(padded_taps, (1, row_count))
    return repeated[:, : row_count * span].reshape(group_count, row_count, span)


def short_features(extended, short_filter, row_count):
    tap_count = short_filter.shape[0]
    features = jnp.zeros((row_count,) + extended.shape[1:], jnp.float32)
    for lag_index in range(tap_count):
        delayed = extended[
            tap_count - 1 - lag_index : tap_count - 1 - lag_index + row_count
        ].astype(jnp.float32)
        features = features + short_filter[lag_index].astype(jnp.float32)[None] * delayed
    return features


def attend(head_queries, query_pos, key_piece, value_piece):
    key_count = key_piece.shape[0]
    head_count = head_queries.shape[1]
    key_heads = key_piece.reshape(key_count, head_count, -1)
    value_heads = value_piece.reshape(key_count, head_count, -1)
    scores = jnp.einsum(
        "qhd,khd->hqk", head_queries, key_heads, preferred_element_type=jnp.float32
    ) * head_queries.shape[2] ** (-0.5)
    key_pos = lax.iota(jnp.int32, key_count)
    allowed = (key_pos[None, :] <= query_pos[:, None])[None]
    peak = jnp.max(jnp.where(allowed, scores, masked_score), axis=2)
    probabilities = jnp.where(allowed, jnp.exp(scores - peak[..., None]), 0.0)
    weight_sum = jnp.sum(probabilities, axis=2)
    mixed = jnp.einsum(
        "hqk,khd->hqd",
        probabilities.astype(jnp.bfloat16),
        value_heads,
        preferred_element_type=jnp.float32,
    )
    result = mixed / weight_sum[..., None]
    return jnp.transpose(result, (1, 0, 2)).reshape(result.shape[1], -1).astype(jnp.bfloat16)


def by_rows(inputs, short_filter, long_filter, skip_gain, queries, key_rows):
    row_count = inputs.shape[0]
    channels = inputs.shape[2]
    groups = long_filter.shape[0]
    tap_count = long_filter.shape[1]
    short_reach = short_filter.shape[0] - 1
    position = lax.axis_index("ctx")
    rim = passed_along(inputs[row_count - short_reach :], "ctx", 1)
    extended = jnp.concatenate([rim, inputs], axis=0)
    features = short_features(extended, short_filter, row_count)
    gate_product = (features[:, 1] * features[:, 2]).astype(jnp.bfloat16)
    gate_prev = passed_along(gate_product[row_count - (tap_count - 1) :], "ctx", 1)
    gate_ext = jnp.concatenate([gate_prev, gate_product], axis=0)
    toeplitz = toeplitz_taps(long_filter, row_count)
    filtered = jnp.einsum(
        "gtr,rgc->tgc",
        toeplitz,
        gate_ext.reshape(row_count + tap_count - 1, groups, channels // groups),
        preferred_element_type=jnp.float32,
    ).reshape(row_count, channels)
    values = (
        features[:, 0] * (filtered + skip_gain[None] * gate_product.astype(jnp.float32))
    ).astype(jnp.bfloat16)
    head_count = channels // HEAD_DIM
    head_queries = queries.reshape(row_count, head_count, HEAD_DIM)
    query_pos = position * row_count + lax.iota(jnp.int32, row_count)
    return attend(
        head_queries,
        query_pos,
        lax.all_gather(key_rows, "ctx", axis=0, tiled=True),
        lax.all_gather(values, "ctx", axis=0, tiled=True),
    )


def delayed(signal, lag):
    if lag == 0:
        return signal
    row = lax.broadcasted_iota(jnp.int32, signal.shape, 0)
    return jnp.where(row < lag, 0.0, pltpu.roll(signal, lag, 0))


def featured(signal, taps):
    total = taps[0] * signal
    for lag in range(1, len(taps)):
        total = total + taps[lag] * delayed(signal, lag)
    return total


def columns_of(block, width):
    return pl.ds(pl.multiple_of(block * width, width), width)


def write_gate(signals, taps, out_ref):
    rows, own = signals[0].shape
    edge_row = lax.broadcasted_iota(jnp.int32, (8, own), 0)
    features = [featured(signal, tap) for signal, tap in zip(signals, taps)]
    edges = [
        jnp.where(edge_row < 2, signal[:8], jnp.where(edge_row < 4, pltpu.roll(signal[rows - 8 :], 4, 0), 0.0))
        for signal in signals
    ]
    out_ref[0:rows] = (features[0] * features[1]).astype(jnp.bfloat16)
    out_ref[rows : rows + EDGE] = jnp.concatenate(edges, axis=0).astype(jnp.bfloat16)


def plain_kernel(inputs_any, queries_any, keys_any, *refs):
    out_refs, sems = refs[:COUNT], refs[COUNT]
    rows, own = queries_any.shape[0], out_refs[0].shape[1]
    position = lax.axis_index("ctx")
    copies = []
    for step in ORDER:
        columns = columns_of(position ^ step, own)
        for index, source in enumerate((queries_any, keys_any, inputs_any.at[0])):
            target = out_refs[step].at[index * rows : (index + 1) * rows]
            copies.append(pltpu.make_async_copy(source.at[:, columns], target, sems.at[len(copies)]))
    for copy in copies:
        copy.start()
    for copy in copies:
        copy.wait()


def gate_kernel(inputs_any, short_any, *refs):
    out_refs, (signal_s, short_s, sems) = refs[:COUNT], refs[COUNT:]
    own = out_refs[0].shape[1]
    position = lax.axis_index("ctx")
    copies = [
        pltpu.make_async_copy(short_any, short_s, sems.at[0]),
        pltpu.make_async_copy(inputs_any.at[1:3], signal_s, sems.at[1]),
    ]
    for copy in copies:
        copy.start()
    for copy in copies:
        copy.wait()
    for step in ORDER:
        columns = columns_of(position ^ step, own)
        signals = [signal_s[stream, :, columns].astype(jnp.float32) for stream in range(2)]
        taps = [
            [short_s[lag, stream : stream + 1, columns].astype(jnp.float32) for lag in range(3)] for stream in (1, 2)
        ]
        write_gate(signals, taps, out_refs[step])


def ready_kernel(filter_ref, weight_any, band_ref, weight_ref, sem):
    rows, span = band_ref.shape
    taps = filter_ref.shape[1]
    groups = rows // taps
    weights = pltpu.make_async_copy(weight_any, weight_ref, sem)
    weights.start()
    source = lax.broadcasted_iota(jnp.int32, (taps, span), 0)
    target = lax.broadcasted_iota(jnp.int32, (taps, span), 1)
    flip = (source + target == taps).astype(jnp.bfloat16)
    first_group = pl.multiple_of(lax.axis_index("ctx") * groups, groups)
    first = jnp.dot(filter_ref[pl.ds(first_group, groups)], flip, preferred_element_type=jnp.float32)
    for group in range(groups):
        repeated = jnp.broadcast_to(first[group : group + 1], (taps, span))
        banded = pltpu.roll(repeated, 0, 1, stride=1, stride_axis=0)
        band_ref[group * taps : (group + 1) * taps] = banded.astype(jnp.bfloat16)
    weights.wait()


def weights_kernel(third_ref, second_ref, near_ref, own_ref, weight_ref, total_ref, query_s, key_s):
    count = COUNT
    rows, own = query_s.shape[1:]
    position = lax.axis_index("ctx")
    for step, given in zip(ORDER, (third_ref, second_ref, near_ref, own_ref)):
        query_s[position ^ step] = given[0:rows]
        key_s[columns_of(position ^ step, rows)] = given[rows : 2 * rows]
    causal = lax.broadcasted_iota(jnp.int32, (rows, rows), 1) <= lax.broadcasted_iota(jnp.int32, (rows, rows), 0)
    for head in range(own // HEAD_DIM):
        columns = slice(head * HEAD_DIM, (head + 1) * HEAD_DIM)
        for block in range(count):
            here, seen = slice(block * rows, (block + 1) * rows), (block + 1) * rows
            scores = lax.dot_general(
                query_s[block, :, columns],
                key_s[0:seen, columns],
                (((1,), (1,)), ((), ())),
                preferred_element_type=jnp.float32,
            ) * HEAD_DIM ** (-0.5)
            own_scores = jnp.where(causal, scores[:, block * rows :], masked_score)
            pieces = [scores[:, : block * rows], own_scores] if block else [own_scores]
            scores = jnp.concatenate(pieces, axis=1)
            weights = jnp.exp(scores - jnp.max(scores, axis=1, keepdims=True))
            total_ref[here, head : head + 1] = jnp.sum(weights, axis=1, keepdims=True)
            weight_ref[head, here, 0:seen] = weights.astype(jnp.bfloat16)
            if seen < count * rows:
                weight_ref[head, here, seen:] = jnp.zeros((rows, count * rows - seen), jnp.bfloat16)


def mix_rows(block, weight_ref, total_ref, value_ref, out_refs):
    rows = sum(out_ref.shape[0] for out_ref in out_refs)
    own = value_ref.shape[1]
    here = columns_of(block, rows)
    for head in range(own // HEAD_DIM):
        columns = slice(head * HEAD_DIM, (head + 1) * HEAD_DIM)
        mixed = jnp.dot(weight_ref[head, here], value_ref[:, columns], preferred_element_type=jnp.float32)
        mixed = (mixed / total_ref[here, head : head + 1]).astype(jnp.bfloat16)
        start = 0
        for out_ref in out_refs:
            out_ref[:, columns] = mixed[start : start + out_ref.shape[0]]
            start += out_ref.shape[0]


def values_kernel(*refs):
    count = COUNT
    plain, gates = refs[:count], refs[count : 2 * count]
    band_ref, short_ref, gain_ref, weight_ref, total_ref = refs[2 * count : 2 * count + 5]
    third_refs, second_refs = refs[2 * count + 5 : 2 * count + 7], refs[2 * count + 7 : 2 * count + 9]
    value_ref, signal_s, gates_s, gate_s = refs[2 * count + 9 :]
    rows, own = plain[0].shape[0] // 3, plain[0].shape[1]
    per_group = own * rows // band_ref.shape[0]
    position = lax.axis_index("ctx")
    mine = columns_of(position, own)
    for step, given, gate in zip(ORDER, plain, gates):
        signal_s[columns_of(position ^ step, rows)] = given[2 * rows :]
        gates_s[position ^ step] = gate[...]
    taps = [
        [short_ref[lag, stream : stream + 1, mine].astype(jnp.float32) for lag in range(3)] for stream in range(3)
    ]
    gate_s[0:rows] = jnp.zeros((rows, own), jnp.bfloat16)
    edge_row = lax.broadcasted_iota(jnp.int32, (8, own), 0)
    head_row = lax.broadcasted_iota(jnp.int32, (16, own), 0)
    for block in range(count):
        gate_s[(block + 1) * rows : (block + 2) * rows] = gates_s[block, 0:rows]
        if block == 0:
            continue
        fixed = 1.0
        before = gates_s[block - 1, rows:].astype(jnp.float32)
        here = gates_s[block, rows:].astype(jnp.float32)
        for which, stream in enumerate((1, 2)):
            old = pltpu.roll(before[8 * which : 8 * which + 8], 6, 0)
            new = pltpu.roll(here[8 * which : 8 * which + 8], 2, 0)
            joined = jnp.where(edge_row < 2, old, new)
            fixed = fixed * (
                taps[stream][0] * pltpu.roll(joined, 6, 0)
                + taps[stream][1] * pltpu.roll(joined, 7, 0)
                + taps[stream][2] * joined
            )
        head = gates_s[block, 0:16].astype(jnp.float32)
        head = jnp.where(head_row < 2, jnp.concatenate([fixed, fixed], axis=0), head)
        gate_s[(block + 1) * rows : (block + 1) * rows + 16] = head.astype(jnp.bfloat16)
    feature = featured(signal_s[...].astype(jnp.float32), taps[0])
    gain = gain_ref[:, mine]
    per_tile = HEAD_DIM // per_group
    lane = lax.broadcasted_iota(jnp.int32, (rows, 2 * HEAD_DIM), 1) % HEAD_DIM // per_group
    for tile in range(own // HEAD_DIM):
        columns = slice(tile * HEAD_DIM, (tile + 1) * HEAD_DIM)
        for block in range(0, count, 2):
            windows = [gate_s[other * rows : (other + 2) * rows, columns] for other in (block, block + 1)]
            mixed = jnp.dot(
                band_ref[tile * per_tile * rows : (tile + 1) * per_tile * rows],
                jnp.concatenate(windows, axis=1),
                preferred_element_type=jnp.float32,
            )
            filtered = mixed[:rows]
            for group in range(1, per_tile):
                filtered = jnp.where(lane == group, mixed[group * rows : (group + 1) * rows], filtered)
            for index in range(2):
                here = slice((block + index) * rows, (block + index + 1) * rows)
                gate = gate_s[(block + index + 1) * rows : (block + index + 2) * rows, columns].astype(jnp.float32)
                part = filtered[:, index * HEAD_DIM : (index + 1) * HEAD_DIM]
                value_ref[here, columns] = (
                    feature[here, columns] * (part + gain[:, columns] * gate)
                ).astype(jnp.bfloat16)
    for step, out_refs in ((3, third_refs), (2, second_refs)):
        mix_rows(position ^ step, weight_ref, total_ref, value_ref, out_refs)


def near_rows_kernel(weight_ref, total_ref, value_ref, *refs):
    position = lax.axis_index("ctx")
    mix_rows(position ^ 1, weight_ref, total_ref, value_ref, refs[0:2])
    mix_rows(position, weight_ref, total_ref, value_ref, refs[2:4])


def project_kernel(masks, *refs):
    outs = len(masks)
    out_refs, attended_s = refs[-outs - 1 : -1], refs[-1]
    own = refs[0].shape[1]
    count = sum(ref.shape[1] == own for ref in refs)
    given, weight_ref = refs[:count], refs[count]
    width = out_refs[0].shape[1]
    position, here = lax.axis_index("ctx"), lax.axis_index("mp")
    start = 0
    for index, piece in enumerate(given):
        rows = piece.shape[0]
        attended_s[start : start + rows, columns_of(position ^ BACK[index % COUNT], own)] = piece[...]
        start += rows if index % COUNT == COUNT - 1 else 0
    for mask, out_ref in zip(masks, out_refs):
        out_ref[...] = jnp.dot(
            attended_s[...], weight_ref[:, columns_of(here ^ mask, width)], preferred_element_type=jnp.float32
        ).astype(jnp.bfloat16)


VMEM_LIMIT = 40 * 1024 * 1024
PLAIN_LIMIT = 53 * 1024 * 1024
GATE_LIMIT = 60 * 1024 * 1024
IN_HBM = pl.BlockSpec(memory_space=pltpu.HBM)
IN_VMEM = pl.BlockSpec(memory_space=pltpu.VMEM)
ANYWHERE = pl.BlockSpec(memory_space=pl.ANY)


def run_kernel(kernel, operands, outputs, scratch=(), spaces=None, limit=VMEM_LIMIT, cost=10**6):
    return pl.pallas_call(
        kernel,
        out_shape=[jax.ShapeDtypeStruct(shape, dtype) for shape, dtype in outputs],
        in_specs=spaces or [IN_VMEM] * len(operands),
        out_specs=[IN_VMEM] * len(outputs),
        scratch_shapes=scratch,
        compiler_params=pltpu.CompilerParams(vmem_limit_bytes=limit),
        cost_estimate=pl.CostEstimate(flops=cost, bytes_accessed=min(2**20, cost), transcendentals=0),
        name=getattr(kernel, "func", kernel).__name__,
    )(*operands)


def swapped(value, axis, step):
    return lax.ppermute(value, axis, [(source, source ^ step) for source in range(lax.axis_size(axis))])


def by_heads(inputs, short_filter, long_filter, skip_gain, queries, key_rows, out_weight):
    rows, streams, channels = inputs.shape
    own = channels // COUNT
    groups, taps = long_filter.shape
    half = jnp.bfloat16
    piece, window = ((rows, own), half), COUNT * rows
    streamed = jnp.transpose(inputs, (1, 0, 2))
    plain = run_kernel(
        plain_kernel,
        (streamed, queries, key_rows),
        [((3 * rows, own), half)] * COUNT,
        [pltpu.SemaphoreType.DMA((3 * COUNT,))],
        [IN_HBM] * 3,
        PLAIN_LIMIT,
    )
    gates = run_kernel(
        gate_kernel,
        (streamed, short_filter),
        [((rows + EDGE, own), half)] * COUNT,
        [
            pltpu.VMEM((2, rows, channels), half),
            pltpu.VMEM(short_filter.shape, half),
            pltpu.SemaphoreType.DMA((2,)),
        ],
        [IN_HBM] * 2,
        GATE_LIMIT,
    )
    plain = [swapped(plain[step], "ctx", step) for step in ORDER[:3]] + [plain[0]]
    gates = [swapped(gates[step], "ctx", step) for step in ORDER[:3]] + [gates[0]]
    band, weight = run_kernel(
        ready_kernel,
        (long_filter, out_weight),
        [((groups // COUNT * taps, 2 * taps), half), (out_weight.shape, half)],
        [pltpu.SemaphoreType.DMA],
        [IN_VMEM, IN_HBM],
    )
    soft, totals = run_kernel(
        weights_kernel,
        plain,
        [((own // HEAD_DIM, window, window), half), ((window, HEAD_DIM), jnp.float32)],
        [pltpu.VMEM((COUNT, rows, own), half), pltpu.VMEM((window, own), half)],
    )
    sides = [((rows // 2, own), half), ((rows // 2, own), half)]
    *far, values = run_kernel(
        values_kernel,
        (*plain, *gates, band, short_filter, skip_gain.reshape(1, channels), soft, totals),
        sides * 2 + [((window, own), half)],
        [
            pltpu.VMEM((window, own), half),
            pltpu.VMEM((COUNT, rows + EDGE, own), half),
            pltpu.VMEM((window + rows, own), half),
        ],
    )
    near = run_kernel(near_rows_kernel, (soft, totals, values), sides * 2)
    halves = [
        [swapped(far[2 + side], "ctx", 2), swapped(far[side], "ctx", 3), swapped(near[side], "ctx", 1), near[2 + side]]
        for side in range(2)
    ]
    return project_and_share(halves, weight)


def projected(attended, out_weight, masks, after, cost):
    rows = sum(piece.shape[0] for piece in attended) // COUNT
    width = out_weight.shape[1] // lax.axis_size("mp")
    return run_kernel(
        functools.partial(project_kernel, masks),
        (*attended, out_weight, *after),
        [((rows, width), jnp.bfloat16)] * len(masks),
        [pltpu.VMEM((rows, out_weight.shape[0]), jnp.bfloat16)],
        [IN_VMEM] * (len(attended) + 1) + [ANYWHERE] * len(after),
        cost=cost,
    )


FAR_COST, NEAR_COST = 10**10, 10**3


def added(*terms):
    total = terms[0].astype(jnp.float32)
    for term in terms[1:]:
        total = total + term.astype(jnp.float32)
    return total.astype(jnp.bfloat16)


def project_and_share(halves, out_weight):
    crossed, after = [], ()
    for pieces in halves:
        (given,) = projected(pieces, out_weight, (3,), after, FAR_COST)
        got = swapped(given, "mp", 1)
        (kept,) = projected(pieces, out_weight, (2,), after, FAR_COST)
        far_sum = added(kept, got)
        after = (far_sum,)
        crossed.append(swapped(far_sum, "mp", 2))
    near_given, near_kept = projected(halves[0] + halves[1], out_weight, (1, 0), after, NEAR_COST)
    half = near_given.shape[0] // 2
    near_got = [swapped(near_given[:half], "mp", 1), swapped(near_given[half:], "mp", 1)]
    return added(near_kept, jnp.concatenate(near_got), jnp.concatenate(crossed))


def per_device(inputs, short_filter, long_filter, skip_gain, queries, key_rows, out_weight):
    rows, _, channels = inputs.shape
    count = lax.axis_size("ctx")
    taps = long_filter.shape[1]
    splits = channels % (count * HEAD_DIM) == 0 and count == COUNT and rows == taps
    if splits and lax.axis_size("mp") == 4:
        return by_heads(inputs, short_filter, long_filter, skip_gain, queries, key_rows, out_weight)
    attended = by_rows(inputs, short_filter, long_filter, skip_gain, queries, key_rows)
    partial_out = jnp.dot(attended, out_weight, preferred_element_type=jnp.float32)
    return lax.psum_scatter(partial_out.astype(jnp.bfloat16), "mp", scatter_dimension=1, tiled=True)


def solution(mesh):
    placed = (
        P(("parts", "ctx"), None, "mp"),
        P(None, None, "mp"),
        P("mp", None),
        P("mp"),
        P(("parts", "ctx"), "mp"),
        P(("parts", "ctx"), "mp"),
        P("mp", None),
    )
    return jax.shard_map(
        per_device, mesh=mesh, in_specs=placed, out_specs=P(("parts", "ctx"), "mp"), check_vma=False
    )
```

```python
import functools

import jax
import jax.numpy as jnp
from jax import lax
from jax.experimental import pallas as pl
from jax.experimental.pallas import tpu as pltpu
from jax.sharding import PartitionSpec as P

HEAD_DIM = 128
COUNT = 4
ORDER = (3, 2, 1, 0)
EDGE = 16


masked_score = -1e30


def passed_along(value, axis, steps):
    count = lax.axis_size(axis)
    initial, last = (max(0, -steps), min(count, count - steps))
    return lax.ppermute(value, axis, [(source, source + steps) for source in range(initial, last)])


def toeplitz_taps(filters, row_count):
    group_count = filters.shape[0]
    tap_count = filters.shape[1]
    span = row_count + tap_count - 1
    flipped = filters[:, ::-1]
    padded_taps = jnp.concatenate(
        [flipped, jnp.zeros((group_count, row_count), filters.dtype)], axis=1
    )
    repeated = jnp.tile(padded_taps, (1, row_count))
    return repeated[:, : row_count * span].reshape(group_count, row_count, span)


def short_features(extended, short_filter, row_count):
    tap_count = short_filter.shape[0]
    features = jnp.zeros((row_count,) + extended.shape[1:], jnp.float32)
    for lag_index in range(tap_count):
        delayed = extended[
            tap_count - 1 - lag_index : tap_count - 1 - lag_index + row_count
        ].astype(jnp.float32)
        features = features + short_filter[lag_index].astype(jnp.float32)[None] * delayed
    return features


def attend(head_queries, query_pos, key_piece, value_piece):
    key_count = key_piece.shape[0]
    head_count = head_queries.shape[1]
    key_heads = key_piece.reshape(key_count, head_count, -1)
    value_heads = value_piece.reshape(key_count, head_count, -1)
    scores = jnp.einsum(
        "qhd,khd->hqk", head_queries, key_heads, preferred_element_type=jnp.float32
    ) * head_queries.shape[2] ** (-0.5)
    key_pos = lax.iota(jnp.int32, key_count)
    allowed = (key_pos[None, :] <= query_pos[:, None])[None]
    peak = jnp.max(jnp.where(allowed, scores, masked_score), axis=2)
    probabilities = jnp.where(allowed, jnp.exp(scores - peak[..., None]), 0.0)
    weight_sum = jnp.sum(probabilities, axis=2)
    mixed = jnp.einsum(
        "hqk,khd->hqd",
        probabilities.astype(jnp.bfloat16),
        value_heads,
        preferred_element_type=jnp.float32,
    )
    result = mixed / weight_sum[..., None]
    return jnp.transpose(result, (1, 0, 2)).reshape(result.shape[1], -1).astype(jnp.bfloat16)


def by_rows(inputs, short_filter, long_filter, skip_gain, queries, key_rows):
    row_count = inputs.shape[0]
    channels = inputs.shape[2]
    groups = long_filter.shape[0]
    tap_count = long_filter.shape[1]
    short_reach = short_filter.shape[0] - 1
    position = lax.axis_index("ctx")
    rim = passed_along(inputs[row_count - short_reach :], "ctx", 1)
    extended = jnp.concatenate([rim, inputs], axis=0)
    features = short_features(extended, short_filter, row_count)
    gate_product = (features[:, 1] * features[:, 2]).astype(jnp.bfloat16)
    gate_prev = passed_along(gate_product[row_count - (tap_count - 1) :], "ctx", 1)
    gate_ext = jnp.concatenate([gate_prev, gate_product], axis=0)
    toeplitz = toeplitz_taps(long_filter, row_count)
    filtered = jnp.einsum(
        "gtr,rgc->tgc",
        toeplitz,
        gate_ext.reshape(row_count + tap_count - 1, groups, channels // groups),
        preferred_element_type=jnp.float32,
    ).reshape(row_count, channels)
    values = (
        features[:, 0] * (filtered + skip_gain[None] * gate_product.astype(jnp.float32))
    ).astype(jnp.bfloat16)
    head_count = channels // HEAD_DIM
    head_queries = queries.reshape(row_count, head_count, HEAD_DIM)
    query_pos = position * row_count + lax.iota(jnp.int32, row_count)
    return attend(
        head_queries,
        query_pos,
        lax.all_gather(key_rows, "ctx", axis=0, tiled=True),
        lax.all_gather(values, "ctx", axis=0, tiled=True),
    )


def delayed(signal, lag):
    if lag == 0:
        return signal
    row = lax.broadcasted_iota(jnp.int32, signal.shape, 0)
    return jnp.where(row < lag, 0.0, pltpu.roll(signal, lag, 0))


def featured(signal, taps):
    total = taps[0] * signal
    for lag in range(1, len(taps)):
        total = total + taps[lag] * delayed(signal, lag)
    return total


def columns_of(block, width):
    return pl.ds(pl.multiple_of(block * width, width), width)


def write_gate(signals, taps, out_ref):
    rows, own = signals[0].shape
    edge_row = lax.broadcasted_iota(jnp.int32, (8, own), 0)
    features = [featured(signal, tap) for signal, tap in zip(signals, taps)]
    edges = [
        jnp.where(edge_row < 2, signal[:8], jnp.where(edge_row < 4, pltpu.roll(signal[rows - 8 :], 4, 0), 0.0))
        for signal in signals
    ]
    out_ref[0:rows] = (features[0] * features[1]).astype(jnp.bfloat16)
    out_ref[rows : rows + EDGE] = jnp.concatenate(edges, axis=0).astype(jnp.bfloat16)


def plain_kernel(inputs_any, queries_any, keys_any, *refs):
    out_refs, sems = refs[:COUNT], refs[COUNT]
    rows, own = queries_any.shape[0], out_refs[0].shape[1]
    position = lax.axis_index("ctx")
    copies = []
    for step in ORDER:
        columns = columns_of(position ^ step, own)
        for index, source in enumerate((queries_any, keys_any, inputs_any.at[0])):
            target = out_refs[step].at[index * rows : (index + 1) * rows]
            copies.append(pltpu.make_async_copy(source.at[:, columns], target, sems.at[len(copies)]))
    for copy in copies:
        copy.start()
    for copy in copies:
        copy.wait()


def gate_kernel(inputs_any, short_any, *refs):
    out_refs, (signal_s, short_s, sems) = refs[:COUNT], refs[COUNT:]
    own = out_refs[0].shape[1]
    position = lax.axis_index("ctx")
    copies = [
        pltpu.make_async_copy(short_any, short_s, sems.at[0]),
        pltpu.make_async_copy(inputs_any.at[1:3], signal_s, sems.at[1]),
    ]
    for copy in copies:
        copy.start()
    for copy in copies:
        copy.wait()
    for step in ORDER:
        columns = columns_of(position ^ step, own)
        signals = [signal_s[stream, :, columns].astype(jnp.float32) for stream in range(2)]
        taps = [
            [short_s[lag, stream : stream + 1, columns].astype(jnp.float32) for lag in range(3)] for stream in (1, 2)
        ]
        write_gate(signals, taps, out_refs[step])


def ready_kernel(filter_ref, weight_any, band_ref, weight_ref, sem):
    rows, span = band_ref.shape
    taps = filter_ref.shape[1]
    groups = rows // taps
    weights = pltpu.make_async_copy(weight_any, weight_ref, sem)
    weights.start()
    source = lax.broadcasted_iota(jnp.int32, (taps, span), 0)
    target = lax.broadcasted_iota(jnp.int32, (taps, span), 1)
    flip = (source + target == taps).astype(jnp.bfloat16)
    first_group = pl.multiple_of(lax.axis_index("ctx") * groups, groups)
    first = jnp.dot(filter_ref[pl.ds(first_group, groups)], flip, preferred_element_type=jnp.float32)
    for group in range(groups):
        repeated = jnp.broadcast_to(first[group : group + 1], (taps, span))
        banded = pltpu.roll(repeated, 0, 1, stride=1, stride_axis=0)
        band_ref[group * taps : (group + 1) * taps] = banded.astype(jnp.bfloat16)
    weights.wait()


def weights_kernel(third_ref, second_ref, near_ref, own_ref, short_ref, weight_ref, total_ref, feature_ref, query_s, key_s, signal_s):
    count = COUNT
    rows, own = query_s.shape[1:]
    position = lax.axis_index("ctx")
    for step, given in zip(ORDER, (third_ref, second_ref, near_ref, own_ref)):
        query_s[position ^ step] = given[0:rows]
        key_s[columns_of(position ^ step, rows)] = given[rows : 2 * rows]
        signal_s[columns_of(position ^ step, rows)] = given[2 * rows :]
    taps = [short_ref[lag, 0:1, columns_of(position, own)].astype(jnp.float32) for lag in range(3)]
    feature_ref[...] = featured(signal_s[...].astype(jnp.float32), taps)
    causal = lax.broadcasted_iota(jnp.int32, (rows, rows), 1) <= lax.broadcasted_iota(jnp.int32, (rows, rows), 0)
    for head in range(own // HEAD_DIM):
        columns = slice(head * HEAD_DIM, (head + 1) * HEAD_DIM)
        for block in range(count):
            here, seen = slice(block * rows, (block + 1) * rows), (block + 1) * rows
            scores = lax.dot_general(
                query_s[block, :, columns],
                key_s[0:seen, columns],
                (((1,), (1,)), ((), ())),
                preferred_element_type=jnp.float32,
            ) * HEAD_DIM ** (-0.5)
            own_scores = jnp.where(causal, scores[:, block * rows :], masked_score)
            pieces = [scores[:, : block * rows], own_scores] if block else [own_scores]
            scores = jnp.concatenate(pieces, axis=1)
            weights = jnp.exp(scores - jnp.max(scores, axis=1, keepdims=True))
            total_ref[here, head : head + 1] = jnp.sum(weights, axis=1, keepdims=True)
            weight_ref[head, here, 0:seen] = weights.astype(jnp.bfloat16)
            if seen < count * rows:
                weight_ref[head, here, seen:] = jnp.zeros((rows, count * rows - seen), jnp.bfloat16)


def mix_rows(block, weight_ref, total_ref, value_ref, out_ref):
    rows = out_ref.shape[0]
    here = columns_of(block, rows)
    for head in range(out_ref.shape[1] // HEAD_DIM):
        columns = slice(head * HEAD_DIM, (head + 1) * HEAD_DIM)
        mixed = jnp.dot(weight_ref[head, here], value_ref[:, columns], preferred_element_type=jnp.float32)
        out_ref[:, columns] = (mixed / total_ref[here, head : head + 1]).astype(jnp.bfloat16)


def values_kernel(*refs):
    count = COUNT
    gates, feature_ref = refs[:count], refs[count]
    band_ref, short_ref, gain_ref, weight_ref, total_ref = refs[count + 1 : count + 6]
    third_ref, second_ref, value_ref = refs[count + 6 : count + 9]
    gates_s, gate_s = refs[count + 9 :]
    rows, own = second_ref.shape
    per_group = own * rows // band_ref.shape[0]
    position = lax.axis_index("ctx")
    mine = columns_of(position, own)
    for step, gate in zip(ORDER, gates):
        gates_s[position ^ step] = gate[...]
    taps = [
        [short_ref[lag, stream : stream + 1, mine].astype(jnp.float32) for lag in range(3)] for stream in range(3)
    ]
    gate_s[0:rows] = jnp.zeros((rows, own), jnp.bfloat16)
    edge_row = lax.broadcasted_iota(jnp.int32, (8, own), 0)
    head_row = lax.broadcasted_iota(jnp.int32, (16, own), 0)
    for block in range(count):
        gate_s[(block + 1) * rows : (block + 2) * rows] = gates_s[block, 0:rows]
        if block == 0:
            continue
        fixed = 1.0
        before = gates_s[block - 1, rows:].astype(jnp.float32)
        here = gates_s[block, rows:].astype(jnp.float32)
        for which, stream in enumerate((1, 2)):
            old = pltpu.roll(before[8 * which : 8 * which + 8], 6, 0)
            new = pltpu.roll(here[8 * which : 8 * which + 8], 2, 0)
            joined = jnp.where(edge_row < 2, old, new)
            fixed = fixed * (
                taps[stream][0] * pltpu.roll(joined, 6, 0)
                + taps[stream][1] * pltpu.roll(joined, 7, 0)
                + taps[stream][2] * joined
            )
        head = gates_s[block, 0:16].astype(jnp.float32)
        head = jnp.where(head_row < 2, jnp.concatenate([fixed, fixed], axis=0), head)
        gate_s[(block + 1) * rows : (block + 1) * rows + 16] = head.astype(jnp.bfloat16)
    gain = gain_ref[:, mine]
    per_tile = HEAD_DIM // per_group
    lane = lax.broadcasted_iota(jnp.int32, (rows, 2 * HEAD_DIM), 1) % HEAD_DIM // per_group
    for tile in range(own // HEAD_DIM):
        columns = slice(tile * HEAD_DIM, (tile + 1) * HEAD_DIM)
        for block in range(0, count, 2):
            windows = [gate_s[other * rows : (other + 2) * rows, columns] for other in (block, block + 1)]
            mixed = jnp.dot(
                band_ref[tile * per_tile * rows : (tile + 1) * per_tile * rows],
                jnp.concatenate(windows, axis=1),
                preferred_element_type=jnp.float32,
            )
            filtered = mixed[:rows]
            for group in range(1, per_tile):
                filtered = jnp.where(lane == group, mixed[group * rows : (group + 1) * rows], filtered)
            for index in range(2):
                here = slice((block + index) * rows, (block + index + 1) * rows)
                gate = gate_s[(block + index + 1) * rows : (block + index + 2) * rows, columns].astype(jnp.float32)
                part = filtered[:, index * HEAD_DIM : (index + 1) * HEAD_DIM]
                value_ref[here, columns] = (
                    feature_ref[here, columns] * (part + gain[:, columns] * gate)
                ).astype(jnp.bfloat16)
    for step, out_ref in ((3, third_ref), (2, second_ref)):
        mix_rows(position ^ step, weight_ref, total_ref, value_ref, out_ref)


def near_rows_kernel(weight_ref, total_ref, value_ref, *refs):
    upper_ref, lower_ref, own_ref, near_s = refs
    half = upper_ref.shape[0]
    position = lax.axis_index("ctx")
    mix_rows(position ^ 1, weight_ref, total_ref, value_ref, near_s)
    upper_ref[...] = near_s[0:half]
    lower_ref[...] = near_s[half:]
    mix_rows(position, weight_ref, total_ref, value_ref, own_ref)


def project_kernel(spans, *refs):
    given, weight_ref = refs[:5], refs[5]
    out_refs, attended_s = refs[-1 - len(spans) : -1], refs[-1]
    second, third, upper, lower, mine = given
    half = upper.shape[0]
    rows, own = mine.shape
    position, here = lax.axis_index("ctx"), lax.axis_index("mp")
    attended_s[0:half, columns_of(position ^ 1, own)] = upper[...]
    attended_s[half:, columns_of(position ^ 1, own)] = lower[...]
    for step, piece in ((0, mine), (2, second), (3, third)):
        attended_s[:, columns_of(position ^ step, own)] = piece[...]
    for (mask, part, parts), out_ref in zip(spans, out_refs):
        columns = columns_of((here ^ mask) * parts + part, out_ref.shape[1])
        out_ref[...] = jnp.dot(
            attended_s[...], weight_ref[:, columns], preferred_element_type=jnp.float32
        ).astype(jnp.bfloat16)


VMEM_LIMIT = 40 * 1024 * 1024
PLAIN_LIMIT = 53 * 1024 * 1024
GATE_LIMIT = 60 * 1024 * 1024
IN_HBM = pl.BlockSpec(memory_space=pltpu.HBM)
IN_VMEM = pl.BlockSpec(memory_space=pltpu.VMEM)
ANYWHERE = pl.BlockSpec(memory_space=pl.ANY)


def run_kernel(kernel, operands, outputs, scratch=(), spaces=None, limit=VMEM_LIMIT, cost=10**6):
    return pl.pallas_call(
        kernel,
        out_shape=[jax.ShapeDtypeStruct(shape, dtype) for shape, dtype in outputs],
        in_specs=spaces or [IN_VMEM] * len(operands),
        out_specs=[IN_VMEM] * len(outputs),
        scratch_shapes=scratch,
        compiler_params=pltpu.CompilerParams(vmem_limit_bytes=limit),
        cost_estimate=pl.CostEstimate(flops=cost, bytes_accessed=2**20, transcendentals=0),
        name=getattr(kernel, "func", kernel).__name__,
    )(*operands)


def swapped(value, axis, step):
    return lax.ppermute(value, axis, [(source, source ^ step) for source in range(lax.axis_size(axis))])


def by_heads(inputs, short_filter, long_filter, skip_gain, queries, key_rows, out_weight):
    rows, streams, channels = inputs.shape
    own = channels // COUNT
    groups, taps = long_filter.shape
    half = jnp.bfloat16
    piece, window = ((rows, own), half), COUNT * rows
    streamed = jnp.transpose(inputs, (1, 0, 2))
    plain = run_kernel(
        plain_kernel,
        (streamed, queries, key_rows),
        [((3 * rows, own), half)] * COUNT,
        [pltpu.SemaphoreType.DMA((3 * COUNT,))],
        [IN_HBM] * 3,
        PLAIN_LIMIT,
    )
    gates = run_kernel(
        gate_kernel,
        (streamed, short_filter),
        [((rows + EDGE, own), half)] * COUNT,
        [
            pltpu.VMEM((2, rows, channels), half),
            pltpu.VMEM(short_filter.shape, half),
            pltpu.SemaphoreType.DMA((2,)),
        ],
        [IN_HBM] * 2,
        GATE_LIMIT,
    )
    plain = [swapped(plain[step], "ctx", step) for step in ORDER[:3]] + [plain[0]]
    gates = [swapped(gates[step], "ctx", step) for step in ORDER[:3]] + [gates[0]]
    band, weight = run_kernel(
        ready_kernel,
        (long_filter, out_weight),
        [((groups // COUNT * taps, 2 * taps), half), (out_weight.shape, half)],
        [pltpu.SemaphoreType.DMA],
        [IN_VMEM, IN_HBM],
    )
    soft, totals, feature = run_kernel(
        weights_kernel,
        (*plain, short_filter),
        [
            ((own // HEAD_DIM, window, window), half),
            ((window, HEAD_DIM), jnp.float32),
            ((window, own), jnp.float32),
        ],
        [
            pltpu.VMEM((COUNT, rows, own), half),
            pltpu.VMEM((window, own), half),
            pltpu.VMEM((window, own), half),
        ],
    )
    third, second, values = run_kernel(
        values_kernel,
        (*gates, feature, band, short_filter, skip_gain.reshape(1, channels), soft, totals),
        [piece, piece, ((window, own), half)],
        [
            pltpu.VMEM((COUNT, rows + EDGE, own), half),
            pltpu.VMEM((window + rows, own), half),
        ],
    )
    third_got, second_got = swapped(third, "ctx", 3), swapped(second, "ctx", 2)
    upper, lower, mine = run_kernel(
        near_rows_kernel,
        (soft, totals, values),
        [((rows // 2, own), half)] * 2 + [piece],
        [pltpu.VMEM((rows, own), half)],
    )
    near = (swapped(upper, "ctx", 1), swapped(lower, "ctx", 1))
    return project_and_share((second_got, third_got, *near, mine), weight)


def projected(attended, out_weight, spans, after=(), cost=10**6):
    rows = attended[-1].shape[0]
    width = out_weight.shape[1] // lax.axis_size("mp")
    return run_kernel(
        functools.partial(project_kernel, spans),
        (*attended, out_weight, *after),
        [((rows, width // parts), jnp.bfloat16) for _, _, parts in spans],
        [pltpu.VMEM((rows, out_weight.shape[0]), jnp.bfloat16)],
        [IN_VMEM] * (len(attended) + 1) + [ANYWHERE] * len(after),
        cost=cost,
    )


FAR_COST, NEAR_COST = 10**6, 10**6


def added(*terms):
    total = terms[0].astype(jnp.float32)
    for term in terms[1:]:
        total = total + term.astype(jnp.float32)
    return total.astype(jnp.bfloat16)


def project_and_share(attended, out_weight):
    crossed, after = [], ()
    for part in range(2):
        given, kept = projected(attended, out_weight, ((3, part, 2), (2, part, 2)), after, FAR_COST)
        after = (given,)
        far_sum = added(kept, swapped(given, "mp", 1))
        crossed.append(swapped(far_sum, "mp", 2))
    near_given, near_kept = projected(attended, out_weight, ((1, 0, 1), (0, 0, 1)), (far_sum,), NEAR_COST)
    half = near_given.shape[0] // 2
    near_got = jnp.concatenate([swapped(near_given[:half], "mp", 1), swapped(near_given[half:], "mp", 1)])
    return added(near_kept, near_got, jnp.concatenate(crossed, axis=1))


def per_device(inputs, short_filter, long_filter, skip_gain, queries, key_rows, out_weight):
    rows, _, channels = inputs.shape
    count = lax.axis_size("ctx")
    taps = long_filter.shape[1]
    splits = channels % (count * HEAD_DIM) == 0 and count == COUNT and rows == taps
    if splits and lax.axis_size("mp") == 4:
        return by_heads(inputs, short_filter, long_filter, skip_gain, queries, key_rows, out_weight)
    attended = by_rows(inputs, short_filter, long_filter, skip_gain, queries, key_rows)
    partial_out = jnp.dot(attended, out_weight, preferred_element_type=jnp.float32)
    return lax.psum_scatter(partial_out.astype(jnp.bfloat16), "mp", scatter_dimension=1, tiled=True)


def solution(mesh):
    placed = (
        P(("parts", "ctx"), None, "mp"),
        P(None, None, "mp"),
        P("mp", None),
        P("mp"),
        P(("parts", "ctx"), "mp"),
        P(("parts", "ctx"), "mp"),
        P("mp", None),
    )
    return jax.shard_map(
        per_device, mesh=mesh, in_specs=placed, out_specs=P(("parts", "ctx"), "mp"), check_vma=False
    )
```

```python
import functools

import jax
import jax.numpy as jnp
from jax import lax
from jax.experimental import pallas as pl
from jax.experimental.pallas import tpu as pltpu
from jax.sharding import PartitionSpec as P

HEAD_DIM = 128
COUNT = 4
ORDER = (3, 2, 1, 0)
EDGE = 16


masked_score = -1e30


def passed_along(value, axis, steps):
    count = lax.axis_size(axis)
    initial, last = (max(0, -steps), min(count, count - steps))
    return lax.ppermute(value, axis, [(source, source + steps) for source in range(initial, last)])


def toeplitz_taps(filters, row_count):
    group_count = filters.shape[0]
    tap_count = filters.shape[1]
    span = row_count + tap_count - 1
    flipped = filters[:, ::-1]
    padded_taps = jnp.concatenate(
        [flipped, jnp.zeros((group_count, row_count), filters.dtype)], axis=1
    )
    repeated = jnp.tile(padded_taps, (1, row_count))
    return repeated[:, : row_count * span].reshape(group_count, row_count, span)


def short_features(extended, short_filter, row_count):
    tap_count = short_filter.shape[0]
    features = jnp.zeros((row_count,) + extended.shape[1:], jnp.float32)
    for lag_index in range(tap_count):
        delayed = extended[
            tap_count - 1 - lag_index : tap_count - 1 - lag_index + row_count
        ].astype(jnp.float32)
        features = features + short_filter[lag_index].astype(jnp.float32)[None] * delayed
    return features


def attend(head_queries, query_pos, key_piece, value_piece):
    key_count = key_piece.shape[0]
    head_count = head_queries.shape[1]
    key_heads = key_piece.reshape(key_count, head_count, -1)
    value_heads = value_piece.reshape(key_count, head_count, -1)
    scores = jnp.einsum(
        "qhd,khd->hqk", head_queries, key_heads, preferred_element_type=jnp.float32
    ) * head_queries.shape[2] ** (-0.5)
    key_pos = lax.iota(jnp.int32, key_count)
    allowed = (key_pos[None, :] <= query_pos[:, None])[None]
    peak = jnp.max(jnp.where(allowed, scores, masked_score), axis=2)
    probabilities = jnp.where(allowed, jnp.exp(scores - peak[..., None]), 0.0)
    weight_sum = jnp.sum(probabilities, axis=2)
    mixed = jnp.einsum(
        "hqk,khd->hqd",
        probabilities.astype(jnp.bfloat16),
        value_heads,
        preferred_element_type=jnp.float32,
    )
    result = mixed / weight_sum[..., None]
    return jnp.transpose(result, (1, 0, 2)).reshape(result.shape[1], -1).astype(jnp.bfloat16)


def by_rows(inputs, short_filter, long_filter, skip_gain, queries, key_rows):
    row_count = inputs.shape[0]
    channels = inputs.shape[2]
    groups = long_filter.shape[0]
    tap_count = long_filter.shape[1]
    short_reach = short_filter.shape[0] - 1
    position = lax.axis_index("ctx")
    rim = passed_along(inputs[row_count - short_reach :], "ctx", 1)
    extended = jnp.concatenate([rim, inputs], axis=0)
    features = short_features(extended, short_filter, row_count)
    gate_product = (features[:, 1] * features[:, 2]).astype(jnp.bfloat16)
    gate_prev = passed_along(gate_product[row_count - (tap_count - 1) :], "ctx", 1)
    gate_ext = jnp.concatenate([gate_prev, gate_product], axis=0)
    toeplitz = toeplitz_taps(long_filter, row_count)
    filtered = jnp.einsum(
        "gtr,rgc->tgc",
        toeplitz,
        gate_ext.reshape(row_count + tap_count - 1, groups, channels // groups),
        preferred_element_type=jnp.float32,
    ).reshape(row_count, channels)
    values = (
        features[:, 0] * (filtered + skip_gain[None] * gate_product.astype(jnp.float32))
    ).astype(jnp.bfloat16)
    head_count = channels // HEAD_DIM
    head_queries = queries.reshape(row_count, head_count, HEAD_DIM)
    query_pos = position * row_count + lax.iota(jnp.int32, row_count)
    return attend(
        head_queries,
        query_pos,
        lax.all_gather(key_rows, "ctx", axis=0, tiled=True),
        lax.all_gather(values, "ctx", axis=0, tiled=True),
    )


def delayed(signal, lag):
    if lag == 0:
        return signal
    row = lax.broadcasted_iota(jnp.int32, signal.shape, 0)
    return jnp.where(row < lag, 0.0, pltpu.roll(signal, lag, 0))


def featured(signal, taps):
    total = taps[0] * signal
    for lag in range(1, len(taps)):
        total = total + taps[lag] * delayed(signal, lag)
    return total


def columns_of(block, width):
    return pl.ds(pl.multiple_of(block * width, width), width)


def write_gate(signals, taps, out_ref):
    rows, own = signals[0].shape
    edge_row = lax.broadcasted_iota(jnp.int32, (8, own), 0)
    features = [featured(signal, tap) for signal, tap in zip(signals, taps)]
    edges = [
        jnp.where(edge_row < 2, signal[:8], jnp.where(edge_row < 4, pltpu.roll(signal[rows - 8 :], 4, 0), 0.0))
        for signal in signals
    ]
    out_ref[0:rows] = (features[0] * features[1]).astype(jnp.bfloat16)
    out_ref[rows : rows + EDGE] = jnp.concatenate(edges, axis=0).astype(jnp.bfloat16)


def plain_copies(sources, out_refs, steps, sems):
    rows, own = sources[0].shape[0], out_refs[0].shape[1]
    position = lax.axis_index("ctx")
    copies = []
    for step, out_ref in zip(steps, out_refs):
        columns = columns_of(position ^ step, own)
        for index, source in enumerate(sources):
            target = out_ref.at[index * rows : (index + 1) * rows]
            copies.append(pltpu.make_async_copy(source.at[:, columns], target, sems.at[len(copies)]))
    for copy in copies:
        copy.start()
    return copies


def plain_kernel(inputs_any, queries_any, keys_any, *refs):
    for copy in plain_copies((queries_any, keys_any, inputs_any.at[0]), refs[:2], ORDER[:2], refs[2]):
        copy.wait()


def gate_kernel(inputs_any, short_any, queries_any, keys_any, *refs):
    out_refs, plain_refs = refs[:COUNT], refs[COUNT : COUNT + 2]
    signal_s, short_s, sems, plain_sems = refs[COUNT + 2 :]
    own = out_refs[0].shape[1]
    position = lax.axis_index("ctx")
    copies = [
        pltpu.make_async_copy(short_any, short_s, sems.at[0]),
        pltpu.make_async_copy(inputs_any.at[1:3], signal_s, sems.at[1]),
    ]
    for copy in copies:
        copy.start()
    plain = plain_copies((queries_any, keys_any, inputs_any.at[0]), plain_refs, ORDER[2:], plain_sems)
    for copy in copies:
        copy.wait()
    for step in ORDER:
        columns = columns_of(position ^ step, own)
        signals = [signal_s[stream, :, columns].astype(jnp.float32) for stream in range(2)]
        taps = [
            [short_s[lag, stream : stream + 1, columns].astype(jnp.float32) for lag in range(3)] for stream in (1, 2)
        ]
        write_gate(signals, taps, out_refs[step])
    for copy in plain:
        copy.wait()


def ready_kernel(filter_ref, weight_any, band_ref, weight_ref, sem):
    rows, span = band_ref.shape
    taps = filter_ref.shape[1]
    groups = rows // taps
    weights = pltpu.make_async_copy(weight_any, weight_ref, sem)
    weights.start()
    source = lax.broadcasted_iota(jnp.int32, (taps, span), 0)
    target = lax.broadcasted_iota(jnp.int32, (taps, span), 1)
    flip = (source + target == taps).astype(jnp.bfloat16)
    first_group = pl.multiple_of(lax.axis_index("ctx") * groups, groups)
    first = jnp.dot(filter_ref[pl.ds(first_group, groups)], flip, preferred_element_type=jnp.float32)
    for group in range(groups):
        repeated = jnp.broadcast_to(first[group : group + 1], (taps, span))
        banded = pltpu.roll(repeated, 0, 1, stride=1, stride_axis=0)
        band_ref[group * taps : (group + 1) * taps] = banded.astype(jnp.bfloat16)
    weights.wait()


def weights_kernel(third_ref, second_ref, near_ref, own_ref, short_ref, weight_ref, total_ref, feature_ref, query_s, key_s, signal_s):
    count = COUNT
    rows, own = query_s.shape[1:]
    position = lax.axis_index("ctx")
    for step, given in zip(ORDER, (third_ref, second_ref, near_ref, own_ref)):
        query_s[position ^ step] = given[0:rows]
        key_s[columns_of(position ^ step, rows)] = given[rows : 2 * rows]
        signal_s[columns_of(position ^ step, rows)] = given[2 * rows :]
    taps = [short_ref[lag, 0:1, columns_of(position, own)].astype(jnp.float32) for lag in range(3)]
    feature_ref[...] = featured(signal_s[...].astype(jnp.float32), taps)
    causal = lax.broadcasted_iota(jnp.int32, (rows, rows), 1) <= lax.broadcasted_iota(jnp.int32, (rows, rows), 0)
    for head in range(own // HEAD_DIM):
        columns = slice(head * HEAD_DIM, (head + 1) * HEAD_DIM)
        for block in range(count):
            here, seen = slice(block * rows, (block + 1) * rows), (block + 1) * rows
            scores = lax.dot_general(
                query_s[block, :, columns],
                key_s[0:seen, columns],
                (((1,), (1,)), ((), ())),
                preferred_element_type=jnp.float32,
            ) * HEAD_DIM ** (-0.5)
            own_scores = jnp.where(causal, scores[:, block * rows :], masked_score)
            pieces = [scores[:, : block * rows], own_scores] if block else [own_scores]
            scores = jnp.concatenate(pieces, axis=1)
            weights = jnp.exp(scores - jnp.max(scores, axis=1, keepdims=True))
            total_ref[here, head : head + 1] = jnp.sum(weights, axis=1, keepdims=True)
            weight_ref[head, here, 0:seen] = weights.astype(jnp.bfloat16)
            if seen < count * rows:
                weight_ref[head, here, seen:] = jnp.zeros((rows, count * rows - seen), jnp.bfloat16)


def mix_rows(block, weight_ref, total_ref, value_ref, out_ref):
    rows = out_ref.shape[0]
    here = columns_of(block, rows)
    for head in range(out_ref.shape[1] // HEAD_DIM):
        columns = slice(head * HEAD_DIM, (head + 1) * HEAD_DIM)
        mixed = jnp.dot(weight_ref[head, here], value_ref[:, columns], preferred_element_type=jnp.float32)
        out_ref[:, columns] = (mixed / total_ref[here, head : head + 1]).astype(jnp.bfloat16)


def values_kernel(*refs):
    count = COUNT
    gates, feature_ref = refs[:count], refs[count]
    band_ref, short_ref, gain_ref, weight_ref, total_ref = refs[count + 1 : count + 6]
    third_ref, second_ref, value_ref = refs[count + 6 : count + 9]
    gates_s, gate_s, filtered_s = refs[count + 9 :]
    rows, own = second_ref.shape
    per_group = own * rows // band_ref.shape[0]
    position = lax.axis_index("ctx")
    mine = columns_of(position, own)
    for step, gate in zip(ORDER, gates):
        gates_s[position ^ step] = gate[...]
    taps = [
        [short_ref[lag, stream : stream + 1, mine].astype(jnp.float32) for lag in range(3)] for stream in range(3)
    ]
    gate_s[0:rows] = jnp.zeros((rows, own), jnp.bfloat16)
    edge_row = lax.broadcasted_iota(jnp.int32, (8, own), 0)
    head_row = lax.broadcasted_iota(jnp.int32, (16, own), 0)
    for block in range(count):
        gate_s[(block + 1) * rows : (block + 2) * rows] = gates_s[block, 0:rows]
        if block == 0:
            continue
        fixed = 1.0
        before = gates_s[block - 1, rows:].astype(jnp.float32)
        here = gates_s[block, rows:].astype(jnp.float32)
        for which, stream in enumerate((1, 2)):
            old = pltpu.roll(before[8 * which : 8 * which + 8], 6, 0)
            new = pltpu.roll(here[8 * which : 8 * which + 8], 2, 0)
            joined = jnp.where(edge_row < 2, old, new)
            fixed = fixed * (
                taps[stream][0] * pltpu.roll(joined, 6, 0)
                + taps[stream][1] * pltpu.roll(joined, 7, 0)
                + taps[stream][2] * joined
            )
        head = gates_s[block, 0:16].astype(jnp.float32)
        head = jnp.where(head_row < 2, jnp.concatenate([fixed, fixed], axis=0), head)
        gate_s[(block + 1) * rows : (block + 1) * rows + 16] = head.astype(jnp.bfloat16)
    gain = gain_ref[:, mine]
    chunk = 2 * HEAD_DIM // count
    in_chunk = chunk // per_group
    lane = lax.broadcasted_iota(jnp.int32, (rows, 2 * HEAD_DIM), 1) % chunk // per_group
    for part in range(own // chunk):
        columns = slice(part * chunk, (part + 1) * chunk)
        windows = [gate_s[block * rows : (block + 2) * rows, columns] for block in range(count)]
        mixed = jnp.dot(
            band_ref[part * in_chunk * rows : (part + 1) * in_chunk * rows],
            jnp.concatenate(windows, axis=1),
            preferred_element_type=jnp.float32,
        )
        filtered = mixed[:rows]
        for group in range(1, in_chunk):
            filtered = jnp.where(lane == group, mixed[group * rows : (group + 1) * rows], filtered)
        for block in range(count):
            filtered_s[block * rows : (block + 1) * rows, columns] = filtered[:, block * chunk : (block + 1) * chunk]
    value_ref[...] = (
        feature_ref[...] * (filtered_s[...] + gain * gate_s[rows:].astype(jnp.float32))
    ).astype(jnp.bfloat16)
    for step, out_ref in ((3, third_ref), (2, second_ref)):
        mix_rows(position ^ step, weight_ref, total_ref, value_ref, out_ref)


def near_rows_kernel(weight_ref, total_ref, value_ref, *refs):
    upper_ref, lower_ref, own_ref, near_s = refs
    half = upper_ref.shape[0]
    position = lax.axis_index("ctx")
    mix_rows(position ^ 1, weight_ref, total_ref, value_ref, near_s)
    upper_ref[...] = near_s[0:half]
    lower_ref[...] = near_s[half:]
    mix_rows(position, weight_ref, total_ref, value_ref, own_ref)


def project_kernel(spans, *refs):
    given, weight_ref = refs[:5], refs[5]
    out_refs, attended_s = refs[-1 - len(spans) : -1], refs[-1]
    second, third, upper, lower, mine = given
    half = upper.shape[0]
    rows, own = mine.shape
    position, here = lax.axis_index("ctx"), lax.axis_index("mp")
    attended_s[0:half, columns_of(position ^ 1, own)] = upper[...]
    attended_s[half:, columns_of(position ^ 1, own)] = lower[...]
    for step, piece in ((0, mine), (2, second), (3, third)):
        attended_s[:, columns_of(position ^ step, own)] = piece[...]
    for (mask, part, parts), out_ref in zip(spans, out_refs):
        columns = columns_of((here ^ mask) * parts + part, out_ref.shape[1])
        out_ref[...] = jnp.dot(
            attended_s[...], weight_ref[:, columns], preferred_element_type=jnp.float32
        ).astype(jnp.bfloat16)


VMEM_LIMIT = 40 * 1024 * 1024
PLAIN_LIMIT = 53 * 1024 * 1024 + 400 * 1024
GATE_LIMIT = 60 * 1024 * 1024
IN_HBM = pl.BlockSpec(memory_space=pltpu.HBM)
IN_VMEM = pl.BlockSpec(memory_space=pltpu.VMEM)
ANYWHERE = pl.BlockSpec(memory_space=pl.ANY)


def run_kernel(kernel, operands, outputs, scratch=(), spaces=None, limit=VMEM_LIMIT, cost=10**6):
    return pl.pallas_call(
        kernel,
        out_shape=[jax.ShapeDtypeStruct(shape, dtype) for shape, dtype in outputs],
        in_specs=spaces or [IN_VMEM] * len(operands),
        out_specs=[IN_VMEM] * len(outputs),
        scratch_shapes=scratch,
        compiler_params=pltpu.CompilerParams(vmem_limit_bytes=limit),
        cost_estimate=pl.CostEstimate(flops=cost, bytes_accessed=2**20, transcendentals=0),
        name=getattr(kernel, "func", kernel).__name__,
    )(*operands)


def swapped(value, axis, step):
    return lax.ppermute(value, axis, [(source, source ^ step) for source in range(lax.axis_size(axis))])


def by_heads(inputs, short_filter, long_filter, skip_gain, queries, key_rows, out_weight):
    rows, streams, channels = inputs.shape
    own = channels // COUNT
    groups, taps = long_filter.shape
    half = jnp.bfloat16
    piece, window = ((rows, own), half), COUNT * rows
    streamed = jnp.transpose(inputs, (1, 0, 2))
    far_plain = run_kernel(
        plain_kernel,
        (streamed, queries, key_rows),
        [((3 * rows, own), half)] * 2,
        [pltpu.SemaphoreType.DMA((6,))],
        [IN_HBM] * 3,
        PLAIN_LIMIT,
    )
    *gates, near_plain, own_plain = run_kernel(
        gate_kernel,
        (streamed, short_filter, queries, key_rows),
        [((rows + EDGE, own), half)] * COUNT + [((3 * rows, own), half)] * 2,
        [
            pltpu.VMEM((2, rows, channels), half),
            pltpu.VMEM(short_filter.shape, half),
            pltpu.SemaphoreType.DMA((2,)),
            pltpu.SemaphoreType.DMA((6,)),
        ],
        [IN_HBM] * 4,
        GATE_LIMIT,
    )
    plain = [own_plain, near_plain, far_plain[1], far_plain[0]]
    plain = [swapped(plain[step], "ctx", step) for step in ORDER[:3]] + [plain[0]]
    gates = [swapped(gates[step], "ctx", step) for step in ORDER[:3]] + [gates[0]]
    band, weight = run_kernel(
        ready_kernel,
        (long_filter, out_weight),
        [((groups // COUNT * taps, 2 * taps), half), (out_weight.shape, half)],
        [pltpu.SemaphoreType.DMA],
        [IN_VMEM, IN_HBM],
    )
    soft, totals, feature = run_kernel(
        weights_kernel,
        (*plain, short_filter),
        [
            ((own // HEAD_DIM, window, window), half),
            ((window, HEAD_DIM), jnp.float32),
            ((window, own), jnp.float32),
        ],
        [
            pltpu.VMEM((COUNT, rows, own), half),
            pltpu.VMEM((window, own), half),
            pltpu.VMEM((window, own), half),
        ],
    )
    third, second, values = run_kernel(
        values_kernel,
        (*gates, feature, band, short_filter, skip_gain.reshape(1, channels), soft, totals),
        [piece, piece, ((window, own), half)],
        [
            pltpu.VMEM((COUNT, rows + EDGE, own), half),
            pltpu.VMEM((window + rows, own), half),
            pltpu.VMEM((window, own), jnp.float32),
        ],
    )
    third_got, second_got = swapped(third, "ctx", 3), swapped(second, "ctx", 2)
    upper, lower, mine = run_kernel(
        near_rows_kernel,
        (soft, totals, values),
        [((rows // 2, own), half)] * 2 + [piece],
        [pltpu.VMEM((rows, own), half)],
    )
    near = (swapped(upper, "ctx", 1), swapped(lower, "ctx", 1))
    return project_and_share((second_got, third_got, *near, mine), weight)


def projected(attended, out_weight, spans, after=(), cost=10**6):
    rows = attended[-1].shape[0]
    width = out_weight.shape[1] // lax.axis_size("mp")
    return run_kernel(
        functools.partial(project_kernel, spans),
        (*attended, out_weight, *after),
        [((rows, width // parts), jnp.bfloat16) for _, _, parts in spans],
        [pltpu.VMEM((rows, out_weight.shape[0]), jnp.bfloat16)],
        [IN_VMEM] * (len(attended) + 1) + [ANYWHERE] * len(after),
        cost=cost,
    )


FAR_COST, NEAR_COST = 10**6, 10**6


def added(*terms):
    total = terms[0].astype(jnp.float32)
    for term in terms[1:]:
        total = total + term.astype(jnp.float32)
    return total.astype(jnp.bfloat16)


def project_and_share(attended, out_weight):
    crossed, after = [], ()
    for part in range(2):
        given, kept = projected(attended, out_weight, ((3, part, 2), (2, part, 2)), after, FAR_COST)
        after = (given,)
        far_sum = added(kept, swapped(given, "mp", 1))
        crossed.append(swapped(far_sum, "mp", 2))
    near_given, near_kept = projected(attended, out_weight, ((1, 0, 1), (0, 0, 1)), (far_sum,), NEAR_COST)
    half = near_given.shape[0] // 2
    near_got = jnp.concatenate([swapped(near_given[:half], "mp", 1), swapped(near_given[half:], "mp", 1)])
    return added(near_kept, near_got, jnp.concatenate(crossed, axis=1))


def per_device(inputs, short_filter, long_filter, skip_gain, queries, key_rows, out_weight):
    rows, _, channels = inputs.shape
    count = lax.axis_size("ctx")
    taps = long_filter.shape[1]
    splits = channels % (count * HEAD_DIM) == 0 and count == COUNT and rows == taps
    if splits and lax.axis_size("mp") == 4:
        return by_heads(inputs, short_filter, long_filter, skip_gain, queries, key_rows, out_weight)
    attended = by_rows(inputs, short_filter, long_filter, skip_gain, queries, key_rows)
    partial_out = jnp.dot(attended, out_weight, preferred_element_type=jnp.float32)
    return lax.psum_scatter(partial_out.astype(jnp.bfloat16), "mp", scatter_dimension=1, tiled=True)


def solution(mesh):
    placed = (
        P(("parts", "ctx"), None, "mp"),
        P(None, None, "mp"),
        P("mp", None),
        P("mp"),
        P(("parts", "ctx"), "mp"),
        P(("parts", "ctx"), "mp"),
        P("mp", None),
    )
    return jax.shard_map(
        per_device, mesh=mesh, in_specs=placed, out_specs=P(("parts", "ctx"), "mp"), check_vma=False
    )
```

```python
import functools

import jax
import jax.numpy as jnp
from jax import lax
from jax.experimental import pallas as pl
from jax.experimental.pallas import tpu as pltpu
from jax.sharding import PartitionSpec as P

HEAD_DIM = 128
COUNT = 4
ORDER = (2, 3, 1, 0)
EDGE = 16


masked_score = -1e30


def passed_along(value, axis, steps):
    count = lax.axis_size(axis)
    initial, last = (max(0, -steps), min(count, count - steps))
    return lax.ppermute(value, axis, [(source, source + steps) for source in range(initial, last)])


def toeplitz_taps(filters, row_count):
    group_count = filters.shape[0]
    tap_count = filters.shape[1]
    span = row_count + tap_count - 1
    flipped = filters[:, ::-1]
    padded_taps = jnp.concatenate(
        [flipped, jnp.zeros((group_count, row_count), filters.dtype)], axis=1
    )
    repeated = jnp.tile(padded_taps, (1, row_count))
    return repeated[:, : row_count * span].reshape(group_count, row_count, span)


def short_features(extended, short_filter, row_count):
    tap_count = short_filter.shape[0]
    features = jnp.zeros((row_count,) + extended.shape[1:], jnp.float32)
    for lag_index in range(tap_count):
        delayed = extended[
            tap_count - 1 - lag_index : tap_count - 1 - lag_index + row_count
        ].astype(jnp.float32)
        features = features + short_filter[lag_index].astype(jnp.float32)[None] * delayed
    return features


def attend(head_queries, query_pos, key_piece, value_piece):
    key_count = key_piece.shape[0]
    head_count = head_queries.shape[1]
    key_heads = key_piece.reshape(key_count, head_count, -1)
    value_heads = value_piece.reshape(key_count, head_count, -1)
    scores = jnp.einsum(
        "qhd,khd->hqk", head_queries, key_heads, preferred_element_type=jnp.float32
    ) * head_queries.shape[2] ** (-0.5)
    key_pos = lax.iota(jnp.int32, key_count)
    allowed = (key_pos[None, :] <= query_pos[:, None])[None]
    peak = jnp.max(jnp.where(allowed, scores, masked_score), axis=2)
    probabilities = jnp.where(allowed, jnp.exp(scores - peak[..., None]), 0.0)
    weight_sum = jnp.sum(probabilities, axis=2)
    mixed = jnp.einsum(
        "hqk,khd->hqd",
        probabilities.astype(jnp.bfloat16),
        value_heads,
        preferred_element_type=jnp.float32,
    )
    result = mixed / weight_sum[..., None]
    return jnp.transpose(result, (1, 0, 2)).reshape(result.shape[1], -1).astype(jnp.bfloat16)


def by_rows(inputs, short_filter, long_filter, skip_gain, queries, key_rows):
    row_count = inputs.shape[0]
    channels = inputs.shape[2]
    groups = long_filter.shape[0]
    tap_count = long_filter.shape[1]
    short_reach = short_filter.shape[0] - 1
    position = lax.axis_index("ctx")
    rim = passed_along(inputs[row_count - short_reach :], "ctx", 1)
    extended = jnp.concatenate([rim, inputs], axis=0)
    features = short_features(extended, short_filter, row_count)
    gate_product = (features[:, 1] * features[:, 2]).astype(jnp.bfloat16)
    gate_prev = passed_along(gate_product[row_count - (tap_count - 1) :], "ctx", 1)
    gate_ext = jnp.concatenate([gate_prev, gate_product], axis=0)
    toeplitz = toeplitz_taps(long_filter, row_count)
    filtered = jnp.einsum(
        "gtr,rgc->tgc",
        toeplitz,
        gate_ext.reshape(row_count + tap_count - 1, groups, channels // groups),
        preferred_element_type=jnp.float32,
    ).reshape(row_count, channels)
    values = (
        features[:, 0] * (filtered + skip_gain[None] * gate_product.astype(jnp.float32))
    ).astype(jnp.bfloat16)
    head_count = channels // HEAD_DIM
    head_queries = queries.reshape(row_count, head_count, HEAD_DIM)
    query_pos = position * row_count + lax.iota(jnp.int32, row_count)
    return attend(
        head_queries,
        query_pos,
        lax.all_gather(key_rows, "ctx", axis=0, tiled=True),
        lax.all_gather(values, "ctx", axis=0, tiled=True),
    )


def delayed(signal, lag):
    if lag == 0:
        return signal
    row = lax.broadcasted_iota(jnp.int32, signal.shape, 0)
    return jnp.where(row < lag, 0.0, pltpu.roll(signal, lag, 0))


def featured(signal, taps):
    total = taps[0] * signal
    for lag in range(1, len(taps)):
        total = total + taps[lag] * delayed(signal, lag)
    return total


def columns_of(block, width):
    return pl.ds(pl.multiple_of(block * width, width), width)


def write_gate(signals, taps, out_ref):
    rows, own = signals[0].shape
    edge_row = lax.broadcasted_iota(jnp.int32, (8, own), 0)
    features = [featured(signal, tap) for signal, tap in zip(signals, taps)]
    edges = [
        jnp.where(edge_row < 2, signal[:8], jnp.where(edge_row < 4, pltpu.roll(signal[rows - 8 :], 4, 0), 0.0))
        for signal in signals
    ]
    out_ref[0:rows] = (features[0] * features[1]).astype(jnp.bfloat16)
    out_ref[rows : rows + EDGE] = jnp.concatenate(edges, axis=0).astype(jnp.bfloat16)


def plain_copies(sources, out_refs, steps, sems):
    rows, own = sources[0].shape[0], out_refs[0].shape[1]
    position = lax.axis_index("ctx")
    copies = []
    for step, out_ref in zip(steps, out_refs):
        columns = columns_of(position ^ step, own)
        for index, source in enumerate(sources):
            target = out_ref.at[index * rows : (index + 1) * rows]
            copies.append(pltpu.make_async_copy(source.at[:, columns], target, sems.at[len(copies)]))
    for copy in copies:
        copy.start()
    return copies


def plain_kernel(inputs_any, queries_any, keys_any, *refs):
    for copy in plain_copies((queries_any, keys_any, inputs_any.at[0]), refs[:2], ORDER[:2], refs[2]):
        copy.wait()


def gate_kernel(inputs_any, short_any, queries_any, keys_any, *refs):
    out_refs, plain_refs = refs[:COUNT], refs[COUNT : COUNT + 2]
    signal_s, short_s, sems, plain_sems = refs[COUNT + 2 :]
    own = out_refs[0].shape[1]
    position = lax.axis_index("ctx")
    copies = [
        pltpu.make_async_copy(short_any, short_s, sems.at[0]),
        pltpu.make_async_copy(inputs_any.at[1:3], signal_s, sems.at[1]),
    ]
    for copy in copies:
        copy.start()
    plain = plain_copies((queries_any, keys_any, inputs_any.at[0]), plain_refs, ORDER[2:], plain_sems)
    for copy in copies:
        copy.wait()
    for step in ORDER:
        columns = columns_of(position ^ step, own)
        signals = [signal_s[stream, :, columns].astype(jnp.float32) for stream in range(2)]
        taps = [
            [short_s[lag, stream : stream + 1, columns].astype(jnp.float32) for lag in range(3)] for stream in (1, 2)
        ]
        write_gate(signals, taps, out_refs[step])
    for copy in plain:
        copy.wait()


def ready_kernel(filter_ref, weight_any, band_ref, weight_ref, sem):
    rows, span = band_ref.shape
    taps = filter_ref.shape[1]
    groups = rows // taps
    weights = pltpu.make_async_copy(weight_any, weight_ref, sem)
    weights.start()
    source = lax.broadcasted_iota(jnp.int32, (taps, span), 0)
    target = lax.broadcasted_iota(jnp.int32, (taps, span), 1)
    flip = (source + target == taps).astype(jnp.bfloat16)
    first_group = pl.multiple_of(lax.axis_index("ctx") * groups, groups)
    first = jnp.dot(filter_ref[pl.ds(first_group, groups)], flip, preferred_element_type=jnp.float32)
    for group in range(groups):
        repeated = jnp.broadcast_to(first[group : group + 1], (taps, span))
        banded = pltpu.roll(repeated, 0, 1, stride=1, stride_axis=0)
        band_ref[group * taps : (group + 1) * taps] = banded.astype(jnp.bfloat16)
    weights.wait()


def weights_kernel(second_ref, third_ref, near_ref, own_ref, short_ref, weight_ref, total_ref, feature_ref, query_s, key_s, signal_s):
    count = COUNT
    rows, own = query_s.shape[1:]
    position = lax.axis_index("ctx")
    for step, given in zip(ORDER, (second_ref, third_ref, near_ref, own_ref)):
        query_s[position ^ step] = given[0:rows]
        key_s[columns_of(position ^ step, rows)] = given[rows : 2 * rows]
        signal_s[columns_of(position ^ step, rows)] = given[2 * rows :]
    taps = [short_ref[lag, 0:1, columns_of(position, own)].astype(jnp.float32) for lag in range(3)]
    feature_ref[...] = featured(signal_s[...].astype(jnp.float32), taps)
    causal = lax.broadcasted_iota(jnp.int32, (rows, rows), 1) <= lax.broadcasted_iota(jnp.int32, (rows, rows), 0)
    for head in range(own // HEAD_DIM):
        columns = slice(head * HEAD_DIM, (head + 1) * HEAD_DIM)
        for block in range(count):
            here, seen = slice(block * rows, (block + 1) * rows), (block + 1) * rows
            scores = lax.dot_general(
                query_s[block, :, columns],
                key_s[0:seen, columns],
                (((1,), (1,)), ((), ())),
                preferred_element_type=jnp.float32,
            ) * HEAD_DIM ** (-0.5)
            own_scores = jnp.where(causal, scores[:, block * rows :], masked_score)
            pieces = [scores[:, : block * rows], own_scores] if block else [own_scores]
            scores = jnp.concatenate(pieces, axis=1)
            weights = jnp.exp(scores - jnp.max(scores, axis=1, keepdims=True))
            total_ref[here, head : head + 1] = jnp.sum(weights, axis=1, keepdims=True)
            weight_ref[head, here, 0:seen] = weights.astype(jnp.bfloat16)
            if seen < count * rows:
                weight_ref[head, here, seen:] = jnp.zeros((rows, count * rows - seen), jnp.bfloat16)


def mix_rows(block, weight_ref, total_ref, value_ref, out_ref):
    rows = out_ref.shape[0]
    here = columns_of(block, rows)
    for head in range(out_ref.shape[1] // HEAD_DIM):
        columns = slice(head * HEAD_DIM, (head + 1) * HEAD_DIM)
        mixed = jnp.dot(weight_ref[head, here], value_ref[:, columns], preferred_element_type=jnp.float32)
        out_ref[:, columns] = (mixed / total_ref[here, head : head + 1]).astype(jnp.bfloat16)


def values_kernel(*refs):
    count = COUNT
    gates, feature_ref = refs[:count], refs[count]
    band_ref, short_ref, gain_ref, weight_ref, total_ref = refs[count + 1 : count + 6]
    third_ref, second_ref, value_ref = refs[count + 6 : count + 9]
    gates_s, gate_s, filtered_s = refs[count + 9 :]
    rows, own = second_ref.shape
    per_group = own * rows // band_ref.shape[0]
    position = lax.axis_index("ctx")
    mine = columns_of(position, own)
    for step, gate in zip(ORDER, gates):
        gates_s[position ^ step] = gate[...]
    taps = [
        [short_ref[lag, stream : stream + 1, mine].astype(jnp.float32) for lag in range(3)] for stream in range(3)
    ]
    gate_s[0:rows] = jnp.zeros((rows, own), jnp.bfloat16)
    edge_row = lax.broadcasted_iota(jnp.int32, (8, own), 0)
    head_row = lax.broadcasted_iota(jnp.int32, (16, own), 0)
    for block in range(count):
        gate_s[(block + 1) * rows : (block + 2) * rows] = gates_s[block, 0:rows]
        if block == 0:
            continue
        fixed = 1.0
        before = gates_s[block - 1, rows:].astype(jnp.float32)
        here = gates_s[block, rows:].astype(jnp.float32)
        for which, stream in enumerate((1, 2)):
            old = pltpu.roll(before[8 * which : 8 * which + 8], 6, 0)
            new = pltpu.roll(here[8 * which : 8 * which + 8], 2, 0)
            joined = jnp.where(edge_row < 2, old, new)
            fixed = fixed * (
                taps[stream][0] * pltpu.roll(joined, 6, 0)
                + taps[stream][1] * pltpu.roll(joined, 7, 0)
                + taps[stream][2] * joined
            )
        head = gates_s[block, 0:16].astype(jnp.float32)
        head = jnp.where(head_row < 2, jnp.concatenate([fixed, fixed], axis=0), head)
        gate_s[(block + 1) * rows : (block + 1) * rows + 16] = head.astype(jnp.bfloat16)
    gain = gain_ref[:, mine]
    chunk = 2 * HEAD_DIM // count
    in_chunk = chunk // per_group
    lane = lax.broadcasted_iota(jnp.int32, (rows, 2 * HEAD_DIM), 1) % chunk // per_group
    for part in range(own // chunk):
        columns = slice(part * chunk, (part + 1) * chunk)
        windows = [gate_s[block * rows : (block + 2) * rows, columns] for block in range(count)]
        mixed = jnp.dot(
            band_ref[part * in_chunk * rows : (part + 1) * in_chunk * rows],
            jnp.concatenate(windows, axis=1),
            preferred_element_type=jnp.float32,
        )
        filtered = mixed[:rows]
        for group in range(1, in_chunk):
            filtered = jnp.where(lane == group, mixed[group * rows : (group + 1) * rows], filtered)
        for block in range(count):
            filtered_s[block * rows : (block + 1) * rows, columns] = filtered[:, block * chunk : (block + 1) * chunk]
    value_ref[...] = (
        feature_ref[...] * (filtered_s[...] + gain * gate_s[rows:].astype(jnp.float32))
    ).astype(jnp.bfloat16)
    for step, out_ref in ((3, third_ref), (2, second_ref)):
        mix_rows(position ^ step, weight_ref, total_ref, value_ref, out_ref)


def near_rows_kernel(weight_ref, total_ref, value_ref, *refs):
    upper_ref, lower_ref, own_ref, near_s = refs
    half = upper_ref.shape[0]
    position = lax.axis_index("ctx")
    mix_rows(position ^ 1, weight_ref, total_ref, value_ref, near_s)
    upper_ref[...] = near_s[0:half]
    lower_ref[...] = near_s[half:]
    mix_rows(position, weight_ref, total_ref, value_ref, own_ref)


def project_kernel(spans, *refs):
    given, weight_ref = refs[:5], refs[5]
    out_refs, attended_s = refs[-1 - len(spans) : -1], refs[-1]
    second, third, upper, lower, mine = given
    half = upper.shape[0]
    rows, own = mine.shape
    position, here = lax.axis_index("ctx"), lax.axis_index("mp")
    attended_s[0:half, columns_of(position ^ 1, own)] = upper[...]
    attended_s[half:, columns_of(position ^ 1, own)] = lower[...]
    for step, piece in ((0, mine), (2, second), (3, third)):
        attended_s[:, columns_of(position ^ step, own)] = piece[...]
    for (mask, part, parts), out_ref in zip(spans, out_refs):
        columns = columns_of((here ^ mask) * parts + part, out_ref.shape[1])
        out_ref[...] = jnp.dot(
            attended_s[...], weight_ref[:, columns], preferred_element_type=jnp.float32
        ).astype(jnp.bfloat16)


VMEM_LIMIT = 40 * 1024 * 1024
PLAIN_LIMIT = 53 * 1024 * 1024 + 400 * 1024
GATE_LIMIT = 60 * 1024 * 1024
IN_HBM = pl.BlockSpec(memory_space=pltpu.HBM)
IN_VMEM = pl.BlockSpec(memory_space=pltpu.VMEM)
ANYWHERE = pl.BlockSpec(memory_space=pl.ANY)


def run_kernel(kernel, operands, outputs, scratch=(), spaces=None, limit=VMEM_LIMIT, cost=10**6):
    return pl.pallas_call(
        kernel,
        out_shape=[jax.ShapeDtypeStruct(shape, dtype) for shape, dtype in outputs],
        in_specs=spaces or [IN_VMEM] * len(operands),
        out_specs=[IN_VMEM] * len(outputs),
        scratch_shapes=scratch,
        compiler_params=pltpu.CompilerParams(vmem_limit_bytes=limit),
        cost_estimate=pl.CostEstimate(flops=cost, bytes_accessed=2**20, transcendentals=0),
        name=getattr(kernel, "func", kernel).__name__,
    )(*operands)


def swapped(value, axis, step):
    return lax.ppermute(value, axis, [(source, source ^ step) for source in range(lax.axis_size(axis))])


def by_heads(inputs, short_filter, long_filter, skip_gain, queries, key_rows, out_weight):
    rows, streams, channels = inputs.shape
    own = channels // COUNT
    groups, taps = long_filter.shape
    half = jnp.bfloat16
    piece, window = ((rows, own), half), COUNT * rows
    streamed = jnp.transpose(inputs, (1, 0, 2))
    far_plain = run_kernel(
        plain_kernel,
        (streamed, queries, key_rows),
        [((3 * rows, own), half)] * 2,
        [pltpu.SemaphoreType.DMA((6,))],
        [IN_HBM] * 3,
        PLAIN_LIMIT,
    )
    *gates, near_plain, own_plain = run_kernel(
        gate_kernel,
        (streamed, short_filter, queries, key_rows),
        [((rows + EDGE, own), half)] * COUNT + [((3 * rows, own), half)] * 2,
        [
            pltpu.VMEM((2, rows, channels), half),
            pltpu.VMEM(short_filter.shape, half),
            pltpu.SemaphoreType.DMA((2,)),
            pltpu.SemaphoreType.DMA((6,)),
        ],
        [IN_HBM] * 4,
        GATE_LIMIT,
    )
    plain = [own_plain, near_plain, *far_plain]
    plain = [swapped(plain[step], "ctx", step) for step in ORDER[:3]] + [plain[0]]
    gates = [swapped(gates[step], "ctx", step) for step in ORDER[:3]] + [gates[0]]
    band, weight = run_kernel(
        ready_kernel,
        (long_filter, out_weight),
        [((groups // COUNT * taps, 2 * taps), half), (out_weight.shape, half)],
        [pltpu.SemaphoreType.DMA],
        [IN_VMEM, IN_HBM],
    )
    soft, totals, feature = run_kernel(
        weights_kernel,
        (*plain, short_filter),
        [
            ((own // HEAD_DIM, window, window), half),
            ((window, HEAD_DIM), jnp.float32),
            ((window, own), jnp.float32),
        ],
        [
            pltpu.VMEM((COUNT, rows, own), half),
            pltpu.VMEM((window, own), half),
            pltpu.VMEM((window, own), half),
        ],
    )
    third, second, values = run_kernel(
        values_kernel,
        (*gates, feature, band, short_filter, skip_gain.reshape(1, channels), soft, totals),
        [piece, piece, ((window, own), half)],
        [
            pltpu.VMEM((COUNT, rows + EDGE, own), half),
            pltpu.VMEM((window + rows, own), half),
            pltpu.VMEM((window, own), jnp.float32),
        ],
    )
    third_got, second_got = swapped(third, "ctx", 3), swapped(second, "ctx", 2)
    upper, lower, mine = run_kernel(
        near_rows_kernel,
        (soft, totals, values),
        [((rows // 2, own), half)] * 2 + [piece],
        [pltpu.VMEM((rows, own), half)],
    )
    near = (swapped(upper, "ctx", 1), swapped(lower, "ctx", 1))
    return project_and_share((second_got, third_got, *near, mine), weight)


def projected(attended, out_weight, spans, after=(), cost=10**6):
    rows = attended[-1].shape[0]
    width = out_weight.shape[1] // lax.axis_size("mp")
    return run_kernel(
        functools.partial(project_kernel, spans),
        (*attended, out_weight, *after),
        [((rows, width // parts), jnp.bfloat16) for _, _, parts in spans],
        [pltpu.VMEM((rows, out_weight.shape[0]), jnp.bfloat16)],
        [IN_VMEM] * (len(attended) + 1) + [ANYWHERE] * len(after),
        cost=cost,
    )


FAR_COST, NEAR_COST = 10**6, 10**6


def added(*terms):
    total = terms[0].astype(jnp.float32)
    for term in terms[1:]:
        total = total + term.astype(jnp.float32)
    return total.astype(jnp.bfloat16)


def project_and_share(attended, out_weight):
    crossed, after = [], ()
    for part in range(2):
        given, kept = projected(attended, out_weight, ((3, part, 2), (2, part, 2)), after, FAR_COST)
        after = (given,)
        far_sum = added(kept, swapped(given, "mp", 1))
        crossed.append(swapped(far_sum, "mp", 2))
    near_given, near_kept = projected(attended, out_weight, ((1, 0, 1), (0, 0, 1)), (far_sum,), NEAR_COST)
    half = near_given.shape[0] // 2
    near_got = jnp.concatenate([swapped(near_given[:half], "mp", 1), swapped(near_given[half:], "mp", 1)])
    return added(near_kept, near_got, jnp.concatenate(crossed, axis=1))


def per_device(inputs, short_filter, long_filter, skip_gain, queries, key_rows, out_weight):
    rows, _, channels = inputs.shape
    count = lax.axis_size("ctx")
    taps = long_filter.shape[1]
    splits = channels % (count * HEAD_DIM) == 0 and count == COUNT and rows == taps
    if splits and lax.axis_size("mp") == 4:
        return by_heads(inputs, short_filter, long_filter, skip_gain, queries, key_rows, out_weight)
    attended = by_rows(inputs, short_filter, long_filter, skip_gain, queries, key_rows)
    partial_out = jnp.dot(attended, out_weight, preferred_element_type=jnp.float32)
    return lax.psum_scatter(partial_out.astype(jnp.bfloat16), "mp", scatter_dimension=1, tiled=True)


def solution(mesh):
    placed = (
        P(("parts", "ctx"), None, "mp"),
        P(None, None, "mp"),
        P("mp", None),
        P("mp"),
        P(("parts", "ctx"), "mp"),
        P(("parts", "ctx"), "mp"),
        P("mp", None),
    )
    return jax.shard_map(
        per_device, mesh=mesh, in_specs=placed, out_specs=P(("parts", "ctx"), "mp"), check_vma=False
    )
```

```python
import functools

import jax
import jax.numpy as jnp
from jax import lax
from jax.experimental import pallas as pl
from jax.experimental.pallas import tpu as pltpu
from jax.sharding import PartitionSpec as P

HEAD_DIM = 128
COUNT = 4
ORDER = (3, 2, 1, 0)
GATE_ORDER = (2, 3, 1, 0)
EDGE = 16


masked_score = -1e30


def passed_along(value, axis, steps):
    count = lax.axis_size(axis)
    initial, last = (max(0, -steps), min(count, count - steps))
    return lax.ppermute(value, axis, [(source, source + steps) for source in range(initial, last)])


def toeplitz_taps(filters, row_count):
    group_count = filters.shape[0]
    tap_count = filters.shape[1]
    span = row_count + tap_count - 1
    flipped = filters[:, ::-1]
    padded_taps = jnp.concatenate(
        [flipped, jnp.zeros((group_count, row_count), filters.dtype)], axis=1
    )
    repeated = jnp.tile(padded_taps, (1, row_count))
    return repeated[:, : row_count * span].reshape(group_count, row_count, span)


def short_features(extended, short_filter, row_count):
    tap_count = short_filter.shape[0]
    features = jnp.zeros((row_count,) + extended.shape[1:], jnp.float32)
    for lag_index in range(tap_count):
        delayed = extended[
            tap_count - 1 - lag_index : tap_count - 1 - lag_index + row_count
        ].astype(jnp.float32)
        features = features + short_filter[lag_index].astype(jnp.float32)[None] * delayed
    return features


def attend(head_queries, query_pos, key_piece, value_piece):
    key_count = key_piece.shape[0]
    head_count = head_queries.shape[1]
    key_heads = key_piece.reshape(key_count, head_count, -1)
    value_heads = value_piece.reshape(key_count, head_count, -1)
    scores = jnp.einsum(
        "qhd,khd->hqk", head_queries, key_heads, preferred_element_type=jnp.float32
    ) * head_queries.shape[2] ** (-0.5)
    key_pos = lax.iota(jnp.int32, key_count)
    allowed = (key_pos[None, :] <= query_pos[:, None])[None]
    peak = jnp.max(jnp.where(allowed, scores, masked_score), axis=2)
    probabilities = jnp.where(allowed, jnp.exp(scores - peak[..., None]), 0.0)
    weight_sum = jnp.sum(probabilities, axis=2)
    mixed = jnp.einsum(
        "hqk,khd->hqd",
        probabilities.astype(jnp.bfloat16),
        value_heads,
        preferred_element_type=jnp.float32,
    )
    result = mixed / weight_sum[..., None]
    return jnp.transpose(result, (1, 0, 2)).reshape(result.shape[1], -1).astype(jnp.bfloat16)


def by_rows(inputs, short_filter, long_filter, skip_gain, queries, key_rows):
    row_count = inputs.shape[0]
    channels = inputs.shape[2]
    groups = long_filter.shape[0]
    tap_count = long_filter.shape[1]
    short_reach = short_filter.shape[0] - 1
    position = lax.axis_index("ctx")
    rim = passed_along(inputs[row_count - short_reach :], "ctx", 1)
    extended = jnp.concatenate([rim, inputs], axis=0)
    features = short_features(extended, short_filter, row_count)
    gate_product = (features[:, 1] * features[:, 2]).astype(jnp.bfloat16)
    gate_prev = passed_along(gate_product[row_count - (tap_count - 1) :], "ctx", 1)
    gate_ext = jnp.concatenate([gate_prev, gate_product], axis=0)
    toeplitz = toeplitz_taps(long_filter, row_count)
    filtered = jnp.einsum(
        "gtr,rgc->tgc",
        toeplitz,
        gate_ext.reshape(row_count + tap_count - 1, groups, channels // groups),
        preferred_element_type=jnp.float32,
    ).reshape(row_count, channels)
    values = (
        features[:, 0] * (filtered + skip_gain[None] * gate_product.astype(jnp.float32))
    ).astype(jnp.bfloat16)
    head_count = channels // HEAD_DIM
    head_queries = queries.reshape(row_count, head_count, HEAD_DIM)
    query_pos = position * row_count + lax.iota(jnp.int32, row_count)
    return attend(
        head_queries,
        query_pos,
        lax.all_gather(key_rows, "ctx", axis=0, tiled=True),
        lax.all_gather(values, "ctx", axis=0, tiled=True),
    )


def delayed(signal, lag):
    if lag == 0:
        return signal
    row = lax.broadcasted_iota(jnp.int32, signal.shape, 0)
    return jnp.where(row < lag, 0.0, pltpu.roll(signal, lag, 0))


def featured(signal, taps):
    total = taps[0] * signal
    for lag in range(1, len(taps)):
        total = total + taps[lag] * delayed(signal, lag)
    return total


def columns_of(block, width):
    return pl.ds(pl.multiple_of(block * width, width), width)


def write_gate(signals, taps, out_ref):
    rows, own = signals[0].shape
    edge_row = lax.broadcasted_iota(jnp.int32, (8, own), 0)
    features = [featured(signal, tap) for signal, tap in zip(signals, taps)]
    edges = [
        jnp.where(edge_row < 2, signal[:8], jnp.where(edge_row < 4, pltpu.roll(signal[rows - 8 :], 4, 0), 0.0))
        for signal in signals
    ]
    out_ref[0:rows] = (features[0] * features[1]).astype(jnp.bfloat16)
    out_ref[rows : rows + EDGE] = jnp.concatenate(edges, axis=0).astype(jnp.bfloat16)


def plain_copies(sources, out_refs, steps, sems):
    rows, own = sources[0].shape[0], out_refs[0].shape[1]
    position = lax.axis_index("ctx")
    copies = []
    for step, out_ref in zip(steps, out_refs):
        columns = columns_of(position ^ step, own)
        for index, source in enumerate(sources):
            target = out_ref.at[index * rows : (index + 1) * rows]
            copies.append(pltpu.make_async_copy(source.at[:, columns], target, sems.at[len(copies)]))
    for copy in copies:
        copy.start()
    return copies


def plain_kernel(inputs_any, queries_any, keys_any, *refs):
    for copy in plain_copies((queries_any, keys_any, inputs_any.at[0]), refs[:2], ORDER[:2], refs[2]):
        copy.wait()


def gate_kernel(inputs_any, short_any, queries_any, keys_any, *refs):
    out_refs, plain_refs = refs[:COUNT], refs[COUNT : COUNT + 2]
    signal_s, short_s, sems, plain_sems = refs[COUNT + 2 :]
    own = out_refs[0].shape[1]
    position = lax.axis_index("ctx")
    copies = [
        pltpu.make_async_copy(short_any, short_s, sems.at[0]),
        pltpu.make_async_copy(inputs_any.at[1:3], signal_s, sems.at[1]),
    ]
    for copy in copies:
        copy.start()
    plain = plain_copies((queries_any, keys_any, inputs_any.at[0]), plain_refs, ORDER[2:], plain_sems)
    for copy in copies:
        copy.wait()
    for step in ORDER:
        columns = columns_of(position ^ step, own)
        signals = [signal_s[stream, :, columns].astype(jnp.float32) for stream in range(2)]
        taps = [
            [short_s[lag, stream : stream + 1, columns].astype(jnp.float32) for lag in range(3)] for stream in (1, 2)
        ]
        write_gate(signals, taps, out_refs[step])
    for copy in plain:
        copy.wait()


def ready_kernel(filter_ref, weight_any, band_ref, weight_ref, sem):
    rows, span = band_ref.shape
    taps = filter_ref.shape[1]
    groups = rows // taps
    weights = pltpu.make_async_copy(weight_any, weight_ref, sem)
    weights.start()
    source = lax.broadcasted_iota(jnp.int32, (taps, span), 0)
    target = lax.broadcasted_iota(jnp.int32, (taps, span), 1)
    flip = (source + target == taps).astype(jnp.bfloat16)
    first_group = pl.multiple_of(lax.axis_index("ctx") * groups, groups)
    first = jnp.dot(filter_ref[pl.ds(first_group, groups)], flip, preferred_element_type=jnp.float32)
    for group in range(groups):
        repeated = jnp.broadcast_to(first[group : group + 1], (taps, span))
        banded = pltpu.roll(repeated, 0, 1, stride=1, stride_axis=0)
        band_ref[group * taps : (group + 1) * taps] = banded.astype(jnp.bfloat16)
    weights.wait()


def weights_kernel(third_ref, second_ref, near_ref, own_ref, short_ref, weight_ref, total_ref, feature_ref, query_s, key_s, signal_s):
    count = COUNT
    rows, own = query_s.shape[1:]
    position = lax.axis_index("ctx")
    for step, given in zip(ORDER, (third_ref, second_ref, near_ref, own_ref)):
        query_s[position ^ step] = given[0:rows]
        key_s[columns_of(position ^ step, rows)] = given[rows : 2 * rows]
        signal_s[columns_of(position ^ step, rows)] = given[2 * rows :]
    taps = [short_ref[lag, 0:1, columns_of(position, own)].astype(jnp.float32) for lag in range(3)]
    feature_ref[...] = featured(signal_s[...].astype(jnp.float32), taps)
    causal = lax.broadcasted_iota(jnp.int32, (rows, rows), 1) <= lax.broadcasted_iota(jnp.int32, (rows, rows), 0)
    for head in range(own // HEAD_DIM):
        columns = slice(head * HEAD_DIM, (head + 1) * HEAD_DIM)
        for block in range(count):
            here, seen = slice(block * rows, (block + 1) * rows), (block + 1) * rows
            scores = lax.dot_general(
                query_s[block, :, columns],
                key_s[0:seen, columns],
                (((1,), (1,)), ((), ())),
                preferred_element_type=jnp.float32,
            ) * HEAD_DIM ** (-0.5)
            own_scores = jnp.where(causal, scores[:, block * rows :], masked_score)
            pieces = [scores[:, : block * rows], own_scores] if block else [own_scores]
            scores = jnp.concatenate(pieces, axis=1)
            weights = jnp.exp(scores - jnp.max(scores, axis=1, keepdims=True))
            total_ref[here, head : head + 1] = jnp.sum(weights, axis=1, keepdims=True)
            weight_ref[head, here, 0:seen] = weights.astype(jnp.bfloat16)
            if seen < count * rows:
                weight_ref[head, here, seen:] = jnp.zeros((rows, count * rows - seen), jnp.bfloat16)


def mix_rows(block, weight_ref, total_ref, value_ref, out_ref):
    rows = out_ref.shape[0]
    here = columns_of(block, rows)
    for head in range(out_ref.shape[1] // HEAD_DIM):
        columns = slice(head * HEAD_DIM, (head + 1) * HEAD_DIM)
        mixed = jnp.dot(weight_ref[head, here], value_ref[:, columns], preferred_element_type=jnp.float32)
        out_ref[:, columns] = (mixed / total_ref[here, head : head + 1]).astype(jnp.bfloat16)


def values_kernel(*refs):
    count = COUNT
    gates, feature_ref = refs[:count], refs[count]
    band_ref, short_ref, gain_ref, weight_ref, total_ref = refs[count + 1 : count + 6]
    third_ref, second_ref, value_ref = refs[count + 6 : count + 9]
    gates_s, gate_s, filtered_s = refs[count + 9 :]
    rows, own = second_ref.shape
    per_group = own * rows // band_ref.shape[0]
    position = lax.axis_index("ctx")
    mine = columns_of(position, own)
    for step, gate in zip(GATE_ORDER, gates):
        gates_s[position ^ step] = gate[...]
    taps = [
        [short_ref[lag, stream : stream + 1, mine].astype(jnp.float32) for lag in range(3)] for stream in range(3)
    ]
    gate_s[0:rows] = jnp.zeros((rows, own), jnp.bfloat16)
    edge_row = lax.broadcasted_iota(jnp.int32, (8, own), 0)
    head_row = lax.broadcasted_iota(jnp.int32, (16, own), 0)
    for block in range(count):
        gate_s[(block + 1) * rows : (block + 2) * rows] = gates_s[block, 0:rows]
        if block == 0:
            continue
        fixed = 1.0
        before = gates_s[block - 1, rows:].astype(jnp.float32)
        here = gates_s[block, rows:].astype(jnp.float32)
        for which, stream in enumerate((1, 2)):
            old = pltpu.roll(before[8 * which : 8 * which + 8], 6, 0)
            new = pltpu.roll(here[8 * which : 8 * which + 8], 2, 0)
            joined = jnp.where(edge_row < 2, old, new)
            fixed = fixed * (
                taps[stream][0] * pltpu.roll(joined, 6, 0)
                + taps[stream][1] * pltpu.roll(joined, 7, 0)
                + taps[stream][2] * joined
            )
        head = gates_s[block, 0:16].astype(jnp.float32)
        head = jnp.where(head_row < 2, jnp.concatenate([fixed, fixed], axis=0), head)
        gate_s[(block + 1) * rows : (block + 1) * rows + 16] = head.astype(jnp.bfloat16)
    gain = gain_ref[:, mine]
    chunk = 2 * HEAD_DIM // count
    in_chunk = chunk // per_group
    lane = lax.broadcasted_iota(jnp.int32, (rows, 2 * HEAD_DIM), 1) % chunk // per_group
    for part in range(own // chunk):
        columns = slice(part * chunk, (part + 1) * chunk)
        windows = [gate_s[block * rows : (block + 2) * rows, columns] for block in range(count)]
        mixed = jnp.dot(
            band_ref[part * in_chunk * rows : (part + 1) * in_chunk * rows],
            jnp.concatenate(windows, axis=1),
            preferred_element_type=jnp.float32,
        )
        filtered = mixed[:rows]
        for group in range(1, in_chunk):
            filtered = jnp.where(lane == group, mixed[group * rows : (group + 1) * rows], filtered)
        for block in range(count):
            filtered_s[block * rows : (block + 1) * rows, columns] = filtered[:, block * chunk : (block + 1) * chunk]
    value_ref[...] = (
        feature_ref[...] * (filtered_s[...] + gain * gate_s[rows:].astype(jnp.float32))
    ).astype(jnp.bfloat16)
    for step, out_ref in ((3, third_ref), (2, second_ref)):
        mix_rows(position ^ step, weight_ref, total_ref, value_ref, out_ref)


def near_rows_kernel(weight_ref, total_ref, value_ref, *refs):
    upper_ref, lower_ref, own_ref, near_s = refs
    half = upper_ref.shape[0]
    position = lax.axis_index("ctx")
    mix_rows(position ^ 1, weight_ref, total_ref, value_ref, near_s)
    upper_ref[...] = near_s[0:half]
    lower_ref[...] = near_s[half:]
    mix_rows(position, weight_ref, total_ref, value_ref, own_ref)


def project_kernel(spans, *refs):
    given, weight_ref = refs[:5], refs[5]
    out_refs, attended_s = refs[-1 - len(spans) : -1], refs[-1]
    second, third, upper, lower, mine = given
    half = upper.shape[0]
    rows, own = mine.shape
    position, here = lax.axis_index("ctx"), lax.axis_index("mp")
    attended_s[0:half, columns_of(position ^ 1, own)] = upper[...]
    attended_s[half:, columns_of(position ^ 1, own)] = lower[...]
    for step, piece in ((0, mine), (2, second), (3, third)):
        attended_s[:, columns_of(position ^ step, own)] = piece[...]
    for (mask, part, parts), out_ref in zip(spans, out_refs):
        columns = columns_of((here ^ mask) * parts + part, out_ref.shape[1])
        out_ref[...] = jnp.dot(
            attended_s[...], weight_ref[:, columns], preferred_element_type=jnp.float32
        ).astype(jnp.bfloat16)


VMEM_LIMIT = 40 * 1024 * 1024
PLAIN_LIMIT = 53 * 1024 * 1024 + 400 * 1024
GATE_LIMIT = 60 * 1024 * 1024
IN_HBM = pl.BlockSpec(memory_space=pltpu.HBM)
IN_VMEM = pl.BlockSpec(memory_space=pltpu.VMEM)
ANYWHERE = pl.BlockSpec(memory_space=pl.ANY)


def run_kernel(kernel, operands, outputs, scratch=(), spaces=None, limit=VMEM_LIMIT, cost=10**6):
    return pl.pallas_call(
        kernel,
        out_shape=[jax.ShapeDtypeStruct(shape, dtype) for shape, dtype in outputs],
        in_specs=spaces or [IN_VMEM] * len(operands),
        out_specs=[IN_VMEM] * len(outputs),
        scratch_shapes=scratch,
        compiler_params=pltpu.CompilerParams(vmem_limit_bytes=limit),
        cost_estimate=pl.CostEstimate(flops=cost, bytes_accessed=2**20, transcendentals=0),
        name=getattr(kernel, "func", kernel).__name__,
    )(*operands)


def swapped(value, axis, step):
    return lax.ppermute(value, axis, [(source, source ^ step) for source in range(lax.axis_size(axis))])


def by_heads(inputs, short_filter, long_filter, skip_gain, queries, key_rows, out_weight):
    rows, streams, channels = inputs.shape
    own = channels // COUNT
    groups, taps = long_filter.shape
    half = jnp.bfloat16
    piece, window = ((rows, own), half), COUNT * rows
    streamed = jnp.transpose(inputs, (1, 0, 2))
    far_plain = run_kernel(
        plain_kernel,
        (streamed, queries, key_rows),
        [((3 * rows, own), half)] * 2,
        [pltpu.SemaphoreType.DMA((6,))],
        [IN_HBM] * 3,
        PLAIN_LIMIT,
    )
    *gates, near_plain, own_plain = run_kernel(
        gate_kernel,
        (streamed, short_filter, queries, key_rows),
        [((rows + EDGE, own), half)] * COUNT + [((3 * rows, own), half)] * 2,
        [
            pltpu.VMEM((2, rows, channels), half),
            pltpu.VMEM(short_filter.shape, half),
            pltpu.SemaphoreType.DMA((2,)),
            pltpu.SemaphoreType.DMA((6,)),
        ],
        [IN_HBM] * 4,
        GATE_LIMIT,
    )
    plain = [own_plain, near_plain, far_plain[1], far_plain[0]]
    plain = [swapped(plain[step], "ctx", step) for step in ORDER[:3]] + [plain[0]]
    gates = [swapped(gates[step], "ctx", step) for step in GATE_ORDER[:3]] + [gates[0]]
    band, weight = run_kernel(
        ready_kernel,
        (long_filter, out_weight),
        [((groups // COUNT * taps, 2 * taps), half), (out_weight.shape, half)],
        [pltpu.SemaphoreType.DMA],
        [IN_VMEM, IN_HBM],
    )
    soft, totals, feature = run_kernel(
        weights_kernel,
        (*plain, short_filter),
        [
            ((own // HEAD_DIM, window, window), half),
            ((window, HEAD_DIM), jnp.float32),
            ((window, own), jnp.float32),
        ],
        [
            pltpu.VMEM((COUNT, rows, own), half),
            pltpu.VMEM((window, own), half),
            pltpu.VMEM((window, own), half),
        ],
    )
    third, second, values = run_kernel(
        values_kernel,
        (*gates, feature, band, short_filter, skip_gain.reshape(1, channels), soft, totals),
        [piece, piece, ((window, own), half)],
        [
            pltpu.VMEM((COUNT, rows + EDGE, own), half),
            pltpu.VMEM((window + rows, own), half),
            pltpu.VMEM((window, own), jnp.float32),
        ],
    )
    third_got, second_got = swapped(third, "ctx", 3), swapped(second, "ctx", 2)
    upper, lower, mine = run_kernel(
        near_rows_kernel,
        (soft, totals, values),
        [((rows // 2, own), half)] * 2 + [piece],
        [pltpu.VMEM((rows, own), half)],
    )
    near = (swapped(upper, "ctx", 1), swapped(lower, "ctx", 1))
    return project_and_share((second_got, third_got, *near, mine), weight)


def projected(attended, out_weight, spans, after=(), cost=10**6):
    rows = attended[-1].shape[0]
    width = out_weight.shape[1] // lax.axis_size("mp")
    return run_kernel(
        functools.partial(project_kernel, spans),
        (*attended, out_weight, *after),
        [((rows, width // parts), jnp.bfloat16) for _, _, parts in spans],
        [pltpu.VMEM((rows, out_weight.shape[0]), jnp.bfloat16)],
        [IN_VMEM] * (len(attended) + 1) + [ANYWHERE] * len(after),
        cost=cost,
    )


FAR_COST, NEAR_COST = 10**6, 10**6


def added(*terms):
    total = terms[0].astype(jnp.float32)
    for term in terms[1:]:
        total = total + term.astype(jnp.float32)
    return total.astype(jnp.bfloat16)


def project_and_share(attended, out_weight):
    crossed, after = [], ()
    for part in range(2):
        given, kept = projected(attended, out_weight, ((3, part, 2), (2, part, 2)), after, FAR_COST)
        after = (given,)
        far_sum = added(kept, swapped(given, "mp", 1))
        crossed.append(swapped(far_sum, "mp", 2))
    near_given, near_kept = projected(attended, out_weight, ((1, 0, 1), (0, 0, 1)), (far_sum,), NEAR_COST)
    half = near_given.shape[0] // 2
    near_got = jnp.concatenate([swapped(near_given[:half], "mp", 1), swapped(near_given[half:], "mp", 1)])
    return added(near_kept, near_got, jnp.concatenate(crossed, axis=1))


def per_device(inputs, short_filter, long_filter, skip_gain, queries, key_rows, out_weight):
    rows, _, channels = inputs.shape
    count = lax.axis_size("ctx")
    taps = long_filter.shape[1]
    splits = channels % (count * HEAD_DIM) == 0 and count == COUNT and rows == taps
    if splits and lax.axis_size("mp") == 4:
        return by_heads(inputs, short_filter, long_filter, skip_gain, queries, key_rows, out_weight)
    attended = by_rows(inputs, short_filter, long_filter, skip_gain, queries, key_rows)
    partial_out = jnp.dot(attended, out_weight, preferred_element_type=jnp.float32)
    return lax.psum_scatter(partial_out.astype(jnp.bfloat16), "mp", scatter_dimension=1, tiled=True)


def solution(mesh):
    placed = (
        P(("parts", "ctx"), None, "mp"),
        P(None, None, "mp"),
        P("mp", None),
        P("mp"),
        P(("parts", "ctx"), "mp"),
        P(("parts", "ctx"), "mp"),
        P("mp", None),
    )
    return jax.shard_map(
        per_device, mesh=mesh, in_specs=placed, out_specs=P(("parts", "ctx"), "mp"), check_vma=False
    )
```

```python
import functools

import jax
import jax.numpy as jnp
from jax import lax
from jax.experimental import pallas as pl
from jax.experimental.pallas import tpu as pltpu
from jax.sharding import PartitionSpec as P

HEAD_DIM = 128
COUNT = 4
ORDER = (3, 2, 1, 0)
EDGE = 16


masked_score = -1e30


def passed_along(value, axis, steps):
    count = lax.axis_size(axis)
    initial, last = (max(0, -steps), min(count, count - steps))
    return lax.ppermute(value, axis, [(source, source + steps) for source in range(initial, last)])


def toeplitz_taps(filters, row_count):
    group_count = filters.shape[0]
    tap_count = filters.shape[1]
    span = row_count + tap_count - 1
    flipped = filters[:, ::-1]
    padded_taps = jnp.concatenate(
        [flipped, jnp.zeros((group_count, row_count), filters.dtype)], axis=1
    )
    repeated = jnp.tile(padded_taps, (1, row_count))
    return repeated[:, : row_count * span].reshape(group_count, row_count, span)


def short_features(extended, short_filter, row_count):
    tap_count = short_filter.shape[0]
    features = jnp.zeros((row_count,) + extended.shape[1:], jnp.float32)
    for lag_index in range(tap_count):
        delayed = extended[
            tap_count - 1 - lag_index : tap_count - 1 - lag_index + row_count
        ].astype(jnp.float32)
        features = features + short_filter[lag_index].astype(jnp.float32)[None] * delayed
    return features


def attend(head_queries, query_pos, key_piece, value_piece):
    key_count = key_piece.shape[0]
    head_count = head_queries.shape[1]
    key_heads = key_piece.reshape(key_count, head_count, -1)
    value_heads = value_piece.reshape(key_count, head_count, -1)
    scores = jnp.einsum(
        "qhd,khd->hqk", head_queries, key_heads, preferred_element_type=jnp.float32
    ) * head_queries.shape[2] ** (-0.5)
    key_pos = lax.iota(jnp.int32, key_count)
    allowed = (key_pos[None, :] <= query_pos[:, None])[None]
    peak = jnp.max(jnp.where(allowed, scores, masked_score), axis=2)
    probabilities = jnp.where(allowed, jnp.exp(scores - peak[..., None]), 0.0)
    weight_sum = jnp.sum(probabilities, axis=2)
    mixed = jnp.einsum(
        "hqk,khd->hqd",
        probabilities.astype(jnp.bfloat16),
        value_heads,
        preferred_element_type=jnp.float32,
    )
    result = mixed / weight_sum[..., None]
    return jnp.transpose(result, (1, 0, 2)).reshape(result.shape[1], -1).astype(jnp.bfloat16)


def by_rows(inputs, short_filter, long_filter, skip_gain, queries, key_rows):
    row_count = inputs.shape[0]
    channels = inputs.shape[2]
    groups = long_filter.shape[0]
    tap_count = long_filter.shape[1]
    short_reach = short_filter.shape[0] - 1
    position = lax.axis_index("ctx")
    rim = passed_along(inputs[row_count - short_reach :], "ctx", 1)
    extended = jnp.concatenate([rim, inputs], axis=0)
    features = short_features(extended, short_filter, row_count)
    gate_product = (features[:, 1] * features[:, 2]).astype(jnp.bfloat16)
    gate_prev = passed_along(gate_product[row_count - (tap_count - 1) :], "ctx", 1)
    gate_ext = jnp.concatenate([gate_prev, gate_product], axis=0)
    toeplitz = toeplitz_taps(long_filter, row_count)
    filtered = jnp.einsum(
        "gtr,rgc->tgc",
        toeplitz,
        gate_ext.reshape(row_count + tap_count - 1, groups, channels // groups),
        preferred_element_type=jnp.float32,
    ).reshape(row_count, channels)
    values = (
        features[:, 0] * (filtered + skip_gain[None] * gate_product.astype(jnp.float32))
    ).astype(jnp.bfloat16)
    head_count = channels // HEAD_DIM
    head_queries = queries.reshape(row_count, head_count, HEAD_DIM)
    query_pos = position * row_count + lax.iota(jnp.int32, row_count)
    return attend(
        head_queries,
        query_pos,
        lax.all_gather(key_rows, "ctx", axis=0, tiled=True),
        lax.all_gather(values, "ctx", axis=0, tiled=True),
    )


def delayed(signal, lag):
    if lag == 0:
        return signal
    row = lax.broadcasted_iota(jnp.int32, signal.shape, 0)
    return jnp.where(row < lag, 0.0, pltpu.roll(signal, lag, 0))


def featured(signal, taps):
    total = taps[0] * signal
    for lag in range(1, len(taps)):
        total = total + taps[lag] * delayed(signal, lag)
    return total


def columns_of(block, width):
    return pl.ds(pl.multiple_of(block * width, width), width)


def write_gate(signals, taps, out_ref):
    rows, own = signals[0].shape
    edge_row = lax.broadcasted_iota(jnp.int32, (8, own), 0)
    features = [featured(signal, tap) for signal, tap in zip(signals, taps)]
    edges = [
        jnp.where(edge_row < 2, signal[:8], jnp.where(edge_row < 4, pltpu.roll(signal[rows - 8 :], 4, 0), 0.0))
        for signal in signals
    ]
    out_ref[0:rows] = (features[0] * features[1]).astype(jnp.bfloat16)
    out_ref[rows : rows + EDGE] = jnp.concatenate(edges, axis=0).astype(jnp.bfloat16)


def plain_copies(sources, out_refs, steps, sems):
    rows, own = sources[0].shape[0], out_refs[0].shape[1]
    position = lax.axis_index("ctx")
    copies = []
    for step, out_ref in zip(steps, out_refs):
        columns = columns_of(position ^ step, own)
        for index, source in enumerate(sources):
            target = out_ref.at[index * rows : (index + 1) * rows]
            copies.append(pltpu.make_async_copy(source.at[:, columns], target, sems.at[len(copies)]))
    for copy in copies:
        copy.start()
    return copies


def plain_kernel(inputs_any, queries_any, keys_any, *refs):
    for copy in plain_copies((queries_any, keys_any, inputs_any.at[0]), refs[:2], ORDER[:2], refs[2]):
        copy.wait()


def gate_kernel(inputs_any, short_any, queries_any, keys_any, *refs):
    out_refs, plain_refs = refs[:COUNT], refs[COUNT : COUNT + 2]
    signal_s, short_s, sems, plain_sems = refs[COUNT + 2 :]
    own = out_refs[0].shape[1]
    position = lax.axis_index("ctx")
    copies = [
        pltpu.make_async_copy(short_any, short_s, sems.at[0]),
        pltpu.make_async_copy(inputs_any.at[1:3], signal_s, sems.at[1]),
    ]
    for copy in copies:
        copy.start()
    plain = plain_copies((queries_any, keys_any, inputs_any.at[0]), plain_refs, ORDER[2:], plain_sems)
    for copy in copies:
        copy.wait()
    for step in ORDER:
        columns = columns_of(position ^ step, own)
        signals = [signal_s[stream, :, columns].astype(jnp.float32) for stream in range(2)]
        taps = [
            [short_s[lag, stream : stream + 1, columns].astype(jnp.float32) for lag in range(3)] for stream in (1, 2)
        ]
        write_gate(signals, taps, out_refs[step])
    for copy in plain:
        copy.wait()


def ready_kernel(filter_ref, weight_any, band_ref, weight_ref, sem):
    rows, span = band_ref.shape
    taps = filter_ref.shape[1]
    groups = rows // taps
    weights = pltpu.make_async_copy(weight_any, weight_ref, sem)
    weights.start()
    source = lax.broadcasted_iota(jnp.int32, (taps, span), 0)
    target = lax.broadcasted_iota(jnp.int32, (taps, span), 1)
    flip = (source + target == taps).astype(jnp.bfloat16)
    first_group = pl.multiple_of(lax.axis_index("ctx") * groups, groups)
    first = jnp.dot(filter_ref[pl.ds(first_group, groups)], flip, preferred_element_type=jnp.float32)
    for group in range(groups):
        repeated = jnp.broadcast_to(first[group : group + 1], (taps, span))
        banded = pltpu.roll(repeated, 0, 1, stride=1, stride_axis=0)
        band_ref[group * taps : (group + 1) * taps] = banded.astype(jnp.bfloat16)
    weights.wait()


def weights_kernel(third_ref, second_ref, near_ref, own_ref, short_ref, weight_ref, total_ref, feature_ref, query_s, key_s, signal_s):
    count = COUNT
    rows, own = query_s.shape[1:]
    position = lax.axis_index("ctx")
    for step, given in zip(ORDER, (third_ref, second_ref, near_ref, own_ref)):
        query_s[position ^ step] = given[0:rows]
        key_s[columns_of(position ^ step, rows)] = given[rows : 2 * rows]
        signal_s[columns_of(position ^ step, rows)] = given[2 * rows :]
    taps = [short_ref[lag, 0:1, columns_of(position, own)].astype(jnp.float32) for lag in range(3)]
    feature_ref[...] = featured(signal_s[...].astype(jnp.float32), taps)
    causal = lax.broadcasted_iota(jnp.int32, (rows, rows), 1) <= lax.broadcasted_iota(jnp.int32, (rows, rows), 0)
    for head in range(own // HEAD_DIM):
        columns = slice(head * HEAD_DIM, (head + 1) * HEAD_DIM)
        for block in range(count):
            here, seen = slice(block * rows, (block + 1) * rows), (block + 1) * rows
            scores = lax.dot_general(
                query_s[block, :, columns],
                key_s[0:seen, columns],
                (((1,), (1,)), ((), ())),
                preferred_element_type=jnp.float32,
            ) * HEAD_DIM ** (-0.5)
            own_scores = jnp.where(causal, scores[:, block * rows :], masked_score)
            pieces = [scores[:, : block * rows], own_scores] if block else [own_scores]
            scores = jnp.concatenate(pieces, axis=1)
            weights = jnp.exp(scores - jnp.max(scores, axis=1, keepdims=True))
            total_ref[here, head : head + 1] = jnp.sum(weights, axis=1, keepdims=True)
            weight_ref[head, here, 0:seen] = weights.astype(jnp.bfloat16)
            if seen < count * rows:
                weight_ref[head, here, seen:] = jnp.zeros((rows, count * rows - seen), jnp.bfloat16)


def mix_rows(block, weight_ref, total_ref, value_ref, out_ref):
    rows = out_ref.shape[0]
    here = columns_of(block, rows)
    for head in range(out_ref.shape[1] // HEAD_DIM):
        columns = slice(head * HEAD_DIM, (head + 1) * HEAD_DIM)
        mixed = jnp.dot(weight_ref[head, here], value_ref[:, columns], preferred_element_type=jnp.float32)
        out_ref[:, columns] = (mixed / total_ref[here, head : head + 1]).astype(jnp.bfloat16)


def values_kernel(*refs):
    count = COUNT
    gates, feature_ref = refs[:count], refs[count]
    band_ref, short_ref, gain_ref, weight_ref, total_ref = refs[count + 1 : count + 6]
    third_ref, second_ref, value_ref = refs[count + 6 : count + 9]
    gates_s, gate_s, filtered_s = refs[count + 9 :]
    rows, own = second_ref.shape
    per_group = own * rows // band_ref.shape[0]
    position = lax.axis_index("ctx")
    mine = columns_of(position, own)
    for step, gate in zip(ORDER, gates):
        gates_s[position ^ step] = gate[...]
    taps = [
        [short_ref[lag, stream : stream + 1, mine].astype(jnp.float32) for lag in range(3)] for stream in range(3)
    ]
    gate_s[0:rows] = jnp.zeros((rows, own), jnp.bfloat16)
    edge_row = lax.broadcasted_iota(jnp.int32, (8, own), 0)
    head_row = lax.broadcasted_iota(jnp.int32, (16, own), 0)
    for block in range(count):
        gate_s[(block + 1) * rows : (block + 2) * rows] = gates_s[block, 0:rows]
        if block == 0:
            continue
        fixed = 1.0
        before = gates_s[block - 1, rows:].astype(jnp.float32)
        here = gates_s[block, rows:].astype(jnp.float32)
        for which, stream in enumerate((1, 2)):
            old = pltpu.roll(before[8 * which : 8 * which + 8], 6, 0)
            new = pltpu.roll(here[8 * which : 8 * which + 8], 2, 0)
            joined = jnp.where(edge_row < 2, old, new)
            fixed = fixed * (
                taps[stream][0] * pltpu.roll(joined, 6, 0)
                + taps[stream][1] * pltpu.roll(joined, 7, 0)
                + taps[stream][2] * joined
            )
        head = gates_s[block, 0:16].astype(jnp.float32)
        head = jnp.where(head_row < 2, jnp.concatenate([fixed, fixed], axis=0), head)
        gate_s[(block + 1) * rows : (block + 1) * rows + 16] = head.astype(jnp.bfloat16)
    gain = gain_ref[:, mine]
    chunk = 2 * HEAD_DIM // count
    in_chunk = chunk // per_group
    lane = lax.broadcasted_iota(jnp.int32, (rows, 2 * HEAD_DIM), 1) % chunk // per_group
    for part in range(own // chunk):
        columns = slice(part * chunk, (part + 1) * chunk)
        windows = [gate_s[block * rows : (block + 2) * rows, columns] for block in range(count)]
        mixed = jnp.dot(
            band_ref[part * in_chunk * rows : (part + 1) * in_chunk * rows],
            jnp.concatenate(windows, axis=1),
            preferred_element_type=jnp.float32,
        )
        filtered = mixed[:rows]
        for group in range(1, in_chunk):
            filtered = jnp.where(lane == group, mixed[group * rows : (group + 1) * rows], filtered)
        for block in range(count):
            filtered_s[block * rows : (block + 1) * rows, columns] = filtered[:, block * chunk : (block + 1) * chunk]
    value_ref[...] = (
        feature_ref[...] * (filtered_s[...] + gain * gate_s[rows:].astype(jnp.float32))
    ).astype(jnp.bfloat16)
    for step, out_ref in ((3, third_ref), (2, second_ref)):
        mix_rows(position ^ step, weight_ref, total_ref, value_ref, out_ref)


def near_rows_kernel(weight_ref, total_ref, value_ref, *refs):
    upper_ref, lower_ref, own_ref, near_s = refs
    half = upper_ref.shape[0]
    position = lax.axis_index("ctx")
    mix_rows(position ^ 1, weight_ref, total_ref, value_ref, near_s)
    upper_ref[...] = near_s[0:half]
    lower_ref[...] = near_s[half:]
    mix_rows(position, weight_ref, total_ref, value_ref, own_ref)


def project_kernel(spans, *refs):
    given, weight_ref = refs[:5], refs[5]
    out_refs, attended_s = refs[-1 - len(spans) : -1], refs[-1]
    second, third, upper, lower, mine = given
    half = upper.shape[0]
    rows, own = mine.shape
    position, here = lax.axis_index("ctx"), lax.axis_index("mp")
    attended_s[0:half, columns_of(position ^ 1, own)] = upper[...]
    attended_s[half:, columns_of(position ^ 1, own)] = lower[...]
    for step, piece in ((0, mine), (2, second), (3, third)):
        attended_s[:, columns_of(position ^ step, own)] = piece[...]
    for (mask, part, parts), out_ref in zip(spans, out_refs):
        columns = columns_of((here ^ mask) * parts + part, out_ref.shape[1])
        out_ref[...] = jnp.dot(
            attended_s[...], weight_ref[:, columns], preferred_element_type=jnp.float32
        ).astype(jnp.bfloat16)


def total_kernel(kept_ref, upper_ref, lower_ref, first_ref, second_ref, out_any, total_s, sems):
    half, cut = upper_ref.shape[0], first_ref.shape[1]
    copies = []
    for index, near_ref in enumerate((upper_ref, lower_ref)):
        here = slice(index * half, (index + 1) * half)
        for columns, crossed_ref in ((slice(0, cut), first_ref), (slice(cut, 2 * cut), second_ref)):
            total = (
                kept_ref[here, columns].astype(jnp.float32)
                + near_ref[:, columns].astype(jnp.float32)
                + crossed_ref[here].astype(jnp.float32)
            )
            total_s[here, columns] = total.astype(jnp.bfloat16)
        copy = pltpu.make_async_copy(total_s.at[here], out_any.at[here], sems.at[index])
        copy.start()
        copies.append(copy)
    for copy in copies:
        copy.wait()


VMEM_LIMIT = 40 * 1024 * 1024
PLAIN_LIMIT = 53 * 1024 * 1024 + 400 * 1024
GATE_LIMIT = 60 * 1024 * 1024
IN_HBM = pl.BlockSpec(memory_space=pltpu.HBM)
IN_VMEM = pl.BlockSpec(memory_space=pltpu.VMEM)
ANYWHERE = pl.BlockSpec(memory_space=pl.ANY)


def run_kernel(kernel, operands, outputs, scratch=(), spaces=None, limit=VMEM_LIMIT, cost=10**6, targets=None):
    return pl.pallas_call(
        kernel,
        out_shape=[jax.ShapeDtypeStruct(shape, dtype) for shape, dtype in outputs],
        in_specs=spaces or [IN_VMEM] * len(operands),
        out_specs=targets or [IN_VMEM] * len(outputs),
        scratch_shapes=scratch,
        compiler_params=pltpu.CompilerParams(vmem_limit_bytes=limit),
        cost_estimate=pl.CostEstimate(flops=cost, bytes_accessed=2**20, transcendentals=0),
        name=getattr(kernel, "func", kernel).__name__,
    )(*operands)


def swapped(value, axis, step):
    return lax.ppermute(value, axis, [(source, source ^ step) for source in range(lax.axis_size(axis))])


def by_heads(inputs, short_filter, long_filter, skip_gain, queries, key_rows, out_weight):
    rows, streams, channels = inputs.shape
    own = channels // COUNT
    groups, taps = long_filter.shape
    half = jnp.bfloat16
    piece, window = ((rows, own), half), COUNT * rows
    streamed = jnp.transpose(inputs, (1, 0, 2))
    far_plain = run_kernel(
        plain_kernel,
        (streamed, queries, key_rows),
        [((3 * rows, own), half)] * 2,
        [pltpu.SemaphoreType.DMA((6,))],
        [IN_HBM] * 3,
        PLAIN_LIMIT,
    )
    *gates, near_plain, own_plain = run_kernel(
        gate_kernel,
        (streamed, short_filter, queries, key_rows),
        [((rows + EDGE, own), half)] * COUNT + [((3 * rows, own), half)] * 2,
        [
            pltpu.VMEM((2, rows, channels), half),
            pltpu.VMEM(short_filter.shape, half),
            pltpu.SemaphoreType.DMA((2,)),
            pltpu.SemaphoreType.DMA((6,)),
        ],
        [IN_HBM] * 4,
        GATE_LIMIT,
    )
    plain = [own_plain, near_plain, far_plain[1], far_plain[0]]
    plain = [swapped(plain[step], "ctx", step) for step in ORDER[:3]] + [plain[0]]
    gates = [swapped(gates[step], "ctx", step) for step in ORDER[:3]] + [gates[0]]
    band, weight = run_kernel(
        ready_kernel,
        (long_filter, out_weight),
        [((groups // COUNT * taps, 2 * taps), half), (out_weight.shape, half)],
        [pltpu.SemaphoreType.DMA],
        [IN_VMEM, IN_HBM],
    )
    soft, totals, feature = run_kernel(
        weights_kernel,
        (*plain, short_filter),
        [
            ((own // HEAD_DIM, window, window), half),
            ((window, HEAD_DIM), jnp.float32),
            ((window, own), jnp.float32),
        ],
        [
            pltpu.VMEM((COUNT, rows, own), half),
            pltpu.VMEM((window, own), half),
            pltpu.VMEM((window, own), half),
        ],
    )
    third, second, values = run_kernel(
        values_kernel,
        (*gates, feature, band, short_filter, skip_gain.reshape(1, channels), soft, totals),
        [piece, piece, ((window, own), half)],
        [
            pltpu.VMEM((COUNT, rows + EDGE, own), half),
            pltpu.VMEM((window + rows, own), half),
            pltpu.VMEM((window, own), jnp.float32),
        ],
    )
    third_got, second_got = swapped(third, "ctx", 3), swapped(second, "ctx", 2)
    upper, lower, mine = run_kernel(
        near_rows_kernel,
        (soft, totals, values),
        [((rows // 2, own), half)] * 2 + [piece],
        [pltpu.VMEM((rows, own), half)],
    )
    near = (swapped(upper, "ctx", 1), swapped(lower, "ctx", 1))
    return project_and_share((second_got, third_got, *near, mine), weight)


def projected(attended, out_weight, spans, after=(), cost=10**6):
    rows = attended[-1].shape[0]
    width = out_weight.shape[1] // lax.axis_size("mp")
    return run_kernel(
        functools.partial(project_kernel, spans),
        (*attended, out_weight, *after),
        [((rows, width // parts), jnp.bfloat16) for _, _, parts in spans],
        [pltpu.VMEM((rows, out_weight.shape[0]), jnp.bfloat16)],
        [IN_VMEM] * (len(attended) + 1) + [ANYWHERE] * len(after),
        cost=cost,
    )


FAR_COST, NEAR_COST = 10**6, 10**6


def added(*terms):
    total = terms[0].astype(jnp.float32)
    for term in terms[1:]:
        total = total + term.astype(jnp.float32)
    return total.astype(jnp.bfloat16)


def project_and_share(attended, out_weight):
    crossed, after = [], ()
    for part in range(2):
        given, kept = projected(attended, out_weight, ((3, part, 2), (2, part, 2)), after, FAR_COST)
        after = (given,)
        far_sum = added(kept, swapped(given, "mp", 1))
        crossed.append(swapped(far_sum, "mp", 2))
    near_given, near_kept = projected(attended, out_weight, ((1, 0, 1), (0, 0, 1)), (far_sum,), NEAR_COST)
    half = near_given.shape[0] // 2
    near_got = [swapped(near_given[:half], "mp", 1), swapped(near_given[half:], "mp", 1)]
    (total,) = run_kernel(
        total_kernel,
        (near_kept, *near_got, *crossed),
        [(near_kept.shape, near_kept.dtype)],
        [pltpu.VMEM(near_kept.shape, near_kept.dtype), pltpu.SemaphoreType.DMA((2,))],
        targets=[IN_HBM],
    )
    return total


def per_device(inputs, short_filter, long_filter, skip_gain, queries, key_rows, out_weight):
    rows, _, channels = inputs.shape
    count = lax.axis_size("ctx")
    taps = long_filter.shape[1]
    splits = channels % (count * HEAD_DIM) == 0 and count == COUNT and rows == taps
    if splits and lax.axis_size("mp") == 4:
        return by_heads(inputs, short_filter, long_filter, skip_gain, queries, key_rows, out_weight)
    attended = by_rows(inputs, short_filter, long_filter, skip_gain, queries, key_rows)
    partial_out = jnp.dot(attended, out_weight, preferred_element_type=jnp.float32)
    return lax.psum_scatter(partial_out.astype(jnp.bfloat16), "mp", scatter_dimension=1, tiled=True)


def solution(mesh):
    placed = (
        P(("parts", "ctx"), None, "mp"),
        P(None, None, "mp"),
        P("mp", None),
        P("mp"),
        P(("parts", "ctx"), "mp"),
        P(("parts", "ctx"), "mp"),
        P("mp", None),
    )
    return jax.shard_map(
        per_device, mesh=mesh, in_specs=placed, out_specs=P(("parts", "ctx"), "mp"), check_vma=False
    )
```

```python
import functools

import jax
import jax.numpy as jnp
from jax import lax
from jax.experimental import pallas as pl
from jax.experimental.pallas import tpu as pltpu
from jax.sharding import PartitionSpec as P

HEAD_DIM = 128
COUNT = 4
ORDER = (3, 2, 1, 0)
EDGE = 16


masked_score = -1e30


def passed_along(value, axis, steps):
    count = lax.axis_size(axis)
    initial, last = (max(0, -steps), min(count, count - steps))
    return lax.ppermute(value, axis, [(source, source + steps) for source in range(initial, last)])


def toeplitz_taps(filters, row_count):
    group_count = filters.shape[0]
    tap_count = filters.shape[1]
    span = row_count + tap_count - 1
    flipped = filters[:, ::-1]
    padded_taps = jnp.concatenate(
        [flipped, jnp.zeros((group_count, row_count), filters.dtype)], axis=1
    )
    repeated = jnp.tile(padded_taps, (1, row_count))
    return repeated[:, : row_count * span].reshape(group_count, row_count, span)


def short_features(extended, short_filter, row_count):
    tap_count = short_filter.shape[0]
    features = jnp.zeros((row_count,) + extended.shape[1:], jnp.float32)
    for lag_index in range(tap_count):
        delayed = extended[
            tap_count - 1 - lag_index : tap_count - 1 - lag_index + row_count
        ].astype(jnp.float32)
        features = features + short_filter[lag_index].astype(jnp.float32)[None] * delayed
    return features


def attend(head_queries, query_pos, key_piece, value_piece):
    key_count = key_piece.shape[0]
    head_count = head_queries.shape[1]
    key_heads = key_piece.reshape(key_count, head_count, -1)
    value_heads = value_piece.reshape(key_count, head_count, -1)
    scores = jnp.einsum(
        "qhd,khd->hqk", head_queries, key_heads, preferred_element_type=jnp.float32
    ) * head_queries.shape[2] ** (-0.5)
    key_pos = lax.iota(jnp.int32, key_count)
    allowed = (key_pos[None, :] <= query_pos[:, None])[None]
    peak = jnp.max(jnp.where(allowed, scores, masked_score), axis=2)
    probabilities = jnp.where(allowed, jnp.exp(scores - peak[..., None]), 0.0)
    weight_sum = jnp.sum(probabilities, axis=2)
    mixed = jnp.einsum(
        "hqk,khd->hqd",
        probabilities.astype(jnp.bfloat16),
        value_heads,
        preferred_element_type=jnp.float32,
    )
    result = mixed / weight_sum[..., None]
    return jnp.transpose(result, (1, 0, 2)).reshape(result.shape[1], -1).astype(jnp.bfloat16)


def by_rows(inputs, short_filter, long_filter, skip_gain, queries, key_rows):
    row_count = inputs.shape[0]
    channels = inputs.shape[2]
    groups = long_filter.shape[0]
    tap_count = long_filter.shape[1]
    short_reach = short_filter.shape[0] - 1
    position = lax.axis_index("ctx")
    rim = passed_along(inputs[row_count - short_reach :], "ctx", 1)
    extended = jnp.concatenate([rim, inputs], axis=0)
    features = short_features(extended, short_filter, row_count)
    gate_product = (features[:, 1] * features[:, 2]).astype(jnp.bfloat16)
    gate_prev = passed_along(gate_product[row_count - (tap_count - 1) :], "ctx", 1)
    gate_ext = jnp.concatenate([gate_prev, gate_product], axis=0)
    toeplitz = toeplitz_taps(long_filter, row_count)
    filtered = jnp.einsum(
        "gtr,rgc->tgc",
        toeplitz,
        gate_ext.reshape(row_count + tap_count - 1, groups, channels // groups),
        preferred_element_type=jnp.float32,
    ).reshape(row_count, channels)
    values = (
        features[:, 0] * (filtered + skip_gain[None] * gate_product.astype(jnp.float32))
    ).astype(jnp.bfloat16)
    head_count = channels // HEAD_DIM
    head_queries = queries.reshape(row_count, head_count, HEAD_DIM)
    query_pos = position * row_count + lax.iota(jnp.int32, row_count)
    return attend(
        head_queries,
        query_pos,
        lax.all_gather(key_rows, "ctx", axis=0, tiled=True),
        lax.all_gather(values, "ctx", axis=0, tiled=True),
    )


def delayed(signal, lag):
    if lag == 0:
        return signal
    row = lax.broadcasted_iota(jnp.int32, signal.shape, 0)
    return jnp.where(row < lag, 0.0, pltpu.roll(signal, lag, 0))


def featured(signal, taps):
    total = taps[0] * signal
    for lag in range(1, len(taps)):
        total = total + taps[lag] * delayed(signal, lag)
    return total


def columns_of(block, width):
    return pl.ds(pl.multiple_of(block * width, width), width)


def write_gate(signals, taps, out_ref):
    rows, own = signals[0].shape
    edge_row = lax.broadcasted_iota(jnp.int32, (8, own), 0)
    features = [featured(signal, tap) for signal, tap in zip(signals, taps)]
    edges = [
        jnp.where(edge_row < 2, signal[:8], jnp.where(edge_row < 4, pltpu.roll(signal[rows - 8 :], 4, 0), 0.0))
        for signal in signals
    ]
    out_ref[0:rows] = (features[0] * features[1]).astype(jnp.bfloat16)
    out_ref[rows : rows + EDGE] = jnp.concatenate(edges, axis=0).astype(jnp.bfloat16)


def plain_copies(sources, out_refs, steps, sems):
    rows, own = sources[0].shape[0], out_refs[0].shape[1]
    position = lax.axis_index("ctx")
    copies = []
    for step, out_ref in zip(steps, out_refs):
        columns = columns_of(position ^ step, own)
        for index, source in enumerate(sources):
            target = out_ref.at[index * rows : (index + 1) * rows]
            copies.append(pltpu.make_async_copy(source.at[:, columns], target, sems.at[len(copies)]))
    for copy in copies:
        copy.start()
    return copies


def plain_kernel(inputs_any, queries_any, keys_any, *refs):
    for copy in plain_copies((queries_any, keys_any, inputs_any.at[0]), refs[:2], ORDER[:2], refs[2]):
        copy.wait()


def gate_kernel(inputs_any, short_any, queries_any, keys_any, *refs):
    out_refs, plain_refs = refs[:COUNT], refs[COUNT : COUNT + 2]
    signal_s, short_s, sems, plain_sems = refs[COUNT + 2 :]
    own = out_refs[0].shape[1]
    position = lax.axis_index("ctx")
    copies = [
        pltpu.make_async_copy(short_any, short_s, sems.at[0]),
        pltpu.make_async_copy(inputs_any.at[1:3], signal_s, sems.at[1]),
    ]
    for copy in copies:
        copy.start()
    plain = plain_copies((queries_any, keys_any, inputs_any.at[0]), plain_refs, ORDER[2:], plain_sems)
    for copy in copies:
        copy.wait()
    for step in ORDER:
        columns = columns_of(position ^ step, own)
        signals = [signal_s[stream, :, columns].astype(jnp.float32) for stream in range(2)]
        taps = [
            [short_s[lag, stream : stream + 1, columns].astype(jnp.float32) for lag in range(3)] for stream in (1, 2)
        ]
        write_gate(signals, taps, out_refs[step])
    for copy in plain:
        copy.wait()


def ready_kernel(filter_ref, weight_any, band_ref, weight_ref, sem):
    rows, span = band_ref.shape
    taps = filter_ref.shape[1]
    groups = rows // taps
    weights = pltpu.make_async_copy(weight_any, weight_ref, sem)
    weights.start()
    source = lax.broadcasted_iota(jnp.int32, (taps, span), 0)
    target = lax.broadcasted_iota(jnp.int32, (taps, span), 1)
    flip = (source + target == taps).astype(jnp.bfloat16)
    first_group = pl.multiple_of(lax.axis_index("ctx") * groups, groups)
    first = jnp.dot(filter_ref[pl.ds(first_group, groups)], flip, preferred_element_type=jnp.float32)
    for group in range(groups):
        repeated = jnp.broadcast_to(first[group : group + 1], (taps, span))
        banded = pltpu.roll(repeated, 0, 1, stride=1, stride_axis=0)
        band_ref[group * taps : (group + 1) * taps] = banded.astype(jnp.bfloat16)
    weights.wait()


def weights_kernel(third_ref, second_ref, near_ref, own_ref, short_ref, weight_ref, total_ref, feature_ref, query_s, key_s, signal_s):
    count = COUNT
    rows, own = query_s.shape[1:]
    position = lax.axis_index("ctx")
    for step, given in zip(ORDER, (third_ref, second_ref, near_ref, own_ref)):
        query_s[position ^ step] = given[0:rows]
        key_s[columns_of(position ^ step, rows)] = given[rows : 2 * rows]
        signal_s[columns_of(position ^ step, rows)] = given[2 * rows :]
    taps = [short_ref[lag, 0:1, columns_of(position, own)].astype(jnp.float32) for lag in range(3)]
    feature_ref[...] = featured(signal_s[...].astype(jnp.float32), taps)
    causal = lax.broadcasted_iota(jnp.int32, (rows, rows), 1) <= lax.broadcasted_iota(jnp.int32, (rows, rows), 0)
    for head in range(own // HEAD_DIM):
        columns = slice(head * HEAD_DIM, (head + 1) * HEAD_DIM)
        for block in range(count):
            here, seen = slice(block * rows, (block + 1) * rows), (block + 1) * rows
            scores = lax.dot_general(
                query_s[block, :, columns],
                key_s[0:seen, columns],
                (((1,), (1,)), ((), ())),
                preferred_element_type=jnp.float32,
            ) * HEAD_DIM ** (-0.5)
            own_scores = jnp.where(causal, scores[:, block * rows :], masked_score)
            pieces = [scores[:, : block * rows], own_scores] if block else [own_scores]
            scores = jnp.concatenate(pieces, axis=1)
            weights = jnp.exp(scores - jnp.max(scores, axis=1, keepdims=True))
            total_ref[here, head : head + 1] = jnp.sum(weights, axis=1, keepdims=True)
            weight_ref[head, here, 0:seen] = weights.astype(jnp.bfloat16)
            if seen < count * rows:
                weight_ref[head, here, seen:] = jnp.zeros((rows, count * rows - seen), jnp.bfloat16)


def mix_rows(block, weight_ref, total_ref, value_ref, out_ref):
    rows = out_ref.shape[0]
    here = columns_of(block, rows)
    for head in range(out_ref.shape[1] // HEAD_DIM):
        columns = slice(head * HEAD_DIM, (head + 1) * HEAD_DIM)
        mixed = jnp.dot(weight_ref[head, here], value_ref[:, columns], preferred_element_type=jnp.float32)
        out_ref[:, columns] = (mixed / total_ref[here, head : head + 1]).astype(jnp.bfloat16)


def values_kernel(*refs):
    count = COUNT
    gates, feature_ref = refs[:count], refs[count]
    band_ref, short_ref, gain_ref, weight_ref, total_ref = refs[count + 1 : count + 6]
    third_ref, second_ref, value_ref = refs[count + 6 : count + 9]
    gates_s, gate_s, filtered_s = refs[count + 9 :]
    rows, own = second_ref.shape
    per_group = own * rows // band_ref.shape[0]
    position = lax.axis_index("ctx")
    mine = columns_of(position, own)
    for step, gate in zip(ORDER, gates):
        gates_s[position ^ step] = gate[...]
    taps = [
        [short_ref[lag, stream : stream + 1, mine].astype(jnp.float32) for lag in range(3)] for stream in range(3)
    ]
    gate_s[0:rows] = jnp.zeros((rows, own), jnp.bfloat16)
    edge_row = lax.broadcasted_iota(jnp.int32, (8, own), 0)
    head_row = lax.broadcasted_iota(jnp.int32, (16, own), 0)
    for block in range(count):
        gate_s[(block + 1) * rows : (block + 2) * rows] = gates_s[block, 0:rows]
        if block == 0:
            continue
        fixed = 1.0
        before = gates_s[block - 1, rows:].astype(jnp.float32)
        here = gates_s[block, rows:].astype(jnp.float32)
        for which, stream in enumerate((1, 2)):
            old = pltpu.roll(before[8 * which : 8 * which + 8], 6, 0)
            new = pltpu.roll(here[8 * which : 8 * which + 8], 2, 0)
            joined = jnp.where(edge_row < 2, old, new)
            fixed = fixed * (
                taps[stream][0] * pltpu.roll(joined, 6, 0)
                + taps[stream][1] * pltpu.roll(joined, 7, 0)
                + taps[stream][2] * joined
            )
        head = gates_s[block, 0:16].astype(jnp.float32)
        head = jnp.where(head_row < 2, jnp.concatenate([fixed, fixed], axis=0), head)
        gate_s[(block + 1) * rows : (block + 1) * rows + 16] = head.astype(jnp.bfloat16)
    gain = gain_ref[:, mine]
    chunk = 2 * HEAD_DIM // count
    in_chunk = chunk // per_group
    lane = lax.broadcasted_iota(jnp.int32, (rows, 2 * HEAD_DIM), 1) % chunk // per_group
    for part in range(own // chunk):
        columns = slice(part * chunk, (part + 1) * chunk)
        windows = [gate_s[block * rows : (block + 2) * rows, columns] for block in range(count)]
        mixed = jnp.dot(
            band_ref[part * in_chunk * rows : (part + 1) * in_chunk * rows],
            jnp.concatenate(windows, axis=1),
            preferred_element_type=jnp.float32,
        )
        filtered = mixed[:rows]
        for group in range(1, in_chunk):
            filtered = jnp.where(lane == group, mixed[group * rows : (group + 1) * rows], filtered)
        for block in range(count):
            filtered_s[block * rows : (block + 1) * rows, columns] = filtered[:, block * chunk : (block + 1) * chunk]
    value_ref[...] = (
        feature_ref[...] * (filtered_s[...] + gain * gate_s[rows:].astype(jnp.float32))
    ).astype(jnp.bfloat16)
    for step, out_ref in ((3, third_ref), (2, second_ref)):
        mix_rows(position ^ step, weight_ref, total_ref, value_ref, out_ref)


def near_rows_kernel(weight_ref, total_ref, value_ref, *refs):
    upper_ref, lower_ref, own_ref, near_s = refs
    half = upper_ref.shape[0]
    position = lax.axis_index("ctx")
    mix_rows(position ^ 1, weight_ref, total_ref, value_ref, near_s)
    upper_ref[...] = near_s[0:half]
    lower_ref[...] = near_s[half:]
    mix_rows(position, weight_ref, total_ref, value_ref, own_ref)


def project_kernel(spans, *refs):
    given, weight_ref = refs[:5], refs[5]
    out_refs, attended_s = refs[-1 - len(spans) : -1], refs[-1]
    second, third, upper, lower, mine = given
    half = upper.shape[0]
    rows, own = mine.shape
    position, here = lax.axis_index("ctx"), lax.axis_index("mp")
    attended_s[0:half, columns_of(position ^ 1, own)] = upper[...]
    attended_s[half:, columns_of(position ^ 1, own)] = lower[...]
    for step, piece in ((0, mine), (2, second), (3, third)):
        attended_s[:, columns_of(position ^ step, own)] = piece[...]
    for (mask, part, parts), out_ref in zip(spans, out_refs):
        columns = columns_of((here ^ mask) * parts + part, out_ref.shape[1])
        out_ref[...] = jnp.dot(
            attended_s[...], weight_ref[:, columns], preferred_element_type=jnp.float32
        ).astype(jnp.bfloat16)


def partial_kernel(second_ref, mine_ref, weight_ref, out_ref):
    own, width = mine_ref.shape[1], out_ref.shape[1] // 2
    position, here = lax.axis_index("ctx"), lax.axis_index("mp")
    for index, mask in enumerate((3, 2)):
        columns = columns_of(here ^ mask, width)
        out_ref[:, index * width : (index + 1) * width] = jnp.dot(
            mine_ref[...], weight_ref[columns_of(position, own), columns], preferred_element_type=jnp.float32
        ) + jnp.dot(
            second_ref[...], weight_ref[columns_of(position ^ 2, own), columns], preferred_element_type=jnp.float32
        )


def project_far_kernel(part, third_ref, upper_ref, lower_ref, partial_ref, weight_ref, *refs):
    given_ref, kept_ref = refs[-2:]
    own, size = third_ref.shape[1], given_ref.shape[1]
    width = partial_ref.shape[1] // 2
    position, here = lax.axis_index("ctx"), lax.axis_index("mp")
    near = jnp.concatenate([upper_ref[...], lower_ref[...]], axis=0)
    for index, (mask, out_ref) in enumerate(((3, given_ref), (2, kept_ref))):
        columns = columns_of((here ^ mask) * (width // size) + part, size)
        start = index * width + part * size
        total = partial_ref[:, start : start + size] + jnp.dot(
            third_ref[...], weight_ref[columns_of(position ^ 3, own), columns], preferred_element_type=jnp.float32
        )
        total = total + jnp.dot(
            near, weight_ref[columns_of(position ^ 1, own), columns], preferred_element_type=jnp.float32
        )
        out_ref[...] = total.astype(jnp.bfloat16)


def total_kernel(kept_ref, upper_ref, lower_ref, first_ref, second_ref, out_any, total_s, sems):
    half, cut = upper_ref.shape[0], first_ref.shape[1]
    copies = []
    for index, near_ref in enumerate((upper_ref, lower_ref)):
        here = slice(index * half, (index + 1) * half)
        for columns, crossed_ref in ((slice(0, cut), first_ref), (slice(cut, 2 * cut), second_ref)):
            total = (
                kept_ref[here, columns].astype(jnp.float32)
                + near_ref[:, columns].astype(jnp.float32)
                + crossed_ref[here].astype(jnp.float32)
            )
            total_s[here, columns] = total.astype(jnp.bfloat16)
        copy = pltpu.make_async_copy(total_s.at[here], out_any.at[here], sems.at[index])
        copy.start()
        copies.append(copy)
    for copy in copies:
        copy.wait()


VMEM_LIMIT = 40 * 1024 * 1024
PLAIN_LIMIT = 53 * 1024 * 1024 + 400 * 1024
GATE_LIMIT = 60 * 1024 * 1024
IN_HBM = pl.BlockSpec(memory_space=pltpu.HBM)
IN_VMEM = pl.BlockSpec(memory_space=pltpu.VMEM)
ANYWHERE = pl.BlockSpec(memory_space=pl.ANY)


def run_kernel(kernel, operands, outputs, scratch=(), spaces=None, limit=VMEM_LIMIT, cost=10**6, targets=None):
    return pl.pallas_call(
        kernel,
        out_shape=[jax.ShapeDtypeStruct(shape, dtype) for shape, dtype in outputs],
        in_specs=spaces or [IN_VMEM] * len(operands),
        out_specs=targets or [IN_VMEM] * len(outputs),
        scratch_shapes=scratch,
        compiler_params=pltpu.CompilerParams(vmem_limit_bytes=limit),
        cost_estimate=pl.CostEstimate(flops=cost, bytes_accessed=2**20, transcendentals=0),
        name=getattr(kernel, "func", kernel).__name__,
    )(*operands)


def swapped(value, axis, step):
    return lax.ppermute(value, axis, [(source, source ^ step) for source in range(lax.axis_size(axis))])


def by_heads(inputs, short_filter, long_filter, skip_gain, queries, key_rows, out_weight):
    rows, streams, channels = inputs.shape
    own = channels // COUNT
    groups, taps = long_filter.shape
    half = jnp.bfloat16
    piece, window = ((rows, own), half), COUNT * rows
    streamed = jnp.transpose(inputs, (1, 0, 2))
    far_plain = run_kernel(
        plain_kernel,
        (streamed, queries, key_rows),
        [((3 * rows, own), half)] * 2,
        [pltpu.SemaphoreType.DMA((6,))],
        [IN_HBM] * 3,
        PLAIN_LIMIT,
    )
    *gates, near_plain, own_plain = run_kernel(
        gate_kernel,
        (streamed, short_filter, queries, key_rows),
        [((rows + EDGE, own), half)] * COUNT + [((3 * rows, own), half)] * 2,
        [
            pltpu.VMEM((2, rows, channels), half),
            pltpu.VMEM(short_filter.shape, half),
            pltpu.SemaphoreType.DMA((2,)),
            pltpu.SemaphoreType.DMA((6,)),
        ],
        [IN_HBM] * 4,
        GATE_LIMIT,
    )
    plain = [own_plain, near_plain, far_plain[1], far_plain[0]]
    plain = [swapped(plain[step], "ctx", step) for step in ORDER[:3]] + [plain[0]]
    gates = [swapped(gates[step], "ctx", step) for step in ORDER[:3]] + [gates[0]]
    band, weight = run_kernel(
        ready_kernel,
        (long_filter, out_weight),
        [((groups // COUNT * taps, 2 * taps), half), (out_weight.shape, half)],
        [pltpu.SemaphoreType.DMA],
        [IN_VMEM, IN_HBM],
    )
    soft, totals, feature = run_kernel(
        weights_kernel,
        (*plain, short_filter),
        [
            ((own // HEAD_DIM, window, window), half),
            ((window, HEAD_DIM), jnp.float32),
            ((window, own), jnp.float32),
        ],
        [
            pltpu.VMEM((COUNT, rows, own), half),
            pltpu.VMEM((window, own), half),
            pltpu.VMEM((window, own), half),
        ],
    )
    third, second, values = run_kernel(
        values_kernel,
        (*gates, feature, band, short_filter, skip_gain.reshape(1, channels), soft, totals),
        [piece, piece, ((window, own), half)],
        [
            pltpu.VMEM((COUNT, rows + EDGE, own), half),
            pltpu.VMEM((window + rows, own), half),
            pltpu.VMEM((window, own), jnp.float32),
        ],
    )
    third_got, second_got = swapped(third, "ctx", 3), swapped(second, "ctx", 2)
    upper, lower, mine = run_kernel(
        near_rows_kernel,
        (soft, totals, values),
        [((rows // 2, own), half)] * 2 + [piece],
        [pltpu.VMEM((rows, own), half)],
    )
    near = (swapped(upper, "ctx", 1), swapped(lower, "ctx", 1))
    return project_and_share((second_got, third_got, *near, mine), weight)


def projected(attended, out_weight, spans, after=(), cost=10**6):
    rows = attended[-1].shape[0]
    width = out_weight.shape[1] // lax.axis_size("mp")
    return run_kernel(
        functools.partial(project_kernel, spans),
        (*attended, out_weight, *after),
        [((rows, width // parts), jnp.bfloat16) for _, _, parts in spans],
        [pltpu.VMEM((rows, out_weight.shape[0]), jnp.bfloat16)],
        [IN_VMEM] * (len(attended) + 1) + [ANYWHERE] * len(after),
        cost=cost,
    )


NEAR_COST = 10**6


def added(*terms):
    total = terms[0].astype(jnp.float32)
    for term in terms[1:]:
        total = total + term.astype(jnp.float32)
    return total.astype(jnp.bfloat16)


def project_and_share(attended, out_weight):
    second, third, upper, lower, mine = attended
    rows = mine.shape[0]
    width = out_weight.shape[1] // lax.axis_size("mp")
    (partial,) = run_kernel(partial_kernel, (second, mine, out_weight), [((rows, 2 * width), jnp.float32)])
    crossed = []
    for part in range(2):
        given, kept = run_kernel(
            functools.partial(project_far_kernel, part),
            (third, upper, lower, partial, out_weight),
            [((rows, width // 2), jnp.bfloat16)] * 2,
        )
        far_sum = added(kept, swapped(given, "mp", 1))
        crossed.append(swapped(far_sum, "mp", 2))
    near_given, near_kept = projected(attended, out_weight, ((1, 0, 1), (0, 0, 1)), (far_sum,), NEAR_COST)
    half = near_given.shape[0] // 2
    near_got = [swapped(near_given[:half], "mp", 1), swapped(near_given[half:], "mp", 1)]
    (total,) = run_kernel(
        total_kernel,
        (near_kept, *near_got, *crossed),
        [(near_kept.shape, near_kept.dtype)],
        [pltpu.VMEM(near_kept.shape, near_kept.dtype), pltpu.SemaphoreType.DMA((2,))],
        targets=[IN_HBM],
    )
    return total


def per_device(inputs, short_filter, long_filter, skip_gain, queries, key_rows, out_weight):
    rows, _, channels = inputs.shape
    count = lax.axis_size("ctx")
    taps = long_filter.shape[1]
    splits = channels % (count * HEAD_DIM) == 0 and count == COUNT and rows == taps
    if splits and lax.axis_size("mp") == 4:
        return by_heads(inputs, short_filter, long_filter, skip_gain, queries, key_rows, out_weight)
    attended = by_rows(inputs, short_filter, long_filter, skip_gain, queries, key_rows)
    partial_out = jnp.dot(attended, out_weight, preferred_element_type=jnp.float32)
    return lax.psum_scatter(partial_out.astype(jnp.bfloat16), "mp", scatter_dimension=1, tiled=True)


def solution(mesh):
    placed = (
        P(("parts", "ctx"), None, "mp"),
        P(None, None, "mp"),
        P("mp", None),
        P("mp"),
        P(("parts", "ctx"), "mp"),
        P(("parts", "ctx"), "mp"),
        P("mp", None),
    )
    return jax.shard_map(
        per_device, mesh=mesh, in_specs=placed, out_specs=P(("parts", "ctx"), "mp"), check_vma=False
    )
```

```python
import functools

import jax
import jax.numpy as jnp
from jax import lax
from jax.experimental import pallas as pl
from jax.experimental.pallas import tpu as pltpu
from jax.sharding import PartitionSpec as P

HEAD_DIM = 128
COUNT = 4
ORDER = (3, 2, 1, 0)
EDGE = 8


masked_score = -1e30


def passed_along(value, axis, steps):
    count = lax.axis_size(axis)
    initial, last = (max(0, -steps), min(count, count - steps))
    return lax.ppermute(value, axis, [(source, source + steps) for source in range(initial, last)])


def toeplitz_taps(filters, row_count):
    group_count = filters.shape[0]
    tap_count = filters.shape[1]
    span = row_count + tap_count - 1
    flipped = filters[:, ::-1]
    padded_taps = jnp.concatenate(
        [flipped, jnp.zeros((group_count, row_count), filters.dtype)], axis=1
    )
    repeated = jnp.tile(padded_taps, (1, row_count))
    return repeated[:, : row_count * span].reshape(group_count, row_count, span)


def short_features(extended, short_filter, row_count):
    tap_count = short_filter.shape[0]
    features = jnp.zeros((row_count,) + extended.shape[1:], jnp.float32)
    for lag_index in range(tap_count):
        delayed = extended[
            tap_count - 1 - lag_index : tap_count - 1 - lag_index + row_count
        ].astype(jnp.float32)
        features = features + short_filter[lag_index].astype(jnp.float32)[None] * delayed
    return features


def attend(head_queries, query_pos, key_piece, value_piece):
    key_count = key_piece.shape[0]
    head_count = head_queries.shape[1]
    key_heads = key_piece.reshape(key_count, head_count, -1)
    value_heads = value_piece.reshape(key_count, head_count, -1)
    scores = jnp.einsum(
        "qhd,khd->hqk", head_queries, key_heads, preferred_element_type=jnp.float32
    ) * head_queries.shape[2] ** (-0.5)
    key_pos = lax.iota(jnp.int32, key_count)
    allowed = (key_pos[None, :] <= query_pos[:, None])[None]
    peak = jnp.max(jnp.where(allowed, scores, masked_score), axis=2)
    probabilities = jnp.where(allowed, jnp.exp(scores - peak[..., None]), 0.0)
    weight_sum = jnp.sum(probabilities, axis=2)
    mixed = jnp.einsum(
        "hqk,khd->hqd",
        probabilities.astype(jnp.bfloat16),
        value_heads,
        preferred_element_type=jnp.float32,
    )
    result = mixed / weight_sum[..., None]
    return jnp.transpose(result, (1, 0, 2)).reshape(result.shape[1], -1).astype(jnp.bfloat16)


def by_rows(inputs, short_filter, long_filter, skip_gain, queries, key_rows):
    row_count = inputs.shape[0]
    channels = inputs.shape[2]
    groups = long_filter.shape[0]
    tap_count = long_filter.shape[1]
    short_reach = short_filter.shape[0] - 1
    position = lax.axis_index("ctx")
    rim = passed_along(inputs[row_count - short_reach :], "ctx", 1)
    extended = jnp.concatenate([rim, inputs], axis=0)
    features = short_features(extended, short_filter, row_count)
    gate_product = (features[:, 1] * features[:, 2]).astype(jnp.bfloat16)
    gate_prev = passed_along(gate_product[row_count - (tap_count - 1) :], "ctx", 1)
    gate_ext = jnp.concatenate([gate_prev, gate_product], axis=0)
    toeplitz = toeplitz_taps(long_filter, row_count)
    filtered = jnp.einsum(
        "gtr,rgc->tgc",
        toeplitz,
        gate_ext.reshape(row_count + tap_count - 1, groups, channels // groups),
        preferred_element_type=jnp.float32,
    ).reshape(row_count, channels)
    values = (
        features[:, 0] * (filtered + skip_gain[None] * gate_product.astype(jnp.float32))
    ).astype(jnp.bfloat16)
    head_count = channels // HEAD_DIM
    head_queries = queries.reshape(row_count, head_count, HEAD_DIM)
    query_pos = position * row_count + lax.iota(jnp.int32, row_count)
    return attend(
        head_queries,
        query_pos,
        lax.all_gather(key_rows, "ctx", axis=0, tiled=True),
        lax.all_gather(values, "ctx", axis=0, tiled=True),
    )


def delayed(signal, lag):
    if lag == 0:
        return signal
    row = lax.broadcasted_iota(jnp.int32, signal.shape, 0)
    return jnp.where(row < lag, 0.0, pltpu.roll(signal, lag, 0))


def featured(signal, taps):
    total = taps[0] * signal
    for lag in range(1, len(taps)):
        total = total + taps[lag] * delayed(signal, lag)
    return total


def columns_of(block, width):
    return pl.ds(pl.multiple_of(block * width, width), width)


def write_gate(signals, taps, out_ref):
    rows, own = signals[0].shape
    tiles = [slice(start, start + HEAD_DIM) for start in range(0, own, HEAD_DIM)]
    edge_row = lax.broadcasted_iota(jnp.int32, (EDGE, own), 0)
    features = [featured(signal, tap) for signal, tap in zip(signals, taps)]
    gate = (features[0] * features[1]).astype(jnp.bfloat16)
    first, second = [
        jnp.where(
            edge_row % 4 < 2, pltpu.roll(signal[:EDGE], turn, 0), pltpu.roll(signal[rows - EDGE :], 4 - turn, 0)
        )
        for signal, turn in zip(signals, (0, 4))
    ]
    edges = jnp.where(edge_row < 4, first, second)
    for index, tile in enumerate(tiles):
        out_ref[index * rows : (index + 1) * rows] = gate[:, tile]
    out_ref[len(tiles) * rows :] = jnp.concatenate([edges[:, tile] for tile in tiles], axis=0).astype(jnp.bfloat16)


def plain_copies(sources, out_refs, steps, sems):
    rows, own = sources[0].shape[0], out_refs[0].shape[1]
    position = lax.axis_index("ctx")
    copies = []
    for step, out_ref in zip(steps, out_refs):
        columns = columns_of(position ^ step, own)
        for index, source in enumerate(sources):
            target = out_ref.at[index * rows : (index + 1) * rows]
            copies.append(pltpu.make_async_copy(source.at[:, columns], target, sems.at[len(copies)]))
    for copy in copies:
        copy.start()
    return copies


def plain_kernel(inputs_any, queries_any, keys_any, *refs):
    for copy in plain_copies((queries_any, keys_any, inputs_any.at[0]), refs[:2], ORDER[:2], refs[2]):
        copy.wait()


def gate_kernel(inputs_any, short_any, queries_any, keys_any, *refs):
    out_refs, plain_refs = refs[:COUNT], refs[COUNT : COUNT + 2]
    signal_s, short_s, sems, plain_sems = refs[COUNT + 2 :]
    own = plain_refs[0].shape[1]
    position = lax.axis_index("ctx")
    copies = [
        pltpu.make_async_copy(short_any, short_s, sems.at[0]),
        pltpu.make_async_copy(inputs_any.at[1:3], signal_s, sems.at[1]),
    ]
    for copy in copies:
        copy.start()
    plain = plain_copies((queries_any, keys_any, inputs_any.at[0]), plain_refs, ORDER[2:], plain_sems)
    for copy in copies:
        copy.wait()
    for step in ORDER:
        columns = columns_of(position ^ step, own)
        signals = [signal_s[stream, :, columns].astype(jnp.float32) for stream in range(2)]
        taps = [
            [short_s[lag, stream : stream + 1, columns].astype(jnp.float32) for lag in range(3)] for stream in (1, 2)
        ]
        write_gate(signals, taps, out_refs[step])
    for copy in plain:
        copy.wait()


def ready_kernel(filter_ref, weight_any, band_ref, weight_ref, sem):
    rows, span = band_ref.shape
    taps = filter_ref.shape[1]
    groups = rows // taps
    weights = pltpu.make_async_copy(weight_any, weight_ref, sem)
    weights.start()
    source = lax.broadcasted_iota(jnp.int32, (taps, span), 0)
    target = lax.broadcasted_iota(jnp.int32, (taps, span), 1)
    flip = (source + target == taps).astype(jnp.bfloat16)
    first_group = pl.multiple_of(lax.axis_index("ctx") * groups, groups)
    first = jnp.dot(filter_ref[pl.ds(first_group, groups)], flip, preferred_element_type=jnp.float32)
    for group in range(groups):
        repeated = jnp.broadcast_to(first[group : group + 1], (taps, span))
        banded = pltpu.roll(repeated, 0, 1, stride=1, stride_axis=0)
        band_ref[group * taps : (group + 1) * taps] = banded.astype(jnp.bfloat16)
    weights.wait()


def weights_kernel(third_ref, second_ref, near_ref, own_ref, short_ref, weight_ref, total_ref, feature_ref, query_s, key_s, signal_s):
    count = COUNT
    rows, own = query_s.shape[1:]
    position = lax.axis_index("ctx")
    for step, given in zip(ORDER, (third_ref, second_ref, near_ref, own_ref)):
        query_s[position ^ step] = given[0:rows]
        key_s[columns_of(position ^ step, rows)] = given[rows : 2 * rows]
        signal_s[columns_of(position ^ step, rows)] = given[2 * rows :]
    taps = [short_ref[lag, 0:1, columns_of(position, own)].astype(jnp.float32) for lag in range(3)]
    feature_ref[...] = featured(signal_s[...].astype(jnp.float32), taps)
    causal = lax.broadcasted_iota(jnp.int32, (rows, rows), 1) <= lax.broadcasted_iota(jnp.int32, (rows, rows), 0)
    for head in range(own // HEAD_DIM):
        columns = slice(head * HEAD_DIM, (head + 1) * HEAD_DIM)
        for block in range(count):
            here, seen = slice(block * rows, (block + 1) * rows), (block + 1) * rows
            scores = lax.dot_general(
                query_s[block, :, columns],
                key_s[0:seen, columns],
                (((1,), (1,)), ((), ())),
                preferred_element_type=jnp.float32,
            ) * HEAD_DIM ** (-0.5)
            own_scores = jnp.where(causal, scores[:, block * rows :], masked_score)
            pieces = [scores[:, : block * rows], own_scores] if block else [own_scores]
            scores = jnp.concatenate(pieces, axis=1)
            weights = jnp.exp(scores - jnp.max(scores, axis=1, keepdims=True))
            total_ref[here, head : head + 1] = jnp.sum(weights, axis=1, keepdims=True)
            weight_ref[head, here, 0:seen] = weights.astype(jnp.bfloat16)
            if seen < count * rows:
                weight_ref[head, here, seen:] = jnp.zeros((rows, count * rows - seen), jnp.bfloat16)


def mix_rows(block, weight_ref, total_ref, value_ref, out_ref):
    rows = out_ref.shape[0]
    here = columns_of(block, rows)
    for head in range(out_ref.shape[1] // HEAD_DIM):
        columns = slice(head * HEAD_DIM, (head + 1) * HEAD_DIM)
        mixed = jnp.dot(weight_ref[head, here], value_ref[:, columns], preferred_element_type=jnp.float32)
        out_ref[:, columns] = (mixed / total_ref[here, head : head + 1]).astype(jnp.bfloat16)


def values_kernel(*refs):
    count = COUNT
    gates, feature_ref = refs[:count], refs[count]
    band_ref, short_ref, gain_ref, weight_ref, total_ref = refs[count + 1 : count + 6]
    third_ref, second_ref, value_ref = refs[count + 6 : count + 9]
    edge_s, gate_s, filtered_s = refs[count + 9 :]
    rows, own = second_ref.shape
    per_group = own * rows // band_ref.shape[0]
    position = lax.axis_index("ctx")
    mine = columns_of(position, own)
    tiles = [slice(start, start + HEAD_DIM) for start in range(0, own, HEAD_DIM)]
    gate_s[0:rows] = jnp.zeros((rows, own), jnp.bfloat16)
    for step, gate in zip(ORDER, gates):
        for index, tile in enumerate(tiles):
            gate_s[columns_of((position ^ step) + 1, rows), tile] = gate[index * rows : (index + 1) * rows]
        edges = gate[len(tiles) * rows :].astype(jnp.float32)
        for index, tile in enumerate(tiles):
            edge_s[position ^ step, :, tile] = edges[index * EDGE : (index + 1) * EDGE]
    taps = [
        [short_ref[lag, stream : stream + 1, mine].astype(jnp.float32) for lag in range(3)] for stream in range(3)
    ]
    edge_row = lax.broadcasted_iota(jnp.int32, (EDGE, own), 0)
    head_row = lax.broadcasted_iota(jnp.int32, (2 * EDGE, own), 0)
    for block in range(1, count):
        fixed = 1.0
        for stream, back, on in ((1, 6, 2), (2, 2, 6)):
            joined = jnp.where(
                edge_row < 2, pltpu.roll(edge_s[block - 1], back, 0), pltpu.roll(edge_s[block], on, 0)
            )
            fixed = fixed * (
                taps[stream][0] * pltpu.roll(joined, 6, 0)
                + taps[stream][1] * pltpu.roll(joined, 7, 0)
                + taps[stream][2] * joined
            )
        here = slice((block + 1) * rows, (block + 1) * rows + 2 * EDGE)
        head = jnp.where(head_row < 2, jnp.concatenate([fixed, fixed], axis=0), gate_s[here].astype(jnp.float32))
        gate_s[here] = head.astype(jnp.bfloat16)
    gain = gain_ref[:, mine]
    chunk = 2 * HEAD_DIM // count
    in_chunk = chunk // per_group
    lane = lax.broadcasted_iota(jnp.int32, (rows, 2 * HEAD_DIM), 1) % chunk // per_group
    for part in range(own // chunk):
        columns = slice(part * chunk, (part + 1) * chunk)
        windows = [gate_s[block * rows : (block + 2) * rows, columns] for block in range(count)]
        mixed = jnp.dot(
            band_ref[part * in_chunk * rows : (part + 1) * in_chunk * rows],
            jnp.concatenate(windows, axis=1),
            preferred_element_type=jnp.float32,
        )
        filtered = mixed[:rows]
        for group in range(1, in_chunk):
            filtered = jnp.where(lane == group, mixed[group * rows : (group + 1) * rows], filtered)
        for block in range(count):
            filtered_s[block * rows : (block + 1) * rows, columns] = filtered[:, block * chunk : (block + 1) * chunk]
    value_ref[...] = (
        feature_ref[...] * (filtered_s[...] + gain * gate_s[rows:].astype(jnp.float32))
    ).astype(jnp.bfloat16)
    for step, out_ref in ((3, third_ref), (2, second_ref)):
        mix_rows(position ^ step, weight_ref, total_ref, value_ref, out_ref)


def near_rows_kernel(weight_ref, total_ref, value_ref, *refs):
    upper_ref, lower_ref, own_ref, near_s = refs
    half = upper_ref.shape[0]
    position = lax.axis_index("ctx")
    mix_rows(position ^ 1, weight_ref, total_ref, value_ref, near_s)
    upper_ref[...] = near_s[0:half]
    lower_ref[...] = near_s[half:]
    mix_rows(position, weight_ref, total_ref, value_ref, own_ref)


def project_kernel(spans, *refs):
    given, weight_ref = refs[:5], refs[5]
    out_refs, attended_s = refs[-1 - len(spans) : -1], refs[-1]
    second, third, upper, lower, mine = given
    half = upper.shape[0]
    rows, own = mine.shape
    position, here = lax.axis_index("ctx"), lax.axis_index("mp")
    attended_s[0:half, columns_of(position ^ 1, own)] = upper[...]
    attended_s[half:, columns_of(position ^ 1, own)] = lower[...]
    for step, piece in ((0, mine), (2, second), (3, third)):
        attended_s[:, columns_of(position ^ step, own)] = piece[...]
    for (mask, part, parts), out_ref in zip(spans, out_refs):
        columns = columns_of((here ^ mask) * parts + part, out_ref.shape[1])
        out_ref[...] = jnp.dot(
            attended_s[...], weight_ref[:, columns], preferred_element_type=jnp.float32
        ).astype(jnp.bfloat16)


def partial_kernel(second_ref, mine_ref, weight_ref, out_ref):
    own, width = mine_ref.shape[1], out_ref.shape[1] // 2
    position, here = lax.axis_index("ctx"), lax.axis_index("mp")
    for index, mask in enumerate((3, 2)):
        columns = columns_of(here ^ mask, width)
        out_ref[:, index * width : (index + 1) * width] = jnp.dot(
            mine_ref[...], weight_ref[columns_of(position, own), columns], preferred_element_type=jnp.float32
        ) + jnp.dot(
            second_ref[...], weight_ref[columns_of(position ^ 2, own), columns], preferred_element_type=jnp.float32
        )


def project_far_kernel(part, third_ref, upper_ref, lower_ref, partial_ref, weight_ref, *refs):
    given_ref, kept_ref = refs[-2:]
    own, size = third_ref.shape[1], given_ref.shape[1]
    width = partial_ref.shape[1] // 2
    position, here = lax.axis_index("ctx"), lax.axis_index("mp")
    near = jnp.concatenate([upper_ref[...], lower_ref[...]], axis=0)
    for index, (mask, out_ref) in enumerate(((3, given_ref), (2, kept_ref))):
        columns = columns_of((here ^ mask) * (width // size) + part, size)
        start = index * width + part * size
        total = partial_ref[:, start : start + size] + jnp.dot(
            third_ref[...], weight_ref[columns_of(position ^ 3, own), columns], preferred_element_type=jnp.float32
        )
        total = total + jnp.dot(
            near, weight_ref[columns_of(position ^ 1, own), columns], preferred_element_type=jnp.float32
        )
        out_ref[...] = total.astype(jnp.bfloat16)


def total_kernel(kept_ref, upper_ref, lower_ref, first_ref, second_ref, out_any, total_s, sems):
    half, cut = upper_ref.shape[0], first_ref.shape[1]
    copies = []
    for index, near_ref in enumerate((upper_ref, lower_ref)):
        here = slice(index * half, (index + 1) * half)
        for columns, crossed_ref in ((slice(0, cut), first_ref), (slice(cut, 2 * cut), second_ref)):
            total = (
                kept_ref[here, columns].astype(jnp.float32)
                + near_ref[:, columns].astype(jnp.float32)
                + crossed_ref[here].astype(jnp.float32)
            )
            total_s[here, columns] = total.astype(jnp.bfloat16)
        copy = pltpu.make_async_copy(total_s.at[here], out_any.at[here], sems.at[index])
        copy.start()
        copies.append(copy)
    for copy in copies:
        copy.wait()


VMEM_LIMIT = 40 * 1024 * 1024
PLAIN_LIMIT = 53 * 1024 * 1024 + 400 * 1024
GATE_LIMIT = 60 * 1024 * 1024
IN_HBM = pl.BlockSpec(memory_space=pltpu.HBM)
IN_VMEM = pl.BlockSpec(memory_space=pltpu.VMEM)
ANYWHERE = pl.BlockSpec(memory_space=pl.ANY)


def run_kernel(kernel, operands, outputs, scratch=(), spaces=None, limit=VMEM_LIMIT, cost=10**6, targets=None):
    return pl.pallas_call(
        kernel,
        out_shape=[jax.ShapeDtypeStruct(shape, dtype) for shape, dtype in outputs],
        in_specs=spaces or [IN_VMEM] * len(operands),
        out_specs=targets or [IN_VMEM] * len(outputs),
        scratch_shapes=scratch,
        compiler_params=pltpu.CompilerParams(vmem_limit_bytes=limit),
        cost_estimate=pl.CostEstimate(flops=cost, bytes_accessed=2**20, transcendentals=0),
        name=getattr(kernel, "func", kernel).__name__,
    )(*operands)


def swapped(value, axis, step):
    return lax.ppermute(value, axis, [(source, source ^ step) for source in range(lax.axis_size(axis))])


def by_heads(inputs, short_filter, long_filter, skip_gain, queries, key_rows, out_weight):
    rows, streams, channels = inputs.shape
    own = channels // COUNT
    groups, taps = long_filter.shape
    half = jnp.bfloat16
    piece, window = ((rows, own), half), COUNT * rows
    streamed = jnp.transpose(inputs, (1, 0, 2))
    far_plain = run_kernel(
        plain_kernel,
        (streamed, queries, key_rows),
        [((3 * rows, own), half)] * 2,
        [pltpu.SemaphoreType.DMA((6,))],
        [IN_HBM] * 3,
        PLAIN_LIMIT,
    )
    *gates, near_plain, own_plain = run_kernel(
        gate_kernel,
        (streamed, short_filter, queries, key_rows),
        [((own // HEAD_DIM * (rows + EDGE), HEAD_DIM), half)] * COUNT + [((3 * rows, own), half)] * 2,
        [
            pltpu.VMEM((2, rows, channels), half),
            pltpu.VMEM(short_filter.shape, half),
            pltpu.SemaphoreType.DMA((2,)),
            pltpu.SemaphoreType.DMA((6,)),
        ],
        [IN_HBM] * 4,
        GATE_LIMIT,
    )
    plain = [own_plain, near_plain, far_plain[1], far_plain[0]]
    plain = [swapped(plain[step], "ctx", step) for step in ORDER[:3]] + [plain[0]]
    gates = [swapped(gates[step], "ctx", step) for step in ORDER[:3]] + [gates[0]]
    band, weight = run_kernel(
        ready_kernel,
        (long_filter, out_weight),
        [((groups // COUNT * taps, 2 * taps), half), (out_weight.shape, half)],
        [pltpu.SemaphoreType.DMA],
        [IN_VMEM, IN_HBM],
    )
    soft, totals, feature = run_kernel(
        weights_kernel,
        (*plain, short_filter),
        [
            ((own // HEAD_DIM, window, window), half),
            ((window, HEAD_DIM), jnp.float32),
            ((window, own), jnp.float32),
        ],
        [
            pltpu.VMEM((COUNT, rows, own), half),
            pltpu.VMEM((window, own), half),
            pltpu.VMEM((window, own), half),
        ],
    )
    third, second, values = run_kernel(
        values_kernel,
        (*gates, feature, band, short_filter, skip_gain.reshape(1, channels), soft, totals),
        [piece, piece, ((window, own), half)],
        [
            pltpu.VMEM((COUNT, EDGE, own), jnp.float32),
            pltpu.VMEM((window + rows, own), half),
            pltpu.VMEM((window, own), jnp.float32),
        ],
    )
    third_got, second_got = swapped(third, "ctx", 3), swapped(second, "ctx", 2)
    upper, lower, mine = run_kernel(
        near_rows_kernel,
        (soft, totals, values),
        [((rows // 2, own), half)] * 2 + [piece],
        [pltpu.VMEM((rows, own), half)],
    )
    near = (swapped(upper, "ctx", 1), swapped(lower, "ctx", 1))
    return project_and_share((second_got, third_got, *near, mine), weight)


def projected(attended, out_weight, spans, after=(), cost=10**6):
    rows = attended[-1].shape[0]
    width = out_weight.shape[1] // lax.axis_size("mp")
    return run_kernel(
        functools.partial(project_kernel, spans),
        (*attended, out_weight, *after),
        [((rows, width // parts), jnp.bfloat16) for _, _, parts in spans],
        [pltpu.VMEM((rows, out_weight.shape[0]), jnp.bfloat16)],
        [IN_VMEM] * (len(attended) + 1) + [ANYWHERE] * len(after),
        cost=cost,
    )


NEAR_COST = 10**6


def added(*terms):
    total = terms[0].astype(jnp.float32)
    for term in terms[1:]:
        total = total + term.astype(jnp.float32)
    return total.astype(jnp.bfloat16)


def project_and_share(attended, out_weight):
    second, third, upper, lower, mine = attended
    rows = mine.shape[0]
    width = out_weight.shape[1] // lax.axis_size("mp")
    (partial,) = run_kernel(partial_kernel, (second, mine, out_weight), [((rows, 2 * width), jnp.float32)])
    crossed = []
    for part in range(2):
        given, kept = run_kernel(
            functools.partial(project_far_kernel, part),
            (third, upper, lower, partial, out_weight),
            [((rows, width // 2), jnp.bfloat16)] * 2,
        )
        far_sum = added(kept, swapped(given, "mp", 1))
        crossed.append(swapped(far_sum, "mp", 2))
    near_given, near_kept = projected(attended, out_weight, ((1, 0, 1), (0, 0, 1)), (far_sum,), NEAR_COST)
    half = near_given.shape[0] // 2
    near_got = [swapped(near_given[:half], "mp", 1), swapped(near_given[half:], "mp", 1)]
    (total,) = run_kernel(
        total_kernel,
        (near_kept, *near_got, *crossed),
        [(near_kept.shape, near_kept.dtype)],
        [pltpu.VMEM(near_kept.shape, near_kept.dtype), pltpu.SemaphoreType.DMA((2,))],
        targets=[IN_HBM],
    )
    return total


def per_device(inputs, short_filter, long_filter, skip_gain, queries, key_rows, out_weight):
    rows, _, channels = inputs.shape
    count = lax.axis_size("ctx")
    taps = long_filter.shape[1]
    splits = channels % (count * HEAD_DIM) == 0 and count == COUNT and rows == taps
    if splits and lax.axis_size("mp") == 4:
        return by_heads(inputs, short_filter, long_filter, skip_gain, queries, key_rows, out_weight)
    attended = by_rows(inputs, short_filter, long_filter, skip_gain, queries, key_rows)
    partial_out = jnp.dot(attended, out_weight, preferred_element_type=jnp.float32)
    return lax.psum_scatter(partial_out.astype(jnp.bfloat16), "mp", scatter_dimension=1, tiled=True)


def solution(mesh):
    placed = (
        P(("parts", "ctx"), None, "mp"),
        P(None, None, "mp"),
        P("mp", None),
        P("mp"),
        P(("parts", "ctx"), "mp"),
        P(("parts", "ctx"), "mp"),
        P("mp", None),
    )
    return jax.shard_map(
        per_device, mesh=mesh, in_specs=placed, out_specs=P(("parts", "ctx"), "mp"), check_vma=False
    )
```

```python
import functools

import jax
import jax.numpy as jnp
from jax import lax
from jax.experimental import pallas as pl
from jax.experimental.pallas import tpu as pltpu
from jax.sharding import PartitionSpec as P

HEAD_DIM = 128
COUNT = 4
ORDER = (3, 2, 1, 0)
EDGE = 8


masked_score = -1e30


def passed_along(value, axis, steps):
    count = lax.axis_size(axis)
    initial, last = (max(0, -steps), min(count, count - steps))
    return lax.ppermute(value, axis, [(source, source + steps) for source in range(initial, last)])


def toeplitz_taps(filters, row_count):
    group_count = filters.shape[0]
    tap_count = filters.shape[1]
    span = row_count + tap_count - 1
    flipped = filters[:, ::-1]
    padded_taps = jnp.concatenate(
        [flipped, jnp.zeros((group_count, row_count), filters.dtype)], axis=1
    )
    repeated = jnp.tile(padded_taps, (1, row_count))
    return repeated[:, : row_count * span].reshape(group_count, row_count, span)


def short_features(extended, short_filter, row_count):
    tap_count = short_filter.shape[0]
    features = jnp.zeros((row_count,) + extended.shape[1:], jnp.float32)
    for lag_index in range(tap_count):
        delayed = extended[
            tap_count - 1 - lag_index : tap_count - 1 - lag_index + row_count
        ].astype(jnp.float32)
        features = features + short_filter[lag_index].astype(jnp.float32)[None] * delayed
    return features


def attend(head_queries, query_pos, key_piece, value_piece):
    key_count = key_piece.shape[0]
    head_count = head_queries.shape[1]
    key_heads = key_piece.reshape(key_count, head_count, -1)
    value_heads = value_piece.reshape(key_count, head_count, -1)
    scores = jnp.einsum(
        "qhd,khd->hqk", head_queries, key_heads, preferred_element_type=jnp.float32
    ) * head_queries.shape[2] ** (-0.5)
    key_pos = lax.iota(jnp.int32, key_count)
    allowed = (key_pos[None, :] <= query_pos[:, None])[None]
    peak = jnp.max(jnp.where(allowed, scores, masked_score), axis=2)
    probabilities = jnp.where(allowed, jnp.exp(scores - peak[..., None]), 0.0)
    weight_sum = jnp.sum(probabilities, axis=2)
    mixed = jnp.einsum(
        "hqk,khd->hqd",
        probabilities.astype(jnp.bfloat16),
        value_heads,
        preferred_element_type=jnp.float32,
    )
    result = mixed / weight_sum[..., None]
    return jnp.transpose(result, (1, 0, 2)).reshape(result.shape[1], -1).astype(jnp.bfloat16)


def by_rows(inputs, short_filter, long_filter, skip_gain, queries, key_rows):
    row_count = inputs.shape[0]
    channels = inputs.shape[2]
    groups = long_filter.shape[0]
    tap_count = long_filter.shape[1]
    short_reach = short_filter.shape[0] - 1
    position = lax.axis_index("ctx")
    rim = passed_along(inputs[row_count - short_reach :], "ctx", 1)
    extended = jnp.concatenate([rim, inputs], axis=0)
    features = short_features(extended, short_filter, row_count)
    gate_product = (features[:, 1] * features[:, 2]).astype(jnp.bfloat16)
    gate_prev = passed_along(gate_product[row_count - (tap_count - 1) :], "ctx", 1)
    gate_ext = jnp.concatenate([gate_prev, gate_product], axis=0)
    toeplitz = toeplitz_taps(long_filter, row_count)
    filtered = jnp.einsum(
        "gtr,rgc->tgc",
        toeplitz,
        gate_ext.reshape(row_count + tap_count - 1, groups, channels // groups),
        preferred_element_type=jnp.float32,
    ).reshape(row_count, channels)
    values = (
        features[:, 0] * (filtered + skip_gain[None] * gate_product.astype(jnp.float32))
    ).astype(jnp.bfloat16)
    head_count = channels // HEAD_DIM
    head_queries = queries.reshape(row_count, head_count, HEAD_DIM)
    query_pos = position * row_count + lax.iota(jnp.int32, row_count)
    return attend(
        head_queries,
        query_pos,
        lax.all_gather(key_rows, "ctx", axis=0, tiled=True),
        lax.all_gather(values, "ctx", axis=0, tiled=True),
    )


def delayed(signal, lag):
    if lag == 0:
        return signal
    row = lax.broadcasted_iota(jnp.int32, signal.shape, 0)
    return jnp.where(row < lag, 0.0, pltpu.roll(signal, lag, 0))


def featured(signal, taps):
    total = taps[0] * signal
    for lag in range(1, len(taps)):
        total = total + taps[lag] * delayed(signal, lag)
    return total


def columns_of(block, width):
    return pl.ds(pl.multiple_of(block * width, width), width)


def write_gate(signals, taps, out_ref):
    rows, own = signals[0].shape
    tiles = [slice(start, start + HEAD_DIM) for start in range(0, own, HEAD_DIM)]
    edge_row = lax.broadcasted_iota(jnp.int32, (EDGE, own), 0)
    features = [featured(signal, tap) for signal, tap in zip(signals, taps)]
    gate = (features[0] * features[1]).astype(jnp.bfloat16)
    first, second = [
        jnp.where(
            edge_row % 4 < 2, pltpu.roll(signal[:EDGE], turn, 0), pltpu.roll(signal[rows - EDGE :], 4 - turn, 0)
        )
        for signal, turn in zip(signals, (0, 4))
    ]
    edges = jnp.where(edge_row < 4, first, second)
    for index, tile in enumerate(tiles):
        out_ref[index * rows : (index + 1) * rows] = gate[:, tile]
    out_ref[len(tiles) * rows :] = jnp.concatenate([edges[:, tile] for tile in tiles], axis=0).astype(jnp.bfloat16)


def plain_copies(sources, out_refs, steps, sems):
    rows, own = sources[0].shape[0], out_refs[0].shape[1]
    position = lax.axis_index("ctx")
    copies = []
    for step, out_ref in zip(steps, out_refs):
        columns = columns_of(position ^ step, own)
        for index, source in enumerate(sources):
            target = out_ref.at[index * rows : (index + 1) * rows]
            copies.append(pltpu.make_async_copy(source.at[:, columns], target, sems.at[len(copies)]))
    for copy in copies:
        copy.start()
    return copies


def plain_kernel(inputs_any, queries_any, keys_any, *refs):
    for copy in plain_copies((queries_any, keys_any, inputs_any.at[0]), refs[:2], ORDER[:2], refs[2]):
        copy.wait()


def gate_kernel(inputs_any, short_any, queries_any, keys_any, *refs):
    out_refs, plain_refs = refs[:COUNT], refs[COUNT : COUNT + 2]
    signal_s, short_s, sems, plain_sems = refs[COUNT + 2 :]
    own = plain_refs[0].shape[1]
    position = lax.axis_index("ctx")
    copies = [
        pltpu.make_async_copy(short_any, short_s, sems.at[0]),
        pltpu.make_async_copy(inputs_any.at[1:3], signal_s, sems.at[1]),
    ]
    for copy in copies:
        copy.start()
    plain = plain_copies((queries_any, keys_any, inputs_any.at[0]), plain_refs, ORDER[2:], plain_sems)
    for copy in copies:
        copy.wait()
    for step in ORDER:
        columns = columns_of(position ^ step, own)
        signals = [signal_s[stream, :, columns].astype(jnp.float32) for stream in range(2)]
        taps = [
            [short_s[lag, stream : stream + 1, columns].astype(jnp.float32) for lag in range(3)] for stream in (1, 2)
        ]
        write_gate(signals, taps, out_refs[step])
    for copy in plain:
        copy.wait()


def ready_kernel(filter_ref, weight_any, band_ref, weight_ref, sem):
    rows, span = band_ref.shape
    taps = filter_ref.shape[1]
    groups = rows // taps
    weights = pltpu.make_async_copy(weight_any, weight_ref, sem)
    weights.start()
    source = lax.broadcasted_iota(jnp.int32, (taps, span), 0)
    target = lax.broadcasted_iota(jnp.int32, (taps, span), 1)
    flip = (source + target == taps).astype(jnp.bfloat16)
    first_group = pl.multiple_of(lax.axis_index("ctx") * groups, groups)
    first = jnp.dot(filter_ref[pl.ds(first_group, groups)], flip, preferred_element_type=jnp.float32)
    for group in range(groups):
        repeated = jnp.broadcast_to(first[group : group + 1], (taps, span))
        banded = pltpu.roll(repeated, 0, 1, stride=1, stride_axis=0)
        band_ref[group * taps : (group + 1) * taps] = banded.astype(jnp.bfloat16)
    weights.wait()


def weights_kernel(third_ref, second_ref, near_ref, own_ref, short_ref, weight_ref, total_ref, feature_ref, query_s, key_s, signal_s):
    count = COUNT
    rows, own = query_s.shape[1:]
    position = lax.axis_index("ctx")
    for step, given in zip(ORDER, (third_ref, second_ref, near_ref, own_ref)):
        query_s[position ^ step] = given[0:rows]
        key_s[columns_of(position ^ step, rows)] = given[rows : 2 * rows]
        signal_s[columns_of(position ^ step, rows)] = given[2 * rows :]
    taps = [short_ref[lag, 0:1, columns_of(position, own)].astype(jnp.float32) for lag in range(3)]
    feature_ref[...] = featured(signal_s[...].astype(jnp.float32), taps)
    causal = lax.broadcasted_iota(jnp.int32, (rows, rows), 1) <= lax.broadcasted_iota(jnp.int32, (rows, rows), 0)
    for head in range(own // HEAD_DIM):
        columns = slice(head * HEAD_DIM, (head + 1) * HEAD_DIM)
        for block in range(count):
            here, seen = slice(block * rows, (block + 1) * rows), (block + 1) * rows
            scores = lax.dot_general(
                query_s[block, :, columns],
                key_s[0:seen, columns],
                (((1,), (1,)), ((), ())),
                preferred_element_type=jnp.float32,
            ) * HEAD_DIM ** (-0.5)
            own_scores = jnp.where(causal, scores[:, block * rows :], masked_score)
            pieces = [scores[:, : block * rows], own_scores] if block else [own_scores]
            scores = jnp.concatenate(pieces, axis=1)
            weights = jnp.exp(scores - jnp.max(scores, axis=1, keepdims=True))
            total_ref[here, head : head + 1] = jnp.sum(weights, axis=1, keepdims=True)
            weight_ref[head, here, 0:seen] = weights.astype(jnp.bfloat16)
            if seen < count * rows:
                weight_ref[head, here, seen:] = jnp.zeros((rows, count * rows - seen), jnp.bfloat16)


def mix_rows(block, weight_ref, total_ref, value_ref, out_ref):
    rows = out_ref.shape[0]
    here = columns_of(block, rows)
    for head in range(out_ref.shape[1] // HEAD_DIM):
        columns = slice(head * HEAD_DIM, (head + 1) * HEAD_DIM)
        mixed = jnp.dot(weight_ref[head, here], value_ref[:, columns], preferred_element_type=jnp.float32)
        out_ref[:, columns] = (mixed / total_ref[here, head : head + 1]).astype(jnp.bfloat16)


def values_kernel(*refs):
    count = COUNT
    gates, feature_ref = refs[:count], refs[count]
    band_ref, short_ref, gain_ref, weight_ref, total_ref = refs[count + 1 : count + 6]
    third_ref, second_ref, value_ref = refs[count + 6 : count + 9]
    edge_s, gate_s, filtered_s = refs[count + 9 :]
    rows, own = second_ref.shape
    per_group = own * rows // band_ref.shape[0]
    position = lax.axis_index("ctx")
    mine = columns_of(position, own)
    tiles = [slice(start, start + HEAD_DIM) for start in range(0, own, HEAD_DIM)]
    gate_s[0:rows] = jnp.zeros((rows, own), jnp.bfloat16)
    for step, gate in zip(ORDER, gates):
        for index, tile in enumerate(tiles):
            gate_s[columns_of((position ^ step) + 1, rows), tile] = gate[index * rows : (index + 1) * rows]
        edges = gate[len(tiles) * rows :].astype(jnp.float32)
        for index, tile in enumerate(tiles):
            edge_s[position ^ step, :, tile] = edges[index * EDGE : (index + 1) * EDGE]
    taps = [
        [short_ref[lag, stream : stream + 1, mine].astype(jnp.float32) for lag in range(3)] for stream in range(3)
    ]
    edge_row = lax.broadcasted_iota(jnp.int32, (EDGE, own), 0)
    head_row = lax.broadcasted_iota(jnp.int32, (2 * EDGE, own), 0)
    for block in range(1, count):
        fixed = 1.0
        for stream, back, on in ((1, 6, 2), (2, 2, 6)):
            joined = jnp.where(
                edge_row < 2, pltpu.roll(edge_s[block - 1], back, 0), pltpu.roll(edge_s[block], on, 0)
            )
            fixed = fixed * (
                taps[stream][0] * pltpu.roll(joined, 6, 0)
                + taps[stream][1] * pltpu.roll(joined, 7, 0)
                + taps[stream][2] * joined
            )
        here = slice((block + 1) * rows, (block + 1) * rows + 2 * EDGE)
        head = jnp.where(head_row < 2, jnp.concatenate([fixed, fixed], axis=0), gate_s[here].astype(jnp.float32))
        gate_s[here] = head.astype(jnp.bfloat16)
    gain = gain_ref[:, mine]
    chunk = 2 * HEAD_DIM // count
    in_chunk = chunk // per_group
    lane = lax.broadcasted_iota(jnp.int32, (rows, 2 * HEAD_DIM), 1) % chunk // per_group
    for part in range(own // chunk):
        columns = slice(part * chunk, (part + 1) * chunk)
        windows = [gate_s[block * rows : (block + 2) * rows, columns] for block in range(count)]
        mixed = jnp.dot(
            band_ref[part * in_chunk * rows : (part + 1) * in_chunk * rows],
            jnp.concatenate(windows, axis=1),
            preferred_element_type=jnp.float32,
        )
        filtered = mixed[:rows]
        for group in range(1, in_chunk):
            filtered = jnp.where(lane == group, mixed[group * rows : (group + 1) * rows], filtered)
        for block in range(count):
            filtered_s[block * rows : (block + 1) * rows, columns] = filtered[:, block * chunk : (block + 1) * chunk]
    value_ref[...] = (
        feature_ref[...] * (filtered_s[...] + gain * gate_s[rows:].astype(jnp.float32))
    ).astype(jnp.bfloat16)
    for step, out_ref in ((3, third_ref), (2, second_ref)):
        mix_rows(position ^ step, weight_ref, total_ref, value_ref, out_ref)


def near_rows_kernel(weight_ref, total_ref, value_ref, near_ref, own_ref):
    position = lax.axis_index("ctx")
    for step, out_ref in ((1, near_ref), (0, own_ref)):
        mix_rows(position ^ step, weight_ref, total_ref, value_ref, out_ref)


def project_kernel(masks, second_ref, third_ref, near_ref, mine_ref, weight_ref, _, *refs):
    out_refs, attended_s = refs[:-1], refs[-1]
    own, width = mine_ref.shape[1], out_refs[0].shape[1]
    position, here = lax.axis_index("ctx"), lax.axis_index("mp")
    for step, piece in ((0, mine_ref), (1, near_ref), (2, second_ref), (3, third_ref)):
        attended_s[:, columns_of(position ^ step, own)] = piece[...]
    for mask, out_ref in zip(masks, out_refs):
        out_ref[...] = jnp.dot(
            attended_s[...], weight_ref[:, columns_of(here ^ mask, width)], preferred_element_type=jnp.float32
        ).astype(jnp.bfloat16)


def partial_kernel(second_ref, mine_ref, weight_ref, out_ref):
    own, width = mine_ref.shape[1], out_ref.shape[1] // 2
    position, here = lax.axis_index("ctx"), lax.axis_index("mp")
    for index, mask in enumerate((3, 2)):
        columns = columns_of(here ^ mask, width)
        out_ref[:, index * width : (index + 1) * width] = jnp.dot(
            mine_ref[...], weight_ref[columns_of(position, own), columns], preferred_element_type=jnp.float32
        ) + jnp.dot(
            second_ref[...], weight_ref[columns_of(position ^ 2, own), columns], preferred_element_type=jnp.float32
        )


def project_far_kernel(part, third_ref, near_ref, partial_ref, weight_ref, given_ref, kept_ref):
    own, size = third_ref.shape[1], given_ref.shape[1]
    width = partial_ref.shape[1] // 2
    position, here = lax.axis_index("ctx"), lax.axis_index("mp")
    for index, (mask, out_ref) in enumerate(((3, given_ref), (2, kept_ref))):
        columns = columns_of((here ^ mask) * (width // size) + part, size)
        start = index * width + part * size
        total = partial_ref[:, start : start + size] + jnp.dot(
            third_ref[...], weight_ref[columns_of(position ^ 3, own), columns], preferred_element_type=jnp.float32
        )
        total = total + jnp.dot(
            near_ref[...], weight_ref[columns_of(position ^ 1, own), columns], preferred_element_type=jnp.float32
        )
        out_ref[...] = total.astype(jnp.bfloat16)


def total_kernel(kept_ref, upper_ref, lower_ref, first_ref, second_ref, out_any, total_s, sems):
    half, cut = upper_ref.shape[0], first_ref.shape[1]
    copies = []
    for index, near_ref in enumerate((upper_ref, lower_ref)):
        here = slice(index * half, (index + 1) * half)
        for columns, crossed_ref in ((slice(0, cut), first_ref), (slice(cut, 2 * cut), second_ref)):
            total = (
                kept_ref[here, columns].astype(jnp.float32)
                + near_ref[:, columns].astype(jnp.float32)
                + crossed_ref[here].astype(jnp.float32)
            )
            total_s[here, columns] = total.astype(jnp.bfloat16)
        copy = pltpu.make_async_copy(total_s.at[here], out_any.at[here], sems.at[index])
        copy.start()
        copies.append(copy)
    for copy in copies:
        copy.wait()


VMEM_LIMIT = 40 * 1024 * 1024
PLAIN_LIMIT = 53 * 1024 * 1024 + 400 * 1024
GATE_LIMIT = 60 * 1024 * 1024
IN_HBM = pl.BlockSpec(memory_space=pltpu.HBM)
IN_VMEM = pl.BlockSpec(memory_space=pltpu.VMEM)
ANYWHERE = pl.BlockSpec(memory_space=pl.ANY)


def run_kernel(kernel, operands, outputs, scratch=(), spaces=None, limit=VMEM_LIMIT, cost=10**6, targets=None):
    return pl.pallas_call(
        kernel,
        out_shape=[jax.ShapeDtypeStruct(shape, dtype) for shape, dtype in outputs],
        in_specs=spaces or [IN_VMEM] * len(operands),
        out_specs=targets or [IN_VMEM] * len(outputs),
        scratch_shapes=scratch,
        compiler_params=pltpu.CompilerParams(vmem_limit_bytes=limit),
        cost_estimate=pl.CostEstimate(flops=cost, bytes_accessed=2**20, transcendentals=0),
        name=getattr(kernel, "func", kernel).__name__,
    )(*operands)


def swapped(value, axis, step):
    return lax.ppermute(value, axis, [(source, source ^ step) for source in range(lax.axis_size(axis))])


def by_heads(inputs, short_filter, long_filter, skip_gain, queries, key_rows, out_weight):
    rows, streams, channels = inputs.shape
    own = channels // COUNT
    groups, taps = long_filter.shape
    half = jnp.bfloat16
    piece, window = ((rows, own), half), COUNT * rows
    streamed = jnp.transpose(inputs, (1, 0, 2))
    far_plain = run_kernel(
        plain_kernel,
        (streamed, queries, key_rows),
        [((3 * rows, own), half)] * 2,
        [pltpu.SemaphoreType.DMA((6,))],
        [IN_HBM] * 3,
        PLAIN_LIMIT,
    )
    *gates, near_plain, own_plain = run_kernel(
        gate_kernel,
        (streamed, short_filter, queries, key_rows),
        [((own // HEAD_DIM * (rows + EDGE), HEAD_DIM), half)] * COUNT + [((3 * rows, own), half)] * 2,
        [
            pltpu.VMEM((2, rows, channels), half),
            pltpu.VMEM(short_filter.shape, half),
            pltpu.SemaphoreType.DMA((2,)),
            pltpu.SemaphoreType.DMA((6,)),
        ],
        [IN_HBM] * 4,
        GATE_LIMIT,
    )
    plain = [own_plain, near_plain, far_plain[1], far_plain[0]]
    plain = [swapped(plain[step], "ctx", step) for step in ORDER[:3]] + [plain[0]]
    gates = [swapped(gates[step], "ctx", step) for step in ORDER[:3]] + [gates[0]]
    band, weight = run_kernel(
        ready_kernel,
        (long_filter, out_weight),
        [((groups // COUNT * taps, 2 * taps), half), (out_weight.shape, half)],
        [pltpu.SemaphoreType.DMA],
        [IN_VMEM, IN_HBM],
    )
    soft, totals, feature = run_kernel(
        weights_kernel,
        (*plain, short_filter),
        [
            ((own // HEAD_DIM, window, window), half),
            ((window, HEAD_DIM), jnp.float32),
            ((window, own), jnp.float32),
        ],
        [
            pltpu.VMEM((COUNT, rows, own), half),
            pltpu.VMEM((window, own), half),
            pltpu.VMEM((window, own), half),
        ],
    )
    third, second, values = run_kernel(
        values_kernel,
        (*gates, feature, band, short_filter, skip_gain.reshape(1, channels), soft, totals),
        [piece, piece, ((window, own), half)],
        [
            pltpu.VMEM((COUNT, EDGE, own), jnp.float32),
            pltpu.VMEM((window + rows, own), half),
            pltpu.VMEM((window, own), jnp.float32),
        ],
    )
    third_got, second_got = swapped(third, "ctx", 3), swapped(second, "ctx", 2)
    near, mine = run_kernel(near_rows_kernel, (soft, totals, values), [piece] * 2)
    return project_and_share((second_got, third_got, swapped(near, "ctx", 1), mine), weight)


def added(*terms):
    total = terms[0].astype(jnp.float32)
    for term in terms[1:]:
        total = total + term.astype(jnp.float32)
    return total.astype(jnp.bfloat16)


def project_and_share(attended, out_weight):
    second, third, near, mine = attended
    rows = mine.shape[0]
    width = out_weight.shape[1] // lax.axis_size("mp")
    (partial,) = run_kernel(partial_kernel, (second, mine, out_weight), [((rows, 2 * width), jnp.float32)])
    crossed = []
    for part in range(2):
        given, kept = run_kernel(
            functools.partial(project_far_kernel, part),
            (third, near, partial, out_weight),
            [((rows, width // 2), jnp.bfloat16)] * 2,
        )
        far_sum = added(kept, swapped(given, "mp", 1))
        crossed.append(swapped(far_sum, "mp", 2))
    near_given, near_kept = run_kernel(
        functools.partial(project_kernel, (1, 0)),
        (*attended, out_weight, far_sum),
        [((rows, width), jnp.bfloat16)] * 2,
        [pltpu.VMEM((rows, out_weight.shape[0]), jnp.bfloat16)],
        [IN_VMEM] * 5 + [ANYWHERE],
    )
    half = near_given.shape[0] // 2
    near_got = [swapped(near_given[:half], "mp", 1), swapped(near_given[half:], "mp", 1)]
    (total,) = run_kernel(
        total_kernel,
        (near_kept, *near_got, *crossed),
        [(near_kept.shape, near_kept.dtype)],
        [pltpu.VMEM(near_kept.shape, near_kept.dtype), pltpu.SemaphoreType.DMA((2,))],
        targets=[IN_HBM],
    )
    return total


def per_device(inputs, short_filter, long_filter, skip_gain, queries, key_rows, out_weight):
    rows, _, channels = inputs.shape
    count = lax.axis_size("ctx")
    taps = long_filter.shape[1]
    splits = channels % (count * HEAD_DIM) == 0 and count == COUNT and rows == taps
    if splits and lax.axis_size("mp") == 4:
        return by_heads(inputs, short_filter, long_filter, skip_gain, queries, key_rows, out_weight)
    attended = by_rows(inputs, short_filter, long_filter, skip_gain, queries, key_rows)
    partial_out = jnp.dot(attended, out_weight, preferred_element_type=jnp.float32)
    return lax.psum_scatter(partial_out.astype(jnp.bfloat16), "mp", scatter_dimension=1, tiled=True)


def solution(mesh):
    placed = (
        P(("parts", "ctx"), None, "mp"),
        P(None, None, "mp"),
        P("mp", None),
        P("mp"),
        P(("parts", "ctx"), "mp"),
        P(("parts", "ctx"), "mp"),
        P("mp", None),
    )
    return jax.shard_map(
        per_device, mesh=mesh, in_specs=placed, out_specs=P(("parts", "ctx"), "mp"), check_vma=False
    )
```

```python
import functools

import jax
import jax.numpy as jnp
from jax import lax
from jax.experimental import pallas as pl
from jax.experimental.pallas import tpu as pltpu
from jax.sharding import PartitionSpec as P

HEAD_DIM = 128
COUNT = 4
ORDER = (3, 2, 1, 0)
EDGE = 8


masked_score = -1e30


def passed_along(value, axis, steps):
    count = lax.axis_size(axis)
    initial, last = (max(0, -steps), min(count, count - steps))
    return lax.ppermute(value, axis, [(source, source + steps) for source in range(initial, last)])


def toeplitz_taps(filters, row_count):
    group_count = filters.shape[0]
    tap_count = filters.shape[1]
    span = row_count + tap_count - 1
    flipped = filters[:, ::-1]
    padded_taps = jnp.concatenate(
        [flipped, jnp.zeros((group_count, row_count), filters.dtype)], axis=1
    )
    repeated = jnp.tile(padded_taps, (1, row_count))
    return repeated[:, : row_count * span].reshape(group_count, row_count, span)


def short_features(extended, short_filter, row_count):
    tap_count = short_filter.shape[0]
    features = jnp.zeros((row_count,) + extended.shape[1:], jnp.float32)
    for lag_index in range(tap_count):
        delayed = extended[
            tap_count - 1 - lag_index : tap_count - 1 - lag_index + row_count
        ].astype(jnp.float32)
        features = features + short_filter[lag_index].astype(jnp.float32)[None] * delayed
    return features


def attend(head_queries, query_pos, key_piece, value_piece):
    key_count = key_piece.shape[0]
    head_count = head_queries.shape[1]
    key_heads = key_piece.reshape(key_count, head_count, -1)
    value_heads = value_piece.reshape(key_count, head_count, -1)
    scores = jnp.einsum(
        "qhd,khd->hqk", head_queries, key_heads, preferred_element_type=jnp.float32
    ) * head_queries.shape[2] ** (-0.5)
    key_pos = lax.iota(jnp.int32, key_count)
    allowed = (key_pos[None, :] <= query_pos[:, None])[None]
    peak = jnp.max(jnp.where(allowed, scores, masked_score), axis=2)
    probabilities = jnp.where(allowed, jnp.exp(scores - peak[..., None]), 0.0)
    weight_sum = jnp.sum(probabilities, axis=2)
    mixed = jnp.einsum(
        "hqk,khd->hqd",
        probabilities.astype(jnp.bfloat16),
        value_heads,
        preferred_element_type=jnp.float32,
    )
    result = mixed / weight_sum[..., None]
    return jnp.transpose(result, (1, 0, 2)).reshape(result.shape[1], -1).astype(jnp.bfloat16)


def by_rows(inputs, short_filter, long_filter, skip_gain, queries, key_rows):
    row_count = inputs.shape[0]
    channels = inputs.shape[2]
    groups = long_filter.shape[0]
    tap_count = long_filter.shape[1]
    short_reach = short_filter.shape[0] - 1
    position = lax.axis_index("ctx")
    rim = passed_along(inputs[row_count - short_reach :], "ctx", 1)
    extended = jnp.concatenate([rim, inputs], axis=0)
    features = short_features(extended, short_filter, row_count)
    gate_product = (features[:, 1] * features[:, 2]).astype(jnp.bfloat16)
    gate_prev = passed_along(gate_product[row_count - (tap_count - 1) :], "ctx", 1)
    gate_ext = jnp.concatenate([gate_prev, gate_product], axis=0)
    toeplitz = toeplitz_taps(long_filter, row_count)
    filtered = jnp.einsum(
        "gtr,rgc->tgc",
        toeplitz,
        gate_ext.reshape(row_count + tap_count - 1, groups, channels // groups),
        preferred_element_type=jnp.float32,
    ).reshape(row_count, channels)
    values = (
        features[:, 0] * (filtered + skip_gain[None] * gate_product.astype(jnp.float32))
    ).astype(jnp.bfloat16)
    head_count = channels // HEAD_DIM
    head_queries = queries.reshape(row_count, head_count, HEAD_DIM)
    query_pos = position * row_count + lax.iota(jnp.int32, row_count)
    return attend(
        head_queries,
        query_pos,
        lax.all_gather(key_rows, "ctx", axis=0, tiled=True),
        lax.all_gather(values, "ctx", axis=0, tiled=True),
    )


def delayed(signal, lag):
    if lag == 0:
        return signal
    row = lax.broadcasted_iota(jnp.int32, signal.shape, 0)
    return jnp.where(row < lag, 0.0, pltpu.roll(signal, lag, 0))


def featured(signal, taps):
    total = taps[0] * signal
    for lag in range(1, len(taps)):
        total = total + taps[lag] * delayed(signal, lag)
    return total


def columns_of(block, width):
    return pl.ds(pl.multiple_of(block * width, width), width)


def write_gate(signals, taps, out_ref):
    rows, own = signals[0].shape
    tiles = [slice(start, start + HEAD_DIM) for start in range(0, own, HEAD_DIM)]
    edge_row = lax.broadcasted_iota(jnp.int32, (EDGE, own), 0)
    features = [featured(signal, tap) for signal, tap in zip(signals, taps)]
    gate = (features[0] * features[1]).astype(jnp.bfloat16)
    first, second = [
        jnp.where(
            edge_row % 4 < 2, pltpu.roll(signal[:EDGE], turn, 0), pltpu.roll(signal[rows - EDGE :], 4 - turn, 0)
        )
        for signal, turn in zip(signals, (0, 4))
    ]
    edges = jnp.where(edge_row < 4, first, second)
    for index, tile in enumerate(tiles):
        out_ref[index * rows : (index + 1) * rows] = gate[:, tile]
    out_ref[len(tiles) * rows :] = jnp.concatenate([edges[:, tile] for tile in tiles], axis=0).astype(jnp.bfloat16)


def plain_copies(sources, out_refs, steps, sems):
    rows, own = sources[0].shape[0], out_refs[0].shape[1]
    position = lax.axis_index("ctx")
    copies = []
    for step, out_ref in zip(steps, out_refs):
        columns = columns_of(position ^ step, own)
        for index, source in enumerate(sources):
            target = out_ref.at[index * rows : (index + 1) * rows]
            copies.append(pltpu.make_async_copy(source.at[:, columns], target, sems.at[len(copies)]))
    for copy in copies:
        copy.start()
    return copies


def plain_kernel(inputs_any, queries_any, keys_any, *refs):
    for copy in plain_copies((queries_any, keys_any, inputs_any.at[0]), refs[:2], ORDER[:2], refs[2]):
        copy.wait()


def gate_kernel(inputs_any, short_any, queries_any, keys_any, *refs):
    out_refs, plain_refs = refs[:COUNT], refs[COUNT : COUNT + 2]
    signal_s, short_s, sems, plain_sems = refs[COUNT + 2 :]
    own = plain_refs[0].shape[1]
    position = lax.axis_index("ctx")
    copies = [
        pltpu.make_async_copy(short_any, short_s, sems.at[0]),
        pltpu.make_async_copy(inputs_any.at[1:3], signal_s, sems.at[1]),
    ]
    for copy in copies:
        copy.start()
    plain = plain_copies((queries_any, keys_any, inputs_any.at[0]), plain_refs, ORDER[2:], plain_sems)
    for copy in copies:
        copy.wait()
    for step in ORDER:
        columns = columns_of(position ^ step, own)
        signals = [signal_s[stream, :, columns].astype(jnp.float32) for stream in range(2)]
        taps = [
            [short_s[lag, stream : stream + 1, columns].astype(jnp.float32) for lag in range(3)] for stream in (1, 2)
        ]
        write_gate(signals, taps, out_refs[step])
    for copy in plain:
        copy.wait()


def ready_kernel(filter_ref, weight_any, band_ref, weight_ref, sem):
    rows, span = band_ref.shape
    taps = filter_ref.shape[1]
    groups = rows // taps
    weights = pltpu.make_async_copy(weight_any, weight_ref, sem)
    weights.start()
    source = lax.broadcasted_iota(jnp.int32, (taps, span), 0)
    target = lax.broadcasted_iota(jnp.int32, (taps, span), 1)
    flip = (source + target == taps).astype(jnp.bfloat16)
    first_group = pl.multiple_of(lax.axis_index("ctx") * groups, groups)
    first = jnp.dot(filter_ref[pl.ds(first_group, groups)], flip, preferred_element_type=jnp.float32)
    for group in range(groups):
        repeated = jnp.broadcast_to(first[group : group + 1], (taps, span))
        banded = pltpu.roll(repeated, 0, 1, stride=1, stride_axis=0)
        band_ref[group * taps : (group + 1) * taps] = banded.astype(jnp.bfloat16)
    weights.wait()


def weights_kernel(third_ref, second_ref, near_ref, own_ref, short_ref, weight_ref, total_ref, feature_ref, query_s, key_s, signal_s):
    count = COUNT
    rows, own = query_s.shape[1:]
    position = lax.axis_index("ctx")
    for step, given in zip(ORDER, (third_ref, second_ref, near_ref, own_ref)):
        query_s[position ^ step] = given[0:rows]
        key_s[columns_of(position ^ step, rows)] = given[rows : 2 * rows]
        signal_s[columns_of(position ^ step, rows)] = given[2 * rows :]
    taps = [short_ref[lag, 0:1, columns_of(position, own)].astype(jnp.float32) for lag in range(3)]
    feature_ref[...] = featured(signal_s[...].astype(jnp.float32), taps)
    causal = lax.broadcasted_iota(jnp.int32, (rows, rows), 1) <= lax.broadcasted_iota(jnp.int32, (rows, rows), 0)
    for head in range(own // HEAD_DIM):
        columns = slice(head * HEAD_DIM, (head + 1) * HEAD_DIM)
        for block in range(count):
            here, seen = slice(block * rows, (block + 1) * rows), (block + 1) * rows
            scores = lax.dot_general(
                query_s[block, :, columns],
                key_s[0:seen, columns],
                (((1,), (1,)), ((), ())),
                preferred_element_type=jnp.float32,
            ) * HEAD_DIM ** (-0.5)
            own_scores = jnp.where(causal, scores[:, block * rows :], masked_score)
            pieces = [scores[:, : block * rows], own_scores] if block else [own_scores]
            scores = jnp.concatenate(pieces, axis=1)
            weights = jnp.exp(scores - jnp.max(scores, axis=1, keepdims=True))
            total_ref[here, head : head + 1] = jnp.sum(weights, axis=1, keepdims=True)
            weight_ref[head, here, 0:seen] = weights.astype(jnp.bfloat16)
            if seen < count * rows:
                weight_ref[head, here, seen:] = jnp.zeros((rows, count * rows - seen), jnp.bfloat16)


def mix_rows(block, weight_ref, total_ref, value_ref, out_ref):
    rows = out_ref.shape[0]
    here = columns_of(block, rows)
    for head in range(out_ref.shape[1] // HEAD_DIM):
        columns = slice(head * HEAD_DIM, (head + 1) * HEAD_DIM)
        mixed = jnp.dot(weight_ref[head, here], value_ref[:, columns], preferred_element_type=jnp.float32)
        out_ref[:, columns] = (mixed / total_ref[here, head : head + 1]).astype(jnp.bfloat16)


def values_kernel(*refs):
    count = COUNT
    gates, feature_ref = refs[:count], refs[count]
    band_ref, short_ref, gain_ref, weight_ref, total_ref = refs[count + 1 : count + 6]
    third_ref, second_ref, value_ref = refs[count + 6 : count + 9]
    edge_s, gate_s, filtered_s = refs[count + 9 :]
    rows, own = second_ref.shape
    per_group = own * rows // band_ref.shape[0]
    position = lax.axis_index("ctx")
    mine = columns_of(position, own)
    tiles = [slice(start, start + HEAD_DIM) for start in range(0, own, HEAD_DIM)]
    gate_s[0:rows] = jnp.zeros((rows, own), jnp.bfloat16)
    for step, gate in zip(ORDER, gates):
        for index, tile in enumerate(tiles):
            gate_s[columns_of((position ^ step) + 1, rows), tile] = gate[index * rows : (index + 1) * rows]
        edges = gate[len(tiles) * rows :].astype(jnp.float32)
        for index, tile in enumerate(tiles):
            edge_s[position ^ step, :, tile] = edges[index * EDGE : (index + 1) * EDGE]
    taps = [
        [short_ref[lag, stream : stream + 1, mine].astype(jnp.float32) for lag in range(3)] for stream in range(3)
    ]
    edge_row = lax.broadcasted_iota(jnp.int32, (EDGE, own), 0)
    head_row = lax.broadcasted_iota(jnp.int32, (2 * EDGE, own), 0)
    for block in range(1, count):
        fixed = 1.0
        for stream, back, on in ((1, 6, 2), (2, 2, 6)):
            joined = jnp.where(
                edge_row < 2, pltpu.roll(edge_s[block - 1], back, 0), pltpu.roll(edge_s[block], on, 0)
            )
            fixed = fixed * (
                taps[stream][0] * pltpu.roll(joined, 6, 0)
                + taps[stream][1] * pltpu.roll(joined, 7, 0)
                + taps[stream][2] * joined
            )
        here = slice((block + 1) * rows, (block + 1) * rows + 2 * EDGE)
        head = jnp.where(head_row < 2, jnp.concatenate([fixed, fixed], axis=0), gate_s[here].astype(jnp.float32))
        gate_s[here] = head.astype(jnp.bfloat16)
    gain = gain_ref[:, mine]
    chunk = 2 * HEAD_DIM // count
    in_chunk = chunk // per_group
    lane = lax.broadcasted_iota(jnp.int32, (rows, 2 * HEAD_DIM), 1) % chunk // per_group
    for part in range(own // chunk):
        columns = slice(part * chunk, (part + 1) * chunk)
        windows = [gate_s[block * rows : (block + 2) * rows, columns] for block in range(count)]
        mixed = jnp.dot(
            band_ref[part * in_chunk * rows : (part + 1) * in_chunk * rows],
            jnp.concatenate(windows, axis=1),
            preferred_element_type=jnp.float32,
        )
        filtered = mixed[:rows]
        for group in range(1, in_chunk):
            filtered = jnp.where(lane == group, mixed[group * rows : (group + 1) * rows], filtered)
        for block in range(count):
            filtered_s[block * rows : (block + 1) * rows, columns] = filtered[:, block * chunk : (block + 1) * chunk]
    value_ref[...] = (
        feature_ref[...] * (filtered_s[...] + gain * gate_s[rows:].astype(jnp.float32))
    ).astype(jnp.bfloat16)
    for step, out_ref in ((3, third_ref), (2, second_ref)):
        mix_rows(position ^ step, weight_ref, total_ref, value_ref, out_ref)


def near_rows_kernel(weight_ref, total_ref, value_ref, near_ref, own_ref):
    position = lax.axis_index("ctx")
    for step, out_ref in ((1, near_ref), (0, own_ref)):
        mix_rows(position ^ step, weight_ref, total_ref, value_ref, out_ref)


def project_kernel(masks, second_ref, third_ref, near_ref, mine_ref, weight_ref, _, *refs):
    out_refs, attended_s = refs[:-1], refs[-1]
    own, width = mine_ref.shape[1], out_refs[0].shape[1]
    position, here = lax.axis_index("ctx"), lax.axis_index("mp")
    for step, piece in ((0, mine_ref), (1, near_ref), (2, second_ref), (3, third_ref)):
        attended_s[:, columns_of(position ^ step, own)] = piece[...]
    for mask, out_ref in zip(masks, out_refs):
        out_ref[...] = jnp.dot(
            attended_s[...], weight_ref[:, columns_of(here ^ mask, width)], preferred_element_type=jnp.float32
        ).astype(jnp.bfloat16)


def partial_kernel(second_ref, mine_ref, weight_ref, out_ref):
    own, width = mine_ref.shape[1], out_ref.shape[1] // 2
    position, here = lax.axis_index("ctx"), lax.axis_index("mp")
    for index, mask in enumerate((3, 2)):
        columns = columns_of(here ^ mask, width)
        out_ref[:, index * width : (index + 1) * width] = jnp.dot(
            mine_ref[...], weight_ref[columns_of(position, own), columns], preferred_element_type=jnp.float32
        ) + jnp.dot(
            second_ref[...], weight_ref[columns_of(position ^ 2, own), columns], preferred_element_type=jnp.float32
        )


def partial_third_kernel(third_ref, partial_ref, weight_ref, out_ref):
    own, width = third_ref.shape[1], out_ref.shape[1] // 2
    position, here = lax.axis_index("ctx"), lax.axis_index("mp")
    for index, mask in enumerate((3, 2)):
        span = slice(index * width, (index + 1) * width)
        out_ref[:, span] = partial_ref[:, span] + jnp.dot(
            third_ref[...],
            weight_ref[columns_of(position ^ 3, own), columns_of(here ^ mask, width)],
            preferred_element_type=jnp.float32,
        )


def project_far_kernel(part, near_ref, partial_ref, weight_ref, given_ref, kept_ref):
    own, size = near_ref.shape[1], given_ref.shape[1]
    width = partial_ref.shape[1] // 2
    position, here = lax.axis_index("ctx"), lax.axis_index("mp")
    for index, (mask, out_ref) in enumerate(((3, given_ref), (2, kept_ref))):
        columns = columns_of((here ^ mask) * (width // size) + part, size)
        start = index * width + part * size
        total = partial_ref[:, start : start + size] + jnp.dot(
            near_ref[...], weight_ref[columns_of(position ^ 1, own), columns], preferred_element_type=jnp.float32
        )
        out_ref[...] = total.astype(jnp.bfloat16)


def total_kernel(part, kept_ref, upper_ref, lower_ref, crossed_ref, *refs):
    out_any, total_s, sem = refs[-3:]
    half, size = upper_ref.shape[0], crossed_ref.shape[1]
    columns = slice(part * size, (part + 1) * size)
    for index, near_ref in enumerate((upper_ref, lower_ref)):
        here = slice(index * half, (index + 1) * half)
        total = (
            kept_ref[here, columns].astype(jnp.float32)
            + near_ref[:, columns].astype(jnp.float32)
            + crossed_ref[here].astype(jnp.float32)
        )
        total_s[here] = total.astype(jnp.bfloat16)
    copy = pltpu.make_async_copy(total_s, out_any.at[:, columns], sem)
    copy.start()
    copy.wait()


VMEM_LIMIT = 40 * 1024 * 1024
PLAIN_LIMIT = 53 * 1024 * 1024 + 400 * 1024
GATE_LIMIT = 60 * 1024 * 1024
IN_HBM = pl.BlockSpec(memory_space=pltpu.HBM)
IN_VMEM = pl.BlockSpec(memory_space=pltpu.VMEM)
ANYWHERE = pl.BlockSpec(memory_space=pl.ANY)


def run_kernel(kernel, operands, outputs, scratch=(), spaces=None, limit=VMEM_LIMIT, cost=10**6, targets=None, aliases=None):
    return pl.pallas_call(
        kernel,
        out_shape=[jax.ShapeDtypeStruct(shape, dtype) for shape, dtype in outputs],
        in_specs=spaces or [IN_VMEM] * len(operands),
        out_specs=targets or [IN_VMEM] * len(outputs),
        scratch_shapes=scratch,
        input_output_aliases=aliases or {},
        compiler_params=pltpu.CompilerParams(vmem_limit_bytes=limit),
        cost_estimate=pl.CostEstimate(flops=cost, bytes_accessed=2**20, transcendentals=0),
        name=getattr(kernel, "func", kernel).__name__,
    )(*operands)


def swapped(value, axis, step):
    return lax.ppermute(value, axis, [(source, source ^ step) for source in range(lax.axis_size(axis))])


def by_heads(inputs, short_filter, long_filter, skip_gain, queries, key_rows, out_weight):
    rows, streams, channels = inputs.shape
    own = channels // COUNT
    groups, taps = long_filter.shape
    half = jnp.bfloat16
    piece, window = ((rows, own), half), COUNT * rows
    streamed = jnp.transpose(inputs, (1, 0, 2))
    far_plain = run_kernel(
        plain_kernel,
        (streamed, queries, key_rows),
        [((3 * rows, own), half)] * 2,
        [pltpu.SemaphoreType.DMA((6,))],
        [IN_HBM] * 3,
        PLAIN_LIMIT,
    )
    *gates, near_plain, own_plain = run_kernel(
        gate_kernel,
        (streamed, short_filter, queries, key_rows),
        [((own // HEAD_DIM * (rows + EDGE), HEAD_DIM), half)] * COUNT + [((3 * rows, own), half)] * 2,
        [
            pltpu.VMEM((2, rows, channels), half),
            pltpu.VMEM(short_filter.shape, half),
            pltpu.SemaphoreType.DMA((2,)),
            pltpu.SemaphoreType.DMA((6,)),
        ],
        [IN_HBM] * 4,
        GATE_LIMIT,
    )
    plain = [own_plain, near_plain, far_plain[1], far_plain[0]]
    plain = [swapped(plain[step], "ctx", step) for step in ORDER[:3]] + [plain[0]]
    gates = [swapped(gates[step], "ctx", step) for step in ORDER[:3]] + [gates[0]]
    band, weight = run_kernel(
        ready_kernel,
        (long_filter, out_weight),
        [((groups // COUNT * taps, 2 * taps), half), (out_weight.shape, half)],
        [pltpu.SemaphoreType.DMA],
        [IN_VMEM, IN_HBM],
    )
    soft, totals, feature = run_kernel(
        weights_kernel,
        (*plain, short_filter),
        [
            ((own // HEAD_DIM, window, window), half),
            ((window, HEAD_DIM), jnp.float32),
            ((window, own), jnp.float32),
        ],
        [
            pltpu.VMEM((COUNT, rows, own), half),
            pltpu.VMEM((window, own), half),
            pltpu.VMEM((window, own), half),
        ],
    )
    third, second, values = run_kernel(
        values_kernel,
        (*gates, feature, band, short_filter, skip_gain.reshape(1, channels), soft, totals),
        [piece, piece, ((window, own), half)],
        [
            pltpu.VMEM((COUNT, EDGE, own), jnp.float32),
            pltpu.VMEM((window + rows, own), half),
            pltpu.VMEM((window, own), jnp.float32),
        ],
    )
    third_got, second_got = swapped(third, "ctx", 3), swapped(second, "ctx", 2)
    near, mine = run_kernel(near_rows_kernel, (soft, totals, values), [piece] * 2)
    return project_and_share((second_got, third_got, swapped(near, "ctx", 1), mine), weight)


def added(*terms):
    total = terms[0].astype(jnp.float32)
    for term in terms[1:]:
        total = total + term.astype(jnp.float32)
    return total.astype(jnp.bfloat16)


def project_and_share(attended, out_weight):
    second, third, near, mine = attended
    rows = mine.shape[0]
    width = out_weight.shape[1] // lax.axis_size("mp")
    (partial,) = run_kernel(partial_kernel, (second, mine, out_weight), [((rows, 2 * width), jnp.float32)])
    (partial,) = run_kernel(
        partial_third_kernel, (third, partial, out_weight), [((rows, 2 * width), jnp.float32)]
    )
    crossed = []
    for part in range(2):
        given, kept = run_kernel(
            functools.partial(project_far_kernel, part),
            (near, partial, out_weight),
            [((rows, width // 2), jnp.bfloat16)] * 2,
        )
        far_sum = added(kept, swapped(given, "mp", 1))
        crossed.append(swapped(far_sum, "mp", 2))
    near_given, near_kept = run_kernel(
        functools.partial(project_kernel, (1, 0)),
        (*attended, out_weight, far_sum),
        [((rows, width), jnp.bfloat16)] * 2,
        [pltpu.VMEM((rows, out_weight.shape[0]), jnp.bfloat16)],
        [IN_VMEM] * 5 + [ANYWHERE],
    )
    half = near_given.shape[0] // 2
    near_got = [swapped(near_given[:half], "mp", 1), swapped(near_given[half:], "mp", 1)]
    total = []
    for part, piece in enumerate(crossed):
        total = run_kernel(
            functools.partial(total_kernel, part),
            (near_kept, *near_got, piece, *total),
            [(near_kept.shape, near_kept.dtype)],
            [pltpu.VMEM(piece.shape, piece.dtype), pltpu.SemaphoreType.DMA],
            [IN_VMEM] * 4 + [IN_HBM] * len(total),
            targets=[IN_HBM],
            aliases={4: 0} if total else {},
        )
    return total[0]


def per_device(inputs, short_filter, long_filter, skip_gain, queries, key_rows, out_weight):
    rows, _, channels = inputs.shape
    count = lax.axis_size("ctx")
    taps = long_filter.shape[1]
    splits = channels % (count * HEAD_DIM) == 0 and count == COUNT and rows == taps
    if splits and lax.axis_size("mp") == 4:
        return by_heads(inputs, short_filter, long_filter, skip_gain, queries, key_rows, out_weight)
    attended = by_rows(inputs, short_filter, long_filter, skip_gain, queries, key_rows)
    partial_out = jnp.dot(attended, out_weight, preferred_element_type=jnp.float32)
    return lax.psum_scatter(partial_out.astype(jnp.bfloat16), "mp", scatter_dimension=1, tiled=True)


def solution(mesh):
    placed = (
        P(("parts", "ctx"), None, "mp"),
        P(None, None, "mp"),
        P("mp", None),
        P("mp"),
        P(("parts", "ctx"), "mp"),
        P(("parts", "ctx"), "mp"),
        P("mp", None),
    )
    return jax.shard_map(
        per_device, mesh=mesh, in_specs=placed, out_specs=P(("parts", "ctx"), "mp"), check_vma=False
    )
```

```python
import functools

import jax
import jax.numpy as jnp
from jax import lax
from jax.experimental import pallas as pl
from jax.experimental.pallas import tpu as pltpu
from jax.sharding import PartitionSpec as P

HEAD_DIM = 128
COUNT = 4
ORDER = (3, 2, 1, 0)
EDGE = 8


masked_score = -1e30


def passed_along(value, axis, steps):
    count = lax.axis_size(axis)
    initial, last = (max(0, -steps), min(count, count - steps))
    return lax.ppermute(value, axis, [(source, source + steps) for source in range(initial, last)])


def toeplitz_taps(filters, row_count):
    group_count = filters.shape[0]
    tap_count = filters.shape[1]
    span = row_count + tap_count - 1
    flipped = filters[:, ::-1]
    padded_taps = jnp.concatenate(
        [flipped, jnp.zeros((group_count, row_count), filters.dtype)], axis=1
    )
    repeated = jnp.tile(padded_taps, (1, row_count))
    return repeated[:, : row_count * span].reshape(group_count, row_count, span)


def short_features(extended, short_filter, row_count):
    tap_count = short_filter.shape[0]
    features = jnp.zeros((row_count,) + extended.shape[1:], jnp.float32)
    for lag_index in range(tap_count):
        delayed = extended[
            tap_count - 1 - lag_index : tap_count - 1 - lag_index + row_count
        ].astype(jnp.float32)
        features = features + short_filter[lag_index].astype(jnp.float32)[None] * delayed
    return features


def attend(head_queries, query_pos, key_piece, value_piece):
    key_count = key_piece.shape[0]
    head_count = head_queries.shape[1]
    key_heads = key_piece.reshape(key_count, head_count, -1)
    value_heads = value_piece.reshape(key_count, head_count, -1)
    scores = jnp.einsum(
        "qhd,khd->hqk", head_queries, key_heads, preferred_element_type=jnp.float32
    ) * head_queries.shape[2] ** (-0.5)
    key_pos = lax.iota(jnp.int32, key_count)
    allowed = (key_pos[None, :] <= query_pos[:, None])[None]
    peak = jnp.max(jnp.where(allowed, scores, masked_score), axis=2)
    probabilities = jnp.where(allowed, jnp.exp(scores - peak[..., None]), 0.0)
    weight_sum = jnp.sum(probabilities, axis=2)
    mixed = jnp.einsum(
        "hqk,khd->hqd",
        probabilities.astype(jnp.bfloat16),
        value_heads,
        preferred_element_type=jnp.float32,
    )
    result = mixed / weight_sum[..., None]
    return jnp.transpose(result, (1, 0, 2)).reshape(result.shape[1], -1).astype(jnp.bfloat16)


def by_rows(inputs, short_filter, long_filter, skip_gain, queries, key_rows):
    row_count = inputs.shape[0]
    channels = inputs.shape[2]
    groups = long_filter.shape[0]
    tap_count = long_filter.shape[1]
    short_reach = short_filter.shape[0] - 1
    position = lax.axis_index("ctx")
    rim = passed_along(inputs[row_count - short_reach :], "ctx", 1)
    extended = jnp.concatenate([rim, inputs], axis=0)
    features = short_features(extended, short_filter, row_count)
    gate_product = (features[:, 1] * features[:, 2]).astype(jnp.bfloat16)
    gate_prev = passed_along(gate_product[row_count - (tap_count - 1) :], "ctx", 1)
    gate_ext = jnp.concatenate([gate_prev, gate_product], axis=0)
    toeplitz = toeplitz_taps(long_filter, row_count)
    filtered = jnp.einsum(
        "gtr,rgc->tgc",
        toeplitz,
        gate_ext.reshape(row_count + tap_count - 1, groups, channels // groups),
        preferred_element_type=jnp.float32,
    ).reshape(row_count, channels)
    values = (
        features[:, 0] * (filtered + skip_gain[None] * gate_product.astype(jnp.float32))
    ).astype(jnp.bfloat16)
    head_count = channels // HEAD_DIM
    head_queries = queries.reshape(row_count, head_count, HEAD_DIM)
    query_pos = position * row_count + lax.iota(jnp.int32, row_count)
    return attend(
        head_queries,
        query_pos,
        lax.all_gather(key_rows, "ctx", axis=0, tiled=True),
        lax.all_gather(values, "ctx", axis=0, tiled=True),
    )


def delayed(signal, lag):
    if lag == 0:
        return signal
    row = lax.broadcasted_iota(jnp.int32, signal.shape, 0)
    return jnp.where(row < lag, 0.0, pltpu.roll(signal, lag, 0))


def featured(signal, taps):
    total = taps[0] * signal
    for lag in range(1, len(taps)):
        total = total + taps[lag] * delayed(signal, lag)
    return total


def columns_of(block, width):
    return pl.ds(pl.multiple_of(block * width, width), width)


def write_gate(signals, taps, out_ref):
    rows, own = signals[0].shape
    tiles = [slice(start, start + HEAD_DIM) for start in range(0, own, HEAD_DIM)]
    edge_row = lax.broadcasted_iota(jnp.int32, (EDGE, own), 0)
    features = [featured(signal, tap) for signal, tap in zip(signals, taps)]
    gate = (features[0] * features[1]).astype(jnp.bfloat16)
    first, second = [
        jnp.where(
            edge_row % 4 < 2, pltpu.roll(signal[:EDGE], turn, 0), pltpu.roll(signal[rows - EDGE :], 4 - turn, 0)
        )
        for signal, turn in zip(signals, (0, 4))
    ]
    edges = jnp.where(edge_row < 4, first, second)
    for index, tile in enumerate(tiles):
        out_ref[index * rows : (index + 1) * rows] = gate[:, tile]
    out_ref[len(tiles) * rows :] = jnp.concatenate([edges[:, tile] for tile in tiles], axis=0).astype(jnp.bfloat16)


def plain_copies(sources, out_refs, steps, sems):
    rows, own = sources[0].shape[0], out_refs[0].shape[1]
    position = lax.axis_index("ctx")
    copies = []
    for step, out_ref in zip(steps, out_refs):
        columns = columns_of(position ^ step, own)
        for index, source in enumerate(sources):
            target = out_ref.at[index * rows : (index + 1) * rows]
            copies.append(pltpu.make_async_copy(source.at[:, columns], target, sems.at[len(copies)]))
    for copy in copies:
        copy.start()
    return copies


def plain_kernel(inputs_any, queries_any, keys_any, *refs):
    for copy in plain_copies((queries_any, keys_any, inputs_any.at[0]), refs[:2], ORDER[:2], refs[2]):
        copy.wait()


def gate_kernel(inputs_any, short_any, queries_any, keys_any, *refs):
    out_refs, plain_refs = refs[:COUNT], refs[COUNT : COUNT + 2]
    signal_s, short_s, sems, plain_sems = refs[COUNT + 2 :]
    own = plain_refs[0].shape[1]
    position = lax.axis_index("ctx")
    copies = [
        pltpu.make_async_copy(short_any, short_s, sems.at[0]),
        pltpu.make_async_copy(inputs_any.at[1:3], signal_s, sems.at[1]),
    ]
    for copy in copies:
        copy.start()
    plain = plain_copies((queries_any, keys_any, inputs_any.at[0]), plain_refs, ORDER[2:], plain_sems)
    for copy in copies:
        copy.wait()
    for step in ORDER:
        columns = columns_of(position ^ step, own)
        signals = [signal_s[stream, :, columns].astype(jnp.float32) for stream in range(2)]
        taps = [
            [short_s[lag, stream : stream + 1, columns].astype(jnp.float32) for lag in range(3)] for stream in (1, 2)
        ]
        write_gate(signals, taps, out_refs[step])
    for copy in plain:
        copy.wait()


def ready_kernel(filter_ref, weight_any, band_ref, weight_ref, sem):
    rows, span = band_ref.shape
    taps = filter_ref.shape[1]
    groups = rows // taps
    weights = pltpu.make_async_copy(weight_any, weight_ref, sem)
    weights.start()
    source = lax.broadcasted_iota(jnp.int32, (taps, span), 0)
    target = lax.broadcasted_iota(jnp.int32, (taps, span), 1)
    flip = (source + target == taps).astype(jnp.bfloat16)
    first_group = pl.multiple_of(lax.axis_index("ctx") * groups, groups)
    first = jnp.dot(filter_ref[pl.ds(first_group, groups)], flip, preferred_element_type=jnp.float32)
    for group in range(groups):
        repeated = jnp.broadcast_to(first[group : group + 1], (taps, span))
        banded = pltpu.roll(repeated, 0, 1, stride=1, stride_axis=0)
        band_ref[group * taps : (group + 1) * taps] = banded.astype(jnp.bfloat16)
    weights.wait()


def weights_kernel(third_ref, second_ref, near_ref, own_ref, short_ref, weight_ref, total_ref, feature_ref, query_s, key_s, signal_s):
    count = COUNT
    rows, own = query_s.shape[1:]
    position = lax.axis_index("ctx")
    for step, given in zip(ORDER, (third_ref, second_ref, near_ref, own_ref)):
        query_s[position ^ step] = given[0:rows]
        key_s[columns_of(position ^ step, rows)] = given[rows : 2 * rows]
        signal_s[columns_of(position ^ step, rows)] = given[2 * rows :]
    taps = [short_ref[lag, 0:1, columns_of(position, own)].astype(jnp.float32) for lag in range(3)]
    feature_ref[...] = featured(signal_s[...].astype(jnp.float32), taps)
    causal = lax.broadcasted_iota(jnp.int32, (rows, rows), 1) <= lax.broadcasted_iota(jnp.int32, (rows, rows), 0)
    for head in range(own // HEAD_DIM):
        columns = slice(head * HEAD_DIM, (head + 1) * HEAD_DIM)
        for block in range(count):
            here, seen = slice(block * rows, (block + 1) * rows), (block + 1) * rows
            scores = lax.dot_general(
                query_s[block, :, columns],
                key_s[0:seen, columns],
                (((1,), (1,)), ((), ())),
                preferred_element_type=jnp.float32,
            ) * HEAD_DIM ** (-0.5)
            own_scores = jnp.where(causal, scores[:, block * rows :], masked_score)
            pieces = [scores[:, : block * rows], own_scores] if block else [own_scores]
            scores = jnp.concatenate(pieces, axis=1)
            weights = jnp.exp(scores - jnp.max(scores, axis=1, keepdims=True))
            total_ref[here, head : head + 1] = jnp.sum(weights, axis=1, keepdims=True)
            weight_ref[head, here, 0:seen] = weights.astype(jnp.bfloat16)
            if seen < count * rows:
                weight_ref[head, here, seen:] = jnp.zeros((rows, count * rows - seen), jnp.bfloat16)


def mix_rows(block, weight_ref, total_ref, value_ref, out_ref):
    rows = out_ref.shape[0]
    here = columns_of(block, rows)
    for head in range(out_ref.shape[1] // HEAD_DIM):
        columns = slice(head * HEAD_DIM, (head + 1) * HEAD_DIM)
        mixed = jnp.dot(weight_ref[head, here], value_ref[:, columns], preferred_element_type=jnp.float32)
        out_ref[:, columns] = (mixed / total_ref[here, head : head + 1]).astype(jnp.bfloat16)


def values_kernel(*refs):
    count = COUNT
    gates, feature_ref = refs[:count], refs[count]
    band_ref, short_ref, gain_ref, weight_ref, total_ref = refs[count + 1 : count + 6]
    second_ref, value_ref = refs[count + 6 : count + 8]
    edge_s, gate_s, filtered_s = refs[count + 8 :]
    rows, own = second_ref.shape
    per_group = own * rows // band_ref.shape[0]
    position = lax.axis_index("ctx")
    mine = columns_of(position, own)
    tiles = [slice(start, start + HEAD_DIM) for start in range(0, own, HEAD_DIM)]
    gate_s[0:rows] = jnp.zeros((rows, own), jnp.bfloat16)
    for step, gate in zip(ORDER, gates):
        for index, tile in enumerate(tiles):
            gate_s[columns_of((position ^ step) + 1, rows), tile] = gate[index * rows : (index + 1) * rows]
        edges = gate[len(tiles) * rows :].astype(jnp.float32)
        for index, tile in enumerate(tiles):
            edge_s[position ^ step, :, tile] = edges[index * EDGE : (index + 1) * EDGE]
    taps = [
        [short_ref[lag, stream : stream + 1, mine].astype(jnp.float32) for lag in range(3)] for stream in range(3)
    ]
    edge_row = lax.broadcasted_iota(jnp.int32, (EDGE, own), 0)
    head_row = lax.broadcasted_iota(jnp.int32, (2 * EDGE, own), 0)
    for block in range(1, count):
        fixed = 1.0
        for stream, back, on in ((1, 6, 2), (2, 2, 6)):
            joined = jnp.where(
                edge_row < 2, pltpu.roll(edge_s[block - 1], back, 0), pltpu.roll(edge_s[block], on, 0)
            )
            fixed = fixed * (
                taps[stream][0] * pltpu.roll(joined, 6, 0)
                + taps[stream][1] * pltpu.roll(joined, 7, 0)
                + taps[stream][2] * joined
            )
        here = slice((block + 1) * rows, (block + 1) * rows + 2 * EDGE)
        head = jnp.where(head_row < 2, jnp.concatenate([fixed, fixed], axis=0), gate_s[here].astype(jnp.float32))
        gate_s[here] = head.astype(jnp.bfloat16)
    gain = gain_ref[:, mine]
    chunk = 2 * HEAD_DIM // count
    in_chunk = chunk // per_group
    lane = lax.broadcasted_iota(jnp.int32, (rows, 2 * HEAD_DIM), 1) % chunk // per_group
    for part in range(own // chunk):
        columns = slice(part * chunk, (part + 1) * chunk)
        windows = [gate_s[block * rows : (block + 2) * rows, columns] for block in range(count)]
        mixed = jnp.dot(
            band_ref[part * in_chunk * rows : (part + 1) * in_chunk * rows],
            jnp.concatenate(windows, axis=1),
            preferred_element_type=jnp.float32,
        )
        filtered = mixed[:rows]
        for group in range(1, in_chunk):
            filtered = jnp.where(lane == group, mixed[group * rows : (group + 1) * rows], filtered)
        for block in range(count):
            filtered_s[block * rows : (block + 1) * rows, columns] = filtered[:, block * chunk : (block + 1) * chunk]
    value_ref[...] = (
        feature_ref[...] * (filtered_s[...] + gain * gate_s[rows:].astype(jnp.float32))
    ).astype(jnp.bfloat16)
    mix_rows(position ^ 2, weight_ref, total_ref, value_ref, second_ref)


def rows_kernel(weight_ref, total_ref, value_ref, *out_refs):
    position = lax.axis_index("ctx")
    for step, out_ref in zip((3, 1, 0), out_refs):
        mix_rows(position ^ step, weight_ref, total_ref, value_ref, out_ref)


def project_kernel(masks, second_ref, third_ref, near_ref, mine_ref, weight_ref, _, *refs):
    out_refs, attended_s = refs[:-1], refs[-1]
    own, width = mine_ref.shape[1], out_refs[0].shape[1]
    position, here = lax.axis_index("ctx"), lax.axis_index("mp")
    for step, piece in ((0, mine_ref), (1, near_ref), (2, second_ref), (3, third_ref)):
        attended_s[:, columns_of(position ^ step, own)] = piece[...]
    for mask, out_ref in zip(masks, out_refs):
        out_ref[...] = jnp.dot(
            attended_s[...], weight_ref[:, columns_of(here ^ mask, width)], preferred_element_type=jnp.float32
        ).astype(jnp.bfloat16)


def partial_kernel(second_ref, mine_ref, weight_ref, out_ref):
    own, width = mine_ref.shape[1], out_ref.shape[1] // 2
    position, here = lax.axis_index("ctx"), lax.axis_index("mp")
    for index, mask in enumerate((3, 2)):
        columns = columns_of(here ^ mask, width)
        out_ref[:, index * width : (index + 1) * width] = jnp.dot(
            mine_ref[...], weight_ref[columns_of(position, own), columns], preferred_element_type=jnp.float32
        ) + jnp.dot(
            second_ref[...], weight_ref[columns_of(position ^ 2, own), columns], preferred_element_type=jnp.float32
        )


def partial_third_kernel(third_ref, partial_ref, weight_ref, out_ref):
    own, width = third_ref.shape[1], out_ref.shape[1] // 2
    position, here = lax.axis_index("ctx"), lax.axis_index("mp")
    for index, mask in enumerate((3, 2)):
        span = slice(index * width, (index + 1) * width)
        out_ref[:, span] = partial_ref[:, span] + jnp.dot(
            third_ref[...],
            weight_ref[columns_of(position ^ 3, own), columns_of(here ^ mask, width)],
            preferred_element_type=jnp.float32,
        )


def project_far_kernel(part, near_ref, partial_ref, weight_ref, given_ref, kept_ref):
    own, size = near_ref.shape[1], given_ref.shape[1]
    width = partial_ref.shape[1] // 2
    position, here = lax.axis_index("ctx"), lax.axis_index("mp")
    for index, (mask, out_ref) in enumerate(((3, given_ref), (2, kept_ref))):
        columns = columns_of((here ^ mask) * (width // size) + part, size)
        start = index * width + part * size
        total = partial_ref[:, start : start + size] + jnp.dot(
            near_ref[...], weight_ref[columns_of(position ^ 1, own), columns], preferred_element_type=jnp.float32
        )
        out_ref[...] = total.astype(jnp.bfloat16)


def total_kernel(part, kept_ref, upper_ref, lower_ref, crossed_ref, *refs):
    out_any, total_s, sem = refs[-3:]
    half, size = upper_ref.shape[0], crossed_ref.shape[1]
    columns = slice(part * size, (part + 1) * size)
    for index, near_ref in enumerate((upper_ref, lower_ref)):
        here = slice(index * half, (index + 1) * half)
        total = (
            kept_ref[here, columns].astype(jnp.float32)
            + near_ref[:, columns].astype(jnp.float32)
            + crossed_ref[here].astype(jnp.float32)
        )
        total_s[here] = total.astype(jnp.bfloat16)
    copy = pltpu.make_async_copy(total_s, out_any.at[:, columns], sem)
    copy.start()
    copy.wait()


VMEM_LIMIT = 40 * 1024 * 1024
PLAIN_LIMIT = 53 * 1024 * 1024 + 400 * 1024
GATE_LIMIT = 60 * 1024 * 1024
IN_HBM = pl.BlockSpec(memory_space=pltpu.HBM)
IN_VMEM = pl.BlockSpec(memory_space=pltpu.VMEM)
ANYWHERE = pl.BlockSpec(memory_space=pl.ANY)


def run_kernel(kernel, operands, outputs, scratch=(), spaces=None, limit=VMEM_LIMIT, cost=10**6, targets=None, aliases=None):
    return pl.pallas_call(
        kernel,
        out_shape=[jax.ShapeDtypeStruct(shape, dtype) for shape, dtype in outputs],
        in_specs=spaces or [IN_VMEM] * len(operands),
        out_specs=targets or [IN_VMEM] * len(outputs),
        scratch_shapes=scratch,
        input_output_aliases=aliases or {},
        compiler_params=pltpu.CompilerParams(vmem_limit_bytes=limit),
        cost_estimate=pl.CostEstimate(flops=cost, bytes_accessed=2**20, transcendentals=0),
        name=getattr(kernel, "func", kernel).__name__,
    )(*operands)


def swapped(value, axis, step):
    return lax.ppermute(value, axis, [(source, source ^ step) for source in range(lax.axis_size(axis))])


def by_heads(inputs, short_filter, long_filter, skip_gain, queries, key_rows, out_weight):
    rows, streams, channels = inputs.shape
    own = channels // COUNT
    groups, taps = long_filter.shape
    half = jnp.bfloat16
    piece, window = ((rows, own), half), COUNT * rows
    streamed = jnp.transpose(inputs, (1, 0, 2))
    far_plain = run_kernel(
        plain_kernel,
        (streamed, queries, key_rows),
        [((3 * rows, own), half)] * 2,
        [pltpu.SemaphoreType.DMA((6,))],
        [IN_HBM] * 3,
        PLAIN_LIMIT,
    )
    *gates, near_plain, own_plain = run_kernel(
        gate_kernel,
        (streamed, short_filter, queries, key_rows),
        [((own // HEAD_DIM * (rows + EDGE), HEAD_DIM), half)] * COUNT + [((3 * rows, own), half)] * 2,
        [
            pltpu.VMEM((2, rows, channels), half),
            pltpu.VMEM(short_filter.shape, half),
            pltpu.SemaphoreType.DMA((2,)),
            pltpu.SemaphoreType.DMA((6,)),
        ],
        [IN_HBM] * 4,
        GATE_LIMIT,
    )
    plain = [own_plain, near_plain, far_plain[1], far_plain[0]]
    plain = [swapped(plain[step], "ctx", step) for step in ORDER[:3]] + [plain[0]]
    gates = [swapped(gates[step], "ctx", step) for step in ORDER[:3]] + [gates[0]]
    band, weight = run_kernel(
        ready_kernel,
        (long_filter, out_weight),
        [((groups // COUNT * taps, 2 * taps), half), (out_weight.shape, half)],
        [pltpu.SemaphoreType.DMA],
        [IN_VMEM, IN_HBM],
    )
    soft, totals, feature = run_kernel(
        weights_kernel,
        (*plain, short_filter),
        [
            ((own // HEAD_DIM, window, window), half),
            ((window, HEAD_DIM), jnp.float32),
            ((window, own), jnp.float32),
        ],
        [
            pltpu.VMEM((COUNT, rows, own), half),
            pltpu.VMEM((window, own), half),
            pltpu.VMEM((window, own), half),
        ],
    )
    second, values = run_kernel(
        values_kernel,
        (*gates, feature, band, short_filter, skip_gain.reshape(1, channels), soft, totals),
        [piece, ((window, own), half)],
        [
            pltpu.VMEM((COUNT, EDGE, own), jnp.float32),
            pltpu.VMEM((window + rows, own), half),
            pltpu.VMEM((window, own), jnp.float32),
        ],
    )
    third, near, mine = run_kernel(rows_kernel, (soft, totals, values), [piece] * 3)
    swaps = [swapped(rows_out, "ctx", step) for step, rows_out in ((2, second), (3, third), (1, near))]
    return project_and_share((*swaps, mine), weight)


def added(*terms):
    total = terms[0].astype(jnp.float32)
    for term in terms[1:]:
        total = total + term.astype(jnp.float32)
    return total.astype(jnp.bfloat16)


def project_and_share(attended, out_weight):
    second, third, near, mine = attended
    rows = mine.shape[0]
    width = out_weight.shape[1] // lax.axis_size("mp")
    (partial,) = run_kernel(partial_kernel, (second, mine, out_weight), [((rows, 2 * width), jnp.float32)])
    (partial,) = run_kernel(
        partial_third_kernel, (third, partial, out_weight), [((rows, 2 * width), jnp.float32)]
    )
    crossed = []
    for part in range(2):
        given, kept = run_kernel(
            functools.partial(project_far_kernel, part),
            (near, partial, out_weight),
            [((rows, width // 2), jnp.bfloat16)] * 2,
        )
        far_sum = added(kept, swapped(given, "mp", 1))
        crossed.append(swapped(far_sum, "mp", 2))
    near_given, near_kept = run_kernel(
        functools.partial(project_kernel, (1, 0)),
        (*attended, out_weight, far_sum),
        [((rows, width), jnp.bfloat16)] * 2,
        [pltpu.VMEM((rows, out_weight.shape[0]), jnp.bfloat16)],
        [IN_VMEM] * 5 + [ANYWHERE],
    )
    half = near_given.shape[0] // 2
    near_got = [swapped(near_given[:half], "mp", 1), swapped(near_given[half:], "mp", 1)]
    total = []
    for part, piece in enumerate(crossed):
        total = run_kernel(
            functools.partial(total_kernel, part),
            (near_kept, *near_got, piece, *total),
            [(near_kept.shape, near_kept.dtype)],
            [pltpu.VMEM(piece.shape, piece.dtype), pltpu.SemaphoreType.DMA],
            [IN_VMEM] * 4 + [IN_HBM] * len(total),
            targets=[IN_HBM],
            aliases={4: 0} if total else {},
        )
    return total[0]


def per_device(inputs, short_filter, long_filter, skip_gain, queries, key_rows, out_weight):
    rows, _, channels = inputs.shape
    count = lax.axis_size("ctx")
    taps = long_filter.shape[1]
    splits = channels % (count * HEAD_DIM) == 0 and count == COUNT and rows == taps
    if splits and lax.axis_size("mp") == 4:
        return by_heads(inputs, short_filter, long_filter, skip_gain, queries, key_rows, out_weight)
    attended = by_rows(inputs, short_filter, long_filter, skip_gain, queries, key_rows)
    partial_out = jnp.dot(attended, out_weight, preferred_element_type=jnp.float32)
    return lax.psum_scatter(partial_out.astype(jnp.bfloat16), "mp", scatter_dimension=1, tiled=True)


def solution(mesh):
    placed = (
        P(("parts", "ctx"), None, "mp"),
        P(None, None, "mp"),
        P("mp", None),
        P("mp"),
        P(("parts", "ctx"), "mp"),
        P(("parts", "ctx"), "mp"),
        P("mp", None),
    )
    return jax.shard_map(
        per_device, mesh=mesh, in_specs=placed, out_specs=P(("parts", "ctx"), "mp"), check_vma=False
    )
```

```python
import functools

import jax
import jax.numpy as jnp
from jax import lax
from jax.experimental import pallas as pl
from jax.experimental.pallas import tpu as pltpu
from jax.sharding import PartitionSpec as P

HEAD_DIM = 128
COUNT = 4
ORDER = (3, 2, 1, 0)
EDGE = 8


masked_score = -1e30


def passed_along(value, axis, steps):
    count = lax.axis_size(axis)
    initial, last = (max(0, -steps), min(count, count - steps))
    return lax.ppermute(value, axis, [(source, source + steps) for source in range(initial, last)])


def toeplitz_taps(filters, row_count):
    group_count = filters.shape[0]
    tap_count = filters.shape[1]
    span = row_count + tap_count - 1
    flipped = filters[:, ::-1]
    padded_taps = jnp.concatenate(
        [flipped, jnp.zeros((group_count, row_count), filters.dtype)], axis=1
    )
    repeated = jnp.tile(padded_taps, (1, row_count))
    return repeated[:, : row_count * span].reshape(group_count, row_count, span)


def short_features(extended, short_filter, row_count):
    tap_count = short_filter.shape[0]
    features = jnp.zeros((row_count,) + extended.shape[1:], jnp.float32)
    for lag_index in range(tap_count):
        delayed = extended[
            tap_count - 1 - lag_index : tap_count - 1 - lag_index + row_count
        ].astype(jnp.float32)
        features = features + short_filter[lag_index].astype(jnp.float32)[None] * delayed
    return features


def attend(head_queries, query_pos, key_piece, value_piece):
    key_count = key_piece.shape[0]
    head_count = head_queries.shape[1]
    key_heads = key_piece.reshape(key_count, head_count, -1)
    value_heads = value_piece.reshape(key_count, head_count, -1)
    scores = jnp.einsum(
        "qhd,khd->hqk", head_queries, key_heads, preferred_element_type=jnp.float32
    ) * head_queries.shape[2] ** (-0.5)
    key_pos = lax.iota(jnp.int32, key_count)
    allowed = (key_pos[None, :] <= query_pos[:, None])[None]
    peak = jnp.max(jnp.where(allowed, scores, masked_score), axis=2)
    probabilities = jnp.where(allowed, jnp.exp(scores - peak[..., None]), 0.0)
    weight_sum = jnp.sum(probabilities, axis=2)
    mixed = jnp.einsum(
        "hqk,khd->hqd",
        probabilities.astype(jnp.bfloat16),
        value_heads,
        preferred_element_type=jnp.float32,
    )
    result = mixed / weight_sum[..., None]
    return jnp.transpose(result, (1, 0, 2)).reshape(result.shape[1], -1).astype(jnp.bfloat16)


def by_rows(inputs, short_filter, long_filter, skip_gain, queries, key_rows):
    row_count = inputs.shape[0]
    channels = inputs.shape[2]
    groups = long_filter.shape[0]
    tap_count = long_filter.shape[1]
    short_reach = short_filter.shape[0] - 1
    position = lax.axis_index("ctx")
    rim = passed_along(inputs[row_count - short_reach :], "ctx", 1)
    extended = jnp.concatenate([rim, inputs], axis=0)
    features = short_features(extended, short_filter, row_count)
    gate_product = (features[:, 1] * features[:, 2]).astype(jnp.bfloat16)
    gate_prev = passed_along(gate_product[row_count - (tap_count - 1) :], "ctx", 1)
    gate_ext = jnp.concatenate([gate_prev, gate_product], axis=0)
    toeplitz = toeplitz_taps(long_filter, row_count)
    filtered = jnp.einsum(
        "gtr,rgc->tgc",
        toeplitz,
        gate_ext.reshape(row_count + tap_count - 1, groups, channels // groups),
        preferred_element_type=jnp.float32,
    ).reshape(row_count, channels)
    values = (
        features[:, 0] * (filtered + skip_gain[None] * gate_product.astype(jnp.float32))
    ).astype(jnp.bfloat16)
    head_count = channels // HEAD_DIM
    head_queries = queries.reshape(row_count, head_count, HEAD_DIM)
    query_pos = position * row_count + lax.iota(jnp.int32, row_count)
    return attend(
        head_queries,
        query_pos,
        lax.all_gather(key_rows, "ctx", axis=0, tiled=True),
        lax.all_gather(values, "ctx", axis=0, tiled=True),
    )


def delayed(signal, lag):
    if lag == 0:
        return signal
    row = lax.broadcasted_iota(jnp.int32, signal.shape, 0)
    return jnp.where(row < lag, 0.0, pltpu.roll(signal, lag, 0))


def featured(signal, taps):
    total = taps[0] * signal
    for lag in range(1, len(taps)):
        total = total + taps[lag] * delayed(signal, lag)
    return total


def columns_of(block, width):
    return pl.ds(pl.multiple_of(block * width, width), width)


def write_gate(signals, taps, out_ref):
    rows, own = signals[0].shape
    tiles = [slice(start, start + HEAD_DIM) for start in range(0, own, HEAD_DIM)]
    edge_row = lax.broadcasted_iota(jnp.int32, (EDGE, own), 0)
    features = [featured(signal, tap) for signal, tap in zip(signals, taps)]
    gate = (features[0] * features[1]).astype(jnp.bfloat16)
    first, second = [
        jnp.where(
            edge_row % 4 < 2, pltpu.roll(signal[:EDGE], turn, 0), pltpu.roll(signal[rows - EDGE :], 4 - turn, 0)
        )
        for signal, turn in zip(signals, (0, 4))
    ]
    edges = jnp.where(edge_row < 4, first, second)
    for index, tile in enumerate(tiles):
        out_ref[index * rows : (index + 1) * rows] = gate[:, tile]
    out_ref[len(tiles) * rows :] = jnp.concatenate([edges[:, tile] for tile in tiles], axis=0).astype(jnp.bfloat16)


def plain_copies(sources, out_refs, steps, sems):
    rows, own = sources[0].shape[0], out_refs[0].shape[1]
    position = lax.axis_index("ctx")
    copies = []
    for step, out_ref in zip(steps, out_refs):
        columns = columns_of(position ^ step, own)
        for index, source in enumerate(sources):
            target = out_ref.at[index * rows : (index + 1) * rows]
            copies.append(pltpu.make_async_copy(source.at[:, columns], target, sems.at[len(copies)]))
    for copy in copies:
        copy.start()
    return copies


def plain_kernel(inputs_any, queries_any, keys_any, *refs):
    for copy in plain_copies((queries_any, keys_any, inputs_any.at[0]), refs[:2], ORDER[:2], refs[2]):
        copy.wait()


def gate_kernel(inputs_any, short_any, queries_any, keys_any, *refs):
    out_refs, plain_refs = refs[:COUNT], refs[COUNT : COUNT + 2]
    signal_s, short_s, sems, plain_sems = refs[COUNT + 2 :]
    own = plain_refs[0].shape[1]
    position = lax.axis_index("ctx")
    copies = [
        pltpu.make_async_copy(short_any, short_s, sems.at[0]),
        pltpu.make_async_copy(inputs_any.at[1:3], signal_s, sems.at[1]),
    ]
    for copy in copies:
        copy.start()
    plain = plain_copies((queries_any, keys_any, inputs_any.at[0]), plain_refs, ORDER[2:], plain_sems)
    for copy in copies:
        copy.wait()
    for step in ORDER:
        columns = columns_of(position ^ step, own)
        signals = [signal_s[stream, :, columns].astype(jnp.float32) for stream in range(2)]
        taps = [
            [short_s[lag, stream : stream + 1, columns].astype(jnp.float32) for lag in range(3)] for stream in (1, 2)
        ]
        write_gate(signals, taps, out_refs[step])
    for copy in plain:
        copy.wait()


def ready_kernel(filter_ref, weight_any, band_ref, weight_ref, sem):
    rows, span = band_ref.shape
    taps = filter_ref.shape[1]
    groups = rows // taps
    weights = pltpu.make_async_copy(weight_any, weight_ref, sem)
    weights.start()
    source = lax.broadcasted_iota(jnp.int32, (taps, span), 0)
    target = lax.broadcasted_iota(jnp.int32, (taps, span), 1)
    flip = (source + target == taps).astype(jnp.bfloat16)
    first_group = pl.multiple_of(lax.axis_index("ctx") * groups, groups)
    first = jnp.dot(filter_ref[pl.ds(first_group, groups)], flip, preferred_element_type=jnp.float32)
    for group in range(groups):
        repeated = jnp.broadcast_to(first[group : group + 1], (taps, span))
        banded = pltpu.roll(repeated, 0, 1, stride=1, stride_axis=0)
        band_ref[group * taps : (group + 1) * taps] = banded.astype(jnp.bfloat16)
    weights.wait()


def weights_kernel(third_ref, second_ref, near_ref, own_ref, short_ref, weight_ref, total_ref, feature_ref, query_s, key_s, signal_s):
    count = COUNT
    rows, own = query_s.shape[1:]
    position = lax.axis_index("ctx")
    for step, given in zip(ORDER, (third_ref, second_ref, near_ref, own_ref)):
        query_s[position ^ step] = given[0:rows]
        key_s[columns_of(position ^ step, rows)] = given[rows : 2 * rows]
        signal_s[columns_of(position ^ step, rows)] = given[2 * rows :]
    taps = [short_ref[lag, 0:1, columns_of(position, own)].astype(jnp.float32) for lag in range(3)]
    feature_ref[...] = featured(signal_s[...].astype(jnp.float32), taps)
    causal = lax.broadcasted_iota(jnp.int32, (rows, rows), 1) <= lax.broadcasted_iota(jnp.int32, (rows, rows), 0)
    for head in range(own // HEAD_DIM):
        columns = slice(head * HEAD_DIM, (head + 1) * HEAD_DIM)
        for block in range(count):
            here, seen = slice(block * rows, (block + 1) * rows), (block + 1) * rows
            scores = lax.dot_general(
                query_s[block, :, columns],
                key_s[0:seen, columns],
                (((1,), (1,)), ((), ())),
                preferred_element_type=jnp.float32,
            ) * HEAD_DIM ** (-0.5)
            own_scores = jnp.where(causal, scores[:, block * rows :], masked_score)
            pieces = [scores[:, : block * rows], own_scores] if block else [own_scores]
            scores = jnp.concatenate(pieces, axis=1)
            weights = jnp.exp(scores - jnp.max(scores, axis=1, keepdims=True))
            total_ref[here, head : head + 1] = jnp.sum(weights, axis=1, keepdims=True)
            weight_ref[head, here, 0:seen] = weights.astype(jnp.bfloat16)
            if seen < count * rows:
                weight_ref[head, here, seen:] = jnp.zeros((rows, count * rows - seen), jnp.bfloat16)


def mix_rows(block, weight_ref, total_ref, value_ref, out_ref):
    rows = out_ref.shape[0]
    here = columns_of(block, rows)
    for head in range(out_ref.shape[1] // HEAD_DIM):
        columns = slice(head * HEAD_DIM, (head + 1) * HEAD_DIM)
        mixed = jnp.dot(weight_ref[head, here], value_ref[:, columns], preferred_element_type=jnp.float32)
        out_ref[:, columns] = (mixed / total_ref[here, head : head + 1]).astype(jnp.bfloat16)


def values_kernel(*refs):
    count = COUNT
    gates, feature_ref = refs[:count], refs[count]
    band_ref, short_ref, gain_ref, weight_ref, total_ref = refs[count + 1 : count + 6]
    third_ref, second_ref, value_ref = refs[count + 6 : count + 9]
    edge_s, gate_s, filtered_s = refs[count + 9 :]
    rows, own = second_ref.shape
    per_group = own * rows // band_ref.shape[0]
    position = lax.axis_index("ctx")
    mine = columns_of(position, own)
    tiles = [slice(start, start + HEAD_DIM) for start in range(0, own, HEAD_DIM)]
    gate_s[0:rows] = jnp.zeros((rows, own), jnp.bfloat16)
    for step, gate in zip(ORDER, gates):
        for index, tile in enumerate(tiles):
            gate_s[columns_of((position ^ step) + 1, rows), tile] = gate[index * rows : (index + 1) * rows]
        edges = gate[len(tiles) * rows :].astype(jnp.float32)
        for index, tile in enumerate(tiles):
            edge_s[position ^ step, :, tile] = edges[index * EDGE : (index + 1) * EDGE]
    taps = [
        [short_ref[lag, stream : stream + 1, mine].astype(jnp.float32) for lag in range(3)] for stream in range(3)
    ]
    edge_row = lax.broadcasted_iota(jnp.int32, (EDGE, own), 0)
    head_row = lax.broadcasted_iota(jnp.int32, (2 * EDGE, own), 0)
    for block in range(1, count):
        fixed = 1.0
        for stream, back, on in ((1, 6, 2), (2, 2, 6)):
            joined = jnp.where(
                edge_row < 2, pltpu.roll(edge_s[block - 1], back, 0), pltpu.roll(edge_s[block], on, 0)
            )
            fixed = fixed * (
                taps[stream][0] * pltpu.roll(joined, 6, 0)
                + taps[stream][1] * pltpu.roll(joined, 7, 0)
                + taps[stream][2] * joined
            )
        here = slice((block + 1) * rows, (block + 1) * rows + 2 * EDGE)
        head = jnp.where(head_row < 2, jnp.concatenate([fixed, fixed], axis=0), gate_s[here].astype(jnp.float32))
        gate_s[here] = head.astype(jnp.bfloat16)
    gain = gain_ref[:, mine]
    chunk = 2 * HEAD_DIM // count
    in_chunk = chunk // per_group
    lane = lax.broadcasted_iota(jnp.int32, (rows, 2 * HEAD_DIM), 1) % chunk // per_group
    for part in range(own // chunk):
        columns = slice(part * chunk, (part + 1) * chunk)
        windows = [gate_s[block * rows : (block + 2) * rows, columns] for block in range(count)]
        mixed = jnp.dot(
            band_ref[part * in_chunk * rows : (part + 1) * in_chunk * rows],
            jnp.concatenate(windows, axis=1),
            preferred_element_type=jnp.float32,
        )
        filtered = mixed[:rows]
        for group in range(1, in_chunk):
            filtered = jnp.where(lane == group, mixed[group * rows : (group + 1) * rows], filtered)
        for block in range(count):
            filtered_s[block * rows : (block + 1) * rows, columns] = filtered[:, block * chunk : (block + 1) * chunk]
    value_ref[...] = (
        feature_ref[...] * (filtered_s[...] + gain * gate_s[rows:].astype(jnp.float32))
    ).astype(jnp.bfloat16)
    for step, out_ref in ((3, third_ref), (2, second_ref)):
        mix_rows(position ^ step, weight_ref, total_ref, value_ref, out_ref)


def near_rows_kernel(weight_ref, total_ref, value_ref, near_ref, own_ref):
    position = lax.axis_index("ctx")
    for step, out_ref in ((1, near_ref), (0, own_ref)):
        mix_rows(position ^ step, weight_ref, total_ref, value_ref, out_ref)


def project_kernel(masks, second_ref, third_ref, near_ref, mine_ref, weight_ref, _, *refs):
    out_refs, attended_s = refs[:-1], refs[-1]
    own, width = mine_ref.shape[1], out_refs[0].shape[1]
    position, here = lax.axis_index("ctx"), lax.axis_index("mp")
    for step, piece in ((0, mine_ref), (1, near_ref), (2, second_ref), (3, third_ref)):
        attended_s[:, columns_of(position ^ step, own)] = piece[...]
    for mask, out_ref in zip(masks, out_refs):
        out_ref[...] = jnp.dot(
            attended_s[...], weight_ref[:, columns_of(here ^ mask, width)], preferred_element_type=jnp.float32
        ).astype(jnp.bfloat16)


def partial_kernel(second_ref, mine_ref, weight_ref, out_ref):
    own, width = mine_ref.shape[1], out_ref.shape[1] // 2
    position, here = lax.axis_index("ctx"), lax.axis_index("mp")
    for index, mask in enumerate((3, 2)):
        columns = columns_of(here ^ mask, width)
        out_ref[:, index * width : (index + 1) * width] = jnp.dot(
            mine_ref[...], weight_ref[columns_of(position, own), columns], preferred_element_type=jnp.float32
        ) + jnp.dot(
            second_ref[...], weight_ref[columns_of(position ^ 2, own), columns], preferred_element_type=jnp.float32
        )


def partial_third_kernel(third_ref, partial_ref, weight_ref, out_ref):
    own, width = third_ref.shape[1], out_ref.shape[1] // 2
    position, here = lax.axis_index("ctx"), lax.axis_index("mp")
    for index, mask in enumerate((3, 2)):
        span = slice(index * width, (index + 1) * width)
        out_ref[:, span] = partial_ref[:, span] + jnp.dot(
            third_ref[...],
            weight_ref[columns_of(position ^ 3, own), columns_of(here ^ mask, width)],
            preferred_element_type=jnp.float32,
        )


def project_far_kernel(part, near_ref, partial_ref, weight_ref, given_ref, kept_ref):
    own, size = near_ref.shape[1], given_ref.shape[1]
    width = partial_ref.shape[1] // 2
    position, here = lax.axis_index("ctx"), lax.axis_index("mp")
    for index, (mask, out_ref) in enumerate(((3, given_ref), (2, kept_ref))):
        columns = columns_of((here ^ mask) * (width // size) + part, size)
        start = index * width + part * size
        total = partial_ref[:, start : start + size] + jnp.dot(
            near_ref[...], weight_ref[columns_of(position ^ 1, own), columns], preferred_element_type=jnp.float32
        )
        out_ref[...] = total.astype(jnp.bfloat16)


def total_kernel(part, kept_ref, upper_ref, lower_ref, crossed_ref, *refs):
    out_any, total_s, sem = refs[-3:]
    half, size = upper_ref.shape[0], crossed_ref.shape[1]
    columns = slice(part * size, (part + 1) * size)
    for index, near_ref in enumerate((upper_ref, lower_ref)):
        here = slice(index * half, (index + 1) * half)
        total = (
            kept_ref[here, columns].astype(jnp.float32)
            + near_ref[:, columns].astype(jnp.float32)
            + crossed_ref[here].astype(jnp.float32)
        )
        total_s[here] = total.astype(jnp.bfloat16)
    copy = pltpu.make_async_copy(total_s, out_any.at[:, columns], sem)
    copy.start()
    copy.wait()


VMEM_LIMIT = 40 * 1024 * 1024
PLAIN_LIMIT = 53 * 1024 * 1024 + 400 * 1024
GATE_LIMIT = 53 * 1024 * 1024 + 200 * 1024
IN_HBM = pl.BlockSpec(memory_space=pltpu.HBM)
IN_VMEM = pl.BlockSpec(memory_space=pltpu.VMEM)
ANYWHERE = pl.BlockSpec(memory_space=pl.ANY)


def run_kernel(kernel, operands, outputs, scratch=(), spaces=None, limit=VMEM_LIMIT, cost=10**6, targets=None, aliases=None):
    return pl.pallas_call(
        kernel,
        out_shape=[jax.ShapeDtypeStruct(shape, dtype) for shape, dtype in outputs],
        in_specs=spaces or [IN_VMEM] * len(operands),
        out_specs=targets or [IN_VMEM] * len(outputs),
        scratch_shapes=scratch,
        input_output_aliases=aliases or {},
        compiler_params=pltpu.CompilerParams(vmem_limit_bytes=limit),
        cost_estimate=pl.CostEstimate(flops=cost, bytes_accessed=2**20, transcendentals=0),
        name=getattr(kernel, "func", kernel).__name__,
    )(*operands)


def swapped(value, axis, step):
    return lax.ppermute(value, axis, [(source, source ^ step) for source in range(lax.axis_size(axis))])


def by_heads(inputs, short_filter, long_filter, skip_gain, queries, key_rows, out_weight):
    rows, streams, channels = inputs.shape
    own = channels // COUNT
    groups, taps = long_filter.shape
    half = jnp.bfloat16
    piece, window = ((rows, own), half), COUNT * rows
    streamed = jnp.transpose(inputs, (1, 0, 2))
    far_plain = run_kernel(
        plain_kernel,
        (streamed, queries, key_rows),
        [((3 * rows, own), half)] * 2,
        [pltpu.SemaphoreType.DMA((6,))],
        [IN_HBM] * 3,
        PLAIN_LIMIT,
    )
    *gates, near_plain, own_plain = run_kernel(
        gate_kernel,
        (streamed, short_filter, queries, key_rows),
        [((own // HEAD_DIM * (rows + EDGE), HEAD_DIM), half)] * COUNT + [((3 * rows, own), half)] * 2,
        [
            pltpu.VMEM((2, rows, channels), half),
            pltpu.VMEM(short_filter.shape, half),
            pltpu.SemaphoreType.DMA((2,)),
            pltpu.SemaphoreType.DMA((6,)),
        ],
        [IN_HBM] * 4,
        GATE_LIMIT,
    )
    plain = [own_plain, near_plain, far_plain[1], far_plain[0]]
    plain = [swapped(plain[step], "ctx", step) for step in ORDER[:3]] + [plain[0]]
    gates = [swapped(gates[step], "ctx", step) for step in ORDER[:3]] + [gates[0]]
    band, weight = run_kernel(
        ready_kernel,
        (long_filter, out_weight),
        [((groups // COUNT * taps, 2 * taps), half), (out_weight.shape, half)],
        [pltpu.SemaphoreType.DMA],
        [IN_VMEM, IN_HBM],
    )
    soft, totals, feature = run_kernel(
        weights_kernel,
        (*plain, short_filter),
        [
            ((own // HEAD_DIM, window, window), half),
            ((window, HEAD_DIM), jnp.float32),
            ((window, own), jnp.float32),
        ],
        [
            pltpu.VMEM((COUNT, rows, own), half),
            pltpu.VMEM((window, own), half),
            pltpu.VMEM((window, own), half),
        ],
    )
    third, second, values = run_kernel(
        values_kernel,
        (*gates, feature, band, short_filter, skip_gain.reshape(1, channels), soft, totals),
        [piece, piece, ((window, own), half)],
        [
            pltpu.VMEM((COUNT, EDGE, own), jnp.float32),
            pltpu.VMEM((window + rows, own), half),
            pltpu.VMEM((window, own), jnp.float32),
        ],
    )
    third_got, second_got = swapped(third, "ctx", 3), swapped(second, "ctx", 2)
    near, mine = run_kernel(near_rows_kernel, (soft, totals, values), [piece] * 2)
    return project_and_share((second_got, third_got, swapped(near, "ctx", 1), mine), weight)


def added(*terms):
    total = terms[0].astype(jnp.float32)
    for term in terms[1:]:
        total = total + term.astype(jnp.float32)
    return total.astype(jnp.bfloat16)


def project_and_share(attended, out_weight):
    second, third, near, mine = attended
    rows = mine.shape[0]
    width = out_weight.shape[1] // lax.axis_size("mp")
    (partial,) = run_kernel(partial_kernel, (second, mine, out_weight), [((rows, 2 * width), jnp.float32)])
    (partial,) = run_kernel(
        partial_third_kernel, (third, partial, out_weight), [((rows, 2 * width), jnp.float32)]
    )
    crossed = []
    for part in range(2):
        given, kept = run_kernel(
            functools.partial(project_far_kernel, part),
            (near, partial, out_weight),
            [((rows, width // 2), jnp.bfloat16)] * 2,
        )
        far_sum = added(kept, swapped(given, "mp", 1))
        crossed.append(swapped(far_sum, "mp", 2))
    near_given, near_kept = run_kernel(
        functools.partial(project_kernel, (1, 0)),
        (*attended, out_weight, far_sum),
        [((rows, width), jnp.bfloat16)] * 2,
        [pltpu.VMEM((rows, out_weight.shape[0]), jnp.bfloat16)],
        [IN_VMEM] * 5 + [ANYWHERE],
    )
    half = near_given.shape[0] // 2
    near_got = [swapped(near_given[:half], "mp", 1), swapped(near_given[half:], "mp", 1)]
    total = []
    for part, piece in enumerate(crossed):
        total = run_kernel(
            functools.partial(total_kernel, part),
            (near_kept, *near_got, piece, *total),
            [(near_kept.shape, near_kept.dtype)],
            [pltpu.VMEM(piece.shape, piece.dtype), pltpu.SemaphoreType.DMA],
            [IN_VMEM] * 4 + [IN_HBM] * len(total),
            targets=[IN_HBM],
            aliases={4: 0} if total else {},
        )
    return total[0]


def per_device(inputs, short_filter, long_filter, skip_gain, queries, key_rows, out_weight):
    rows, _, channels = inputs.shape
    count = lax.axis_size("ctx")
    taps = long_filter.shape[1]
    splits = channels % (count * HEAD_DIM) == 0 and count == COUNT and rows == taps
    if splits and lax.axis_size("mp") == 4:
        return by_heads(inputs, short_filter, long_filter, skip_gain, queries, key_rows, out_weight)
    attended = by_rows(inputs, short_filter, long_filter, skip_gain, queries, key_rows)
    partial_out = jnp.dot(attended, out_weight, preferred_element_type=jnp.float32)
    return lax.psum_scatter(partial_out.astype(jnp.bfloat16), "mp", scatter_dimension=1, tiled=True)


def solution(mesh):
    placed = (
        P(("parts", "ctx"), None, "mp"),
        P(None, None, "mp"),
        P("mp", None),
        P("mp"),
        P(("parts", "ctx"), "mp"),
        P(("parts", "ctx"), "mp"),
        P("mp", None),
    )
    return jax.shard_map(
        per_device, mesh=mesh, in_specs=placed, out_specs=P(("parts", "ctx"), "mp"), check_vma=False
    )
```

```python
import functools

import jax
import jax.numpy as jnp
from jax import lax
from jax.experimental import pallas as pl
from jax.experimental.pallas import tpu as pltpu
from jax.sharding import PartitionSpec as P

HEAD_DIM = 128
COUNT = 4
ORDER = (3, 2, 1, 0)
EDGE = 8


masked_score = -1e30


def passed_along(value, axis, steps):
    count = lax.axis_size(axis)
    initial, last = (max(0, -steps), min(count, count - steps))
    return lax.ppermute(value, axis, [(source, source + steps) for source in range(initial, last)])


def toeplitz_taps(filters, row_count):
    group_count = filters.shape[0]
    tap_count = filters.shape[1]
    span = row_count + tap_count - 1
    flipped = filters[:, ::-1]
    padded_taps = jnp.concatenate(
        [flipped, jnp.zeros((group_count, row_count), filters.dtype)], axis=1
    )
    repeated = jnp.tile(padded_taps, (1, row_count))
    return repeated[:, : row_count * span].reshape(group_count, row_count, span)


def short_features(extended, short_filter, row_count):
    tap_count = short_filter.shape[0]
    features = jnp.zeros((row_count,) + extended.shape[1:], jnp.float32)
    for lag_index in range(tap_count):
        delayed = extended[
            tap_count - 1 - lag_index : tap_count - 1 - lag_index + row_count
        ].astype(jnp.float32)
        features = features + short_filter[lag_index].astype(jnp.float32)[None] * delayed
    return features


def attend(head_queries, query_pos, key_piece, value_piece):
    key_count = key_piece.shape[0]
    head_count = head_queries.shape[1]
    key_heads = key_piece.reshape(key_count, head_count, -1)
    value_heads = value_piece.reshape(key_count, head_count, -1)
    scores = jnp.einsum(
        "qhd,khd->hqk", head_queries, key_heads, preferred_element_type=jnp.float32
    ) * head_queries.shape[2] ** (-0.5)
    key_pos = lax.iota(jnp.int32, key_count)
    allowed = (key_pos[None, :] <= query_pos[:, None])[None]
    peak = jnp.max(jnp.where(allowed, scores, masked_score), axis=2)
    probabilities = jnp.where(allowed, jnp.exp(scores - peak[..., None]), 0.0)
    weight_sum = jnp.sum(probabilities, axis=2)
    mixed = jnp.einsum(
        "hqk,khd->hqd",
        probabilities.astype(jnp.bfloat16),
        value_heads,
        preferred_element_type=jnp.float32,
    )
    result = mixed / weight_sum[..., None]
    return jnp.transpose(result, (1, 0, 2)).reshape(result.shape[1], -1).astype(jnp.bfloat16)


def by_rows(inputs, short_filter, long_filter, skip_gain, queries, key_rows):
    row_count = inputs.shape[0]
    channels = inputs.shape[2]
    groups = long_filter.shape[0]
    tap_count = long_filter.shape[1]
    short_reach = short_filter.shape[0] - 1
    position = lax.axis_index("ctx")
    rim = passed_along(inputs[row_count - short_reach :], "ctx", 1)
    extended = jnp.concatenate([rim, inputs], axis=0)
    features = short_features(extended, short_filter, row_count)
    gate_product = (features[:, 1] * features[:, 2]).astype(jnp.bfloat16)
    gate_prev = passed_along(gate_product[row_count - (tap_count - 1) :], "ctx", 1)
    gate_ext = jnp.concatenate([gate_prev, gate_product], axis=0)
    toeplitz = toeplitz_taps(long_filter, row_count)
    filtered = jnp.einsum(
        "gtr,rgc->tgc",
        toeplitz,
        gate_ext.reshape(row_count + tap_count - 1, groups, channels // groups),
        preferred_element_type=jnp.float32,
    ).reshape(row_count, channels)
    values = (
        features[:, 0] * (filtered + skip_gain[None] * gate_product.astype(jnp.float32))
    ).astype(jnp.bfloat16)
    head_count = channels // HEAD_DIM
    head_queries = queries.reshape(row_count, head_count, HEAD_DIM)
    query_pos = position * row_count + lax.iota(jnp.int32, row_count)
    return attend(
        head_queries,
        query_pos,
        lax.all_gather(key_rows, "ctx", axis=0, tiled=True),
        lax.all_gather(values, "ctx", axis=0, tiled=True),
    )


def delayed(signal, lag):
    if lag == 0:
        return signal
    row = lax.broadcasted_iota(jnp.int32, signal.shape, 0)
    return jnp.where(row < lag, 0.0, pltpu.roll(signal, lag, 0))


def featured(signal, taps):
    total = taps[0] * signal
    for lag in range(1, len(taps)):
        total = total + taps[lag] * delayed(signal, lag)
    return total


def columns_of(block, width):
    return pl.ds(pl.multiple_of(block * width, width), width)


def write_gate(signals, taps, out_ref):
    rows, own = signals[0].shape
    tiles = [slice(start, start + HEAD_DIM) for start in range(0, own, HEAD_DIM)]
    edge_row = lax.broadcasted_iota(jnp.int32, (EDGE, own), 0)
    features = [featured(signal, tap) for signal, tap in zip(signals, taps)]
    gate = (features[0] * features[1]).astype(jnp.bfloat16)
    first, second = [
        jnp.where(
            edge_row % 4 < 2, pltpu.roll(signal[:EDGE], turn, 0), pltpu.roll(signal[rows - EDGE :], 4 - turn, 0)
        )
        for signal, turn in zip(signals, (0, 4))
    ]
    edges = jnp.where(edge_row < 4, first, second)
    for index, tile in enumerate(tiles):
        out_ref[index * rows : (index + 1) * rows] = gate[:, tile]
    out_ref[len(tiles) * rows :] = jnp.concatenate([edges[:, tile] for tile in tiles], axis=0).astype(jnp.bfloat16)


def plain_copies(sources, out_refs, steps, sems):
    rows, own = sources[0].shape[0], out_refs[0].shape[1]
    position = lax.axis_index("ctx")
    copies = []
    for step, out_ref in zip(steps, out_refs):
        columns = columns_of(position ^ step, own)
        for index, source in enumerate(sources):
            target = out_ref.at[index * rows : (index + 1) * rows]
            copies.append(pltpu.make_async_copy(source.at[:, columns], target, sems.at[len(copies)]))
    for copy in copies:
        copy.start()
    return copies


def plain_kernel(inputs_any, queries_any, keys_any, *refs):
    for copy in plain_copies((queries_any, keys_any, inputs_any.at[0]), refs[:2], ORDER[:2], refs[2]):
        copy.wait()


def gate_kernel(inputs_any, short_any, queries_any, keys_any, *refs):
    out_refs, plain_refs = refs[:COUNT], refs[COUNT : COUNT + 2]
    signal_s, short_s, sems, plain_sems = refs[COUNT + 2 :]
    own = plain_refs[0].shape[1]
    position = lax.axis_index("ctx")
    copies = [
        pltpu.make_async_copy(short_any, short_s, sems.at[0]),
        pltpu.make_async_copy(inputs_any.at[1:3], signal_s, sems.at[1]),
    ]
    for copy in copies:
        copy.start()
    plain = plain_copies((queries_any, keys_any, inputs_any.at[0]), plain_refs, ORDER[2:], plain_sems)
    for copy in copies:
        copy.wait()
    for step in ORDER:
        columns = columns_of(position ^ step, own)
        signals = [signal_s[stream, :, columns].astype(jnp.float32) for stream in range(2)]
        taps = [
            [short_s[lag, stream : stream + 1, columns].astype(jnp.float32) for lag in range(3)] for stream in (1, 2)
        ]
        write_gate(signals, taps, out_refs[step])
    for copy in plain:
        copy.wait()


def ready_kernel(filter_ref, weight_any, band_ref, weight_ref, sem):
    rows, span = band_ref.shape
    taps = filter_ref.shape[1]
    groups = rows // taps
    weights = pltpu.make_async_copy(weight_any, weight_ref, sem)
    weights.start()
    source = lax.broadcasted_iota(jnp.int32, (taps, span), 0)
    target = lax.broadcasted_iota(jnp.int32, (taps, span), 1)
    flip = (source + target == taps).astype(jnp.bfloat16)
    first_group = pl.multiple_of(lax.axis_index("ctx") * groups, groups)
    first = jnp.dot(filter_ref[pl.ds(first_group, groups)], flip, preferred_element_type=jnp.float32)
    for group in range(groups):
        repeated = jnp.broadcast_to(first[group : group + 1], (taps, span))
        banded = pltpu.roll(repeated, 0, 1, stride=1, stride_axis=0)
        band_ref[group * taps : (group + 1) * taps] = banded.astype(jnp.bfloat16)
    weights.wait()


def weights_kernel(third_ref, second_ref, near_ref, own_ref, short_ref, weight_ref, total_ref, feature_ref, query_s, key_s, signal_s):
    count = COUNT
    rows, own = query_s.shape[1:]
    position = lax.axis_index("ctx")
    for step, given in zip(ORDER, (third_ref, second_ref, near_ref, own_ref)):
        query_s[position ^ step] = given[0:rows]
        key_s[columns_of(position ^ step, rows)] = given[rows : 2 * rows]
        signal_s[columns_of(position ^ step, rows)] = given[2 * rows :]
    taps = [short_ref[lag, 0:1, columns_of(position, own)].astype(jnp.float32) for lag in range(3)]
    feature_ref[...] = featured(signal_s[...].astype(jnp.float32), taps)
    causal = lax.broadcasted_iota(jnp.int32, (rows, rows), 1) <= lax.broadcasted_iota(jnp.int32, (rows, rows), 0)
    for head in range(own // HEAD_DIM):
        columns = slice(head * HEAD_DIM, (head + 1) * HEAD_DIM)
        for block in range(count):
            here, seen = slice(block * rows, (block + 1) * rows), (block + 1) * rows
            scores = lax.dot_general(
                query_s[block, :, columns],
                key_s[0:seen, columns],
                (((1,), (1,)), ((), ())),
                preferred_element_type=jnp.float32,
            ) * HEAD_DIM ** (-0.5)
            own_scores = jnp.where(causal, scores[:, block * rows :], masked_score)
            pieces = [scores[:, : block * rows], own_scores] if block else [own_scores]
            scores = jnp.concatenate(pieces, axis=1)
            weights = jnp.exp(scores - jnp.max(scores, axis=1, keepdims=True))
            total_ref[here, head : head + 1] = jnp.sum(weights, axis=1, keepdims=True)
            weight_ref[head, here, 0:seen] = weights.astype(jnp.bfloat16)
            if seen < count * rows:
                weight_ref[head, here, seen:] = jnp.zeros((rows, count * rows - seen), jnp.bfloat16)


def mix_rows(block, weight_ref, total_ref, value_ref, out_ref):
    rows = out_ref.shape[0]
    here = columns_of(block, rows)
    for head in range(out_ref.shape[1] // HEAD_DIM):
        columns = slice(head * HEAD_DIM, (head + 1) * HEAD_DIM)
        mixed = jnp.dot(weight_ref[head, here], value_ref[:, columns], preferred_element_type=jnp.float32)
        out_ref[:, columns] = (mixed / total_ref[here, head : head + 1]).astype(jnp.bfloat16)


def values_kernel(*refs):
    count = COUNT
    gates, feature_ref = refs[:count], refs[count]
    band_ref, short_ref, gain_ref, weight_ref, total_ref = refs[count + 1 : count + 6]
    third_ref, second_ref, value_ref = refs[count + 6 : count + 9]
    edge_s, gate_s, filtered_s = refs[count + 9 :]
    rows, own = second_ref.shape
    per_group = own * rows // band_ref.shape[0]
    position = lax.axis_index("ctx")
    mine = columns_of(position, own)
    tiles = [slice(start, start + HEAD_DIM) for start in range(0, own, HEAD_DIM)]
    gate_s[0:rows] = jnp.zeros((rows, own), jnp.bfloat16)
    for step, gate in zip(ORDER, gates):
        for index, tile in enumerate(tiles):
            gate_s[columns_of((position ^ step) + 1, rows), tile] = gate[index * rows : (index + 1) * rows]
        edges = gate[len(tiles) * rows :].astype(jnp.float32)
        for index, tile in enumerate(tiles):
            edge_s[position ^ step, :, tile] = edges[index * EDGE : (index + 1) * EDGE]
    taps = [
        [short_ref[lag, stream : stream + 1, mine].astype(jnp.float32) for lag in range(3)] for stream in range(3)
    ]
    edge_row = lax.broadcasted_iota(jnp.int32, (EDGE, own), 0)
    head_row = lax.broadcasted_iota(jnp.int32, (2 * EDGE, own), 0)
    for block in range(1, count):
        fixed = 1.0
        for stream, back, on in ((1, 6, 2), (2, 2, 6)):
            joined = jnp.where(
                edge_row < 2, pltpu.roll(edge_s[block - 1], back, 0), pltpu.roll(edge_s[block], on, 0)
            )
            fixed = fixed * (
                taps[stream][0] * pltpu.roll(joined, 6, 0)
                + taps[stream][1] * pltpu.roll(joined, 7, 0)
                + taps[stream][2] * joined
            )
        here = slice((block + 1) * rows, (block + 1) * rows + 2 * EDGE)
        head = jnp.where(head_row < 2, jnp.concatenate([fixed, fixed], axis=0), gate_s[here].astype(jnp.float32))
        gate_s[here] = head.astype(jnp.bfloat16)
    gain = gain_ref[:, mine]
    chunk = 2 * HEAD_DIM // count
    in_chunk = chunk // per_group
    lane = lax.broadcasted_iota(jnp.int32, (rows, 2 * HEAD_DIM), 1) % chunk // per_group
    for part in range(own // chunk):
        columns = slice(part * chunk, (part + 1) * chunk)
        windows = [gate_s[block * rows : (block + 2) * rows, columns] for block in range(count)]
        mixed = jnp.dot(
            band_ref[part * in_chunk * rows : (part + 1) * in_chunk * rows],
            jnp.concatenate(windows, axis=1),
            preferred_element_type=jnp.float32,
        )
        filtered = mixed[:rows]
        for group in range(1, in_chunk):
            filtered = jnp.where(lane == group, mixed[group * rows : (group + 1) * rows], filtered)
        for block in range(count):
            filtered_s[block * rows : (block + 1) * rows, columns] = filtered[:, block * chunk : (block + 1) * chunk]
    value_ref[...] = (
        feature_ref[...] * (filtered_s[...] + gain * gate_s[rows:].astype(jnp.float32))
    ).astype(jnp.bfloat16)
    for step, out_ref in ((3, third_ref), (2, second_ref)):
        mix_rows(position ^ step, weight_ref, total_ref, value_ref, out_ref)


def near_rows_kernel(weight_ref, total_ref, value_ref, near_ref, own_ref):
    position = lax.axis_index("ctx")
    for step, out_ref in ((1, near_ref), (0, own_ref)):
        mix_rows(position ^ step, weight_ref, total_ref, value_ref, out_ref)


def project_kernel(masks, second_ref, third_ref, near_ref, mine_ref, weight_ref, *refs):
    out_refs, attended_s = refs[2:-1], refs[-1]
    own, width = mine_ref.shape[1], out_refs[0].shape[1]
    position, here = lax.axis_index("ctx"), lax.axis_index("mp")
    for step, piece in ((0, mine_ref), (1, near_ref), (2, second_ref), (3, third_ref)):
        attended_s[:, columns_of(position ^ step, own)] = piece[...]
    for mask, out_ref in zip(masks, out_refs):
        out_ref[...] = jnp.dot(
            attended_s[...], weight_ref[:, columns_of(here ^ mask, width)], preferred_element_type=jnp.float32
        ).astype(jnp.bfloat16)


def partial_kernel(second_ref, mine_ref, weight_ref, out_ref):
    own, width = mine_ref.shape[1], out_ref.shape[1] // 2
    position, here = lax.axis_index("ctx"), lax.axis_index("mp")
    for index, mask in enumerate((3, 2)):
        columns = columns_of(here ^ mask, width)
        out_ref[:, index * width : (index + 1) * width] = jnp.dot(
            mine_ref[...], weight_ref[columns_of(position, own), columns], preferred_element_type=jnp.float32
        ) + jnp.dot(
            second_ref[...], weight_ref[columns_of(position ^ 2, own), columns], preferred_element_type=jnp.float32
        )


def partial_third_kernel(third_ref, partial_ref, weight_ref, out_ref):
    own, width = third_ref.shape[1], out_ref.shape[1] // 2
    position, here = lax.axis_index("ctx"), lax.axis_index("mp")
    for index, mask in enumerate((3, 2)):
        span = slice(index * width, (index + 1) * width)
        out_ref[:, span] = partial_ref[:, span] + jnp.dot(
            third_ref[...],
            weight_ref[columns_of(position ^ 3, own), columns_of(here ^ mask, width)],
            preferred_element_type=jnp.float32,
        )


def project_far_kernel(part, masks, near_ref, partial_ref, weight_ref, *out_refs):
    own, size = near_ref.shape[1], out_refs[0].shape[1]
    width = partial_ref.shape[1] // 2
    position, here = lax.axis_index("ctx"), lax.axis_index("mp")
    for mask, out_ref in zip(masks, out_refs):
        columns = columns_of((here ^ mask) * (width // size) + part, size)
        start = (3 - mask) * width + part * size
        total = partial_ref[:, start : start + size] + jnp.dot(
            near_ref[...], weight_ref[columns_of(position ^ 1, own), columns], preferred_element_type=jnp.float32
        )
        out_ref[...] = total.astype(jnp.bfloat16)


def total_kernel(part, kept_ref, upper_ref, lower_ref, crossed_ref, *refs):
    out_any, total_s, sem = refs[-3:]
    half, size = upper_ref.shape[0], crossed_ref.shape[1]
    columns = slice(part * size, (part + 1) * size)
    for index, near_ref in enumerate((upper_ref, lower_ref)):
        here = slice(index * half, (index + 1) * half)
        total = (
            kept_ref[here, columns].astype(jnp.float32)
            + near_ref[:, columns].astype(jnp.float32)
            + crossed_ref[here].astype(jnp.float32)
        )
        total_s[here] = total.astype(jnp.bfloat16)
    copy = pltpu.make_async_copy(total_s, out_any.at[:, columns], sem)
    copy.start()
    copy.wait()


VMEM_LIMIT = 40 * 1024 * 1024
PLAIN_LIMIT = 53 * 1024 * 1024 + 400 * 1024
GATE_LIMIT = 53 * 1024 * 1024 + 200 * 1024
IN_HBM = pl.BlockSpec(memory_space=pltpu.HBM)
IN_VMEM = pl.BlockSpec(memory_space=pltpu.VMEM)
ANYWHERE = pl.BlockSpec(memory_space=pl.ANY)


def run_kernel(kernel, operands, outputs, scratch=(), spaces=None, limit=VMEM_LIMIT, cost=10**6, targets=None, aliases=None):
    return pl.pallas_call(
        kernel,
        out_shape=[jax.ShapeDtypeStruct(shape, dtype) for shape, dtype in outputs],
        in_specs=spaces or [IN_VMEM] * len(operands),
        out_specs=targets or [IN_VMEM] * len(outputs),
        scratch_shapes=scratch,
        input_output_aliases=aliases or {},
        compiler_params=pltpu.CompilerParams(vmem_limit_bytes=limit),
        cost_estimate=pl.CostEstimate(flops=cost, bytes_accessed=2**20, transcendentals=0),
        name=getattr(kernel, "func", kernel).__name__,
    )(*operands)


def swapped(value, axis, step):
    return lax.ppermute(value, axis, [(source, source ^ step) for source in range(lax.axis_size(axis))])


def by_heads(inputs, short_filter, long_filter, skip_gain, queries, key_rows, out_weight):
    rows, streams, channels = inputs.shape
    own = channels // COUNT
    groups, taps = long_filter.shape
    half = jnp.bfloat16
    piece, window = ((rows, own), half), COUNT * rows
    streamed = jnp.transpose(inputs, (1, 0, 2))
    far_plain = run_kernel(
        plain_kernel,
        (streamed, queries, key_rows),
        [((3 * rows, own), half)] * 2,
        [pltpu.SemaphoreType.DMA((6,))],
        [IN_HBM] * 3,
        PLAIN_LIMIT,
    )
    *gates, near_plain, own_plain = run_kernel(
        gate_kernel,
        (streamed, short_filter, queries, key_rows),
        [((own // HEAD_DIM * (rows + EDGE), HEAD_DIM), half)] * COUNT + [((3 * rows, own), half)] * 2,
        [
            pltpu.VMEM((2, rows, channels), half),
            pltpu.VMEM(short_filter.shape, half),
            pltpu.SemaphoreType.DMA((2,)),
            pltpu.SemaphoreType.DMA((6,)),
        ],
        [IN_HBM] * 4,
        GATE_LIMIT,
    )
    plain = [own_plain, near_plain, far_plain[1], far_plain[0]]
    plain = [swapped(plain[step], "ctx", step) for step in ORDER[:3]] + [plain[0]]
    gates = [swapped(gates[step], "ctx", step) for step in ORDER[:3]] + [gates[0]]
    band, weight = run_kernel(
        ready_kernel,
        (long_filter, out_weight),
        [((groups // COUNT * taps, 2 * taps), half), (out_weight.shape, half)],
        [pltpu.SemaphoreType.DMA],
        [IN_VMEM, IN_HBM],
    )
    soft, totals, feature = run_kernel(
        weights_kernel,
        (*plain, short_filter),
        [
            ((own // HEAD_DIM, window, window), half),
            ((window, HEAD_DIM), jnp.float32),
            ((window, own), jnp.float32),
        ],
        [
            pltpu.VMEM((COUNT, rows, own), half),
            pltpu.VMEM((window, own), half),
            pltpu.VMEM((window, own), half),
        ],
    )
    third, second, values = run_kernel(
        values_kernel,
        (*gates, feature, band, short_filter, skip_gain.reshape(1, channels), soft, totals),
        [piece, piece, ((window, own), half)],
        [
            pltpu.VMEM((COUNT, EDGE, own), jnp.float32),
            pltpu.VMEM((window + rows, own), half),
            pltpu.VMEM((window, own), jnp.float32),
        ],
    )
    third_got, second_got = swapped(third, "ctx", 3), swapped(second, "ctx", 2)
    near, mine = run_kernel(near_rows_kernel, (soft, totals, values), [piece] * 2)
    return project_and_share((second_got, third_got, swapped(near, "ctx", 1), mine), weight)


def added(*terms):
    total = terms[0].astype(jnp.float32)
    for term in terms[1:]:
        total = total + term.astype(jnp.float32)
    return total.astype(jnp.bfloat16)


def project_and_share(attended, out_weight):
    second, third, near, mine = attended
    rows = mine.shape[0]
    width = out_weight.shape[1] // lax.axis_size("mp")
    (partial,) = run_kernel(partial_kernel, (second, mine, out_weight), [((rows, 2 * width), jnp.float32)])
    (partial,) = run_kernel(
        partial_third_kernel, (third, partial, out_weight), [((rows, 2 * width), jnp.float32)]
    )
    crossed, sums = [], []
    for part in range(2):
        given, kept = [
            block
            for masks in ((3,), (2,))
            for block in run_kernel(
                functools.partial(project_far_kernel, part, masks),
                (near, partial, out_weight),
                [((rows, width // 2), jnp.bfloat16)] * len(masks),
            )
        ]
        far_sum = added(kept, swapped(given, "mp", 1))
        sums.append(far_sum)
        crossed.append(swapped(far_sum, "mp", 2))
    near_given, near_kept = run_kernel(
        functools.partial(project_kernel, (1, 0)),
        (*attended, out_weight, *sums),
        [((rows, width), jnp.bfloat16)] * 2,
        [pltpu.VMEM((rows, out_weight.shape[0]), jnp.bfloat16)],
        [IN_VMEM] * 5 + [ANYWHERE] * 2,
    )
    half = near_given.shape[0] // 2
    near_got = [swapped(near_given[:half], "mp", 1), swapped(near_given[half:], "mp", 1)]
    total = []
    for part, piece in enumerate(crossed):
        total = run_kernel(
            functools.partial(total_kernel, part),
            (near_kept, *near_got, piece, *total),
            [(near_kept.shape, near_kept.dtype)],
            [pltpu.VMEM(piece.shape, piece.dtype), pltpu.SemaphoreType.DMA],
            [IN_VMEM] * 4 + [IN_HBM] * len(total),
            targets=[IN_HBM],
            aliases={4: 0} if total else {},
        )
    return total[0]


def per_device(inputs, short_filter, long_filter, skip_gain, queries, key_rows, out_weight):
    rows, _, channels = inputs.shape
    count = lax.axis_size("ctx")
    taps = long_filter.shape[1]
    splits = channels % (count * HEAD_DIM) == 0 and count == COUNT and rows == taps
    if splits and lax.axis_size("mp") == 4:
        return by_heads(inputs, short_filter, long_filter, skip_gain, queries, key_rows, out_weight)
    attended = by_rows(inputs, short_filter, long_filter, skip_gain, queries, key_rows)
    partial_out = jnp.dot(attended, out_weight, preferred_element_type=jnp.float32)
    return lax.psum_scatter(partial_out.astype(jnp.bfloat16), "mp", scatter_dimension=1, tiled=True)


def solution(mesh):
    placed = (
        P(("parts", "ctx"), None, "mp"),
        P(None, None, "mp"),
        P("mp", None),
        P("mp"),
        P(("parts", "ctx"), "mp"),
        P(("parts", "ctx"), "mp"),
        P("mp", None),
    )
    return jax.shard_map(
        per_device, mesh=mesh, in_specs=placed, out_specs=P(("parts", "ctx"), "mp"), check_vma=False
    )
```

```python
import functools

import jax
import jax.numpy as jnp
from jax import lax
from jax.experimental import pallas as pl
from jax.experimental.pallas import tpu as pltpu
from jax.sharding import PartitionSpec as P

HEAD_DIM = 128
COUNT = 4
ORDER = (3, 2, 1, 0)
EDGE = 8


masked_score = -1e30


def passed_along(value, axis, steps):
    count = lax.axis_size(axis)
    initial, last = (max(0, -steps), min(count, count - steps))
    return lax.ppermute(value, axis, [(source, source + steps) for source in range(initial, last)])


def toeplitz_taps(filters, row_count):
    group_count = filters.shape[0]
    tap_count = filters.shape[1]
    span = row_count + tap_count - 1
    flipped = filters[:, ::-1]
    padded_taps = jnp.concatenate(
        [flipped, jnp.zeros((group_count, row_count), filters.dtype)], axis=1
    )
    repeated = jnp.tile(padded_taps, (1, row_count))
    return repeated[:, : row_count * span].reshape(group_count, row_count, span)


def short_features(extended, short_filter, row_count):
    tap_count = short_filter.shape[0]
    features = jnp.zeros((row_count,) + extended.shape[1:], jnp.float32)
    for lag_index in range(tap_count):
        delayed = extended[
            tap_count - 1 - lag_index : tap_count - 1 - lag_index + row_count
        ].astype(jnp.float32)
        features = features + short_filter[lag_index].astype(jnp.float32)[None] * delayed
    return features


def attend(head_queries, query_pos, key_piece, value_piece):
    key_count = key_piece.shape[0]
    head_count = head_queries.shape[1]
    key_heads = key_piece.reshape(key_count, head_count, -1)
    value_heads = value_piece.reshape(key_count, head_count, -1)
    scores = jnp.einsum(
        "qhd,khd->hqk", head_queries, key_heads, preferred_element_type=jnp.float32
    ) * head_queries.shape[2] ** (-0.5)
    key_pos = lax.iota(jnp.int32, key_count)
    allowed = (key_pos[None, :] <= query_pos[:, None])[None]
    peak = jnp.max(jnp.where(allowed, scores, masked_score), axis=2)
    probabilities = jnp.where(allowed, jnp.exp(scores - peak[..., None]), 0.0)
    weight_sum = jnp.sum(probabilities, axis=2)
    mixed = jnp.einsum(
        "hqk,khd->hqd",
        probabilities.astype(jnp.bfloat16),
        value_heads,
        preferred_element_type=jnp.float32,
    )
    result = mixed / weight_sum[..., None]
    return jnp.transpose(result, (1, 0, 2)).reshape(result.shape[1], -1).astype(jnp.bfloat16)


def by_rows(inputs, short_filter, long_filter, skip_gain, queries, key_rows):
    row_count = inputs.shape[0]
    channels = inputs.shape[2]
    groups = long_filter.shape[0]
    tap_count = long_filter.shape[1]
    short_reach = short_filter.shape[0] - 1
    position = lax.axis_index("ctx")
    rim = passed_along(inputs[row_count - short_reach :], "ctx", 1)
    extended = jnp.concatenate([rim, inputs], axis=0)
    features = short_features(extended, short_filter, row_count)
    gate_product = (features[:, 1] * features[:, 2]).astype(jnp.bfloat16)
    gate_prev = passed_along(gate_product[row_count - (tap_count - 1) :], "ctx", 1)
    gate_ext = jnp.concatenate([gate_prev, gate_product], axis=0)
    toeplitz = toeplitz_taps(long_filter, row_count)
    filtered = jnp.einsum(
        "gtr,rgc->tgc",
        toeplitz,
        gate_ext.reshape(row_count + tap_count - 1, groups, channels // groups),
        preferred_element_type=jnp.float32,
    ).reshape(row_count, channels)
    values = (
        features[:, 0] * (filtered + skip_gain[None] * gate_product.astype(jnp.float32))
    ).astype(jnp.bfloat16)
    head_count = channels // HEAD_DIM
    head_queries = queries.reshape(row_count, head_count, HEAD_DIM)
    query_pos = position * row_count + lax.iota(jnp.int32, row_count)
    return attend(
        head_queries,
        query_pos,
        lax.all_gather(key_rows, "ctx", axis=0, tiled=True),
        lax.all_gather(values, "ctx", axis=0, tiled=True),
    )


def delayed(signal, lag):
    if lag == 0:
        return signal
    row = lax.broadcasted_iota(jnp.int32, signal.shape, 0)
    return jnp.where(row < lag, 0.0, pltpu.roll(signal, lag, 0))


def featured(signal, taps):
    total = taps[0] * signal
    for lag in range(1, len(taps)):
        total = total + taps[lag] * delayed(signal, lag)
    return total


def columns_of(block, width):
    return pl.ds(pl.multiple_of(block * width, width), width)


def write_gate(signals, taps, out_ref):
    rows, own = signals[0].shape
    tiles = [slice(start, start + HEAD_DIM) for start in range(0, own, HEAD_DIM)]
    edge_row = lax.broadcasted_iota(jnp.int32, (EDGE, own), 0)
    features = [featured(signal, tap) for signal, tap in zip(signals, taps)]
    gate = (features[0] * features[1]).astype(jnp.bfloat16)
    first, second = [
        jnp.where(
            edge_row % 4 < 2, pltpu.roll(signal[:EDGE], turn, 0), pltpu.roll(signal[rows - EDGE :], 4 - turn, 0)
        )
        for signal, turn in zip(signals, (0, 4))
    ]
    edges = jnp.where(edge_row < 4, first, second)
    for index, tile in enumerate(tiles):
        out_ref[index * rows : (index + 1) * rows] = gate[:, tile]
    out_ref[len(tiles) * rows :] = jnp.concatenate([edges[:, tile] for tile in tiles], axis=0).astype(jnp.bfloat16)


def plain_copies(sources, out_refs, steps, sems):
    rows, own = sources[0].shape[0], out_refs[0].shape[1]
    position = lax.axis_index("ctx")
    copies = []
    for step, out_ref in zip(steps, out_refs):
        columns = columns_of(position ^ step, own)
        for index, source in enumerate(sources):
            target = out_ref.at[index * rows : (index + 1) * rows]
            copies.append(pltpu.make_async_copy(source.at[:, columns], target, sems.at[len(copies)]))
    for copy in copies:
        copy.start()
    return copies


def plain_kernel(inputs_any, queries_any, keys_any, third_ref, second_ref, pair_s, sems):
    rows, own = pair_s.shape[1], third_ref.shape[1]
    position = lax.axis_index("ctx")
    columns = columns_of((position ^ 2) // 2, 2 * own)
    copies = [
        pltpu.make_async_copy(source.at[:, columns], pair_s.at[index], sems.at[index])
        for index, source in enumerate((queries_any, keys_any, inputs_any.at[0]))
    ]
    for copy in copies:
        copy.start()
    for index, copy in enumerate(copies):
        copy.wait()
        for step, out_ref in ((3, third_ref), (2, second_ref)):
            out_ref[index * rows : (index + 1) * rows] = pair_s[index, :, columns_of((position ^ step) % 2, own)]


def gate_kernel(inputs_any, short_any, queries_any, keys_any, *refs):
    out_refs, plain_refs = refs[:COUNT], refs[COUNT : COUNT + 2]
    signal_s, short_s, sems, plain_sems = refs[COUNT + 2 :]
    own = plain_refs[0].shape[1]
    position = lax.axis_index("ctx")
    copies = [
        pltpu.make_async_copy(short_any, short_s, sems.at[0]),
        pltpu.make_async_copy(inputs_any.at[1:3], signal_s, sems.at[1]),
    ]
    for copy in copies:
        copy.start()
    plain = plain_copies((queries_any, keys_any, inputs_any.at[0]), plain_refs, ORDER[2:], plain_sems)
    for copy in copies:
        copy.wait()
    for step in ORDER:
        columns = columns_of(position ^ step, own)
        signals = [signal_s[stream, :, columns].astype(jnp.float32) for stream in range(2)]
        taps = [
            [short_s[lag, stream : stream + 1, columns].astype(jnp.float32) for lag in range(3)] for stream in (1, 2)
        ]
        write_gate(signals, taps, out_refs[step])
    for copy in plain:
        copy.wait()


def ready_kernel(filter_ref, weight_any, band_ref, weight_ref, sem):
    rows, span = band_ref.shape
    taps = filter_ref.shape[1]
    groups = rows // taps
    weights = pltpu.make_async_copy(weight_any, weight_ref, sem)
    weights.start()
    source = lax.broadcasted_iota(jnp.int32, (taps, span), 0)
    target = lax.broadcasted_iota(jnp.int32, (taps, span), 1)
    flip = (source + target == taps).astype(jnp.bfloat16)
    first_group = pl.multiple_of(lax.axis_index("ctx") * groups, groups)
    first = jnp.dot(filter_ref[pl.ds(first_group, groups)], flip, preferred_element_type=jnp.float32)
    for group in range(groups):
        repeated = jnp.broadcast_to(first[group : group + 1], (taps, span))
        banded = pltpu.roll(repeated, 0, 1, stride=1, stride_axis=0)
        band_ref[group * taps : (group + 1) * taps] = banded.astype(jnp.bfloat16)
    weights.wait()


def weights_kernel(third_ref, second_ref, near_ref, own_ref, short_ref, weight_ref, total_ref, feature_ref, query_s, key_s, signal_s):
    count = COUNT
    rows, own = query_s.shape[1:]
    position = lax.axis_index("ctx")
    for step, given in zip(ORDER, (third_ref, second_ref, near_ref, own_ref)):
        query_s[position ^ step] = given[0:rows]
        key_s[columns_of(position ^ step, rows)] = given[rows : 2 * rows]
        signal_s[columns_of(position ^ step, rows)] = given[2 * rows :]
    taps = [short_ref[lag, 0:1, columns_of(position, own)].astype(jnp.float32) for lag in range(3)]
    feature_ref[...] = featured(signal_s[...].astype(jnp.float32), taps)
    causal = lax.broadcasted_iota(jnp.int32, (rows, rows), 1) <= lax.broadcasted_iota(jnp.int32, (rows, rows), 0)
    for head in range(own // HEAD_DIM):
        columns = slice(head * HEAD_DIM, (head + 1) * HEAD_DIM)
        for block in range(count):
            here, seen = slice(block * rows, (block + 1) * rows), (block + 1) * rows
            scores = lax.dot_general(
                query_s[block, :, columns],
                key_s[0:seen, columns],
                (((1,), (1,)), ((), ())),
                preferred_element_type=jnp.float32,
            ) * HEAD_DIM ** (-0.5)
            own_scores = jnp.where(causal, scores[:, block * rows :], masked_score)
            pieces = [scores[:, : block * rows], own_scores] if block else [own_scores]
            scores = jnp.concatenate(pieces, axis=1)
            weights = jnp.exp(scores - jnp.max(scores, axis=1, keepdims=True))
            total_ref[here, head : head + 1] = jnp.sum(weights, axis=1, keepdims=True)
            weight_ref[head, here, 0:seen] = weights.astype(jnp.bfloat16)
            if seen < count * rows:
                weight_ref[head, here, seen:] = jnp.zeros((rows, count * rows - seen), jnp.bfloat16)


def mix_rows(block, weight_ref, total_ref, value_ref, out_ref):
    rows = out_ref.shape[0]
    here = columns_of(block, rows)
    for head in range(out_ref.shape[1] // HEAD_DIM):
        columns = slice(head * HEAD_DIM, (head + 1) * HEAD_DIM)
        mixed = jnp.dot(weight_ref[head, here], value_ref[:, columns], preferred_element_type=jnp.float32)
        out_ref[:, columns] = (mixed / total_ref[here, head : head + 1]).astype(jnp.bfloat16)


def values_kernel(*refs):
    count = COUNT
    gates, feature_ref = refs[:count], refs[count]
    band_ref, short_ref, gain_ref, weight_ref, total_ref = refs[count + 1 : count + 6]
    third_ref, second_ref, value_ref = refs[count + 6 : count + 9]
    edge_s, gate_s, filtered_s = refs[count + 9 :]
    rows, own = second_ref.shape
    per_group = own * rows // band_ref.shape[0]
    position = lax.axis_index("ctx")
    mine = columns_of(position, own)
    tiles = [slice(start, start + HEAD_DIM) for start in range(0, own, HEAD_DIM)]
    gate_s[0:rows] = jnp.zeros((rows, own), jnp.bfloat16)
    for step, gate in zip(ORDER, gates):
        for index, tile in enumerate(tiles):
            gate_s[columns_of((position ^ step) + 1, rows), tile] = gate[index * rows : (index + 1) * rows]
        edges = gate[len(tiles) * rows :].astype(jnp.float32)
        for index, tile in enumerate(tiles):
            edge_s[position ^ step, :, tile] = edges[index * EDGE : (index + 1) * EDGE]
    taps = [
        [short_ref[lag, stream : stream + 1, mine].astype(jnp.float32) for lag in range(3)] for stream in range(3)
    ]
    edge_row = lax.broadcasted_iota(jnp.int32, (EDGE, own), 0)
    head_row = lax.broadcasted_iota(jnp.int32, (2 * EDGE, own), 0)
    for block in range(1, count):
        fixed = 1.0
        for stream, back, on in ((1, 6, 2), (2, 2, 6)):
            joined = jnp.where(
                edge_row < 2, pltpu.roll(edge_s[block - 1], back, 0), pltpu.roll(edge_s[block], on, 0)
            )
            fixed = fixed * (
                taps[stream][0] * pltpu.roll(joined, 6, 0)
                + taps[stream][1] * pltpu.roll(joined, 7, 0)
                + taps[stream][2] * joined
            )
        here = slice((block + 1) * rows, (block + 1) * rows + 2 * EDGE)
        head = jnp.where(head_row < 2, jnp.concatenate([fixed, fixed], axis=0), gate_s[here].astype(jnp.float32))
        gate_s[here] = head.astype(jnp.bfloat16)
    gain = gain_ref[:, mine]
    chunk = 2 * HEAD_DIM // count
    in_chunk = chunk // per_group
    lane = lax.broadcasted_iota(jnp.int32, (rows, 2 * HEAD_DIM), 1) % chunk // per_group
    for part in range(own // chunk):
        columns = slice(part * chunk, (part + 1) * chunk)
        windows = [gate_s[block * rows : (block + 2) * rows, columns] for block in range(count)]
        mixed = jnp.dot(
            band_ref[part * in_chunk * rows : (part + 1) * in_chunk * rows],
            jnp.concatenate(windows, axis=1),
            preferred_element_type=jnp.float32,
        )
        filtered = mixed[:rows]
        for group in range(1, in_chunk):
            filtered = jnp.where(lane == group, mixed[group * rows : (group + 1) * rows], filtered)
        for block in range(count):
            filtered_s[block * rows : (block + 1) * rows, columns] = filtered[:, block * chunk : (block + 1) * chunk]
    value_ref[...] = (
        feature_ref[...] * (filtered_s[...] + gain * gate_s[rows:].astype(jnp.float32))
    ).astype(jnp.bfloat16)
    for step, out_ref in ((3, third_ref), (2, second_ref)):
        mix_rows(position ^ step, weight_ref, total_ref, value_ref, out_ref)


def near_rows_kernel(weight_ref, total_ref, value_ref, near_ref, own_ref):
    position = lax.axis_index("ctx")
    for step, out_ref in ((1, near_ref), (0, own_ref)):
        mix_rows(position ^ step, weight_ref, total_ref, value_ref, out_ref)


def project_kernel(masks, second_ref, third_ref, near_ref, mine_ref, weight_ref, *refs):
    out_refs, attended_s = refs[2:-1], refs[-1]
    own, width = mine_ref.shape[1], out_refs[0].shape[1]
    position, here = lax.axis_index("ctx"), lax.axis_index("mp")
    for step, piece in ((0, mine_ref), (1, near_ref), (2, second_ref), (3, third_ref)):
        attended_s[:, columns_of(position ^ step, own)] = piece[...]
    for mask, out_ref in zip(masks, out_refs):
        out_ref[...] = jnp.dot(
            attended_s[...], weight_ref[:, columns_of(here ^ mask, width)], preferred_element_type=jnp.float32
        ).astype(jnp.bfloat16)


def partial_kernel(second_ref, mine_ref, weight_ref, out_ref):
    own, width = mine_ref.shape[1], out_ref.shape[1] // 2
    position, here = lax.axis_index("ctx"), lax.axis_index("mp")
    for index, mask in enumerate((3, 2)):
        columns = columns_of(here ^ mask, width)
        out_ref[:, index * width : (index + 1) * width] = jnp.dot(
            mine_ref[...], weight_ref[columns_of(position, own), columns], preferred_element_type=jnp.float32
        ) + jnp.dot(
            second_ref[...], weight_ref[columns_of(position ^ 2, own), columns], preferred_element_type=jnp.float32
        )


def partial_third_kernel(third_ref, partial_ref, weight_ref, out_ref):
    own, width = third_ref.shape[1], out_ref.shape[1] // 2
    position, here = lax.axis_index("ctx"), lax.axis_index("mp")
    for index, mask in enumerate((3, 2)):
        span = slice(index * width, (index + 1) * width)
        out_ref[:, span] = partial_ref[:, span] + jnp.dot(
            third_ref[...],
            weight_ref[columns_of(position ^ 3, own), columns_of(here ^ mask, width)],
            preferred_element_type=jnp.float32,
        )


def project_far_kernel(part, masks, near_ref, partial_ref, weight_ref, *out_refs):
    own, size = near_ref.shape[1], out_refs[0].shape[1]
    width = partial_ref.shape[1] // 2
    position, here = lax.axis_index("ctx"), lax.axis_index("mp")
    for mask, out_ref in zip(masks, out_refs):
        columns = columns_of((here ^ mask) * (width // size) + part, size)
        start = (3 - mask) * width + part * size
        total = partial_ref[:, start : start + size] + jnp.dot(
            near_ref[...], weight_ref[columns_of(position ^ 1, own), columns], preferred_element_type=jnp.float32
        )
        out_ref[...] = total.astype(jnp.bfloat16)


def total_kernel(part, kept_ref, upper_ref, lower_ref, crossed_ref, *refs):
    out_any, total_s, sem = refs[-3:]
    half, size = upper_ref.shape[0], crossed_ref.shape[1]
    columns = slice(part * size, (part + 1) * size)
    for index, near_ref in enumerate((upper_ref, lower_ref)):
        here = slice(index * half, (index + 1) * half)
        total = (
            kept_ref[here, columns].astype(jnp.float32)
            + near_ref[:, columns].astype(jnp.float32)
            + crossed_ref[here].astype(jnp.float32)
        )
        total_s[here] = total.astype(jnp.bfloat16)
    copy = pltpu.make_async_copy(total_s, out_any.at[:, columns], sem)
    copy.start()
    copy.wait()


VMEM_LIMIT = 40 * 1024 * 1024
PLAIN_LIMIT = 53 * 1024 * 1024 + 400 * 1024
GATE_LIMIT = 53 * 1024 * 1024 + 200 * 1024
IN_HBM = pl.BlockSpec(memory_space=pltpu.HBM)
IN_VMEM = pl.BlockSpec(memory_space=pltpu.VMEM)
ANYWHERE = pl.BlockSpec(memory_space=pl.ANY)


def run_kernel(kernel, operands, outputs, scratch=(), spaces=None, limit=VMEM_LIMIT, cost=10**6, targets=None, aliases=None):
    return pl.pallas_call(
        kernel,
        out_shape=[jax.ShapeDtypeStruct(shape, dtype) for shape, dtype in outputs],
        in_specs=spaces or [IN_VMEM] * len(operands),
        out_specs=targets or [IN_VMEM] * len(outputs),
        scratch_shapes=scratch,
        input_output_aliases=aliases or {},
        compiler_params=pltpu.CompilerParams(vmem_limit_bytes=limit),
        cost_estimate=pl.CostEstimate(flops=cost, bytes_accessed=2**20, transcendentals=0),
        name=getattr(kernel, "func", kernel).__name__,
    )(*operands)


def swapped(value, axis, step):
    return lax.ppermute(value, axis, [(source, source ^ step) for source in range(lax.axis_size(axis))])


def by_heads(inputs, short_filter, long_filter, skip_gain, queries, key_rows, out_weight):
    rows, streams, channels = inputs.shape
    own = channels // COUNT
    groups, taps = long_filter.shape
    half = jnp.bfloat16
    piece, window = ((rows, own), half), COUNT * rows
    streamed = jnp.transpose(inputs, (1, 0, 2))
    far_plain = run_kernel(
        plain_kernel,
        (streamed, queries, key_rows),
        [((3 * rows, own), half)] * 2,
        [pltpu.VMEM((3, rows, 2 * own), half), pltpu.SemaphoreType.DMA((3,))],
        [IN_HBM] * 3,
        PLAIN_LIMIT,
    )
    *gates, near_plain, own_plain = run_kernel(
        gate_kernel,
        (streamed, short_filter, queries, key_rows),
        [((own // HEAD_DIM * (rows + EDGE), HEAD_DIM), half)] * COUNT + [((3 * rows, own), half)] * 2,
        [
            pltpu.VMEM((2, rows, channels), half),
            pltpu.VMEM(short_filter.shape, half),
            pltpu.SemaphoreType.DMA((2,)),
            pltpu.SemaphoreType.DMA((6,)),
        ],
        [IN_HBM] * 4,
        GATE_LIMIT,
    )
    plain = [own_plain, near_plain, far_plain[1], far_plain[0]]
    plain = [swapped(plain[step], "ctx", step) for step in ORDER[:3]] + [plain[0]]
    gates = [swapped(gates[step], "ctx", step) for step in ORDER[:3]] + [gates[0]]
    band, weight = run_kernel(
        ready_kernel,
        (long_filter, out_weight),
        [((groups // COUNT * taps, 2 * taps), half), (out_weight.shape, half)],
        [pltpu.SemaphoreType.DMA],
        [IN_VMEM, IN_HBM],
    )
    soft, totals, feature = run_kernel(
        weights_kernel,
        (*plain, short_filter),
        [
            ((own // HEAD_DIM, window, window), half),
            ((window, HEAD_DIM), jnp.float32),
            ((window, own), jnp.float32),
        ],
        [
            pltpu.VMEM((COUNT, rows, own), half),
            pltpu.VMEM((window, own), half),
            pltpu.VMEM((window, own), half),
        ],
    )
    third, second, values = run_kernel(
        values_kernel,
        (*gates, feature, band, short_filter, skip_gain.reshape(1, channels), soft, totals),
        [piece, piece, ((window, own), half)],
        [
            pltpu.VMEM((COUNT, EDGE, own), jnp.float32),
            pltpu.VMEM((window + rows, own), half),
            pltpu.VMEM((window, own), jnp.float32),
        ],
    )
    third_got, second_got = swapped(third, "ctx", 3), swapped(second, "ctx", 2)
    near, mine = run_kernel(near_rows_kernel, (soft, totals, values), [piece] * 2)
    return project_and_share((second_got, third_got, swapped(near, "ctx", 1), mine), weight)


def added(*terms):
    total = terms[0].astype(jnp.float32)
    for term in terms[1:]:
        total = total + term.astype(jnp.float32)
    return total.astype(jnp.bfloat16)


def project_and_share(attended, out_weight):
    second, third, near, mine = attended
    rows = mine.shape[0]
    width = out_weight.shape[1] // lax.axis_size("mp")
    (partial,) = run_kernel(partial_kernel, (second, mine, out_weight), [((rows, 2 * width), jnp.float32)])
    (partial,) = run_kernel(
        partial_third_kernel, (third, partial, out_weight), [((rows, 2 * width), jnp.float32)]
    )
    crossed, sums = [], []
    for part in range(2):
        given, kept = [
            block
            for masks in ((3,), (2,))
            for block in run_kernel(
                functools.partial(project_far_kernel, part, masks),
                (near, partial, out_weight),
                [((rows, width // 2), jnp.bfloat16)] * len(masks),
            )
        ]
        far_sum = added(kept, swapped(given, "mp", 1))
        sums.append(far_sum)
        crossed.append(swapped(far_sum, "mp", 2))
    near_given, near_kept = run_kernel(
        functools.partial(project_kernel, (1, 0)),
        (*attended, out_weight, *sums),
        [((rows, width), jnp.bfloat16)] * 2,
        [pltpu.VMEM((rows, out_weight.shape[0]), jnp.bfloat16)],
        [IN_VMEM] * 5 + [ANYWHERE] * 2,
    )
    half = near_given.shape[0] // 2
    near_got = [swapped(near_given[:half], "mp", 1), swapped(near_given[half:], "mp", 1)]
    total = []
    for part, piece in enumerate(crossed):
        total = run_kernel(
            functools.partial(total_kernel, part),
            (near_kept, *near_got, piece, *total),
            [(near_kept.shape, near_kept.dtype)],
            [pltpu.VMEM(piece.shape, piece.dtype), pltpu.SemaphoreType.DMA],
            [IN_VMEM] * 4 + [IN_HBM] * len(total),
            targets=[IN_HBM],
            aliases={4: 0} if total else {},
        )
    return total[0]


def per_device(inputs, short_filter, long_filter, skip_gain, queries, key_rows, out_weight):
    rows, _, channels = inputs.shape
    count = lax.axis_size("ctx")
    taps = long_filter.shape[1]
    splits = channels % (count * HEAD_DIM) == 0 and count == COUNT and rows == taps
    if splits and lax.axis_size("mp") == 4:
        return by_heads(inputs, short_filter, long_filter, skip_gain, queries, key_rows, out_weight)
    attended = by_rows(inputs, short_filter, long_filter, skip_gain, queries, key_rows)
    partial_out = jnp.dot(attended, out_weight, preferred_element_type=jnp.float32)
    return lax.psum_scatter(partial_out.astype(jnp.bfloat16), "mp", scatter_dimension=1, tiled=True)


def solution(mesh):
    placed = (
        P(("parts", "ctx"), None, "mp"),
        P(None, None, "mp"),
        P("mp", None),
        P("mp"),
        P(("parts", "ctx"), "mp"),
        P(("parts", "ctx"), "mp"),
        P("mp", None),
    )
    return jax.shard_map(
        per_device, mesh=mesh, in_specs=placed, out_specs=P(("parts", "ctx"), "mp"), check_vma=False
    )
```

```python
import functools

import jax
import jax.numpy as jnp
from jax import lax
from jax.experimental import pallas as pl
from jax.experimental.pallas import tpu as pltpu
from jax.sharding import PartitionSpec as P

HEAD_DIM = 128
COUNT = 4
ORDER = (3, 2, 1, 0)
EDGE = 8


masked_score = -1e30


def passed_along(value, axis, steps):
    count = lax.axis_size(axis)
    initial, last = (max(0, -steps), min(count, count - steps))
    return lax.ppermute(value, axis, [(source, source + steps) for source in range(initial, last)])


def toeplitz_taps(filters, row_count):
    group_count = filters.shape[0]
    tap_count = filters.shape[1]
    span = row_count + tap_count - 1
    flipped = filters[:, ::-1]
    padded_taps = jnp.concatenate(
        [flipped, jnp.zeros((group_count, row_count), filters.dtype)], axis=1
    )
    repeated = jnp.tile(padded_taps, (1, row_count))
    return repeated[:, : row_count * span].reshape(group_count, row_count, span)


def short_features(extended, short_filter, row_count):
    tap_count = short_filter.shape[0]
    features = jnp.zeros((row_count,) + extended.shape[1:], jnp.float32)
    for lag_index in range(tap_count):
        delayed = extended[
            tap_count - 1 - lag_index : tap_count - 1 - lag_index + row_count
        ].astype(jnp.float32)
        features = features + short_filter[lag_index].astype(jnp.float32)[None] * delayed
    return features


def attend(head_queries, query_pos, key_piece, value_piece):
    key_count = key_piece.shape[0]
    head_count = head_queries.shape[1]
    key_heads = key_piece.reshape(key_count, head_count, -1)
    value_heads = value_piece.reshape(key_count, head_count, -1)
    scores = jnp.einsum(
        "qhd,khd->hqk", head_queries, key_heads, preferred_element_type=jnp.float32
    ) * head_queries.shape[2] ** (-0.5)
    key_pos = lax.iota(jnp.int32, key_count)
    allowed = (key_pos[None, :] <= query_pos[:, None])[None]
    peak = jnp.max(jnp.where(allowed, scores, masked_score), axis=2)
    probabilities = jnp.where(allowed, jnp.exp(scores - peak[..., None]), 0.0)
    weight_sum = jnp.sum(probabilities, axis=2)
    mixed = jnp.einsum(
        "hqk,khd->hqd",
        probabilities.astype(jnp.bfloat16),
        value_heads,
        preferred_element_type=jnp.float32,
    )
    result = mixed / weight_sum[..., None]
    return jnp.transpose(result, (1, 0, 2)).reshape(result.shape[1], -1).astype(jnp.bfloat16)


def by_rows(inputs, short_filter, long_filter, skip_gain, queries, key_rows):
    row_count = inputs.shape[0]
    channels = inputs.shape[2]
    groups = long_filter.shape[0]
    tap_count = long_filter.shape[1]
    short_reach = short_filter.shape[0] - 1
    position = lax.axis_index("ctx")
    rim = passed_along(inputs[row_count - short_reach :], "ctx", 1)
    extended = jnp.concatenate([rim, inputs], axis=0)
    features = short_features(extended, short_filter, row_count)
    gate_product = (features[:, 1] * features[:, 2]).astype(jnp.bfloat16)
    gate_prev = passed_along(gate_product[row_count - (tap_count - 1) :], "ctx", 1)
    gate_ext = jnp.concatenate([gate_prev, gate_product], axis=0)
    toeplitz = toeplitz_taps(long_filter, row_count)
    filtered = jnp.einsum(
        "gtr,rgc->tgc",
        toeplitz,
        gate_ext.reshape(row_count + tap_count - 1, groups, channels // groups),
        preferred_element_type=jnp.float32,
    ).reshape(row_count, channels)
    values = (
        features[:, 0] * (filtered + skip_gain[None] * gate_product.astype(jnp.float32))
    ).astype(jnp.bfloat16)
    head_count = channels // HEAD_DIM
    head_queries = queries.reshape(row_count, head_count, HEAD_DIM)
    query_pos = position * row_count + lax.iota(jnp.int32, row_count)
    return attend(
        head_queries,
        query_pos,
        lax.all_gather(key_rows, "ctx", axis=0, tiled=True),
        lax.all_gather(values, "ctx", axis=0, tiled=True),
    )


def delayed(signal, lag):
    if lag == 0:
        return signal
    row = lax.broadcasted_iota(jnp.int32, signal.shape, 0)
    return jnp.where(row < lag, 0.0, pltpu.roll(signal, lag, 0))


def featured(signal, taps):
    total = taps[0] * signal
    for lag in range(1, len(taps)):
        total = total + taps[lag] * delayed(signal, lag)
    return total


def columns_of(block, width):
    return pl.ds(pl.multiple_of(block * width, width), width)


def write_gate(signals, taps, out_ref):
    rows, own = signals[0].shape
    tiles = [slice(start, start + HEAD_DIM) for start in range(0, own, HEAD_DIM)]
    edge_row = lax.broadcasted_iota(jnp.int32, (EDGE, own), 0)
    features = [featured(signal, tap) for signal, tap in zip(signals, taps)]
    gate = (features[0] * features[1]).astype(jnp.bfloat16)
    first, second = [
        jnp.where(
            edge_row % 4 < 2, pltpu.roll(signal[:EDGE], turn, 0), pltpu.roll(signal[rows - EDGE :], 4 - turn, 0)
        )
        for signal, turn in zip(signals, (0, 4))
    ]
    edges = jnp.where(edge_row < 4, first, second)
    for index, tile in enumerate(tiles):
        out_ref[index * rows : (index + 1) * rows] = gate[:, tile]
    out_ref[len(tiles) * rows :] = jnp.concatenate([edges[:, tile] for tile in tiles], axis=0).astype(jnp.bfloat16)


def plain_copies(sources, out_refs, steps, sems):
    rows, own = sources[0].shape[0], out_refs[0].shape[1]
    position = lax.axis_index("ctx")
    copies = []
    for step, out_ref in zip(steps, out_refs):
        columns = columns_of(position ^ step, own)
        for index, source in enumerate(sources):
            target = out_ref.at[index * rows : (index + 1) * rows]
            copies.append(pltpu.make_async_copy(source.at[:, columns], target, sems.at[len(copies)]))
    for copy in copies:
        copy.start()
    return copies


def plain_kernel(inputs_any, queries_any, keys_any, *refs):
    for copy in plain_copies((queries_any, keys_any, inputs_any.at[0]), refs[:2], ORDER[:2], refs[2]):
        copy.wait()


def gate_kernel(inputs_any, short_any, queries_any, keys_any, *refs):
    out_refs, plain_refs = refs[:COUNT], refs[COUNT : COUNT + 2]
    signal_s, short_s, sems, plain_sems = refs[COUNT + 2 :]
    own = plain_refs[0].shape[1]
    position = lax.axis_index("ctx")
    copies = [
        pltpu.make_async_copy(short_any, short_s, sems.at[0]),
        pltpu.make_async_copy(inputs_any.at[1:3], signal_s, sems.at[1]),
    ]
    for copy in copies:
        copy.start()
    plain = plain_copies((queries_any, keys_any, inputs_any.at[0]), plain_refs, ORDER[2:], plain_sems)
    for copy in copies:
        copy.wait()
    for step in ORDER:
        columns = columns_of(position ^ step, own)
        signals = [signal_s[stream, :, columns].astype(jnp.float32) for stream in range(2)]
        taps = [
            [short_s[lag, stream : stream + 1, columns].astype(jnp.float32) for lag in range(3)] for stream in (1, 2)
        ]
        write_gate(signals, taps, out_refs[step])
    for copy in plain:
        copy.wait()


def ready_kernel(filter_ref, weight_any, band_ref, weight_ref, sem):
    rows, span = band_ref.shape
    taps = filter_ref.shape[1]
    groups = rows // taps
    weights = pltpu.make_async_copy(weight_any, weight_ref, sem)
    weights.start()
    source = lax.broadcasted_iota(jnp.int32, (taps, span), 0)
    target = lax.broadcasted_iota(jnp.int32, (taps, span), 1)
    flip = (source + target == taps).astype(jnp.bfloat16)
    first_group = pl.multiple_of(lax.axis_index("ctx") * groups, groups)
    first = jnp.dot(filter_ref[pl.ds(first_group, groups)], flip, preferred_element_type=jnp.float32)
    for group in range(groups):
        repeated = jnp.broadcast_to(first[group : group + 1], (taps, span))
        banded = pltpu.roll(repeated, 0, 1, stride=1, stride_axis=0)
        band_ref[group * taps : (group + 1) * taps] = banded.astype(jnp.bfloat16)
    weights.wait()


def weights_kernel(third_ref, second_ref, near_ref, own_ref, short_ref, weight_ref, total_ref, feature_ref, query_s, key_s, signal_s):
    count = COUNT
    rows, own = query_s.shape[1:]
    position = lax.axis_index("ctx")
    for step, given in zip(ORDER, (third_ref, second_ref, near_ref, own_ref)):
        query_s[position ^ step] = given[0:rows]
        key_s[columns_of(position ^ step, rows)] = given[rows : 2 * rows]
        signal_s[columns_of(position ^ step, rows)] = given[2 * rows :]
    taps = [short_ref[lag, 0:1, columns_of(position, own)].astype(jnp.float32) for lag in range(3)]
    feature_ref[...] = featured(signal_s[...].astype(jnp.float32), taps)
    causal = lax.broadcasted_iota(jnp.int32, (rows, rows), 1) <= lax.broadcasted_iota(jnp.int32, (rows, rows), 0)
    for head in range(own // HEAD_DIM):
        columns = slice(head * HEAD_DIM, (head + 1) * HEAD_DIM)
        for block in range(count):
            here, seen = slice(block * rows, (block + 1) * rows), (block + 1) * rows
            scores = lax.dot_general(
                query_s[block, :, columns],
                key_s[0:seen, columns],
                (((1,), (1,)), ((), ())),
                preferred_element_type=jnp.float32,
            ) * HEAD_DIM ** (-0.5)
            own_scores = jnp.where(causal, scores[:, block * rows :], masked_score)
            pieces = [scores[:, : block * rows], own_scores] if block else [own_scores]
            scores = jnp.concatenate(pieces, axis=1)
            weights = jnp.exp(scores - jnp.max(scores, axis=1, keepdims=True))
            total_ref[here, head : head + 1] = jnp.sum(weights, axis=1, keepdims=True)
            weight_ref[head, here, 0:seen] = weights.astype(jnp.bfloat16)
            if seen < count * rows:
                weight_ref[head, here, seen:] = jnp.zeros((rows, count * rows - seen), jnp.bfloat16)


def mix_rows(block, weight_ref, total_ref, value_ref, out_ref):
    rows = out_ref.shape[0]
    here = columns_of(block, rows)
    for head in range(out_ref.shape[1] // HEAD_DIM):
        columns = slice(head * HEAD_DIM, (head + 1) * HEAD_DIM)
        mixed = jnp.dot(weight_ref[head, here], value_ref[:, columns], preferred_element_type=jnp.float32)
        out_ref[:, columns] = (mixed / total_ref[here, head : head + 1]).astype(jnp.bfloat16)


def values_kernel(*refs):
    count = COUNT
    gates, feature_ref = refs[:count], refs[count]
    band_ref, short_ref, gain_ref, weight_ref, total_ref = refs[count + 1 : count + 6]
    third_ref, second_ref, value_ref = refs[count + 6 : count + 9]
    edge_s, gate_s, filtered_s = refs[count + 9 :]
    rows, own = second_ref.shape
    per_group = own * rows // band_ref.shape[0]
    position = lax.axis_index("ctx")
    mine = columns_of(position, own)
    tiles = [slice(start, start + HEAD_DIM) for start in range(0, own, HEAD_DIM)]
    gate_s[0:rows] = jnp.zeros((rows, own), jnp.bfloat16)
    for step, gate in zip(ORDER, gates):
        for index, tile in enumerate(tiles):
            gate_s[columns_of((position ^ step) + 1, rows), tile] = gate[index * rows : (index + 1) * rows]
        edges = gate[len(tiles) * rows :].astype(jnp.float32)
        for index, tile in enumerate(tiles):
            edge_s[position ^ step, :, tile] = edges[index * EDGE : (index + 1) * EDGE]
    taps = [
        [short_ref[lag, stream : stream + 1, mine].astype(jnp.float32) for lag in range(3)] for stream in range(3)
    ]
    edge_row = lax.broadcasted_iota(jnp.int32, (EDGE, own), 0)
    head_row = lax.broadcasted_iota(jnp.int32, (2 * EDGE, own), 0)
    for block in range(1, count):
        fixed = 1.0
        for stream, back, on in ((1, 6, 2), (2, 2, 6)):
            joined = jnp.where(
                edge_row < 2, pltpu.roll(edge_s[block - 1], back, 0), pltpu.roll(edge_s[block], on, 0)
            )
            fixed = fixed * (
                taps[stream][0] * pltpu.roll(joined, 6, 0)
                + taps[stream][1] * pltpu.roll(joined, 7, 0)
                + taps[stream][2] * joined
            )
        here = slice((block + 1) * rows, (block + 1) * rows + 2 * EDGE)
        head = jnp.where(head_row < 2, jnp.concatenate([fixed, fixed], axis=0), gate_s[here].astype(jnp.float32))
        gate_s[here] = head.astype(jnp.bfloat16)
    gain = gain_ref[:, mine]
    chunk = 2 * HEAD_DIM // count
    in_chunk = chunk // per_group
    lane = lax.broadcasted_iota(jnp.int32, (rows, 2 * HEAD_DIM), 1) % chunk // per_group
    for part in range(own // chunk):
        columns = slice(part * chunk, (part + 1) * chunk)
        windows = [gate_s[block * rows : (block + 2) * rows, columns] for block in range(count)]
        mixed = jnp.dot(
            band_ref[part * in_chunk * rows : (part + 1) * in_chunk * rows],
            jnp.concatenate(windows, axis=1),
            preferred_element_type=jnp.float32,
        )
        filtered = mixed[:rows]
        for group in range(1, in_chunk):
            filtered = jnp.where(lane == group, mixed[group * rows : (group + 1) * rows], filtered)
        for block in range(count):
            filtered_s[block * rows : (block + 1) * rows, columns] = filtered[:, block * chunk : (block + 1) * chunk]
    for block in range(count):
        here = slice(block * rows, (block + 1) * rows)
        gate = gate_s[(block + 1) * rows : (block + 2) * rows].astype(jnp.float32)
        value_ref[here] = (feature_ref[here] * (filtered_s[here] + gain * gate)).astype(jnp.bfloat16)
    for step, out_ref in ((3, third_ref), (2, second_ref)):
        mix_rows(position ^ step, weight_ref, total_ref, value_ref, out_ref)


def near_rows_kernel(weight_ref, total_ref, value_ref, near_ref, own_ref):
    position = lax.axis_index("ctx")
    for step, out_ref in ((1, near_ref), (0, own_ref)):
        mix_rows(position ^ step, weight_ref, total_ref, value_ref, out_ref)


def project_kernel(masks, second_ref, third_ref, near_ref, mine_ref, weight_ref, *refs):
    out_refs, attended_s = refs[2:-1], refs[-1]
    own, width = mine_ref.shape[1], out_refs[0].shape[1]
    position, here = lax.axis_index("ctx"), lax.axis_index("mp")
    for step, piece in ((0, mine_ref), (1, near_ref), (2, second_ref), (3, third_ref)):
        attended_s[:, columns_of(position ^ step, own)] = piece[...]
    for mask, out_ref in zip(masks, out_refs):
        out_ref[...] = jnp.dot(
            attended_s[...], weight_ref[:, columns_of(here ^ mask, width)], preferred_element_type=jnp.float32
        ).astype(jnp.bfloat16)


def partial_kernel(second_ref, mine_ref, weight_ref, out_ref):
    own, width = mine_ref.shape[1], out_ref.shape[1] // 2
    position, here = lax.axis_index("ctx"), lax.axis_index("mp")
    for index, mask in enumerate((3, 2)):
        columns = columns_of(here ^ mask, width)
        out_ref[:, index * width : (index + 1) * width] = jnp.dot(
            mine_ref[...], weight_ref[columns_of(position, own), columns], preferred_element_type=jnp.float32
        ) + jnp.dot(
            second_ref[...], weight_ref[columns_of(position ^ 2, own), columns], preferred_element_type=jnp.float32
        )


def partial_third_kernel(third_ref, partial_ref, weight_ref, out_ref):
    own, width = third_ref.shape[1], out_ref.shape[1] // 2
    position, here = lax.axis_index("ctx"), lax.axis_index("mp")
    for index, mask in enumerate((3, 2)):
        span = slice(index * width, (index + 1) * width)
        out_ref[:, span] = partial_ref[:, span] + jnp.dot(
            third_ref[...],
            weight_ref[columns_of(position ^ 3, own), columns_of(here ^ mask, width)],
            preferred_element_type=jnp.float32,
        )


def project_far_kernel(part, masks, near_ref, partial_ref, weight_ref, *out_refs):
    own, size = near_ref.shape[1], out_refs[0].shape[1]
    width = partial_ref.shape[1] // 2
    position, here = lax.axis_index("ctx"), lax.axis_index("mp")
    for mask, out_ref in zip(masks, out_refs):
        columns = columns_of((here ^ mask) * (width // size) + part, size)
        start = (3 - mask) * width + part * size
        total = partial_ref[:, start : start + size] + jnp.dot(
            near_ref[...], weight_ref[columns_of(position ^ 1, own), columns], preferred_element_type=jnp.float32
        )
        out_ref[...] = total.astype(jnp.bfloat16)


def total_kernel(part, kept_ref, upper_ref, lower_ref, crossed_ref, *refs):
    out_any, total_s, sem = refs[-3:]
    half, size = upper_ref.shape[0], crossed_ref.shape[1]
    columns = slice(part * size, (part + 1) * size)
    for index, near_ref in enumerate((upper_ref, lower_ref)):
        here = slice(index * half, (index + 1) * half)
        total = (
            kept_ref[here, columns].astype(jnp.float32)
            + near_ref[:, columns].astype(jnp.float32)
            + crossed_ref[here].astype(jnp.float32)
        )
        total_s[here] = total.astype(jnp.bfloat16)
    copy = pltpu.make_async_copy(total_s, out_any.at[:, columns], sem)
    copy.start()
    copy.wait()


VMEM_LIMIT = 40 * 1024 * 1024
PLAIN_LIMIT = 53 * 1024 * 1024 + 400 * 1024
GATE_LIMIT = 53 * 1024 * 1024 + 200 * 1024
IN_HBM = pl.BlockSpec(memory_space=pltpu.HBM)
IN_VMEM = pl.BlockSpec(memory_space=pltpu.VMEM)
ANYWHERE = pl.BlockSpec(memory_space=pl.ANY)


def run_kernel(kernel, operands, outputs, scratch=(), spaces=None, limit=VMEM_LIMIT, cost=10**6, targets=None, aliases=None):
    return pl.pallas_call(
        kernel,
        out_shape=[jax.ShapeDtypeStruct(shape, dtype) for shape, dtype in outputs],
        in_specs=spaces or [IN_VMEM] * len(operands),
        out_specs=targets or [IN_VMEM] * len(outputs),
        scratch_shapes=scratch,
        input_output_aliases=aliases or {},
        compiler_params=pltpu.CompilerParams(vmem_limit_bytes=limit),
        cost_estimate=pl.CostEstimate(flops=cost, bytes_accessed=2**20, transcendentals=0),
        name=getattr(kernel, "func", kernel).__name__,
    )(*operands)


def swapped(value, axis, step):
    return lax.ppermute(value, axis, [(source, source ^ step) for source in range(lax.axis_size(axis))])


def by_heads(inputs, short_filter, long_filter, skip_gain, queries, key_rows, out_weight):
    rows, streams, channels = inputs.shape
    own = channels // COUNT
    groups, taps = long_filter.shape
    half = jnp.bfloat16
    piece, window = ((rows, own), half), COUNT * rows
    streamed = jnp.transpose(inputs, (1, 0, 2))
    far_plain = run_kernel(
        plain_kernel,
        (streamed, queries, key_rows),
        [((3 * rows, own), half)] * 2,
        [pltpu.SemaphoreType.DMA((6,))],
        [IN_HBM] * 3,
        PLAIN_LIMIT,
    )
    *gates, near_plain, own_plain = run_kernel(
        gate_kernel,
        (streamed, short_filter, queries, key_rows),
        [((own // HEAD_DIM * (rows + EDGE), HEAD_DIM), half)] * COUNT + [((3 * rows, own), half)] * 2,
        [
            pltpu.VMEM((2, rows, channels), half),
            pltpu.VMEM(short_filter.shape, half),
            pltpu.SemaphoreType.DMA((2,)),
            pltpu.SemaphoreType.DMA((6,)),
        ],
        [IN_HBM] * 4,
        GATE_LIMIT,
    )
    plain = [own_plain, near_plain, far_plain[1], far_plain[0]]
    plain = [swapped(plain[step], "ctx", step) for step in ORDER[:3]] + [plain[0]]
    gates = [swapped(gates[step], "ctx", step) for step in ORDER[:3]] + [gates[0]]
    band, weight = run_kernel(
        ready_kernel,
        (long_filter, out_weight),
        [((groups // COUNT * taps, 2 * taps), half), (out_weight.shape, half)],
        [pltpu.SemaphoreType.DMA],
        [IN_VMEM, IN_HBM],
    )
    soft, totals, feature = run_kernel(
        weights_kernel,
        (*plain, short_filter),
        [
            ((own // HEAD_DIM, window, window), half),
            ((window, HEAD_DIM), jnp.float32),
            ((window, own), jnp.float32),
        ],
        [
            pltpu.VMEM((COUNT, rows, own), half),
            pltpu.VMEM((window, own), half),
            pltpu.VMEM((window, own), half),
        ],
    )
    third, second, values = run_kernel(
        values_kernel,
        (*gates, feature, band, short_filter, skip_gain.reshape(1, channels), soft, totals),
        [piece, piece, ((window, own), half)],
        [
            pltpu.VMEM((COUNT, EDGE, own), jnp.float32),
            pltpu.VMEM((window + rows, own), half),
            pltpu.VMEM((window, own), jnp.float32),
        ],
    )
    third_got, second_got = swapped(third, "ctx", 3), swapped(second, "ctx", 2)
    near, mine = run_kernel(near_rows_kernel, (soft, totals, values), [piece] * 2)
    return project_and_share((second_got, third_got, swapped(near, "ctx", 1), mine), weight)


def added(*terms):
    total = terms[0].astype(jnp.float32)
    for term in terms[1:]:
        total = total + term.astype(jnp.float32)
    return total.astype(jnp.bfloat16)


def project_and_share(attended, out_weight):
    second, third, near, mine = attended
    rows = mine.shape[0]
    width = out_weight.shape[1] // lax.axis_size("mp")
    (partial,) = run_kernel(partial_kernel, (second, mine, out_weight), [((rows, 2 * width), jnp.float32)])
    (partial,) = run_kernel(
        partial_third_kernel, (third, partial, out_weight), [((rows, 2 * width), jnp.float32)]
    )
    crossed, sums = [], []
    for part in range(2):
        given, kept = [
            block
            for masks in ((3,), (2,))
            for block in run_kernel(
                functools.partial(project_far_kernel, part, masks),
                (near, partial, out_weight),
                [((rows, width // 2), jnp.bfloat16)] * len(masks),
            )
        ]
        far_sum = added(kept, swapped(given, "mp", 1))
        sums.append(far_sum)
        crossed.append(swapped(far_sum, "mp", 2))
    near_given, near_kept = run_kernel(
        functools.partial(project_kernel, (1, 0)),
        (*attended, out_weight, *sums),
        [((rows, width), jnp.bfloat16)] * 2,
        [pltpu.VMEM((rows, out_weight.shape[0]), jnp.bfloat16)],
        [IN_VMEM] * 5 + [ANYWHERE] * 2,
    )
    half = near_given.shape[0] // 2
    near_got = [swapped(near_given[:half], "mp", 1), swapped(near_given[half:], "mp", 1)]
    total = []
    for part, piece in enumerate(crossed):
        total = run_kernel(
            functools.partial(total_kernel, part),
            (near_kept, *near_got, piece, *total),
            [(near_kept.shape, near_kept.dtype)],
            [pltpu.VMEM(piece.shape, piece.dtype), pltpu.SemaphoreType.DMA],
            [IN_VMEM] * 4 + [IN_HBM] * len(total),
            targets=[IN_HBM],
            aliases={4: 0} if total else {},
        )
    return total[0]


def per_device(inputs, short_filter, long_filter, skip_gain, queries, key_rows, out_weight):
    rows, _, channels = inputs.shape
    count = lax.axis_size("ctx")
    taps = long_filter.shape[1]
    splits = channels % (count * HEAD_DIM) == 0 and count == COUNT and rows == taps
    if splits and lax.axis_size("mp") == 4:
        return by_heads(inputs, short_filter, long_filter, skip_gain, queries, key_rows, out_weight)
    attended = by_rows(inputs, short_filter, long_filter, skip_gain, queries, key_rows)
    partial_out = jnp.dot(attended, out_weight, preferred_element_type=jnp.float32)
    return lax.psum_scatter(partial_out.astype(jnp.bfloat16), "mp", scatter_dimension=1, tiled=True)


def solution(mesh):
    placed = (
        P(("parts", "ctx"), None, "mp"),
        P(None, None, "mp"),
        P("mp", None),
        P("mp"),
        P(("parts", "ctx"), "mp"),
        P(("parts", "ctx"), "mp"),
        P("mp", None),
    )
    return jax.shard_map(
        per_device, mesh=mesh, in_specs=placed, out_specs=P(("parts", "ctx"), "mp"), check_vma=False
    )
```
